32 devices in a mesh: pix: 8 (over z, y), ch: 4 (over x, core).
Axes of the slice: x: 2, y: 2, z: 4, core: 2. Of those that a mesh axis runs over, the one named last changes fastest.
Arguments:
- features: bfloat16 [32, 128, 2048], P('pix', None, 'ch'), may hold values from -7.5 to 7.5
- valid_mask: int32 [32, 128], P('pix'), may hold values from 0 to 1, as said below
- sem_label: int32 [32, 128], P('pix'), may hold values from 0 to 18
- depth_target: float32 [32, 128], P('pix'), may hold values from -6 to 6
- normal_target: float32 [3, 32, 128], P(None, 'pix'), may hold values from -6 to 6
- label_mask: int32 [3, 32, 128], P(None, 'pix'), may hold values from 0 to 1, as said below
- w_reduce: float32 [2048, 512], P('ch', 'pix'), may hold values from -0.125 to 0.125
- m_reduce: float32 [2048, 512], P('ch', 'pix'), may hold values from -2.3841858e-06 to 2.3841858e-06
- v_reduce: float32 [2048, 512], P('ch', 'pix'), may hold values from 5.0711002e-17 to 2.0284401e-16
- w_dilated: float32 [9, 512, 512], P(None, 'pix', 'ch'), may hold values from -0.09375 to 0.09375
- m_dilated: float32 [9, 512, 512], P(None, 'pix', 'ch'), may hold values from -2.3841858e-06 to 2.3841858e-06
- v_dilated: float32 [9, 512, 512], P(None, 'pix', 'ch'), may hold values from 6.761467e-17 to 2.7045868e-16
- w_expand: float32 [512, 2048], P('pix', 'ch'), may hold values from -0.25 to 0.25
- m_expand: float32 [512, 2048], P('pix', 'ch'), may hold values from -2.3841858e-06 to 2.3841858e-06
- v_expand: float32 [512, 2048], P('pix', 'ch'), may hold values from 2.5355501e-17 to 1.01422005e-16
- head_weight: float32 [2048, 768], P('ch', 'pix'), may hold values from -0.125 to 0.125
- m_head: float32 [2048, 768], P('ch', 'pix'), may hold values from -2.3841858e-06 to 2.3841858e-06
- v_head: float32 [2048, 768], P('ch', 'pix'), may hold values from 2.02844e-15 to 8.11376e-15
- head_rates: float32 [3, 9, 768, 2048], P(None, None, 'pix', 'ch'), may hold values from -0.046875 to 0.046875
- m_rates: float32 [3, 9, 768, 2048], P(None, None, 'pix', 'ch'), may hold values from -2.3841858e-06 to 2.3841858e-06
- v_rates: float32 [3, 9, 768, 2048], P(None, None, 'pix', 'ch'), may hold values from 2.02844e-15 to 8.11376e-15
- head_proj: float32 [3, 1024, 256], P(None, 'pix'), may hold values from -0.1875 to 0.1875
- m_proj: float32 [3, 1024, 256], P(None, 'pix'), may hold values from -2.3841858e-06 to 2.3841858e-06
- v_proj: float32 [3, 1024, 256], P(None, 'pix'), may hold values from 2.02844e-15 to 8.11376e-15
- norm_params: float32 [2, 3072], replicated, may hold values from -0.6 to 1.8, as said below
- norm_m: float32 [2, 3072], replicated, may hold values from -2.3841858e-06 to 2.3841858e-06
- norm_v: float32 [2, 3072], replicated, may hold values from 4.0568802e-17 to 1.6227521e-16
- head_small: float32 [9751], replicated, may hold values from -1.2 to 1.2
- small_m: float32 [9751], replicated, may hold values from -2.3841858e-06 to 2.3841858e-06
- small_v: float32 [9751], replicated, may hold values from 2.02844e-15 to 8.11376e-15
Outputs:
- block_out: bfloat16 [32, 128, 2048], P('pix', None, 'ch')
- input_grad: float32 [32, 128, 2048], P('pix', None, 'ch')
- grad_norm: float32 [], replicated
- reduce_new: float32 [2048, 512], P('ch', 'pix')
- reduce_first: float32 [2048, 512], P('ch', 'pix')
- reduce_second: float32 [2048, 512], P('ch', 'pix')
- reduce_copy: bfloat16 [2048, 512], P('ch', 'pix')
- dilated_new: float32 [9, 512, 512], P(None, 'pix', 'ch')
- dilated_first: float32 [9, 512, 512], P(None, 'pix', 'ch')
- dilated_second: float32 [9, 512, 512], P(None, 'pix', 'ch')
- dilated_copy: bfloat16 [9, 512, 512], P(None, 'pix', 'ch')
- expand_new: float32 [512, 2048], P('pix', 'ch')
- expand_first: float32 [512, 2048], P('pix', 'ch')
- expand_second: float32 [512, 2048], P('pix', 'ch')
- expand_copy: bfloat16 [512, 2048], P('pix', 'ch')
- head_new: float32 [2048, 768], P('ch', 'pix')
- head_first: float32 [2048, 768], P('ch', 'pix')
- head_second: float32 [2048, 768], P('ch', 'pix')
- head_copy: bfloat16 [2048, 768], P('ch', 'pix')
- rates_new: float32 [3, 9, 768, 2048], P(None, None, 'pix', 'ch')
- rates_first: float32 [3, 9, 768, 2048], P(None, None, 'pix', 'ch')
- rates_second: float32 [3, 9, 768, 2048], P(None, None, 'pix', 'ch')
- rates_copy: bfloat16 [3, 9, 768, 2048], P(None, None, 'pix', 'ch')
- proj_new: float32 [3, 1024, 256], P(None, 'pix')
- proj_first: float32 [3, 1024, 256], P(None, 'pix')
- proj_second: float32 [3, 1024, 256], P(None, 'pix')
- proj_copy: bfloat16 [3, 1024, 256], P(None, 'pix')
- norm_new: float32 [2, 3072], replicated
- norm_first: float32 [2, 3072], replicated
- norm_second: float32 [2, 3072], replicated
- small_new: float32 [9751], replicated
- small_first: float32 [9751], replicated
- small_second: float32 [9751], replicated
- depth_bias_grad: float32 [], replicated
The draws below stay inside these ranges and needn't reach their ends.
Inputs may be any that keep to these rules, and one draw needn't show every extreme that they name: `valid_mask`: in each band of 4 rows a run of 4 columns (shorter at the right edge) is 0, the rest 1. `label_mask`: the share of valid labels grows from about a quarter in the first rows to about three quarters in the last. `norm_params`: gains are positive.
All inputs are finite; a program needn't handle non-finite values.
Results may differ from the reference program's by a relative error of at most 0.015.
Values may be sent and summed in bfloat16 or wider, within the bound.
A program may use at most 320 MiB of HBM per device.

```python
import math
from functools import partial
import jax
import jax.numpy as jnp
from jax import lax

C = 2048
M = 512
HID = 256
NCLS = 19
DILATION_RATE = 4
STEP = 10
CANVAS_ROWS = 32
CANVAS_COLUMNS = 128
NORMW = 3072
HSMALL = 9751
NPARAM = 49298967


def draw_features(key, part):
    row_place = jnp.arange(CANVAS_ROWS, dtype=jnp.float32)[:, None, None] / CANVAS_ROWS
    values = jnp.clip(jax.random.normal(key, (CANVAS_ROWS, CANVAS_COLUMNS, C), jnp.float32), -5.0, 5.0)
    return (values * (0.5 + row_place)).astype(jnp.bfloat16)


def draw_valid_mask(key, part):
    bands = (CANVAS_ROWS + 3) // 4
    cuts = jax.random.randint(key, (bands,), 0, CANVAS_COLUMNS)
    band_index = jnp.arange(CANVAS_ROWS, dtype=jnp.int32) // 4
    cut_rows = cuts[band_index][:, None]
    columns = jnp.arange(CANVAS_COLUMNS, dtype=jnp.int32)[None, :]
    offset = columns - cut_rows
    return jnp.where((offset >= 0) & (offset < 4), 0, 1).astype(jnp.int32)


def draw_label_mask(key, part):
    row_index = jnp.arange(CANVAS_ROWS, dtype=jnp.int32)[None, :, None]
    tickets = jax.random.randint(key, (3, CANVAS_ROWS, CANVAS_COLUMNS), 0, 4 * CANVAS_ROWS)
    return (tickets < CANVAS_ROWS + 2 * row_index).astype(jnp.int32)


def draw_norm_params(key, part):
    gain_key, shift_key = jax.random.split(key)
    columns = jnp.arange(2 * M + C, dtype=jnp.float32)
    place = jnp.where(columns < M, columns / M, jnp.where(columns < 2 * M, (columns - M) / M, (columns - 2 * M) / C))
    factor = jax.random.uniform(gain_key, (2 * M + C,), jnp.float32, 0.8, 1.2)
    gain_row = (0.5 + place) * factor
    shift_row = jax.random.uniform(shift_key, (2 * M + C,), jnp.float32, -0.5, 0.5)
    return jnp.stack([gain_row, shift_row])


def draw_head_small(key, part):
    keys = jax.random.split(key, 8)
    shapes = (12 * HID, 3 * HID, HID * NCLS, HID, HID * 3, NCLS, 1, 3)
    scales = (0.3, 0.3, 3.0 / HID ** 0.5, 1.0 / HID ** 0.5, 1.0 / HID ** 0.5, 0.3, 0.3, 0.3)
    pieces = []
    for index_key, length, scale in zip(keys, shapes, scales):
        pieces.append(scale * jnp.clip(jax.random.normal(index_key, (length,), jnp.float32), -4.0, 4.0))
    return jnp.concatenate(pieces)


def plant(result, stream_key, low, high):
    extent = result.shape
    index_at = [jax.random.randint(jax.random.fold_in(stream_key, axis), (), 0, extent[axis]) for axis in range(len(extent))]
    result = result.at[tuple(index_at)].set(low)
    longest = extent.index(max(extent))
    index_at[longest] = (index_at[longest] + 1) % extent[longest]
    return result.at[tuple(index_at)].set(high)


def steps_of(stream_key, shape, cuts, smallest, high):
    factor_of, own = 1.0, jax.random.fold_in(stream_key, 6)
    for axis_at, parts in cuts:
        draws = jnp.exp(jax.random.uniform(jax.random.fold_in(own, axis_at), (parts,), jnp.float32, smallest / len(cuts), high / len(cuts)))
        factor_of = factor_of * jnp.repeat(draws, shape[axis_at] // parts).reshape([-1 if axis == axis_at else 1 for axis in range(len(shape))])
    return factor_of


def bell_draw(own_key, extent, scale, limit, cuts=(), kind=jnp.bfloat16):
    values = jax.random.normal(own_key, extent, jnp.float32) * scale
    if len(cuts) > 0:
        values = steps_of(own_key, extent, cuts, -0.22, 0.18) * values
    return jnp.clip(values, min=-limit, max=limit).astype(kind)


def setup_inputs(seed: int = 0) -> dict:
    seeds = jax.random.split(jax.random.key(seed), 31)
    features = draw_features(jax.random.fold_in(seeds[30], 71), 0)
    valid_mask = draw_valid_mask(jax.random.fold_in(seeds[30], 71), 0)
    sem_label = plant(jax.random.randint(seeds[2], (CANVAS_ROWS, CANVAS_COLUMNS), 0, NCLS), jax.random.fold_in(seeds[2], 1), 0, NCLS - 1).astype(jnp.int32)
    depth_target = bell_draw(seeds[3], (CANVAS_ROWS, CANVAS_COLUMNS), 1.0, 6.0, ((0, 8),), jnp.float32)
    normal_target = bell_draw(seeds[4], (3, CANVAS_ROWS, CANVAS_COLUMNS), 1.0, 6.0, ((1, 8),), jnp.float32)
    label_mask = draw_label_mask(jax.random.fold_in(seeds[30], 71), 0)
    w_reduce = bell_draw(seeds[6], (C, M), C ** -0.5, 0.125, ((0, 4), (1, 8)), jnp.float32)
    m_reduce = bell_draw(seeds[7], (C, M), (0.00111 / NPARAM ** 0.5), 2.384185791015625e-06, ((0, 4), (1, 8)), jnp.float32)
    v_reduce = jnp.clip(jnp.exp(math.log(2.0284400913711162e-16) - 1.3862944 * jax.random.uniform(seeds[8], (C, M), jnp.float32) ** steps_of(seeds[8], (C, M), ((0, 4), (1, 8)), -0.2, 0.2)), 5.0711002284277906e-17, 2.0284400913711162e-16)
    w_dilated = bell_draw(seeds[9], (9, M, M), (9 * M) ** -0.5, 0.09375, ((1, 8), (2, 4)), jnp.float32)
    m_dilated = bell_draw(seeds[10], (9, M, M), (0.00111 / NPARAM ** 0.5), 2.384185791015625e-06, ((1, 8), (2, 4)), jnp.float32)
    v_dilated = jnp.clip(jnp.exp(math.log(2.7045867884948217e-16) - 1.3862944 * jax.random.uniform(seeds[11], (9, M, M), jnp.float32) ** steps_of(seeds[11], (9, M, M), ((1, 8), (2, 4)), -0.2, 0.2)), 6.761466971237054e-17, 2.7045867884948217e-16)
    w_expand = bell_draw(seeds[12], (M, C), M ** -0.5, 0.25, ((0, 8), (1, 4)), jnp.float32)
    m_expand = bell_draw(seeds[13], (M, C), (0.00111 / NPARAM ** 0.5), 2.384185791015625e-06, ((0, 8), (1, 4)), jnp.float32)
    v_expand = jnp.clip(jnp.exp(math.log(1.0142200456855581e-16) - 1.3862944 * jax.random.uniform(seeds[14], (M, C), jnp.float32) ** steps_of(seeds[14], (M, C), ((0, 8), (1, 4)), -0.2, 0.2)), 2.5355501142138953e-17, 1.0142200456855581e-16)
    head_weight = bell_draw(seeds[15], (C, 3 * HID), C ** -0.5, 0.125, ((0, 4), (1, 8)), jnp.float32)
    m_head = bell_draw(seeds[16], (C, 3 * HID), (0.00111 / NPARAM ** 0.5), 2.384185791015625e-06, ((0, 4), (1, 8)), jnp.float32)
    v_head = jnp.clip(jnp.exp(math.log(8.113759941967991e-15) - 1.3862944 * jax.random.uniform(seeds[17], (C, 3 * HID), jnp.float32) ** steps_of(seeds[17], (C, 3 * HID), ((0, 4), (1, 8)), -0.2, 0.2)), 2.028439985491998e-15, 8.113759941967991e-15)
    head_rates = bell_draw(seeds[18], (3, 9, 3 * HID, C), (9 * C) ** -0.5, 0.046875, ((2, 8), (3, 4)), jnp.float32)
    m_rates = bell_draw(seeds[19], (3, 9, 3 * HID, C), (0.00111 / NPARAM ** 0.5), 2.384185791015625e-06, ((2, 8), (3, 4)), jnp.float32)
    v_rates = jnp.clip(jnp.exp(math.log(8.113759941967991e-15) - 1.3862944 * jax.random.uniform(seeds[20], (3, 9, 3 * HID, C), jnp.float32) ** steps_of(seeds[20], (3, 9, 3 * HID, C), ((2, 8), (3, 4)), -0.2, 0.2)), 2.028439985491998e-15, 8.113759941967991e-15)
    head_proj = bell_draw(seeds[21], (3, 4 * HID, HID), (4 * HID) ** -0.5, 0.1875, ((1, 8),), jnp.float32)
    m_proj = bell_draw(seeds[22], (3, 4 * HID, HID), (0.00111 / NPARAM ** 0.5), 2.384185791015625e-06, ((1, 8),), jnp.float32)
    v_proj = jnp.clip(jnp.exp(math.log(8.113759941967991e-15) - 1.3862944 * jax.random.uniform(seeds[23], (3, 4 * HID, HID), jnp.float32) ** steps_of(seeds[23], (3, 4 * HID, HID), ((1, 8),), -0.2, 0.2)), 2.028439985491998e-15, 8.113759941967991e-15)
    norm_params = draw_norm_params(jax.random.fold_in(seeds[30], 71), 0)
    norm_m = bell_draw(seeds[25], (2, NORMW), (0.00111 / NPARAM ** 0.5), 2.384185791015625e-06, (), jnp.float32)
    norm_v = jnp.clip(jnp.exp(jax.random.uniform(seeds[26], (2, NORMW), jnp.float32, math.log(4.0568801827422325e-17), math.log(1.622752073096893e-16))), 4.0568801827422325e-17, 1.622752073096893e-16)
    head_small = draw_head_small(jax.random.fold_in(seeds[30], 71), 0)
    small_m = bell_draw(seeds[28], (HSMALL,), (0.00111 / NPARAM ** 0.5), 2.384185791015625e-06, (), jnp.float32)
    small_v = jnp.clip(jnp.exp(jax.random.uniform(seeds[29], (HSMALL,), jnp.float32, math.log(2.028439985491998e-15), math.log(8.113759941967991e-15))), 2.028439985491998e-15, 8.113759941967991e-15)
    return {"features": features, "valid_mask": valid_mask, "sem_label": sem_label, "depth_target": depth_target, "normal_target": normal_target, "label_mask": label_mask, "w_reduce": w_reduce, "m_reduce": m_reduce, "v_reduce": v_reduce, "w_dilated": w_dilated, "m_dilated": m_dilated, "v_dilated": v_dilated, "w_expand": w_expand, "m_expand": m_expand, "v_expand": v_expand, "head_weight": head_weight, "m_head": m_head, "v_head": v_head, "head_rates": head_rates, "m_rates": m_rates, "v_rates": v_rates, "head_proj": head_proj, "m_proj": m_proj, "v_proj": v_proj, "norm_params": norm_params, "norm_m": norm_m, "norm_v": norm_v, "head_small": head_small, "small_m": small_m, "small_v": small_v}


@jax.custom_vjp
def low(v):
    return lax.optimization_barrier(v.astype(jnp.bfloat16)).astype(jnp.float32)

@jax.custom_vjp
def low_back(v):
    return v

def low_keep(v):
    return (low(v), None)

def low_pass(kept, grad):
    return (grad,)

def back_keep(v):
    return (v, None)

def back_low(kept, grad):
    return (low(grad),)
low.defvjp(low_keep, low_pass)
low_back.defvjp(back_keep, back_low)
EPS_NORM = 1e-05
BETA_ONE = 0.9
BETA_TWO = 0.999
ADAM_EPS = 1e-08
RATE_MATRIX = 0.02
RATE_SMALL = 0.2
DECAY = 0.01
CLIP_NORM = 0.01
aspp_rates = (12, 24, 36)

def product(left, right):
    return jnp.dot(left, right, precision=lax.Precision.HIGHEST, preferred_element_type=jnp.float32)

def smooth(values):
    return jax.nn.gelu(values, approximate=True)

def normalize(inputs, gain_row, shift_row):
    mean_row = lax.optimization_barrier(jnp.mean(inputs, axis=0))
    second = lax.optimization_barrier(jnp.mean(inputs * inputs, axis=0))
    scale_row = lax.rsqrt(second - mean_row * mean_row + EPS_NORM)
    return (inputs - mean_row) * scale_row * gain_row + shift_row

def dilated(receptive_area, kernel):
    padded_canvas = jnp.pad(receptive_area, ((DILATION_RATE, DILATION_RATE), (DILATION_RATE, DILATION_RATE), (0, 0)))
    summed = jnp.zeros((CANVAS_ROWS * CANVAS_COLUMNS, kernel.shape[2]), jnp.float32)
    for tap_index in range(9):
        kernel_row, kernel_column = divmod(tap_index, 3)
        sliding_patch = padded_canvas[kernel_row * DILATION_RATE:kernel_row * DILATION_RATE + CANVAS_ROWS, kernel_column * DILATION_RATE:kernel_column * DILATION_RATE + CANVAS_COLUMNS]
        summed = summed + product(sliding_patch.reshape(CANVAS_ROWS * CANVAS_COLUMNS, M), kernel[tap_index])
    return summed

def shifted_taps(grid, kernel, rate):
    padded_canvas = jnp.pad(grid, ((rate, rate), (rate, rate), (0, 0)))
    summed = jnp.zeros((CANVAS_ROWS * CANVAS_COLUMNS, kernel.shape[2]), jnp.float32)
    for tap_index in range(9):
        kernel_row, kernel_column = divmod(tap_index, 3)
        sliding_patch = padded_canvas[kernel_row * rate:kernel_row * rate + CANVAS_ROWS, kernel_column * rate:kernel_column * rate + CANVAS_COLUMNS]
        summed = summed + product(sliding_patch.reshape(CANVAS_ROWS * CANVAS_COLUMNS, grid.shape[2]), kernel[tap_index])
    return summed

def unpack_small(vector):
    lengths = (12 * HID, 3 * HID, HID * NCLS, HID, HID * 3, NCLS, 1, 3)
    pieces = []
    offset = 0
    for length in lengths:
        pieces.append(lax.slice_in_dim(vector, offset, offset + length, axis=0))
        offset = offset + length
    return (pieces[0].reshape(4, 3 * HID), pieces[1].reshape(3, HID), pieces[2].reshape(HID, NCLS), pieces[3].reshape(HID, 1), pieces[4].reshape(HID, 3), pieces[5], pieces[6], pieces[7])

def block(flat_in, mask_flat, w_reduce, w_dilated, w_expand, norm_params):
    gains = norm_params[0]
    shifts = norm_params[1]
    reduced = low_back(product(flat_in, low(w_reduce)))
    first = low(smooth(normalize(reduced, gains[:M], shifts[:M])) * mask_flat[:, None])
    middle = low_back(dilated(first.reshape(CANVAS_ROWS, CANVAS_COLUMNS, M), low(w_dilated)))
    second = low(smooth(normalize(middle, gains[M:2 * M], shifts[M:2 * M])))
    expanded = low_back(product(second, low(w_expand)))
    return low(smooth(normalize(expanded, gains[2 * M:], shifts[2 * M:]) + flat_in))

def task_loss(task_index, shared, head_weight, head_rates, head_small, head_proj, sem_label, depth_target, normal_target, label_mask, counts):
    branch_bias, proj_bias, sem_w, depth_w, normal_w, sem_b, depth_b, normal_b = unpack_small(head_small)
    first_col = task_index * HID
    last_col = first_col + HID
    grid = shared.reshape(CANVAS_ROWS, CANVAS_COLUMNS, C)
    sums = [product(shared, low(head_weight[:, first_col:last_col]))]
    for rate_index in range(3):
        kernel = jnp.swapaxes(low(head_rates[rate_index, :, first_col:last_col, :]), 1, 2)
        sums.append(jax.checkpoint(partial(shifted_taps, rate=aspp_rates[rate_index]))(grid, kernel))
    hidden = [low(smooth(low_back(sums[branch] + branch_bias[branch, first_col:last_col]))) for branch in range(4)]
    joined = jnp.concatenate(hidden, axis=1)
    top = low(smooth(low_back(product(joined, low(head_proj[task_index])) + proj_bias[task_index])))
    mask_row = label_mask[task_index].reshape(-1).astype(jnp.float32)
    if task_index == 0:
        logits = low_back(product(top, low(sem_w)) + sem_b)
        classes = lax.broadcasted_iota(jnp.int32, (1, NCLS), 1)
        onehot = (sem_label.reshape(-1, 1) == classes).astype(jnp.float32)
        highest = lax.optimization_barrier(jnp.max(logits, axis=1, keepdims=True))
        log_total = jnp.log(lax.optimization_barrier(jnp.sum(jnp.exp(logits - highest), axis=1))) + highest[:, 0]
        picked = lax.optimization_barrier(jnp.sum(logits * onehot, axis=1))
        return jnp.sum(mask_row * (log_total - picked)) / counts[0]
    if task_index == 1:
        depth_pred = low_back(product(top, low(depth_w)) + depth_b)
        depth_gap = depth_pred[:, 0] - depth_target.reshape(-1)
        return jnp.sum(mask_row * (jnp.sqrt(depth_gap * depth_gap + 1.0) - 1.0)) / counts[1]
    normal_pred = low_back(product(top, low(normal_w)) + normal_b)
    normal_gap = normal_pred - normal_target.reshape(3, -1).T
    return jnp.sum(mask_row * 0.5 * lax.optimization_barrier(jnp.sum(normal_gap * normal_gap, axis=1))) / counts[2]

def imtl_weights(gram):
    lengths = jnp.sqrt(jnp.diagonal(gram) + 1e-12)

    def pairing(row_task, col_task):
        return gram[0, 0] / lengths[0] - gram[0, col_task] / lengths[col_task] - gram[row_task, 0] / lengths[0] + gram[row_task, col_task] / lengths[col_task]
    right_one = gram[0, 0] / lengths[0] - gram[0, 1] / lengths[1]
    right_two = gram[0, 0] / lengths[0] - gram[0, 2] / lengths[2]
    upper_left = pairing(1, 1)
    upper_right = pairing(1, 2)
    lower_left = pairing(2, 1)
    lower_right = pairing(2, 2)
    determinant = upper_left * lower_right - upper_right * lower_left
    alpha_one = (right_one * lower_right - right_two * lower_left) / determinant
    alpha_two = (right_two * upper_left - right_one * upper_right) / determinant
    return jnp.stack([1.0 - alpha_one - alpha_two, alpha_one, alpha_two])

def adam_step(weight, first, second, grad, rate, decay):
    first_new = BETA_ONE * first + (1.0 - BETA_ONE) * grad
    second_new = BETA_TWO * second + (1.0 - BETA_TWO) * grad * grad
    first_hat = first_new / (1.0 - BETA_ONE ** STEP)
    second_hat = second_new / (1.0 - BETA_TWO ** STEP)
    weight_new = weight - rate * (first_hat / (jnp.sqrt(second_hat) + ADAM_EPS) + decay * weight)
    return (weight_new, first_new, second_new)

def reference(features, valid_mask, sem_label, depth_target, normal_target, label_mask, w_reduce, m_reduce, v_reduce, w_dilated, m_dilated, v_dilated, w_expand, m_expand, v_expand, head_weight, m_head, v_head, head_rates, m_rates, v_rates, head_proj, m_proj, v_proj, norm_params, norm_m, norm_v, head_small, small_m, small_v):
    flat_in = features.astype(jnp.float32).reshape(CANVAS_ROWS * CANVAS_COLUMNS, C)
    mask_flat = valid_mask.reshape(-1).astype(jnp.float32)
    counts = jnp.maximum(lax.optimization_barrier(jnp.sum(label_mask.astype(jnp.float32), axis=(1, 2))), 1.0)

    def run_block(inputs, first_w, middle_w, last_w, norms):
        return block(inputs, mask_flat, first_w, middle_w, last_w, norms)
    shared, block_back = jax.vjp(run_block, flat_in, w_reduce, w_dilated, w_expand, norm_params)
    task_grads = []
    head_grad = jnp.zeros_like(head_weight)
    rates_grad = jnp.zeros_like(head_rates)
    small_grad = jnp.zeros_like(head_small)
    proj_grad = jnp.zeros_like(head_proj)
    for task_index in range(3):

        def run_task(inputs, weight, rates, vector, proj):
            return task_loss(task_index, inputs, weight, rates, vector, proj, sem_label, depth_target, normal_target, label_mask, counts)
        value, task_back = jax.vjp(run_task, shared, head_weight, head_rates, head_small, head_proj)
        shared_grad, weight_grad, rate_grad, vector_grad, proj_part = task_back(jnp.ones_like(value))
        task_grads.append(shared_grad)
        head_grad = head_grad + weight_grad
        rates_grad = rates_grad + rate_grad
        small_grad = small_grad + vector_grad
        proj_grad = proj_grad + proj_part
    gram = jnp.stack([jnp.stack([jnp.sum(task_grads[row_task] * task_grads[col_task]) for col_task in range(3)]) for row_task in range(3)])
    alphas = imtl_weights(gram)
    combined = alphas[0] * task_grads[0] + alphas[1] * task_grads[1] + alphas[2] * task_grads[2]
    input_grad, reduce_grad, dilated_grad, expand_grad, norm_grad = block_back(combined)
    squares = jnp.sum(reduce_grad * reduce_grad) + jnp.sum(dilated_grad * dilated_grad) + jnp.sum(expand_grad * expand_grad) + jnp.sum(head_grad * head_grad) + jnp.sum(rates_grad * rates_grad) + jnp.sum(proj_grad * proj_grad) + jnp.sum(norm_grad * norm_grad) + jnp.sum(small_grad * small_grad)
    grad_norm = jnp.sqrt(squares)
    factor = jnp.minimum(1.0, CLIP_NORM / (grad_norm + 1e-06))
    reduce_new, reduce_first, reduce_second = adam_step(w_reduce, m_reduce, v_reduce, reduce_grad * factor, RATE_MATRIX, DECAY)
    dilated_new, dilated_first, dilated_second = adam_step(w_dilated, m_dilated, v_dilated, dilated_grad * factor, RATE_MATRIX, DECAY)
    expand_new, expand_first, expand_second = adam_step(w_expand, m_expand, v_expand, expand_grad * factor, RATE_MATRIX, DECAY)
    head_new, head_first, head_second = adam_step(head_weight, m_head, v_head, head_grad * factor, RATE_MATRIX, DECAY)
    rates_new, rates_first, rates_second = adam_step(head_rates, m_rates, v_rates, rates_grad * factor, RATE_MATRIX, DECAY)
    proj_new, proj_first, proj_second = adam_step(head_proj, m_proj, v_proj, proj_grad * factor, RATE_MATRIX, DECAY)
    norm_new, norm_first, norm_second = adam_step(norm_params, norm_m, norm_v, norm_grad * factor, RATE_SMALL, 0.0)
    small_new, small_first, small_second = adam_step(head_small, small_m, small_v, small_grad * factor, RATE_SMALL, 0.0)
    depth_bias_grad = small_grad[HSMALL - 4]
    return (shared.reshape(CANVAS_ROWS, CANVAS_COLUMNS, C).astype(jnp.bfloat16), input_grad.reshape(CANVAS_ROWS, CANVAS_COLUMNS, C), grad_norm, reduce_new, reduce_first, reduce_second, reduce_new.astype(jnp.bfloat16), dilated_new, dilated_first, dilated_second, dilated_new.astype(jnp.bfloat16), expand_new, expand_first, expand_second, expand_new.astype(jnp.bfloat16), head_new, head_first, head_second, head_new.astype(jnp.bfloat16), rates_new, rates_first, rates_second, rates_new.astype(jnp.bfloat16), proj_new, proj_first, proj_second, proj_new.astype(jnp.bfloat16), norm_new, norm_first, norm_second, small_new, small_first, small_second, depth_bias_grad)
```

```python
import jax
import jax.numpy as jnp
from jax import lax
from jax.experimental import pallas as pl
from jax.experimental.pallas import tpu as pltpu
from jax.sharding import PartitionSpec as P

C = 2048
M = 512
HID = 256
NCLS = 19
DILATION_RATE = 4
STEP = 10


EPS_NORM = 1e-05
BETA_ONE = 0.9
BETA_TWO = 0.999
ADAM_EPS = 1e-08
RATE_MATRIX = 0.02
RATE_SMALL = 0.2
DECAY = 0.01
CLIP_NORM = 0.01
aspp_rates = (12, 24, 36)


def shifted(value, axis, steps):
    count = lax.axis_size(axis)
    leading, last = (max(0, -steps), min(count, count - steps))
    return lax.ppermute(value, axis, [(source, source + steps) for source in range(leading, last)])


def with_halo(cells, sides, width):
    for axis, dim in sides:
        count = lax.axis_size(axis)
        ends = count - 1
        head = lax.slice_in_dim(cells, 0, width, axis=dim)
        tail = lax.slice_in_dim(cells, cells.shape[dim] - width, cells.shape[dim], axis=dim)
        cells = jnp.concatenate(
            [
                lax.ppermute(tail, axis, [(i, (i + 1) % count) for i in range(ends)]),
                cells,
                lax.ppermute(head, axis, [((i + 1) % count, i) for i in range(ends)]),
            ],
            axis=dim,
        )
    return cells


def smooth(values):
    return jax.nn.gelu(values, approximate=True)


def smooth_slope(values):
    return jax.vjp(smooth, values)[1](jnp.ones_like(values))[0]


def contract_first(left, right):
    return lax.dot_general(
        left, right, (((0,), (0,)), ((), ())), preferred_element_type=jnp.float32
    )


def contract_last(left, right):
    return lax.dot_general(
        left, right, (((1,), (1,)), ((), ())), preferred_element_type=jnp.float32
    )


def split_tasks(slopes, weight):
    pixels = slopes.shape[0]
    return lax.dot_general(
        slopes.reshape(pixels, 3, -1),
        weight.reshape(weight.shape[0], 3, -1),
        (((2,), (2,)), ((1,), (1,))),
        preferred_element_type=jnp.float32,
    )


def split_tasks_rows(slopes, weight):
    pixels = slopes.shape[0]
    return lax.dot_general(
        slopes.reshape(pixels, 3, -1),
        weight.reshape(3, -1, weight.shape[1]),
        (((2,), (1,)), ((1,), (0,))),
        preferred_element_type=jnp.float32,
    )


def unpack_small(vector):
    lengths = (12 * HID, 3 * HID, HID * NCLS, HID, HID * 3, NCLS, 1, 3)
    pieces = []
    offset = 0
    for length in lengths:
        pieces.append(lax.slice_in_dim(vector, offset, offset + length, axis=0))
        offset = offset + length
    return (
        pieces[0].reshape(4, 3 * HID),
        pieces[1].reshape(3, HID),
        pieces[2].reshape(HID, NCLS),
        pieces[3].reshape(HID, 1),
        pieces[4].reshape(HID, 3),
        pieces[5],
        pieces[6],
        pieces[7],
    )


def pack_small(pieces):
    return jnp.concatenate([piece.reshape(-1) for piece in pieces])


def fetch_rows(grid, step):
    if abs(step) >= lax.axis_size("pix"):
        return jnp.zeros_like(grid)
    return shifted(grid, "pix", -step)


def fetch_grads(grid, step):
    if abs(step) >= lax.axis_size("pix"):
        return jnp.zeros_like(grid)
    return shifted(grid, "pix", -step)


def row_view(grid, offset, fetch):
    height = grid.shape[0]
    lead, rest = divmod(offset, height)
    return fetch(grid, lead)


def column_view(grid, offset):
    width = grid.shape[1]
    reach = abs(offset)
    if reach == 0:
        return grid
    padded_canvas = jnp.pad(grid, ((0, 0), (reach, reach), (0, 0)))
    return padded_canvas[:, reach + offset : reach + offset + width]


def imtl_weights(gram):
    lengths = jnp.sqrt(jnp.diagonal(gram) + 1e-12)

    def pairing(row_task, col_task):
        return (
            gram[0, 0] / lengths[0]
            - gram[0, col_task] / lengths[col_task]
            - gram[row_task, 0] / lengths[0]
            + gram[row_task, col_task] / lengths[col_task]
        )

    right_one = gram[0, 0] / lengths[0] - gram[0, 1] / lengths[1]
    right_two = gram[0, 0] / lengths[0] - gram[0, 2] / lengths[2]
    upper_left = pairing(1, 1)
    upper_right = pairing(1, 2)
    lower_left = pairing(2, 1)
    lower_right = pairing(2, 2)
    determinant = upper_left * lower_right - upper_right * lower_left
    alpha_one = (right_one * lower_right - right_two * lower_left) / determinant
    alpha_two = (right_two * upper_left - right_one * upper_right) / determinant
    return jnp.stack([1.0 - alpha_one - alpha_two, alpha_one, alpha_two])


def adam_step(weight, first, second, grad, rate, decay):
    first_new = BETA_ONE * first + (1.0 - BETA_ONE) * grad
    second_new = BETA_TWO * second + (1.0 - BETA_TWO) * grad * grad
    first_hat = first_new / (1.0 - BETA_ONE**STEP)
    second_hat = second_new / (1.0 - BETA_TWO**STEP)
    weight_new = weight - rate * (first_hat / (jnp.sqrt(second_hat) + ADAM_EPS) + decay * weight)
    return (weight_new, first_new, second_new)


def pixel_sums(first, second):
    return lax.psum((first, second), "pix")


def back_pair(first, second):
    return lax.psum((first, second), "pix")


def channel_gather(piece):
    return lax.all_gather(piece, "ch", axis=1, tiled=True)


def channel_parts(partial_sum):
    return lax.psum_scatter(partial_sum, "ch", scatter_dimension=1, tiled=True)


def forward_norm(inputs, sums, squares, count, gain_row, shift_row):
    mean_row = sums / count
    scale_row = lax.rsqrt(squares / count - mean_row * mean_row + EPS_NORM)
    normed = (inputs - mean_row) * scale_row
    return (normed * gain_row + shift_row, normed, scale_row)


def backward_norm(upstream, normed, scale_row, count, gain_row):
    shift_grad, gain_grad = back_pair(jnp.sum(upstream, axis=0), jnp.sum(upstream * normed, axis=0))
    inner = gain_row * scale_row * (upstream - shift_grad / count - normed * (gain_grad / count))
    return (inner, gain_grad, shift_grad)


def loss_slopes(
    logits, depth_pred, normal_pred, sem_label, depth_target, normal_target, label_mask, counts
):
    masks = label_mask.reshape(3, -1).astype(jnp.float32)
    classes = lax.broadcasted_iota(jnp.int32, (1, NCLS), 1)
    onehot = (sem_label.reshape(-1, 1) == classes).astype(jnp.float32)
    highest = jnp.max(logits, axis=1, keepdims=True)
    raised = jnp.exp(logits - highest)
    probs = raised / jnp.sum(raised, axis=1, keepdims=True)
    sem_slope = masks[0][:, None] * (probs - onehot) / counts[0]
    depth_gap = depth_pred[:, 0] - depth_target.reshape(-1)
    depth_slope = (masks[1] * depth_gap / jnp.sqrt(depth_gap * depth_gap + 1.0) / counts[1])[
        :, None
    ]
    normal_slope = masks[2][:, None] * (normal_pred - normal_target.reshape(3, -1).T) / counts[2]
    return (
        sem_slope.astype(jnp.bfloat16),
        depth_slope.astype(jnp.bfloat16),
        normal_slope.astype(jnp.bfloat16),
    )


def per_device_plain(
    features,
    valid_mask,
    sem_label,
    depth_target,
    normal_target,
    label_mask,
    w_reduce,
    m_reduce,
    v_reduce,
    w_dilated,
    m_dilated,
    v_dilated,
    w_expand,
    m_expand,
    v_expand,
    head_weight,
    m_head,
    v_head,
    head_rates,
    m_rates,
    v_rates,
    head_proj,
    m_proj,
    v_proj,
    norm_params,
    norm_m,
    norm_v,
    head_small,
    small_m,
    small_v,
):
    rows_per_shard, columns_per_shard, wide_dev = features.shape
    pixels = rows_per_shard * columns_per_shard
    groups = lax.axis_size("ch")
    block_id = lax.axis_index("ch")
    pix_devices = lax.axis_size("pix")
    middle_per_shard = M // groups
    count_all = float(pixels * pix_devices)
    flat_in = features.reshape(pixels, wide_dev)
    mask_flat = valid_mask.reshape(pixels).astype(jnp.float32)
    gains = norm_params[0]
    shifts = norm_params[1]

    def owned(vector, offset, width):
        return lax.dynamic_slice_in_dim(vector, offset + block_id * width, width)

    reduce_w, dilated_w, expand_w, heads_w, rates_w, proj_w = (
        lax.all_gather(w_reduce.astype(jnp.bfloat16), "pix", axis=1, tiled=True),
        lax.all_gather(w_dilated.astype(jnp.bfloat16), "pix", axis=1, tiled=True),
        lax.all_gather(w_expand.astype(jnp.bfloat16), "pix", axis=0, tiled=True),
        lax.all_gather(head_weight.astype(jnp.bfloat16), "pix", axis=1, tiled=True),
        lax.all_gather(head_rates.astype(jnp.bfloat16), "pix", axis=2, tiled=True),
        lax.all_gather(head_proj.astype(jnp.bfloat16), "pix", axis=1, tiled=True),
    )
    reduced = lax.psum_scatter(
        jnp.dot(flat_in, reduce_w, preferred_element_type=jnp.float32),
        "ch",
        scatter_dimension=1,
        tiled=True,
    )
    local_counts = jnp.sum(label_mask.astype(jnp.float32), axis=(1, 2))
    reduced_sum = jnp.sum(reduced, axis=0)
    reduced_sq = jnp.sum(reduced * reduced, axis=0)
    reduced_sum, reduced_sq = lax.psum((reduced_sum, reduced_sq), "pix")
    task_counts = lax.psum(local_counts, "pix")
    task_counts = jnp.maximum(task_counts, 1.0)
    gain_one = owned(gains, 0, middle_per_shard)
    norm_one, hat_one, scale_one = forward_norm(
        reduced, reduced_sum, reduced_sq, count_all, gain_one, owned(shifts, 0, middle_per_shard)
    )
    first = (smooth(norm_one) * mask_flat[:, None]).astype(jnp.bfloat16)
    first_gathered = channel_gather(first).reshape(rows_per_shard, columns_per_shard, M)
    bordered_input = with_halo(first_gathered, (("pix", 0),), DILATION_RATE)
    bordered_input = jnp.pad(bordered_input, ((0, 0), (DILATION_RATE, DILATION_RATE), (0, 0)))
    middle = jnp.zeros((pixels, middle_per_shard), jnp.float32)
    for tap_index in range(9):
        kernel_row, kernel_column = divmod(tap_index, 3)
        sliding_patch = bordered_input[
            kernel_row * DILATION_RATE : kernel_row * DILATION_RATE + rows_per_shard,
            kernel_column * DILATION_RATE : kernel_column * DILATION_RATE + columns_per_shard,
        ].reshape(pixels, M)
        middle = middle + jnp.dot(
            sliding_patch, dilated_w[tap_index], preferred_element_type=jnp.float32
        )
    gain_two = owned(gains, M, middle_per_shard)
    middle_sum, middle_sq = pixel_sums(jnp.sum(middle, axis=0), jnp.sum(middle * middle, axis=0))
    norm_two, hat_two, scale_two = forward_norm(
        middle, middle_sum, middle_sq, count_all, gain_two, owned(shifts, M, middle_per_shard)
    )
    second = smooth(norm_two).astype(jnp.bfloat16)
    second_all = channel_gather(second)
    expanded = jnp.dot(second_all, expand_w, preferred_element_type=jnp.float32)
    gain_three = owned(gains, 2 * M, wide_dev)
    expand_sum, expand_sq = pixel_sums(
        jnp.sum(expanded, axis=0), jnp.sum(expanded * expanded, axis=0)
    )
    norm_three, hat_three, scale_three = forward_norm(
        expanded, expand_sum, expand_sq, count_all, gain_three, owned(shifts, 2 * M, wide_dev)
    )
    summed_in = norm_three + flat_in.astype(jnp.float32)
    shared = smooth(summed_in).astype(jnp.bfloat16)
    branch_bias, proj_bias, sem_w, depth_w, normal_w, sem_b, depth_b, normal_b = unpack_small(
        head_small
    )
    out_weights = (
        sem_w.astype(jnp.bfloat16),
        depth_w.astype(jnp.bfloat16),
        normal_w.astype(jnp.bfloat16),
    )
    grid_shared = shared.reshape(rows_per_shard, columns_per_shard, wide_dev)
    row_views = []
    pre_list = [jnp.dot(shared, heads_w, preferred_element_type=jnp.float32)]
    for rate_index, rate in enumerate(aspp_rates):
        views = (
            row_view(grid_shared, -rate, fetch_rows),
            grid_shared,
            row_view(grid_shared, rate, fetch_rows),
        )
        row_views.append(views)
        summed = jnp.zeros((pixels, 3 * HID), jnp.float32)
        for tap_index in range(9):
            kernel_row, kernel_column = divmod(tap_index, 3)
            sliding_patch = column_view(views[kernel_row], (kernel_column - 1) * rate).reshape(
                pixels, wide_dev
            )
            summed = summed + contract_last(sliding_patch, rates_w[rate_index, tap_index])
        pre_list.append(summed)
    pre_parts = jnp.stack(pre_list, axis=1)
    before = lax.psum(pre_parts, "ch") + branch_bias[None]
    hidden = smooth(before).astype(jnp.bfloat16)
    branch_slope = smooth_slope(before).reshape(pixels, 4, 3, HID)
    joined_list = []
    projected_list = []
    top_list = []
    produced = []
    for task_index in range(3):
        joined = hidden[:, :, task_index * HID : (task_index + 1) * HID].reshape(pixels, 4 * HID)
        projected = (
            jnp.dot(joined, proj_w[task_index], preferred_element_type=jnp.float32)
            + proj_bias[task_index]
        )
        top = smooth(projected).astype(jnp.bfloat16)
        produced.append(jnp.dot(top, out_weights[task_index], preferred_element_type=jnp.float32))
        joined_list.append(joined)
        projected_list.append(projected)
        top_list.append(top)
    logits = produced[0] + sem_b
    depth_pred = produced[1] + depth_b
    normal_pred = produced[2] + normal_b
    slopes = loss_slopes(
        logits,
        depth_pred,
        normal_pred,
        sem_label,
        depth_target,
        normal_target,
        label_mask,
        task_counts,
    )
    out_grads = []
    out_bias_grads = []
    proj_grads = []
    proj_bias_grads = []
    joined_backs = []
    for task_index in range(3):
        top_back = contract_last(slopes[task_index], out_weights[task_index])
        proj_back = (top_back * smooth_slope(projected_list[task_index])).astype(jnp.bfloat16)
        out_grads.append(contract_first(top_list[task_index], slopes[task_index]))
        out_bias_grads.append(jnp.sum(slopes[task_index], axis=0, dtype=jnp.float32))
        proj_grads.append(contract_first(joined_list[task_index], proj_back))
        proj_bias_grads.append(jnp.sum(proj_back, axis=0, dtype=jnp.float32))
        joined_backs.append(contract_last(proj_back, proj_w[task_index]).reshape(pixels, 4, HID))
    joined_back = jnp.stack(joined_backs, axis=2)
    pre_grad = (joined_back * branch_slope).astype(jnp.bfloat16).reshape(pixels, 4, 3 * HID)
    small_term = (
        pack_small(
            [jnp.sum(pre_grad, axis=0, dtype=jnp.float32), jnp.stack(proj_bias_grads)]
            + out_grads
            + out_bias_grads
        )
        / groups
    )
    proj_grad = jnp.stack(proj_grads)
    first_branch = pre_grad[:, 0]
    task_sum = split_tasks(first_branch, heads_w)
    rates_list = []
    for rate_index, rate in enumerate(aspp_rates):
        flat_back = pre_grad[:, rate_index + 1]
        rate_back = flat_back.reshape(rows_per_shard, columns_per_shard, 3 * HID)
        back_views = (
            row_view(rate_back, rate, fetch_grads),
            rate_back,
            row_view(rate_back, -rate, fetch_grads),
        )
        for tap_index in range(9):
            kernel_row, kernel_column = divmod(tap_index, 3)
            sliding_patch = column_view(
                row_views[rate_index][kernel_row], (kernel_column - 1) * rate
            ).reshape(pixels, wide_dev)
            rates_list.append(contract_first(flat_back, sliding_patch))
            spread = column_view(back_views[kernel_row], (1 - kernel_column) * rate).reshape(
                pixels, 3 * HID
            )
            task_sum = task_sum + split_tasks_rows(spread, rates_w[rate_index, tap_index])
    rates_grad = jnp.stack(rates_list).reshape(3, 9, 3 * HID, wide_dev)
    task_grads = [task_sum[0], task_sum[1], task_sum[2]]
    head_grad = contract_first(shared, first_branch)
    local_gram = jnp.stack(
        [
            jnp.stack(
                [jnp.sum(task_grads[row_task] * task_grads[col_task]) for col_task in range(3)]
            )
            for row_task in range(3)
        ]
    )
    gram = lax.psum(local_gram, ("pix", "ch"))
    alphas = imtl_weights(gram)
    combined = alphas[0] * task_grads[0] + alphas[1] * task_grads[1] + alphas[2] * task_grads[2]
    shared_slope = combined * smooth_slope(summed_in)
    expand_up, gain_three_grad, shift_three_grad = backward_norm(
        shared_slope, hat_three, scale_three, count_all, gain_three
    )
    expand_back = expand_up.astype(jnp.bfloat16)
    expand_grad = contract_first(second_all, expand_back)
    second_back = channel_parts(contract_last(expand_back, expand_w))
    middle_up, gain_two_grad, shift_two_grad = backward_norm(
        second_back * smooth_slope(norm_two), hat_two, scale_two, count_all, gain_two
    )
    middle_gradient = middle_up.astype(jnp.bfloat16)
    dilated_list = []
    for tap_index in range(9):
        kernel_row, kernel_column = divmod(tap_index, 3)
        sliding_patch = bordered_input[
            kernel_row * DILATION_RATE : kernel_row * DILATION_RATE + rows_per_shard,
            kernel_column * DILATION_RATE : kernel_column * DILATION_RATE + columns_per_shard,
        ].reshape(pixels, M)
        dilated_list.append(contract_first(sliding_patch, middle_gradient))
    dilated_grad = jnp.stack(dilated_list)
    canvas_gradient = with_halo(
        middle_gradient.reshape(rows_per_shard, columns_per_shard, middle_per_shard),
        (("pix", 0),),
        DILATION_RATE,
    )
    canvas_gradient = jnp.pad(canvas_gradient, ((0, 0), (DILATION_RATE, DILATION_RATE), (0, 0)))
    first_part = jnp.zeros((pixels, M), jnp.float32)
    for tap_index in range(9):
        kernel_row, kernel_column = divmod(tap_index, 3)
        sliding_patch = canvas_gradient[
            (2 - kernel_row) * DILATION_RATE : (2 - kernel_row) * DILATION_RATE + rows_per_shard,
            (2 - kernel_column) * DILATION_RATE : (2 - kernel_column) * DILATION_RATE
            + columns_per_shard,
        ].reshape(pixels, middle_per_shard)
        first_part = first_part + contract_last(sliding_patch, dilated_w[tap_index])
    first_back = channel_parts(first_part) * mask_flat[:, None] * smooth_slope(norm_one)
    reduce_up, gain_one_grad, shift_one_grad = backward_norm(
        first_back, hat_one, scale_one, count_all, gain_one
    )
    reduce_all = channel_gather(reduce_up.astype(jnp.bfloat16))
    reduce_grad = contract_first(flat_in, reduce_all)
    input_grad = contract_last(reduce_all, reduce_w) + shared_slope
    reduce_shard, dilated_shard, expand_shard, head_shard, rates_shard, proj_shard = (
        lax.psum_scatter(reduce_grad, "pix", scatter_dimension=1, tiled=True),
        lax.psum_scatter(dilated_grad, "pix", scatter_dimension=1, tiled=True),
        lax.psum_scatter(expand_grad, "pix", scatter_dimension=0, tiled=True),
        lax.psum_scatter(head_grad, "pix", scatter_dimension=1, tiled=True),
        lax.psum_scatter(rates_grad, "pix", scatter_dimension=2, tiled=True),
        lax.psum_scatter(proj_grad, "pix", scatter_dimension=1, tiled=True),
    )
    norm_local = jnp.zeros((2, 2 * M + C), jnp.float32)
    for offset, width, gain_grad, shift_grad in (
        (0, middle_per_shard, gain_one_grad, shift_one_grad),
        (M, middle_per_shard, gain_two_grad, shift_two_grad),
        (2 * M, wide_dev, gain_three_grad, shift_three_grad),
    ):
        norm_local = lax.dynamic_update_slice(
            norm_local, jnp.stack([gain_grad, shift_grad]), (0, offset + block_id * width)
        )
    big_local = (
        jnp.sum(reduce_shard * reduce_shard)
        + jnp.sum(dilated_shard * dilated_shard)
        + jnp.sum(expand_shard * expand_shard)
        + jnp.sum(head_shard * head_shard)
        + jnp.sum(rates_shard * rates_shard)
        + jnp.sum(proj_shard * proj_shard) / groups
    )
    big_squares, norm_grad, small_grad = lax.psum(
        (big_local, norm_local / pix_devices, small_term), ("pix", "ch")
    )
    grad_norm = jnp.sqrt(
        big_squares + jnp.sum(norm_grad * norm_grad) + jnp.sum(small_grad * small_grad)
    )
    factor = jnp.minimum(1.0, CLIP_NORM / (grad_norm + 1e-06))
    reduce_new, reduce_first, reduce_second = adam_step(
        w_reduce, m_reduce, v_reduce, reduce_shard * factor, RATE_MATRIX, DECAY
    )
    dilated_new, dilated_first, dilated_second = adam_step(
        w_dilated, m_dilated, v_dilated, dilated_shard * factor, RATE_MATRIX, DECAY
    )
    expand_new, expand_first, expand_second = adam_step(
        w_expand, m_expand, v_expand, expand_shard * factor, RATE_MATRIX, DECAY
    )
    head_new, head_first, head_second = adam_step(
        head_weight, m_head, v_head, head_shard * factor, RATE_MATRIX, DECAY
    )
    rates_new, rates_first, rates_second = adam_step(
        head_rates, m_rates, v_rates, rates_shard * factor, RATE_MATRIX, DECAY
    )
    proj_new, proj_first, proj_second = adam_step(
        head_proj, m_proj, v_proj, proj_shard * factor, RATE_MATRIX, DECAY
    )
    norm_new, norm_first, norm_second = adam_step(
        norm_params, norm_m, norm_v, norm_grad * factor, RATE_SMALL, 0.0
    )
    small_new, small_first, small_second = adam_step(
        head_small, small_m, small_v, small_grad * factor, RATE_SMALL, 0.0
    )
    depth_bias_grad = small_grad[small_grad.shape[0] - 4]
    return (
        shared.reshape(rows_per_shard, columns_per_shard, wide_dev),
        input_grad.reshape(rows_per_shard, columns_per_shard, wide_dev),
        grad_norm,
        reduce_new,
        reduce_first,
        reduce_second,
        reduce_new.astype(jnp.bfloat16),
        dilated_new,
        dilated_first,
        dilated_second,
        dilated_new.astype(jnp.bfloat16),
        expand_new,
        expand_first,
        expand_second,
        expand_new.astype(jnp.bfloat16),
        head_new,
        head_first,
        head_second,
        head_new.astype(jnp.bfloat16),
        rates_new,
        rates_first,
        rates_second,
        rates_new.astype(jnp.bfloat16),
        proj_new,
        proj_first,
        proj_second,
        proj_new.astype(jnp.bfloat16),
        norm_new,
        norm_first,
        norm_second,
        small_new,
        small_first,
        small_second,
        depth_bias_grad,
    )


MESH = pl.DeviceIdType.MESH
BF = jnp.bfloat16
F32 = jnp.float32
NPIX = 8
NCH = 4
ROWS = 4
WIDTH = 128
PX = ROWS * WIDTH
CIN = C // NCH
COLS = 3 * HID // NPIX
SEGS = COLS // 32
VMEM_LIMIT = 60 * 2**20


def row_groups():
    groups = []
    for rate_index, rate in enumerate(aspp_rates):
        for step in (-1, 0, 1):
            if abs(step) * rate // ROWS < NPIX:
                groups.append((rate_index, step))
    return groups


GROUPS = row_groups()
TAPS = 1 + 3 * len(GROUPS)
SEG_ROWS = TAPS * 32


def whole_vmem():
    return pl.BlockSpec(memory_space=pltpu.VMEM)


def slide(tile, steps):
    lane = lax.broadcasted_iota(jnp.int32, tile.shape, 1)
    if steps == 0:
        return tile
    rolled = pltpu.roll(tile, steps % WIDTH, 1)
    if steps > 0:
        return jnp.where(lane >= steps, rolled, 0.0)
    return jnp.where(lane < WIDTH + steps, rolled, 0.0)


def tanh_parts(values):
    root = 0.7978845608028654
    inner = jnp.tanh(root * (values + 0.044715 * values * values * values))
    return root, inner


def gelu_of(values):
    _, inner = tanh_parts(values)
    return 0.5 * values * (1.0 + inner)


def gelu_slope(values):
    root, inner = tanh_parts(values)
    return 0.5 * (1.0 + inner) + 0.5 * values * (1.0 - inner * inner) * root * (
        1.0 + 3.0 * 0.044715 * values * values
    )


def nt_dot(left, right):
    return lax.dot_general(left, right, (((1,), (1,)), ((), ())), preferred_element_type=F32)


def nn_dot(left, right):
    return lax.dot_general(left, right, (((1,), (0,)), ((), ())), preferred_element_type=F32)


def greet(targets):
    barrier = pltpu.get_barrier_semaphore()
    for target in targets:
        pl.semaphore_signal(barrier, inc=1, device_id=target, device_id_type=MESH)
    pl.semaphore_wait(barrier, len(targets))


def remote(src, dst, send_sem, recv_sem, target):
    return pltpu.make_async_remote_copy(
        src, dst, send_sem, recv_sem, device_id=target, device_id_type=MESH
    )


def place():
    p = lax.axis_index("pix")
    c = lax.axis_index("ch")
    return p, c, p // 2, lax.rem(p, 2), c // 2, lax.rem(c, 2)


def heads_forward_kernel(
    x_ref, w_ref, q_ref, xall_ref,
    acc, y_tmp, core_buf, core_in, x_buf, x_in, row_buf, local_sem,
    zr_send, zl_send, z_recv, y_send, y_recv, core_send, core_recv, x_send, x_recv, row_send, row_recv,
):
    p, c, z, y, x, core = place()
    zcount = NPIX // 2
    up = (2 * lax.rem(z + 1, zcount) + y, c)
    down = (2 * lax.rem(z + zcount - 1, zcount) + y, c)
    other_y = (2 * z + 1 - y, c)
    other_core = (p, 2 * x + 1 - core)
    other_x = (p, 2 * (1 - x) + core)
    row_targets = [(lax.rem(p + d, NPIX), c) for d in range(1, NPIX)]
    greet(row_targets + [other_core, other_x])

    own = pltpu.make_async_copy(x_ref, xall_ref.at[p], local_sem.at[0])
    own.start()

    def to_up(source):
        return remote(xall_ref.at[source], xall_ref.at[source], zr_send.at[source // 2], z_recv.at[source // 2], up)

    def to_down(source):
        return remote(xall_ref.at[source], xall_ref.at[source], zl_send.at[source // 2], z_recv.at[source // 2], down)

    def to_y(source):
        return remote(xall_ref.at[source], xall_ref.at[source], y_send.at[source // 2], y_recv.at[source // 2], other_y)

    def step_of(i):
        near = jnp.where(z == 0, i, jnp.where(z == 3, 3 - i, 0))
        one = jnp.where(i == 0, 1, jnp.where(i == 1, 0, i))
        two = jnp.where(i == 0, 2, jnp.where(i == 1, 3, 3 - i))
        two = jnp.where(i == 2, 1, jnp.where(i == 3, 0, two))
        return jnp.where(z == 1, one, jnp.where(z == 2, two, near))

    acc[...] = jnp.zeros_like(acc)
    own.wait()

    def process(src):
        xb = xall_ref[src]

        def one_seg(s, carry):
            y_tmp[...] = nt_dot(w_ref[s], xb)

            def add_group(dest, branch, first_tap, taps):
                rows = pl.ds(pl.multiple_of(branch * COLS + s * 32, 32), 32)
                for r in range(ROWS):
                    lanes = pl.ds(r * WIDTH, WIDTH)
                    total = acc[dest, rows, lanes]
                    for i, shift in enumerate(taps):
                        tile = y_tmp[pl.ds((first_tap + i) * 32, 32), lanes]
                        total = total + slide(tile, shift)
                    acc[dest, rows, lanes] = total

            add_group(src, 0, 0, (0,))
            for g, (rate_index, step) in enumerate(GROUPS):
                rate = aspp_rates[rate_index]
                dest = src - step * (rate // ROWS)
                shifts = (rate, 0, -rate)
                if step == 0:
                    add_group(dest, rate_index + 1, 1 + 3 * g, shifts)
                else:

                    @pl.when((dest >= 0) & (dest < NPIX))
                    def _():
                        add_group(dest, rate_index + 1, 1 + 3 * g, shifts)

            return carry

        lax.fori_loop(0, SEGS, one_seg, 0)

    def gather_step(i, carry):
        zs = step_of(i)
        mine = 2 * zs + y
        theirs = 2 * zs + 1 - y

        @pl.when(i > 0)
        def _():
            to_up(mine).wait_recv()

        @pl.when((zs <= z) & (z < zcount - 1))
        def _():
            to_up(mine).start()

        @pl.when((zs >= z) & (z > 0))
        def _():
            to_down(mine).start()

        to_y(mine).start()
        process(mine)
        to_y(theirs).wait_recv()
        process(theirs)
        return carry

    lax.fori_loop(0, zcount, gather_step, 0)

    def drain(zs, carry):
        mine = 2 * zs + y

        @pl.when((zs <= z) & (z < zcount - 1))
        def _():
            to_up(mine).wait_send()

        @pl.when((zs >= z) & (z > 0))
        def _():
            to_down(mine).wait_send()

        to_y(mine).wait_send()
        return carry

    lax.fori_loop(0, zcount, drain, 0)

    def lanes_of(ch):
        return pl.ds(pl.multiple_of(ch * WIDTH, WIDTH), WIDTH)

    def core_copy(b):
        return remote(core_buf.at[b], core_in.at[b], core_send.at[b], core_recv.at[b], other_core)

    def x_copy(b):
        return remote(x_buf.at[b], x_in.at[b], x_send.at[b], x_recv.at[b], other_x)

    def row_copy(b, slot):
        return remote(
            row_buf.at[b],
            q_ref.at[:, pl.ds(pl.multiple_of(COLS * p, 32), COLS), :],
            row_send.at[slot],
            row_recv.at[slot],
            (b, c),
        )

    def core_step(d, carry):
        b = lax.rem(p + d, NPIX)
        for xx in range(2):
            core_buf[b, xx] = acc[b, :, lanes_of(2 * xx + 1 - core)].astype(BF)
        core_copy(b).start()
        return carry

    lax.fori_loop(0, NPIX, core_step, 0)

    def x_step(d, carry):
        b = lax.rem(p + d, NPIX)
        core_copy(b).wait_recv()
        x_buf[b] = (acc[b, :, lanes_of(2 * (1 - x) + core)] + core_in[b, 1 - x].astype(F32)).astype(BF)
        x_copy(b).start()
        return carry

    lax.fori_loop(0, NPIX, x_step, 0)

    def finish(b):
        x_copy(b).wait_recv()
        total = acc[b, :, lanes_of(c)] + core_in[b, x].astype(F32) + x_in[b].astype(F32)
        return total.astype(BF).reshape(4, COLS, WIDTH)

    def row_step(d, carry):
        b = lax.rem(p + d, NPIX)
        row_buf[b] = finish(b)
        row_copy(b, d - 1).start()
        return carry

    lax.fori_loop(1, NPIX, row_step, 0)
    q_ref[:, pl.ds(pl.multiple_of(COLS * p, 32), COLS), :] = finish(p)

    def settle(d, carry):
        b = lax.rem(p + d, NPIX)
        row_copy(b, d - 1).wait()
        return carry

    lax.fori_loop(1, NPIX, settle, 0)

    def settle_more(b, carry):
        core_copy(b).wait_send()
        x_copy(b).wait_send()
        return carry

    lax.fori_loop(0, NPIX, settle_more, 0)


def heads_forward(block_out, w_seg):
    dma = pltpu.SemaphoreType.DMA
    zc = NPIX // 2
    return pl.pallas_call(
        heads_forward_kernel,
        out_shape=(
            jax.ShapeDtypeStruct((4, 3 * HID, WIDTH), BF),
            jax.ShapeDtypeStruct((NPIX, PX, CIN), BF),
        ),
        in_specs=[whole_vmem()] * 2,
        out_specs=[whole_vmem()] * 2,
        scratch_shapes=[
            pltpu.VMEM((NPIX, 4 * COLS, PX), F32),
            pltpu.VMEM((SEG_ROWS, PX), F32),
            pltpu.VMEM((NPIX, 2, 4 * COLS, WIDTH), BF),
            pltpu.VMEM((NPIX, 2, 4 * COLS, WIDTH), BF),
            pltpu.VMEM((NPIX, 4 * COLS, WIDTH), BF),
            pltpu.VMEM((NPIX, 4 * COLS, WIDTH), BF),
            pltpu.VMEM((NPIX, 4, COLS, WIDTH), BF),
            dma((1,)),
            dma((zc,)), dma((zc,)), dma((zc,)), dma((zc,)), dma((zc,)),
            dma((NPIX,)), dma((NPIX,)), dma((NPIX,)), dma((NPIX,)),
            dma((NPIX - 1,)), dma((NPIX - 1,)),
        ],
        compiler_params=pltpu.CompilerParams(
            collective_id=1, has_side_effects=True, vmem_limit_bytes=VMEM_LIMIT
        ),
        name="heads_forward",
    )(block_out, w_seg)


def heads_middle_kernel(
    q_ref, bias_ref, pbias_ref, wpt_ref, wot_ref, obias_ref, label_ref, target_ref, mask_ref, count_ref,
    dq_ref, dwp_ref, dwo_ref, rows_ref, obg_ref,
    hid,
):
    ones = jnp.ones((8, WIDTH), BF)
    for k in range(4):
        hid[k] = gelu_of(q_ref[k].astype(F32) + bias_ref[:, k : k + 1]).astype(BF)
    row = lax.broadcasted_iota(jnp.int32, (32, WIDTH), 0)
    for t in range(3):
        cols = slice(t * HID, (t + 1) * HID)
        zt = pbias_ref[:, t : t + 1] + jnp.zeros((HID, WIDTH), F32)
        for k in range(4):
            zt = zt + nn_dot(wpt_ref[t, :, k * HID : (k + 1) * HID], hid[k, cols, :])
        ut = gelu_of(zt).astype(BF)
        out = lax.dot_general(
            wot_ref[t], ut, (((0,), (0,)), ((), ())), preferred_element_type=F32
        ) + obias_ref[:, t : t + 1]
        scale = mask_ref[t : t + 1, :] / count_ref[t : t + 1, :]
        if t == 0:
            live = row < NCLS
            highest = jnp.max(jnp.where(live, out, -1e30), axis=0, keepdims=True)
            raised = jnp.where(live, jnp.exp(jnp.minimum(out - highest, 0.0)), 0.0)
            probs = raised / jnp.sum(raised, axis=0, keepdims=True)
            onehot = (row == label_ref[0:1, :]).astype(F32)
            slope = scale * (probs - onehot)
        elif t == 1:
            gap = out - target_ref[0:1, :]
            slope = jnp.where(row < 1, scale * gap / jnp.sqrt(gap * gap + 1.0), 0.0)
        else:
            target = jnp.zeros((32, WIDTH), F32)
            for i in range(3):
                target = jnp.where(row == i, target_ref[1 + i : 2 + i, :], target)
            slope = jnp.where(row < 3, scale * (out - target), 0.0)
        ot = slope.astype(BF)
        dwo_ref[t] = nt_dot(ot, ut)
        obg_ref[t] = nt_dot(ones, ot)
        dz = (nn_dot(wot_ref[t], ot) * gelu_slope(zt)).astype(BF)
        rows_ref[4, :, cols] = nt_dot(ones, dz)
        for k in range(4):
            part = hid[k, cols, :]
            dwp_ref[t, k * HID : (k + 1) * HID, :] = nt_dot(part, dz)
            dcat = lax.dot_general(
                wpt_ref[t, :, k * HID : (k + 1) * HID], dz, (((0,), (0,)), ((), ())),
                preferred_element_type=F32,
            )
            before = q_ref[k, cols, :].astype(F32) + bias_ref[cols, k : k + 1]
            dq_ref[k, cols, :] = (dcat * gelu_slope(before)).astype(BF)
    for k in range(4):
        rows_ref[k] = nt_dot(ones, dq_ref[k])


def heads_middle(q, bias, pbias, wpt, wot, obias, label, target, mask, count):
    return pl.pallas_call(
        heads_middle_kernel,
        out_shape=(
            jax.ShapeDtypeStruct((4, 3 * HID, WIDTH), BF),
            jax.ShapeDtypeStruct((3, 4 * HID, HID), F32),
            jax.ShapeDtypeStruct((3, 32, HID), F32),
            jax.ShapeDtypeStruct((5, 8, 3 * HID), F32),
            jax.ShapeDtypeStruct((3, 8, 32), F32),
        ),
        in_specs=[whole_vmem()] * 10,
        out_specs=[whole_vmem()] * 5,
        scratch_shapes=[pltpu.VMEM((4, 3 * HID, WIDTH), BF)],
        compiler_params=pltpu.CompilerParams(vmem_limit_bytes=VMEM_LIMIT),
        name="heads_middle",
    )(q, bias, pbias, wpt, wot, obias, label, target, mask, count)


def low_task(zplane):
    return (2 * zplane * COLS) // HID


def heads_backward_kernel(
    dq_ref, xall_ref, w_ref, dw_ref, gz_ref,
    dq_all, wt, dcol, parts, y_in, z_buf, z_in, gram_own, gram_ch, gram_px, gsum,
    local_sem, row_send, row_recv, x_send, x_recv, ca_send, ca_recv, cb_send, cb_recv,
    y_send, y_recv, z_send, z_recv, gc_send, gc_recv, gp_send, gp_recv,
):
    p, c, z, y, x, core = place()
    zcount = NPIX // 2
    other_y = (2 * z + 1 - y, c)
    other_core = (p, 2 * x + 1 - core)
    other_x = (p, 2 * (1 - x) + core)
    pix_targets = [(lax.rem(p + d, NPIX), c) for d in range(1, NPIX)]
    ch_targets = [(p, lax.rem(c + d, NCH)) for d in range(1, NCH)]
    greet(pix_targets + ch_targets)

    def cols_of(b):
        return pl.ds(pl.multiple_of(COLS * b, 32), COLS)

    def row_copy(d):
        b = lax.rem(p + d, NPIX)
        return remote(dq_ref.at[:, cols_of(b), :], dq_all.at[p, c], row_send.at[d - 1], row_recv.at[d - 1], (b, c))

    for d in range(1, NPIX):
        row_copy(d).start()
    own = pltpu.make_async_copy(dq_ref.at[:, cols_of(p), :], dq_all.at[p, c], local_sem.at[0])
    own.start()
    for s in range(SEGS):
        wt[s] = jnp.transpose(w_ref[s].astype(F32)).astype(BF)
    dw_ref[...] = jnp.zeros_like(dw_ref)
    own.wait()

    def x_copy(d, b, ch):
        return remote(dq_all.at[b, ch], dq_all.at[b, ch], x_send.at[d], x_recv.at[d], other_x)

    def ca_copy(d, b, ch):
        return remote(dq_all.at[b, ch], dq_all.at[b, ch], ca_send.at[d], ca_recv.at[d], other_core)

    def cb_copy(d, b, ch):
        return remote(dq_all.at[b, ch], dq_all.at[b, ch], cb_send.at[d], cb_recv.at[d], other_core)

    far = 2 * (1 - x) + core
    for d in range(NPIX):
        b = lax.rem(p + NPIX - d, NPIX)
        if d > 0:
            row_copy(d).wait_recv()
        x_copy(d, b, c).start()
        ca_copy(d, b, c).start()
    for d in range(NPIX):
        b = lax.rem(p + NPIX - d, NPIX)
        x_copy(d, b, far).wait_recv()
        cb_copy(d, b, far).start()
    for d in range(NPIX):
        b = lax.rem(p + NPIX - d, NPIX)
        ca_copy(d, b, 2 * x + 1 - core).wait_recv()
        cb_copy(d, b, 2 * (1 - x) + 1 - core).wait_recv()

    def task_of(pixel_device, s):
        return (SEGS * pixel_device + s) // (HID // 32)

    in_low = [task_of(p, s) == low_task(z) for s in range(SEGS)]
    other_p = 2 * z + 1 - y

    def has_low(device):
        return task_of(device, 0) == low_task(z)

    def has_high(device):
        return task_of(device, SEGS - 1) != low_task(z)

    def y_copy(zz, slot):
        return remote(
            parts.at[2 * zz + 1 - y, slot], y_in.at[zz, slot],
            y_send.at[zz, slot], y_recv.at[zz, slot], other_y,
        )

    def block_step(i, carry):
        zz = lax.rem(i, zcount)
        b = jnp.where(i < zcount, 2 * zz + 1 - y, 2 * zz + y)

        def fill(source, branch, first_tap, shifts):
            for r in range(ROWS):
                lanes = pl.ds(r * WIDTH, WIDTH)
                tile = dq_all[source, r, branch].astype(F32)
                for t, shift in enumerate(shifts):
                    moved = slide(tile, shift).astype(BF)
                    for s in range(SEGS):
                        dcol[s, pl.ds((first_tap + t) * 32, 32), lanes] = moved[s * 32 : (s + 1) * 32]

        fill(b, 0, 0, (0,))
        for g, (rate_index, step) in enumerate(GROUPS):
            rate = aspp_rates[rate_index]
            source = b - step * (rate // ROWS)
            shifts = (-rate, 0, rate)
            if step == 0:
                fill(source, rate_index + 1, 1 + 3 * g, shifts)
            else:
                inside = (source >= 0) & (source < NPIX)

                @pl.when(inside)
                def _():
                    fill(source, rate_index + 1, 1 + 3 * g, shifts)

                @pl.when(jnp.logical_not(inside))
                def _():
                    for s in range(SEGS):
                        dcol[s, pl.ds((1 + 3 * g) * 32, 96), :] = jnp.zeros((96, PX), BF)

        def product_rows(m, inner):
            rows = pl.ds(pl.multiple_of(m * 128, 128), 128)
            low = jnp.zeros((128, PX), F32)
            high = jnp.zeros((128, PX), F32)
            for s in range(SEGS):
                value = nn_dot(wt[s, rows, :], dcol[s])
                low = low + jnp.where(in_low[s], value, 0.0)
                high = high + jnp.where(in_low[s], 0.0, value)
            parts[b, 0, rows, :] = low.astype(BF)
            parts[b, 1, rows, :] = high.astype(BF)
            return inner

        lax.fori_loop(0, CIN // 128, product_rows, 0)

        @pl.when((i < zcount) & has_low(p))
        def _():
            y_copy(zz, 0).start()

        @pl.when((i < zcount) & has_high(p))
        def _():
            y_copy(zz, 1).start()

        def weight_rows(m, inner):
            s = m // 2
            rows = pl.ds(pl.multiple_of(lax.rem(m, 2) * (SEG_ROWS // 2), 32), SEG_ROWS // 2)
            dw_ref[s, rows, :] += nn_dot(dcol[s, rows, :], xall_ref[b])
            return inner

        lax.fori_loop(0, 2 * SEGS, weight_rows, 0)
        return carry

    lax.fori_loop(0, NPIX, block_step, 0)

    def z_copy(d, slot):
        zz = lax.rem(z + d, zcount)
        return remote(
            z_buf.at[zz, slot], z_in.at[z, slot],
            z_send.at[d - 1, slot], z_recv.at[d - 1, slot], (2 * zz + y, c),
        )

    pair_high = (z == 1) | (z == 2)
    for d in (1, 2, 3, 0):
        zz = lax.rem(z + d, zcount)
        for slot in range(2):
            theirs = has_low(other_p) if slot == 0 else has_high(other_p)
            there = pair_high if slot else (z >= 0)

            @pl.when(theirs)
            def _():
                y_copy(zz, slot).wait_recv()
                z_buf[zz, slot] = (
                    parts[2 * zz + y, slot].astype(F32) + y_in[zz, slot].astype(F32)
                ).astype(BF)

            @pl.when(jnp.logical_not(theirs))
            def _():
                z_buf[zz, slot] = parts[2 * zz + y, slot]

            if d > 0:

                @pl.when(there)
                def _():
                    z_copy(d, slot).start()

    for slot in range(2):
        z_in[z, slot] = z_buf[z, slot]
    for d in range(1, zcount):
        source = lax.rem(z + zcount - d, zcount)
        for slot in range(2):
            has = (source == 1) | (source == 2) if slot else (source >= 0)

            @pl.when(has)
            def _():
                z_copy(d, slot).wait_recv()

    def task_grads(rows):
        first = z_in[0, 0, rows, :].astype(F32) + z_in[1, 0, rows, :].astype(F32)
        second = z_in[1, 1, rows, :].astype(F32) + z_in[2, 0, rows, :].astype(F32)
        third = z_in[2, 1, rows, :].astype(F32) + z_in[3, 0, rows, :].astype(F32)
        return first, second, third

    pairs = ((0, 0), (0, 1), (0, 2), (1, 1), (1, 2), (2, 2))
    gram_own[...] = jnp.zeros_like(gram_own)

    def gram_rows(m, carry):
        rows = pl.ds(pl.multiple_of(m * 32, 32), 32)
        grads = task_grads(rows)
        for i, (a, b) in enumerate(pairs):
            product = grads[a] * grads[b]
            gram_own[i] += fold(product)
        return carry

    def fold(product):
        total = product[0:8, 0:128]
        for r in range(4):
            for l in range(4):
                if r or l:
                    total = total + product[8 * r : 8 * r + 8, 128 * l : 128 * l + 128]
        return total

    lax.fori_loop(0, CIN // 32, gram_rows, 0)

    def gc_copy(d):
        return remote(gram_own, gram_ch.at[d - 1], gc_send.at[d - 1], gc_recv.at[d - 1], ch_targets[d - 1])

    for d in range(1, NCH):
        gc_copy(d).start()
    for d in range(1, NCH):
        gc_copy(d).wait()
    gsum[...] = gram_own[...] + gram_ch[0] + gram_ch[1] + gram_ch[2]

    def gp_copy(d):
        return remote(gsum, gram_px.at[d - 1], gp_send.at[d - 1], gp_recv.at[d - 1], pix_targets[d - 1])

    for d in range(1, NPIX):
        gp_copy(d).start()
    for d in range(1, NPIX):
        gp_copy(d).wait()
    entry = {}
    for i, (a, b) in enumerate(pairs):
        total = gsum[i]
        for d in range(NPIX - 1):
            total = total + gram_px[d, i]
        value = jnp.sum(total, axis=0, keepdims=True)
        value = jnp.sum(value, axis=1, keepdims=True)
        entry[(a, b)] = value
        entry[(b, a)] = value
    lengths = [jnp.sqrt(entry[(t, t)] + 1e-12) for t in range(3)]

    def pairing(row_task, col_task):
        return (
            entry[(0, 0)] / lengths[0]
            - entry[(0, col_task)] / lengths[col_task]
            - entry[(row_task, 0)] / lengths[0]
            + entry[(row_task, col_task)] / lengths[col_task]
        )

    right_one = entry[(0, 0)] / lengths[0] - entry[(0, 1)] / lengths[1]
    right_two = entry[(0, 0)] / lengths[0] - entry[(0, 2)] / lengths[2]
    upper_left, upper_right = pairing(1, 1), pairing(1, 2)
    lower_left, lower_right = pairing(2, 1), pairing(2, 2)
    determinant = upper_left * lower_right - upper_right * lower_left
    alpha_one = (right_one * lower_right - right_two * lower_left) / determinant
    alpha_two = (right_two * upper_left - right_one * upper_right) / determinant
    alpha_zero = 1.0 - alpha_one - alpha_two

    for m in range(CIN // 128):
        first, second, third = task_grads(pl.ds(m * 128, 128))
        mixed = alpha_zero * first + alpha_one * second + alpha_two * third
        gz_ref[:, m * 128 : (m + 1) * 128] = jnp.transpose(mixed)

    for d in range(1, NPIX):
        row_copy(d).wait_send()
    for d in range(NPIX):
        b = lax.rem(p + NPIX - d, NPIX)
        x_copy(d, b, c).wait_send()
        ca_copy(d, b, c).wait_send()
        cb_copy(d, b, far).wait_send()
    for zz in range(zcount):

        @pl.when(has_low(p))
        def _():
            y_copy(zz, 0).wait_send()

        @pl.when(has_high(p))
        def _():
            y_copy(zz, 1).wait_send()

    for d in range(1, zcount):
        z_copy(d, 0).wait_send()

        @pl.when(pair_high)
        def _():
            z_copy(d, 1).wait_send()


def heads_backward(dq, xall, w_seg):
    dma = pltpu.SemaphoreType.DMA
    zc = NPIX // 2
    return pl.pallas_call(
        heads_backward_kernel,
        out_shape=(
            jax.ShapeDtypeStruct((SEGS, SEG_ROWS, CIN), F32),
            jax.ShapeDtypeStruct((PX, CIN), F32),
        ),
        in_specs=[whole_vmem()] * 3,
        out_specs=[whole_vmem()] * 2,
        scratch_shapes=[
            pltpu.VMEM((NPIX, NCH, 4, COLS, WIDTH), BF),
            pltpu.VMEM((SEGS, CIN, SEG_ROWS), BF),
            pltpu.VMEM((SEGS, SEG_ROWS, PX), BF),
            pltpu.VMEM((NPIX, 2, CIN, PX), BF),
            pltpu.VMEM((zc, 2, CIN, PX), BF),
            pltpu.VMEM((zc, 2, CIN, PX), BF),
            pltpu.VMEM((zc, 2, CIN, PX), BF),
            pltpu.VMEM((6, 8, 128), F32),
            pltpu.VMEM((NCH - 1, 6, 8, 128), F32),
            pltpu.VMEM((NPIX - 1, 6, 8, 128), F32),
            pltpu.VMEM((6, 8, 128), F32),
            dma((1,)),
            dma((NPIX - 1,)), dma((NPIX - 1,)),
            dma((NPIX,)), dma((NPIX,)), dma((NPIX,)), dma((NPIX,)), dma((NPIX,)), dma((NPIX,)),
            dma((zc, 2)), dma((zc, 2)),
            dma((zc - 1, 2)), dma((zc - 1, 2)),
            dma((NCH - 1,)), dma((NCH - 1,)),
            dma((NPIX - 1,)), dma((NPIX - 1,)),
        ],
        compiler_params=pltpu.CompilerParams(
            collective_id=2, has_side_effects=True, vmem_limit_bytes=VMEM_LIMIT
        ),
        name="heads_backward",
    )(dq, xall, w_seg)


def tap_weights(head_weight, head_rates):
    rates = head_rates.astype(BF)
    pieces = [jnp.transpose(head_weight.astype(BF))[None]]
    for rate_index, step in GROUPS:
        pieces.append(rates[rate_index, 3 * (step + 1) : 3 * (step + 2)])
    taps = jnp.concatenate(pieces, axis=0)
    taps = taps.reshape(TAPS, SEGS, 32, CIN).transpose(1, 0, 2, 3)
    return taps.reshape(SEGS, SEG_ROWS, CIN)


def tap_grads(dw):
    taps = dw.reshape(SEGS, TAPS, 32, CIN).transpose(1, 0, 2, 3).reshape(TAPS, COLS, CIN)
    head = jnp.transpose(taps[0])
    rates = []
    for rate_index in range(3):
        for step in (-1, 0, 1):
            if (rate_index, step) in GROUPS:
                g = GROUPS.index((rate_index, step))
                rates.append(taps[1 + 3 * g : 4 + 3 * g])
            else:
                rates.append(jnp.zeros((3, COLS, CIN), F32))
    return head, jnp.stack(rates).reshape(3, 9, COLS, CIN)


def per_device_rows(
    features,
    valid_mask,
    sem_label,
    depth_target,
    normal_target,
    label_mask,
    w_reduce,
    m_reduce,
    v_reduce,
    w_dilated,
    m_dilated,
    v_dilated,
    w_expand,
    m_expand,
    v_expand,
    head_weight,
    m_head,
    v_head,
    head_rates,
    m_rates,
    v_rates,
    head_proj,
    m_proj,
    v_proj,
    norm_params,
    norm_m,
    norm_v,
    head_small,
    small_m,
    small_v,
):
    rows_per_shard, columns_per_shard, wide_dev = features.shape
    pixels = rows_per_shard * columns_per_shard
    groups = lax.axis_size("ch")
    block_id = lax.axis_index("ch")
    pix_devices = lax.axis_size("pix")
    middle_per_shard = M // groups
    count_all = float(pixels * pix_devices)
    flat_in = features.reshape(pixels, wide_dev)
    mask_flat = valid_mask.reshape(pixels).astype(jnp.float32)
    gains = norm_params[0]
    shifts = norm_params[1]

    def owned(vector, offset, width):
        return lax.dynamic_slice_in_dim(vector, offset + block_id * width, width)

    reduce_w, dilated_w, expand_w = (
        lax.all_gather(w_reduce.astype(jnp.bfloat16), "pix", axis=1, tiled=True),
        lax.all_gather(w_dilated.astype(jnp.bfloat16), "pix", axis=1, tiled=True),
        lax.all_gather(w_expand.astype(jnp.bfloat16), "pix", axis=0, tiled=True),
    )
    reduced = lax.psum_scatter(
        jnp.dot(flat_in, reduce_w, preferred_element_type=jnp.float32),
        "ch",
        scatter_dimension=1,
        tiled=True,
    )
    local_counts = jnp.sum(label_mask.astype(jnp.float32), axis=(1, 2))
    reduced_sum = jnp.sum(reduced, axis=0)
    reduced_sq = jnp.sum(reduced * reduced, axis=0)
    reduced_sum, reduced_sq = lax.psum((reduced_sum, reduced_sq), "pix")
    task_counts = lax.psum(local_counts, "pix")
    task_counts = jnp.maximum(task_counts, 1.0)
    gain_one = owned(gains, 0, middle_per_shard)
    norm_one, hat_one, scale_one = forward_norm(
        reduced, reduced_sum, reduced_sq, count_all, gain_one, owned(shifts, 0, middle_per_shard)
    )
    first = (smooth(norm_one) * mask_flat[:, None]).astype(jnp.bfloat16)
    first_gathered = channel_gather(first).reshape(rows_per_shard, columns_per_shard, M)
    bordered_input = with_halo(first_gathered, (("pix", 0),), DILATION_RATE)
    bordered_input = jnp.pad(bordered_input, ((0, 0), (DILATION_RATE, DILATION_RATE), (0, 0)))
    middle = jnp.zeros((pixels, middle_per_shard), jnp.float32)
    for tap_index in range(9):
        kernel_row, kernel_column = divmod(tap_index, 3)
        sliding_patch = bordered_input[
            kernel_row * DILATION_RATE : kernel_row * DILATION_RATE + rows_per_shard,
            kernel_column * DILATION_RATE : kernel_column * DILATION_RATE + columns_per_shard,
        ].reshape(pixels, M)
        middle = middle + jnp.dot(
            sliding_patch, dilated_w[tap_index], preferred_element_type=jnp.float32
        )
    gain_two = owned(gains, M, middle_per_shard)
    middle_sum, middle_sq = pixel_sums(jnp.sum(middle, axis=0), jnp.sum(middle * middle, axis=0))
    norm_two, hat_two, scale_two = forward_norm(
        middle, middle_sum, middle_sq, count_all, gain_two, owned(shifts, M, middle_per_shard)
    )
    second = smooth(norm_two).astype(jnp.bfloat16)
    second_all = channel_gather(second)
    expanded = jnp.dot(second_all, expand_w, preferred_element_type=jnp.float32)
    gain_three = owned(gains, 2 * M, wide_dev)
    expand_sum, expand_sq = pixel_sums(
        jnp.sum(expanded, axis=0), jnp.sum(expanded * expanded, axis=0)
    )
    norm_three, hat_three, scale_three = forward_norm(
        expanded, expand_sum, expand_sq, count_all, gain_three, owned(shifts, 2 * M, wide_dev)
    )
    summed_in = norm_three + flat_in.astype(jnp.float32)
    shared = smooth(summed_in).astype(jnp.bfloat16)
    branch_bias, proj_bias, sem_w, depth_w, normal_w, sem_b, depth_b, normal_b = unpack_small(
        head_small
    )
    out_weights = (
        sem_w.astype(jnp.bfloat16),
        depth_w.astype(jnp.bfloat16),
        normal_w.astype(jnp.bfloat16),
    )
    own_row = lambda array, axis: lax.dynamic_slice_in_dim(array, block_id, 1, axis=axis)
    w_seg = tap_weights(head_weight, head_rates)
    q_rows, shared_all = heads_forward(shared, w_seg)
    proj_t = lax.all_gather(
        jnp.transpose(head_proj.astype(jnp.bfloat16), (0, 2, 1)), "pix", axis=2, tiled=True
    )
    out_stack = jnp.stack(
        [jnp.pad(weight, ((0, 0), (0, 32 - weight.shape[1]))) for weight in out_weights]
    )
    out_bias = jnp.stack(
        [jnp.pad(bias, (0, 32 - bias.shape[0])) for bias in (sem_b, depth_b, normal_b)], axis=1
    )
    targets = jnp.concatenate([own_row(depth_target, 0), own_row(normal_target, 1)[:, 0]], axis=0)
    pre_grad, proj_grad, out_grad, bias_rows, out_bias_rows = heads_middle(
        q_rows,
        branch_bias.T,
        proj_bias.T,
        proj_t,
        out_stack,
        out_bias,
        own_row(sem_label, 0),
        targets,
        own_row(label_mask, 1)[:, 0].astype(jnp.float32),
        jnp.broadcast_to(task_counts[:, None], (3, columns_per_shard)),
    )
    small_term = pack_small(
        [bias_rows[:4, 0], bias_rows[4, 0]]
        + [out_grad[0, :NCLS].T, out_grad[1, :1].T, out_grad[2, :3].T]
        + [out_bias_rows[0, 0, :NCLS], out_bias_rows[1, 0, :1], out_bias_rows[2, 0, :3]]
    )
    tap_sums, combined = heads_backward(pre_grad, shared_all, w_seg)
    head_shard, rates_shard = tap_grads(tap_sums)
    shared_slope = combined * smooth_slope(summed_in)
    expand_up, gain_three_grad, shift_three_grad = backward_norm(
        shared_slope, hat_three, scale_three, count_all, gain_three
    )
    expand_back = expand_up.astype(jnp.bfloat16)
    expand_grad = contract_first(second_all, expand_back)
    second_back = channel_parts(contract_last(expand_back, expand_w))
    middle_up, gain_two_grad, shift_two_grad = backward_norm(
        second_back * smooth_slope(norm_two), hat_two, scale_two, count_all, gain_two
    )
    middle_gradient = middle_up.astype(jnp.bfloat16)
    dilated_list = []
    for tap_index in range(9):
        kernel_row, kernel_column = divmod(tap_index, 3)
        sliding_patch = bordered_input[
            kernel_row * DILATION_RATE : kernel_row * DILATION_RATE + rows_per_shard,
            kernel_column * DILATION_RATE : kernel_column * DILATION_RATE + columns_per_shard,
        ].reshape(pixels, M)
        dilated_list.append(contract_first(sliding_patch, middle_gradient))
    dilated_grad = jnp.stack(dilated_list)
    canvas_gradient = with_halo(
        middle_gradient.reshape(rows_per_shard, columns_per_shard, middle_per_shard),
        (("pix", 0),),
        DILATION_RATE,
    )
    canvas_gradient = jnp.pad(canvas_gradient, ((0, 0), (DILATION_RATE, DILATION_RATE), (0, 0)))
    first_part = jnp.zeros((pixels, M), jnp.float32)
    for tap_index in range(9):
        kernel_row, kernel_column = divmod(tap_index, 3)
        sliding_patch = canvas_gradient[
            (2 - kernel_row) * DILATION_RATE : (2 - kernel_row) * DILATION_RATE + rows_per_shard,
            (2 - kernel_column) * DILATION_RATE : (2 - kernel_column) * DILATION_RATE
            + columns_per_shard,
        ].reshape(pixels, middle_per_shard)
        first_part = first_part + contract_last(sliding_patch, dilated_w[tap_index])
    first_back = channel_parts(first_part) * mask_flat[:, None] * smooth_slope(norm_one)
    reduce_up, gain_one_grad, shift_one_grad = backward_norm(
        first_back, hat_one, scale_one, count_all, gain_one
    )
    reduce_all = channel_gather(reduce_up.astype(jnp.bfloat16))
    reduce_grad = contract_first(flat_in, reduce_all)
    input_grad = contract_last(reduce_all, reduce_w) + shared_slope
    reduce_shard, dilated_shard, expand_shard, proj_shard = (
        lax.psum_scatter(reduce_grad, "pix", scatter_dimension=1, tiled=True),
        lax.psum_scatter(dilated_grad, "pix", scatter_dimension=1, tiled=True),
        lax.psum_scatter(expand_grad, "pix", scatter_dimension=0, tiled=True),
        lax.psum_scatter(lax.psum(proj_grad, "ch"), "pix", scatter_dimension=1, tiled=True),
    )
    norm_local = jnp.zeros((2, 2 * M + C), jnp.float32)
    for offset, width, gain_grad, shift_grad in (
        (0, middle_per_shard, gain_one_grad, shift_one_grad),
        (M, middle_per_shard, gain_two_grad, shift_two_grad),
        (2 * M, wide_dev, gain_three_grad, shift_three_grad),
    ):
        norm_local = lax.dynamic_update_slice(
            norm_local, jnp.stack([gain_grad, shift_grad]), (0, offset + block_id * width)
        )
    big_local = (
        jnp.sum(reduce_shard * reduce_shard)
        + jnp.sum(dilated_shard * dilated_shard)
        + jnp.sum(expand_shard * expand_shard)
        + jnp.sum(head_shard * head_shard)
        + jnp.sum(rates_shard * rates_shard)
        + jnp.sum(proj_shard * proj_shard) / groups
    )
    big_squares, norm_grad, small_grad = lax.psum(
        (big_local, norm_local / pix_devices, small_term), ("pix", "ch")
    )
    grad_norm = jnp.sqrt(
        big_squares + jnp.sum(norm_grad * norm_grad) + jnp.sum(small_grad * small_grad)
    )
    factor = jnp.minimum(1.0, CLIP_NORM / (grad_norm + 1e-06))
    reduce_new, reduce_first, reduce_second = adam_step(
        w_reduce, m_reduce, v_reduce, reduce_shard * factor, RATE_MATRIX, DECAY
    )
    dilated_new, dilated_first, dilated_second = adam_step(
        w_dilated, m_dilated, v_dilated, dilated_shard * factor, RATE_MATRIX, DECAY
    )
    expand_new, expand_first, expand_second = adam_step(
        w_expand, m_expand, v_expand, expand_shard * factor, RATE_MATRIX, DECAY
    )
    head_new, head_first, head_second = adam_step(
        head_weight, m_head, v_head, head_shard * factor, RATE_MATRIX, DECAY
    )
    rates_new, rates_first, rates_second = adam_step(
        head_rates, m_rates, v_rates, rates_shard * factor, RATE_MATRIX, DECAY
    )
    proj_new, proj_first, proj_second = adam_step(
        head_proj, m_proj, v_proj, proj_shard * factor, RATE_MATRIX, DECAY
    )
    norm_new, norm_first, norm_second = adam_step(
        norm_params, norm_m, norm_v, norm_grad * factor, RATE_SMALL, 0.0
    )
    small_new, small_first, small_second = adam_step(
        head_small, small_m, small_v, small_grad * factor, RATE_SMALL, 0.0
    )
    depth_bias_grad = small_grad[small_grad.shape[0] - 4]
    return (
        shared.reshape(rows_per_shard, columns_per_shard, wide_dev),
        input_grad.reshape(rows_per_shard, columns_per_shard, wide_dev),
        grad_norm,
        reduce_new,
        reduce_first,
        reduce_second,
        reduce_new.astype(jnp.bfloat16),
        dilated_new,
        dilated_first,
        dilated_second,
        dilated_new.astype(jnp.bfloat16),
        expand_new,
        expand_first,
        expand_second,
        expand_new.astype(jnp.bfloat16),
        head_new,
        head_first,
        head_second,
        head_new.astype(jnp.bfloat16),
        rates_new,
        rates_first,
        rates_second,
        rates_new.astype(jnp.bfloat16),
        proj_new,
        proj_first,
        proj_second,
        proj_new.astype(jnp.bfloat16),
        norm_new,
        norm_first,
        norm_second,
        small_new,
        small_first,
        small_second,
        depth_bias_grad,
    )


def per_device(features, *rest):
    sizes = (lax.axis_size("pix"), lax.axis_size("ch"))
    if sizes == (NPIX, NCH) and features.shape == (ROWS, WIDTH, CIN):
        return per_device_rows(features, *rest)
    return per_device_plain(features, *rest)


def solution(mesh):
    placed = (
        P("pix", None, "ch"),
        P("pix", None),
        P("pix", None),
        P("pix", None),
        P(None, "pix", None),
        P(None, "pix", None),
        P("ch", "pix"),
        P("ch", "pix"),
        P("ch", "pix"),
        P(None, "pix", "ch"),
        P(None, "pix", "ch"),
        P(None, "pix", "ch"),
        P("pix", "ch"),
        P("pix", "ch"),
        P("pix", "ch"),
        P("ch", "pix"),
        P("ch", "pix"),
        P("ch", "pix"),
        P(None, None, "pix", "ch"),
        P(None, None, "pix", "ch"),
        P(None, None, "pix", "ch"),
        P(None, "pix", None),
        P(None, "pix", None),
        P(None, "pix", None),
        P(),
        P(),
        P(),
        P(),
        P(),
        P(),
    )
    return jax.shard_map(
        per_device,
        mesh=mesh,
        in_specs=placed,
        out_specs=(
            P("pix", None, "ch"),
            P("pix", None, "ch"),
            P(),
            P("ch", "pix"),
            P("ch", "pix"),
            P("ch", "pix"),
            P("ch", "pix"),
            P(None, "pix", "ch"),
            P(None, "pix", "ch"),
            P(None, "pix", "ch"),
            P(None, "pix", "ch"),
            P("pix", "ch"),
            P("pix", "ch"),
            P("pix", "ch"),
            P("pix", "ch"),
            P("ch", "pix"),
            P("ch", "pix"),
            P("ch", "pix"),
            P("ch", "pix"),
            P(None, None, "pix", "ch"),
            P(None, None, "pix", "ch"),
            P(None, None, "pix", "ch"),
            P(None, None, "pix", "ch"),
            P(None, "pix", None),
            P(None, "pix", None),
            P(None, "pix", None),
            P(None, "pix", None),
            P(),
            P(),
            P(),
            P(),
            P(),
            P(),
            P(),
        ),
        check_vma=False,
    )
```

```python
import jax
import jax.numpy as jnp
from jax import lax
from jax.experimental import pallas as pl
from jax.experimental.pallas import tpu as pltpu
from jax.sharding import PartitionSpec as P

C = 2048
M = 512
HID = 256
NCLS = 19
DILATION_RATE = 4
STEP = 10


EPS_NORM = 1e-05
BETA_ONE = 0.9
BETA_TWO = 0.999
ADAM_EPS = 1e-08
RATE_MATRIX = 0.02
RATE_SMALL = 0.2
DECAY = 0.01
CLIP_NORM = 0.01
aspp_rates = (12, 24, 36)


def shifted(value, axis, steps):
    count = lax.axis_size(axis)
    leading, last = (max(0, -steps), min(count, count - steps))
    return lax.ppermute(value, axis, [(source, source + steps) for source in range(leading, last)])


def with_halo(cells, sides, width):
    for axis, dim in sides:
        count = lax.axis_size(axis)
        ends = count - 1
        head = lax.slice_in_dim(cells, 0, width, axis=dim)
        tail = lax.slice_in_dim(cells, cells.shape[dim] - width, cells.shape[dim], axis=dim)
        cells = jnp.concatenate(
            [
                lax.ppermute(tail, axis, [(i, (i + 1) % count) for i in range(ends)]),
                cells,
                lax.ppermute(head, axis, [((i + 1) % count, i) for i in range(ends)]),
            ],
            axis=dim,
        )
    return cells


def smooth(values):
    return jax.nn.gelu(values, approximate=True)


def smooth_slope(values):
    return jax.vjp(smooth, values)[1](jnp.ones_like(values))[0]


def contract_first(left, right):
    return lax.dot_general(
        left, right, (((0,), (0,)), ((), ())), preferred_element_type=jnp.float32
    )


def contract_last(left, right):
    return lax.dot_general(
        left, right, (((1,), (1,)), ((), ())), preferred_element_type=jnp.float32
    )


def split_tasks(slopes, weight):
    pixels = slopes.shape[0]
    return lax.dot_general(
        slopes.reshape(pixels, 3, -1),
        weight.reshape(weight.shape[0], 3, -1),
        (((2,), (2,)), ((1,), (1,))),
        preferred_element_type=jnp.float32,
    )


def split_tasks_rows(slopes, weight):
    pixels = slopes.shape[0]
    return lax.dot_general(
        slopes.reshape(pixels, 3, -1),
        weight.reshape(3, -1, weight.shape[1]),
        (((2,), (1,)), ((1,), (0,))),
        preferred_element_type=jnp.float32,
    )


def unpack_small(vector):
    lengths = (12 * HID, 3 * HID, HID * NCLS, HID, HID * 3, NCLS, 1, 3)
    pieces = []
    offset = 0
    for length in lengths:
        pieces.append(lax.slice_in_dim(vector, offset, offset + length, axis=0))
        offset = offset + length
    return (
        pieces[0].reshape(4, 3 * HID),
        pieces[1].reshape(3, HID),
        pieces[2].reshape(HID, NCLS),
        pieces[3].reshape(HID, 1),
        pieces[4].reshape(HID, 3),
        pieces[5],
        pieces[6],
        pieces[7],
    )


def pack_small(pieces):
    return jnp.concatenate([piece.reshape(-1) for piece in pieces])


def fetch_rows(grid, step):
    if abs(step) >= lax.axis_size("pix"):
        return jnp.zeros_like(grid)
    return shifted(grid, "pix", -step)


def fetch_grads(grid, step):
    if abs(step) >= lax.axis_size("pix"):
        return jnp.zeros_like(grid)
    return shifted(grid, "pix", -step)


def row_view(grid, offset, fetch):
    height = grid.shape[0]
    lead, rest = divmod(offset, height)
    return fetch(grid, lead)


def column_view(grid, offset):
    width = grid.shape[1]
    reach = abs(offset)
    if reach == 0:
        return grid
    padded_canvas = jnp.pad(grid, ((0, 0), (reach, reach), (0, 0)))
    return padded_canvas[:, reach + offset : reach + offset + width]


def imtl_weights(gram):
    lengths = jnp.sqrt(jnp.diagonal(gram) + 1e-12)

    def pairing(row_task, col_task):
        return (
            gram[0, 0] / lengths[0]
            - gram[0, col_task] / lengths[col_task]
            - gram[row_task, 0] / lengths[0]
            + gram[row_task, col_task] / lengths[col_task]
        )

    right_one = gram[0, 0] / lengths[0] - gram[0, 1] / lengths[1]
    right_two = gram[0, 0] / lengths[0] - gram[0, 2] / lengths[2]
    upper_left = pairing(1, 1)
    upper_right = pairing(1, 2)
    lower_left = pairing(2, 1)
    lower_right = pairing(2, 2)
    determinant = upper_left * lower_right - upper_right * lower_left
    alpha_one = (right_one * lower_right - right_two * lower_left) / determinant
    alpha_two = (right_two * upper_left - right_one * upper_right) / determinant
    return jnp.stack([1.0 - alpha_one - alpha_two, alpha_one, alpha_two])


def adam_step(weight, first, second, grad, rate, decay):
    first_new = BETA_ONE * first + (1.0 - BETA_ONE) * grad
    second_new = BETA_TWO * second + (1.0 - BETA_TWO) * grad * grad
    first_hat = first_new / (1.0 - BETA_ONE**STEP)
    second_hat = second_new / (1.0 - BETA_TWO**STEP)
    weight_new = weight - rate * (first_hat / (jnp.sqrt(second_hat) + ADAM_EPS) + decay * weight)
    return (weight_new, first_new, second_new)


def pixel_sums(first, second):
    return lax.psum((first, second), "pix")


def back_pair(first, second):
    return lax.psum((first, second), "pix")


def channel_gather(piece):
    return lax.all_gather(piece, "ch", axis=1, tiled=True)


def channel_parts(partial_sum):
    return lax.psum_scatter(partial_sum, "ch", scatter_dimension=1, tiled=True)


def forward_norm(inputs, sums, squares, count, gain_row, shift_row):
    mean_row = sums / count
    scale_row = lax.rsqrt(squares / count - mean_row * mean_row + EPS_NORM)
    normed = (inputs - mean_row) * scale_row
    return (normed * gain_row + shift_row, normed, scale_row)


def backward_norm(upstream, normed, scale_row, count, gain_row):
    shift_grad, gain_grad = back_pair(jnp.sum(upstream, axis=0), jnp.sum(upstream * normed, axis=0))
    inner = gain_row * scale_row * (upstream - shift_grad / count - normed * (gain_grad / count))
    return (inner, gain_grad, shift_grad)


def loss_slopes(
    logits, depth_pred, normal_pred, sem_label, depth_target, normal_target, label_mask, counts
):
    masks = label_mask.reshape(3, -1).astype(jnp.float32)
    classes = lax.broadcasted_iota(jnp.int32, (1, NCLS), 1)
    onehot = (sem_label.reshape(-1, 1) == classes).astype(jnp.float32)
    highest = jnp.max(logits, axis=1, keepdims=True)
    raised = jnp.exp(logits - highest)
    probs = raised / jnp.sum(raised, axis=1, keepdims=True)
    sem_slope = masks[0][:, None] * (probs - onehot) / counts[0]
    depth_gap = depth_pred[:, 0] - depth_target.reshape(-1)
    depth_slope = (masks[1] * depth_gap / jnp.sqrt(depth_gap * depth_gap + 1.0) / counts[1])[
        :, None
    ]
    normal_slope = masks[2][:, None] * (normal_pred - normal_target.reshape(3, -1).T) / counts[2]
    return (
        sem_slope.astype(jnp.bfloat16),
        depth_slope.astype(jnp.bfloat16),
        normal_slope.astype(jnp.bfloat16),
    )


def per_device_plain(
    features,
    valid_mask,
    sem_label,
    depth_target,
    normal_target,
    label_mask,
    w_reduce,
    m_reduce,
    v_reduce,
    w_dilated,
    m_dilated,
    v_dilated,
    w_expand,
    m_expand,
    v_expand,
    head_weight,
    m_head,
    v_head,
    head_rates,
    m_rates,
    v_rates,
    head_proj,
    m_proj,
    v_proj,
    norm_params,
    norm_m,
    norm_v,
    head_small,
    small_m,
    small_v,
):
    rows_per_shard, columns_per_shard, wide_dev = features.shape
    pixels = rows_per_shard * columns_per_shard
    groups = lax.axis_size("ch")
    block_id = lax.axis_index("ch")
    pix_devices = lax.axis_size("pix")
    middle_per_shard = M // groups
    count_all = float(pixels * pix_devices)
    flat_in = features.reshape(pixels, wide_dev)
    mask_flat = valid_mask.reshape(pixels).astype(jnp.float32)
    gains = norm_params[0]
    shifts = norm_params[1]

    def owned(vector, offset, width):
        return lax.dynamic_slice_in_dim(vector, offset + block_id * width, width)

    reduce_w, dilated_w, expand_w, heads_w, rates_w, proj_w = (
        lax.all_gather(w_reduce.astype(jnp.bfloat16), "pix", axis=1, tiled=True),
        lax.all_gather(w_dilated.astype(jnp.bfloat16), "pix", axis=1, tiled=True),
        lax.all_gather(w_expand.astype(jnp.bfloat16), "pix", axis=0, tiled=True),
        lax.all_gather(head_weight.astype(jnp.bfloat16), "pix", axis=1, tiled=True),
        lax.all_gather(head_rates.astype(jnp.bfloat16), "pix", axis=2, tiled=True),
        lax.all_gather(head_proj.astype(jnp.bfloat16), "pix", axis=1, tiled=True),
    )
    reduced = lax.psum_scatter(
        jnp.dot(flat_in, reduce_w, preferred_element_type=jnp.float32),
        "ch",
        scatter_dimension=1,
        tiled=True,
    )
    local_counts = jnp.sum(label_mask.astype(jnp.float32), axis=(1, 2))
    reduced_sum = jnp.sum(reduced, axis=0)
    reduced_sq = jnp.sum(reduced * reduced, axis=0)
    reduced_sum, reduced_sq = lax.psum((reduced_sum, reduced_sq), "pix")
    task_counts = lax.psum(local_counts, "pix")
    task_counts = jnp.maximum(task_counts, 1.0)
    gain_one = owned(gains, 0, middle_per_shard)
    norm_one, hat_one, scale_one = forward_norm(
        reduced, reduced_sum, reduced_sq, count_all, gain_one, owned(shifts, 0, middle_per_shard)
    )
    first = (smooth(norm_one) * mask_flat[:, None]).astype(jnp.bfloat16)
    first_gathered = channel_gather(first).reshape(rows_per_shard, columns_per_shard, M)
    bordered_input = with_halo(first_gathered, (("pix", 0),), DILATION_RATE)
    bordered_input = jnp.pad(bordered_input, ((0, 0), (DILATION_RATE, DILATION_RATE), (0, 0)))
    middle = jnp.zeros((pixels, middle_per_shard), jnp.float32)
    for tap_index in range(9):
        kernel_row, kernel_column = divmod(tap_index, 3)
        sliding_patch = bordered_input[
            kernel_row * DILATION_RATE : kernel_row * DILATION_RATE + rows_per_shard,
            kernel_column * DILATION_RATE : kernel_column * DILATION_RATE + columns_per_shard,
        ].reshape(pixels, M)
        middle = middle + jnp.dot(
            sliding_patch, dilated_w[tap_index], preferred_element_type=jnp.float32
        )
    gain_two = owned(gains, M, middle_per_shard)
    middle_sum, middle_sq = pixel_sums(jnp.sum(middle, axis=0), jnp.sum(middle * middle, axis=0))
    norm_two, hat_two, scale_two = forward_norm(
        middle, middle_sum, middle_sq, count_all, gain_two, owned(shifts, M, middle_per_shard)
    )
    second = smooth(norm_two).astype(jnp.bfloat16)
    second_all = channel_gather(second)
    expanded = jnp.dot(second_all, expand_w, preferred_element_type=jnp.float32)
    gain_three = owned(gains, 2 * M, wide_dev)
    expand_sum, expand_sq = pixel_sums(
        jnp.sum(expanded, axis=0), jnp.sum(expanded * expanded, axis=0)
    )
    norm_three, hat_three, scale_three = forward_norm(
        expanded, expand_sum, expand_sq, count_all, gain_three, owned(shifts, 2 * M, wide_dev)
    )
    summed_in = norm_three + flat_in.astype(jnp.float32)
    shared = smooth(summed_in).astype(jnp.bfloat16)
    branch_bias, proj_bias, sem_w, depth_w, normal_w, sem_b, depth_b, normal_b = unpack_small(
        head_small
    )
    out_weights = (
        sem_w.astype(jnp.bfloat16),
        depth_w.astype(jnp.bfloat16),
        normal_w.astype(jnp.bfloat16),
    )
    grid_shared = shared.reshape(rows_per_shard, columns_per_shard, wide_dev)
    row_views = []
    pre_list = [jnp.dot(shared, heads_w, preferred_element_type=jnp.float32)]
    for rate_index, rate in enumerate(aspp_rates):
        views = (
            row_view(grid_shared, -rate, fetch_rows),
            grid_shared,
            row_view(grid_shared, rate, fetch_rows),
        )
        row_views.append(views)
        summed = jnp.zeros((pixels, 3 * HID), jnp.float32)
        for tap_index in range(9):
            kernel_row, kernel_column = divmod(tap_index, 3)
            sliding_patch = column_view(views[kernel_row], (kernel_column - 1) * rate).reshape(
                pixels, wide_dev
            )
            summed = summed + contract_last(sliding_patch, rates_w[rate_index, tap_index])
        pre_list.append(summed)
    pre_parts = jnp.stack(pre_list, axis=1)
    before = lax.psum(pre_parts, "ch") + branch_bias[None]
    hidden = smooth(before).astype(jnp.bfloat16)
    branch_slope = smooth_slope(before).reshape(pixels, 4, 3, HID)
    joined_list = []
    projected_list = []
    top_list = []
    produced = []
    for task_index in range(3):
        joined = hidden[:, :, task_index * HID : (task_index + 1) * HID].reshape(pixels, 4 * HID)
        projected = (
            jnp.dot(joined, proj_w[task_index], preferred_element_type=jnp.float32)
            + proj_bias[task_index]
        )
        top = smooth(projected).astype(jnp.bfloat16)
        produced.append(jnp.dot(top, out_weights[task_index], preferred_element_type=jnp.float32))
        joined_list.append(joined)
        projected_list.append(projected)
        top_list.append(top)
    logits = produced[0] + sem_b
    depth_pred = produced[1] + depth_b
    normal_pred = produced[2] + normal_b
    slopes = loss_slopes(
        logits,
        depth_pred,
        normal_pred,
        sem_label,
        depth_target,
        normal_target,
        label_mask,
        task_counts,
    )
    out_grads = []
    out_bias_grads = []
    proj_grads = []
    proj_bias_grads = []
    joined_backs = []
    for task_index in range(3):
        top_back = contract_last(slopes[task_index], out_weights[task_index])
        proj_back = (top_back * smooth_slope(projected_list[task_index])).astype(jnp.bfloat16)
        out_grads.append(contract_first(top_list[task_index], slopes[task_index]))
        out_bias_grads.append(jnp.sum(slopes[task_index], axis=0, dtype=jnp.float32))
        proj_grads.append(contract_first(joined_list[task_index], proj_back))
        proj_bias_grads.append(jnp.sum(proj_back, axis=0, dtype=jnp.float32))
        joined_backs.append(contract_last(proj_back, proj_w[task_index]).reshape(pixels, 4, HID))
    joined_back = jnp.stack(joined_backs, axis=2)
    pre_grad = (joined_back * branch_slope).astype(jnp.bfloat16).reshape(pixels, 4, 3 * HID)
    small_term = (
        pack_small(
            [jnp.sum(pre_grad, axis=0, dtype=jnp.float32), jnp.stack(proj_bias_grads)]
            + out_grads
            + out_bias_grads
        )
        / groups
    )
    proj_grad = jnp.stack(proj_grads)
    first_branch = pre_grad[:, 0]
    task_sum = split_tasks(first_branch, heads_w)
    rates_list = []
    for rate_index, rate in enumerate(aspp_rates):
        flat_back = pre_grad[:, rate_index + 1]
        rate_back = flat_back.reshape(rows_per_shard, columns_per_shard, 3 * HID)
        back_views = (
            row_view(rate_back, rate, fetch_grads),
            rate_back,
            row_view(rate_back, -rate, fetch_grads),
        )
        for tap_index in range(9):
            kernel_row, kernel_column = divmod(tap_index, 3)
            sliding_patch = column_view(
                row_views[rate_index][kernel_row], (kernel_column - 1) * rate
            ).reshape(pixels, wide_dev)
            rates_list.append(contract_first(flat_back, sliding_patch))
            spread = column_view(back_views[kernel_row], (1 - kernel_column) * rate).reshape(
                pixels, 3 * HID
            )
            task_sum = task_sum + split_tasks_rows(spread, rates_w[rate_index, tap_index])
    rates_grad = jnp.stack(rates_list).reshape(3, 9, 3 * HID, wide_dev)
    task_grads = [task_sum[0], task_sum[1], task_sum[2]]
    head_grad = contract_first(shared, first_branch)
    local_gram = jnp.stack(
        [
            jnp.stack(
                [jnp.sum(task_grads[row_task] * task_grads[col_task]) for col_task in range(3)]
            )
            for row_task in range(3)
        ]
    )
    gram = lax.psum(local_gram, ("pix", "ch"))
    alphas = imtl_weights(gram)
    combined = alphas[0] * task_grads[0] + alphas[1] * task_grads[1] + alphas[2] * task_grads[2]
    shared_slope = combined * smooth_slope(summed_in)
    expand_up, gain_three_grad, shift_three_grad = backward_norm(
        shared_slope, hat_three, scale_three, count_all, gain_three
    )
    expand_back = expand_up.astype(jnp.bfloat16)
    expand_grad = contract_first(second_all, expand_back)
    second_back = channel_parts(contract_last(expand_back, expand_w))
    middle_up, gain_two_grad, shift_two_grad = backward_norm(
        second_back * smooth_slope(norm_two), hat_two, scale_two, count_all, gain_two
    )
    middle_gradient = middle_up.astype(jnp.bfloat16)
    dilated_list = []
    for tap_index in range(9):
        kernel_row, kernel_column = divmod(tap_index, 3)
        sliding_patch = bordered_input[
            kernel_row * DILATION_RATE : kernel_row * DILATION_RATE + rows_per_shard,
            kernel_column * DILATION_RATE : kernel_column * DILATION_RATE + columns_per_shard,
        ].reshape(pixels, M)
        dilated_list.append(contract_first(sliding_patch, middle_gradient))
    dilated_grad = jnp.stack(dilated_list)
    canvas_gradient = with_halo(
        middle_gradient.reshape(rows_per_shard, columns_per_shard, middle_per_shard),
        (("pix", 0),),
        DILATION_RATE,
    )
    canvas_gradient = jnp.pad(canvas_gradient, ((0, 0), (DILATION_RATE, DILATION_RATE), (0, 0)))
    first_part = jnp.zeros((pixels, M), jnp.float32)
    for tap_index in range(9):
        kernel_row, kernel_column = divmod(tap_index, 3)
        sliding_patch = canvas_gradient[
            (2 - kernel_row) * DILATION_RATE : (2 - kernel_row) * DILATION_RATE + rows_per_shard,
            (2 - kernel_column) * DILATION_RATE : (2 - kernel_column) * DILATION_RATE
            + columns_per_shard,
        ].reshape(pixels, middle_per_shard)
        first_part = first_part + contract_last(sliding_patch, dilated_w[tap_index])
    first_back = channel_parts(first_part) * mask_flat[:, None] * smooth_slope(norm_one)
    reduce_up, gain_one_grad, shift_one_grad = backward_norm(
        first_back, hat_one, scale_one, count_all, gain_one
    )
    reduce_all = channel_gather(reduce_up.astype(jnp.bfloat16))
    reduce_grad = contract_first(flat_in, reduce_all)
    input_grad = contract_last(reduce_all, reduce_w) + shared_slope
    reduce_shard, dilated_shard, expand_shard, head_shard, rates_shard, proj_shard = (
        lax.psum_scatter(reduce_grad, "pix", scatter_dimension=1, tiled=True),
        lax.psum_scatter(dilated_grad, "pix", scatter_dimension=1, tiled=True),
        lax.psum_scatter(expand_grad, "pix", scatter_dimension=0, tiled=True),
        lax.psum_scatter(head_grad, "pix", scatter_dimension=1, tiled=True),
        lax.psum_scatter(rates_grad, "pix", scatter_dimension=2, tiled=True),
        lax.psum_scatter(proj_grad, "pix", scatter_dimension=1, tiled=True),
    )
    norm_local = jnp.zeros((2, 2 * M + C), jnp.float32)
    for offset, width, gain_grad, shift_grad in (
        (0, middle_per_shard, gain_one_grad, shift_one_grad),
        (M, middle_per_shard, gain_two_grad, shift_two_grad),
        (2 * M, wide_dev, gain_three_grad, shift_three_grad),
    ):
        norm_local = lax.dynamic_update_slice(
            norm_local, jnp.stack([gain_grad, shift_grad]), (0, offset + block_id * width)
        )
    big_local = (
        jnp.sum(reduce_shard * reduce_shard)
        + jnp.sum(dilated_shard * dilated_shard)
        + jnp.sum(expand_shard * expand_shard)
        + jnp.sum(head_shard * head_shard)
        + jnp.sum(rates_shard * rates_shard)
        + jnp.sum(proj_shard * proj_shard) / groups
    )
    big_squares, norm_grad, small_grad = lax.psum(
        (big_local, norm_local / pix_devices, small_term), ("pix", "ch")
    )
    grad_norm = jnp.sqrt(
        big_squares + jnp.sum(norm_grad * norm_grad) + jnp.sum(small_grad * small_grad)
    )
    factor = jnp.minimum(1.0, CLIP_NORM / (grad_norm + 1e-06))
    reduce_new, reduce_first, reduce_second = adam_step(
        w_reduce, m_reduce, v_reduce, reduce_shard * factor, RATE_MATRIX, DECAY
    )
    dilated_new, dilated_first, dilated_second = adam_step(
        w_dilated, m_dilated, v_dilated, dilated_shard * factor, RATE_MATRIX, DECAY
    )
    expand_new, expand_first, expand_second = adam_step(
        w_expand, m_expand, v_expand, expand_shard * factor, RATE_MATRIX, DECAY
    )
    head_new, head_first, head_second = adam_step(
        head_weight, m_head, v_head, head_shard * factor, RATE_MATRIX, DECAY
    )
    rates_new, rates_first, rates_second = adam_step(
        head_rates, m_rates, v_rates, rates_shard * factor, RATE_MATRIX, DECAY
    )
    proj_new, proj_first, proj_second = adam_step(
        head_proj, m_proj, v_proj, proj_shard * factor, RATE_MATRIX, DECAY
    )
    norm_new, norm_first, norm_second = adam_step(
        norm_params, norm_m, norm_v, norm_grad * factor, RATE_SMALL, 0.0
    )
    small_new, small_first, small_second = adam_step(
        head_small, small_m, small_v, small_grad * factor, RATE_SMALL, 0.0
    )
    depth_bias_grad = small_grad[small_grad.shape[0] - 4]
    return (
        shared.reshape(rows_per_shard, columns_per_shard, wide_dev),
        input_grad.reshape(rows_per_shard, columns_per_shard, wide_dev),
        grad_norm,
        reduce_new,
        reduce_first,
        reduce_second,
        reduce_new.astype(jnp.bfloat16),
        dilated_new,
        dilated_first,
        dilated_second,
        dilated_new.astype(jnp.bfloat16),
        expand_new,
        expand_first,
        expand_second,
        expand_new.astype(jnp.bfloat16),
        head_new,
        head_first,
        head_second,
        head_new.astype(jnp.bfloat16),
        rates_new,
        rates_first,
        rates_second,
        rates_new.astype(jnp.bfloat16),
        proj_new,
        proj_first,
        proj_second,
        proj_new.astype(jnp.bfloat16),
        norm_new,
        norm_first,
        norm_second,
        small_new,
        small_first,
        small_second,
        depth_bias_grad,
    )


MESH = pl.DeviceIdType.MESH
BF = jnp.bfloat16
F32 = jnp.float32
NPIX = 8
NCH = 4
ROWS = 4
WIDTH = 128
PX = ROWS * WIDTH
CIN = C // NCH
COLS = 3 * HID // NPIX
SEGS = COLS // 32
VMEM_LIMIT = 60 * 2**20


def row_groups():
    groups = []
    for rate_index, rate in enumerate(aspp_rates):
        for step in (-1, 0, 1):
            if abs(step) * rate // ROWS < NPIX:
                groups.append((rate_index, step))
    return groups


GROUPS = row_groups()
TAPS = 1 + 3 * len(GROUPS)
SEG_ROWS = TAPS * 32


def whole_vmem():
    return pl.BlockSpec(memory_space=pltpu.VMEM)


def slide(tile, steps):
    lane = lax.broadcasted_iota(jnp.int32, tile.shape, 1)
    if steps == 0:
        return tile
    rolled = pltpu.roll(tile, steps % WIDTH, 1)
    if steps > 0:
        return jnp.where(lane >= steps, rolled, 0.0)
    return jnp.where(lane < WIDTH + steps, rolled, 0.0)


def tanh_parts(values):
    root = 0.7978845608028654
    inner = jnp.tanh(root * (values + 0.044715 * values * values * values))
    return root, inner


def gelu_of(values):
    _, inner = tanh_parts(values)
    return 0.5 * values * (1.0 + inner)


def gelu_slope(values):
    root, inner = tanh_parts(values)
    return 0.5 * (1.0 + inner) + 0.5 * values * (1.0 - inner * inner) * root * (
        1.0 + 3.0 * 0.044715 * values * values
    )


def nt_dot(left, right):
    return lax.dot_general(left, right, (((1,), (1,)), ((), ())), preferred_element_type=F32)


def nn_dot(left, right):
    return lax.dot_general(left, right, (((1,), (0,)), ((), ())), preferred_element_type=F32)


def greet(targets):
    barrier = pltpu.get_barrier_semaphore()
    for target in targets:
        pl.semaphore_signal(barrier, inc=1, device_id=target, device_id_type=MESH)
    pl.semaphore_wait(barrier, len(targets))


def remote(src, dst, send_sem, recv_sem, target):
    return pltpu.make_async_remote_copy(
        src, dst, send_sem, recv_sem, device_id=target, device_id_type=MESH
    )


def place():
    p = lax.axis_index("pix")
    c = lax.axis_index("ch")
    return p, c, p // 2, lax.rem(p, 2), c // 2, lax.rem(c, 2)


def heads_forward_kernel(
    x_ref, w_ref, q_ref, xall_ref,
    acc, y_tmp, core_buf, core_in, x_buf, x_in, row_buf, local_sem,
    zr_send, zl_send, z_recv, y_send, y_recv, core_send, core_recv, x_send, x_recv, row_send, row_recv,
):
    p, c, z, y, x, core = place()
    zcount = NPIX // 2
    up = (2 * lax.rem(z + 1, zcount) + y, c)
    down = (2 * lax.rem(z + zcount - 1, zcount) + y, c)
    other_y = (2 * z + 1 - y, c)
    other_core = (p, 2 * x + 1 - core)
    other_x = (p, 2 * (1 - x) + core)
    row_targets = [(lax.rem(p + d, NPIX), c) for d in range(1, NPIX)]
    greet(row_targets + [other_core, other_x])

    own = pltpu.make_async_copy(x_ref, xall_ref.at[p], local_sem.at[0])
    own.start()

    def to_up(source):
        return remote(xall_ref.at[source], xall_ref.at[source], zr_send.at[source // 2], z_recv.at[source // 2], up)

    def to_down(source):
        return remote(xall_ref.at[source], xall_ref.at[source], zl_send.at[source // 2], z_recv.at[source // 2], down)

    def to_y(source):
        return remote(xall_ref.at[source], xall_ref.at[source], y_send.at[source // 2], y_recv.at[source // 2], other_y)

    def step_of(i):
        near = jnp.where(z == 0, i, jnp.where(z == 3, 3 - i, 0))
        one = jnp.where(i == 0, 1, jnp.where(i == 1, 0, i))
        two = jnp.where(i == 0, 2, jnp.where(i == 1, 3, 3 - i))
        two = jnp.where(i == 2, 1, jnp.where(i == 3, 0, two))
        return jnp.where(z == 1, one, jnp.where(z == 2, two, near))

    acc[...] = jnp.zeros_like(acc)
    own.wait()

    def process(src):
        xb = xall_ref[src]

        def one_seg(s, carry):
            y_tmp[...] = nt_dot(w_ref[s], xb)

            def add_group(dest, branch, first_tap, taps):
                rows = pl.ds(pl.multiple_of(branch * COLS + s * 32, 32), 32)
                for r in range(ROWS):
                    lanes = pl.ds(r * WIDTH, WIDTH)
                    total = acc[dest, rows, lanes]
                    for i, shift in enumerate(taps):
                        tile = y_tmp[pl.ds((first_tap + i) * 32, 32), lanes]
                        total = total + slide(tile, shift)
                    acc[dest, rows, lanes] = total

            add_group(src, 0, 0, (0,))
            for g, (rate_index, step) in enumerate(GROUPS):
                rate = aspp_rates[rate_index]
                dest = src - step * (rate // ROWS)
                shifts = (rate, 0, -rate)
                if step == 0:
                    add_group(dest, rate_index + 1, 1 + 3 * g, shifts)
                else:

                    @pl.when((dest >= 0) & (dest < NPIX))
                    def _():
                        add_group(dest, rate_index + 1, 1 + 3 * g, shifts)

            return carry

        lax.fori_loop(0, SEGS, one_seg, 0)

    def gather_step(i, carry):
        zs = step_of(i)
        mine = 2 * zs + y
        theirs = 2 * zs + 1 - y

        @pl.when(i > 0)
        def _():
            to_up(mine).wait_recv()

        @pl.when((zs <= z) & (z < zcount - 1))
        def _():
            to_up(mine).start()

        @pl.when((zs >= z) & (z > 0))
        def _():
            to_down(mine).start()

        to_y(mine).start()
        process(mine)
        to_y(theirs).wait_recv()
        process(theirs)
        return carry

    lax.fori_loop(0, zcount, gather_step, 0)

    def drain(zs, carry):
        mine = 2 * zs + y

        @pl.when((zs <= z) & (z < zcount - 1))
        def _():
            to_up(mine).wait_send()

        @pl.when((zs >= z) & (z > 0))
        def _():
            to_down(mine).wait_send()

        to_y(mine).wait_send()
        return carry

    lax.fori_loop(0, zcount, drain, 0)

    def lanes_of(ch):
        return pl.ds(pl.multiple_of(ch * WIDTH, WIDTH), WIDTH)

    def core_copy(b):
        return remote(core_buf.at[b], core_in.at[b], core_send.at[b], core_recv.at[b], other_core)

    def x_copy(b):
        return remote(x_buf.at[b], x_in.at[b], x_send.at[b], x_recv.at[b], other_x)

    def row_copy(b, slot):
        return remote(
            row_buf.at[b],
            q_ref.at[:, pl.ds(pl.multiple_of(COLS * p, 32), COLS), :],
            row_send.at[slot],
            row_recv.at[slot],
            (b, c),
        )

    def core_step(d, carry):
        b = lax.rem(p + d, NPIX)
        for xx in range(2):
            core_buf[b, xx] = acc[b, :, lanes_of(2 * xx + 1 - core)].astype(BF)
        core_copy(b).start()
        return carry

    lax.fori_loop(0, NPIX, core_step, 0)

    def x_step(d, carry):
        b = lax.rem(p + d, NPIX)
        core_copy(b).wait_recv()
        x_buf[b] = (acc[b, :, lanes_of(2 * (1 - x) + core)] + core_in[b, 1 - x].astype(F32)).astype(BF)
        x_copy(b).start()
        return carry

    lax.fori_loop(0, NPIX, x_step, 0)

    def finish(b):
        x_copy(b).wait_recv()
        total = acc[b, :, lanes_of(c)] + core_in[b, x].astype(F32) + x_in[b].astype(F32)
        return total.astype(BF).reshape(4, COLS, WIDTH)

    def row_step(d, carry):
        b = lax.rem(p + d, NPIX)
        row_buf[b] = finish(b)
        row_copy(b, d - 1).start()
        return carry

    lax.fori_loop(1, NPIX, row_step, 0)
    q_ref[:, pl.ds(pl.multiple_of(COLS * p, 32), COLS), :] = finish(p)

    def settle(d, carry):
        b = lax.rem(p + d, NPIX)
        row_copy(b, d - 1).wait()
        return carry

    lax.fori_loop(1, NPIX, settle, 0)

    def settle_more(b, carry):
        core_copy(b).wait_send()
        x_copy(b).wait_send()
        return carry

    lax.fori_loop(0, NPIX, settle_more, 0)


def heads_forward(block_out, w_seg):
    dma = pltpu.SemaphoreType.DMA
    zc = NPIX // 2
    return pl.pallas_call(
        heads_forward_kernel,
        out_shape=(
            jax.ShapeDtypeStruct((4, 3 * HID, WIDTH), BF),
            jax.ShapeDtypeStruct((NPIX, PX, CIN), BF),
        ),
        in_specs=[whole_vmem()] * 2,
        out_specs=[whole_vmem()] * 2,
        scratch_shapes=[
            pltpu.VMEM((NPIX, 4 * COLS, PX), F32),
            pltpu.VMEM((SEG_ROWS, PX), F32),
            pltpu.VMEM((NPIX, 2, 4 * COLS, WIDTH), BF),
            pltpu.VMEM((NPIX, 2, 4 * COLS, WIDTH), BF),
            pltpu.VMEM((NPIX, 4 * COLS, WIDTH), BF),
            pltpu.VMEM((NPIX, 4 * COLS, WIDTH), BF),
            pltpu.VMEM((NPIX, 4, COLS, WIDTH), BF),
            dma((1,)),
            dma((zc,)), dma((zc,)), dma((zc,)), dma((zc,)), dma((zc,)),
            dma((NPIX,)), dma((NPIX,)), dma((NPIX,)), dma((NPIX,)),
            dma((NPIX - 1,)), dma((NPIX - 1,)),
        ],
        compiler_params=pltpu.CompilerParams(
            collective_id=1, has_side_effects=True, vmem_limit_bytes=VMEM_LIMIT
        ),
        name="heads_forward",
    )(block_out, w_seg)


def heads_middle_kernel(
    q_ref, bias_ref, pbias_ref, wpt_ref, wot_ref, obias_ref, label_ref, target_ref, mask_ref, count_ref,
    dq_ref, dwp_ref, dwo_ref, rows_ref, obg_ref,
    hid,
):
    ones = jnp.ones((8, WIDTH), BF)
    for k in range(4):
        hid[k] = gelu_of(q_ref[k].astype(F32) + bias_ref[:, k : k + 1]).astype(BF)
    row = lax.broadcasted_iota(jnp.int32, (32, WIDTH), 0)
    for t in range(3):
        cols = slice(t * HID, (t + 1) * HID)
        zt = pbias_ref[:, t : t + 1] + jnp.zeros((HID, WIDTH), F32)
        for k in range(4):
            zt = zt + nn_dot(wpt_ref[t, :, k * HID : (k + 1) * HID], hid[k, cols, :])
        ut = gelu_of(zt).astype(BF)
        out = lax.dot_general(
            wot_ref[t], ut, (((0,), (0,)), ((), ())), preferred_element_type=F32
        ) + obias_ref[:, t : t + 1]
        scale = mask_ref[t : t + 1, :] / count_ref[t : t + 1, :]
        if t == 0:
            live = row < NCLS
            highest = jnp.max(jnp.where(live, out, -1e30), axis=0, keepdims=True)
            raised = jnp.where(live, jnp.exp(jnp.minimum(out - highest, 0.0)), 0.0)
            probs = raised / jnp.sum(raised, axis=0, keepdims=True)
            onehot = (row == label_ref[0:1, :]).astype(F32)
            slope = scale * (probs - onehot)
        elif t == 1:
            gap = out - target_ref[0:1, :]
            slope = jnp.where(row < 1, scale * gap / jnp.sqrt(gap * gap + 1.0), 0.0)
        else:
            target = jnp.zeros((32, WIDTH), F32)
            for i in range(3):
                target = jnp.where(row == i, target_ref[1 + i : 2 + i, :], target)
            slope = jnp.where(row < 3, scale * (out - target), 0.0)
        ot = slope.astype(BF)
        dwo_ref[t] = nt_dot(ot, ut)
        obg_ref[t] = nt_dot(ones, ot)
        dz = (nn_dot(wot_ref[t], ot) * gelu_slope(zt)).astype(BF)
        rows_ref[4, :, cols] = nt_dot(ones, dz)
        for k in range(4):
            part = hid[k, cols, :]
            dwp_ref[t, k * HID : (k + 1) * HID, :] = nt_dot(part, dz)
            dcat = lax.dot_general(
                wpt_ref[t, :, k * HID : (k + 1) * HID], dz, (((0,), (0,)), ((), ())),
                preferred_element_type=F32,
            )
            before = q_ref[k, cols, :].astype(F32) + bias_ref[cols, k : k + 1]
            dq_ref[k, cols, :] = (dcat * gelu_slope(before)).astype(BF)
    for k in range(4):
        rows_ref[k] = nt_dot(ones, dq_ref[k])


def heads_middle(q, bias, pbias, wpt, wot, obias, label, target, mask, count):
    return pl.pallas_call(
        heads_middle_kernel,
        out_shape=(
            jax.ShapeDtypeStruct((4, 3 * HID, WIDTH), BF),
            jax.ShapeDtypeStruct((3, 4 * HID, HID), F32),
            jax.ShapeDtypeStruct((3, 32, HID), F32),
            jax.ShapeDtypeStruct((5, 8, 3 * HID), F32),
            jax.ShapeDtypeStruct((3, 8, 32), F32),
        ),
        in_specs=[whole_vmem()] * 10,
        out_specs=[whole_vmem()] * 5,
        scratch_shapes=[pltpu.VMEM((4, 3 * HID, WIDTH), BF)],
        compiler_params=pltpu.CompilerParams(vmem_limit_bytes=VMEM_LIMIT),
        name="heads_middle",
    )(q, bias, pbias, wpt, wot, obias, label, target, mask, count)


def fold(values):
    rows, lanes = values.shape
    total = values[0:8, 0:128]
    for r in range(rows // 8):
        for l in range(lanes // 128):
            if r or l:
                total = total + values[8 * r : 8 * r + 8, 128 * l : 128 * l + 128]
    return total


def low_task(zplane):
    return (2 * zplane * COLS) // HID


def heads_backward_kernel(
    dq_ref, xall_ref, w_ref, dw_ref, gz_ref, square_ref,
    dq_all, wt, dcol, parts, y_in, z_buf, z_in, gram_own, gram_ch, gram_px, gsum,
    local_sem, row_send, row_recv, x_send, x_recv, ca_send, ca_recv, cb_send, cb_recv,
    y_send, y_recv, z_send, z_recv, gc_send, gc_recv, gp_send, gp_recv,
):
    p, c, z, y, x, core = place()
    zcount = NPIX // 2
    other_y = (2 * z + 1 - y, c)
    other_core = (p, 2 * x + 1 - core)
    other_x = (p, 2 * (1 - x) + core)
    pix_targets = [(lax.rem(p + d, NPIX), c) for d in range(1, NPIX)]
    ch_targets = [(p, lax.rem(c + d, NCH)) for d in range(1, NCH)]
    greet(pix_targets + ch_targets)

    def cols_of(b):
        return pl.ds(pl.multiple_of(COLS * b, 32), COLS)

    def row_copy(d):
        b = lax.rem(p + d, NPIX)
        return remote(dq_ref.at[:, cols_of(b), :], dq_all.at[p, c], row_send.at[d - 1], row_recv.at[d - 1], (b, c))

    for d in range(1, NPIX):
        row_copy(d).start()
    own = pltpu.make_async_copy(dq_ref.at[:, cols_of(p), :], dq_all.at[p, c], local_sem.at[0])
    own.start()
    for s in range(SEGS):
        wt[s] = jnp.transpose(w_ref[s].astype(F32)).astype(BF)
    dw_ref[...] = jnp.zeros_like(dw_ref)
    own.wait()

    def x_copy(d, b, ch):
        return remote(dq_all.at[b, ch], dq_all.at[b, ch], x_send.at[d], x_recv.at[d], other_x)

    def ca_copy(d, b, ch):
        return remote(dq_all.at[b, ch], dq_all.at[b, ch], ca_send.at[d], ca_recv.at[d], other_core)

    def cb_copy(d, b, ch):
        return remote(dq_all.at[b, ch], dq_all.at[b, ch], cb_send.at[d], cb_recv.at[d], other_core)

    far = 2 * (1 - x) + core
    for d in range(NPIX):
        b = lax.rem(p + NPIX - d, NPIX)
        if d > 0:
            row_copy(d).wait_recv()
        x_copy(d, b, c).start()
        ca_copy(d, b, c).start()
    for d in range(NPIX):
        b = lax.rem(p + NPIX - d, NPIX)
        x_copy(d, b, far).wait_recv()
        cb_copy(d, b, far).start()
    for d in range(NPIX):
        b = lax.rem(p + NPIX - d, NPIX)
        ca_copy(d, b, 2 * x + 1 - core).wait_recv()
        cb_copy(d, b, 2 * (1 - x) + 1 - core).wait_recv()

    def task_of(pixel_device, s):
        return (SEGS * pixel_device + s) // (HID // 32)

    in_low = [task_of(p, s) == low_task(z) for s in range(SEGS)]
    other_p = 2 * z + 1 - y

    def has_low(device):
        return task_of(device, 0) == low_task(z)

    def has_high(device):
        return task_of(device, SEGS - 1) != low_task(z)

    def y_copy(zz, slot):
        return remote(
            parts.at[2 * zz + 1 - y, slot], y_in.at[zz, slot],
            y_send.at[zz, slot], y_recv.at[zz, slot], other_y,
        )

    def block_step(i, carry):
        zz = lax.rem(i, zcount)
        b = jnp.where(i < zcount, 2 * zz + 1 - y, 2 * zz + y)

        def fill(source, branch, first_tap, shifts):
            for r in range(ROWS):
                lanes = pl.ds(r * WIDTH, WIDTH)
                tile = dq_all[source, r, branch].astype(F32)
                for t, shift in enumerate(shifts):
                    moved = slide(tile, shift).astype(BF)
                    for s in range(SEGS):
                        dcol[s, pl.ds((first_tap + t) * 32, 32), lanes] = moved[s * 32 : (s + 1) * 32]

        fill(b, 0, 0, (0,))
        for g, (rate_index, step) in enumerate(GROUPS):
            rate = aspp_rates[rate_index]
            source = b - step * (rate // ROWS)
            shifts = (-rate, 0, rate)
            if step == 0:
                fill(source, rate_index + 1, 1 + 3 * g, shifts)
            else:
                inside = (source >= 0) & (source < NPIX)

                @pl.when(inside)
                def _():
                    fill(source, rate_index + 1, 1 + 3 * g, shifts)

                @pl.when(jnp.logical_not(inside))
                def _():
                    for s in range(SEGS):
                        dcol[s, pl.ds((1 + 3 * g) * 32, 96), :] = jnp.zeros((96, PX), BF)

        def product_rows(m, inner):
            rows = pl.ds(pl.multiple_of(m * 128, 128), 128)
            low = jnp.zeros((128, PX), F32)
            high = jnp.zeros((128, PX), F32)
            for s in range(SEGS):
                value = nn_dot(wt[s, rows, :], dcol[s])
                low = low + jnp.where(in_low[s], value, 0.0)
                high = high + jnp.where(in_low[s], 0.0, value)
            parts[b, 0, rows, :] = low.astype(BF)
            parts[b, 1, rows, :] = high.astype(BF)
            return inner

        lax.fori_loop(0, CIN // 128, product_rows, 0)

        @pl.when((i < zcount) & has_low(p))
        def _():
            y_copy(zz, 0).start()

        @pl.when((i < zcount) & has_high(p))
        def _():
            y_copy(zz, 1).start()

        def weight_rows(m, inner):
            s = m // 2
            rows = pl.ds(pl.multiple_of(lax.rem(m, 2) * (SEG_ROWS // 2), 32), SEG_ROWS // 2)
            dw_ref[s, rows, :] += nn_dot(dcol[s, rows, :], xall_ref[b])
            return inner

        lax.fori_loop(0, 2 * SEGS, weight_rows, 0)
        return carry

    lax.fori_loop(0, NPIX, block_step, 0)

    square_ref[...] = jnp.zeros_like(square_ref)

    def square_rows(m, carry):
        s = m // TAPS
        part = dw_ref[s, pl.ds(pl.multiple_of(lax.rem(m, TAPS) * 32, 32), 32), :]
        square_ref[...] += fold(part * part)
        return carry

    def z_copy(d, slot):
        zz = lax.rem(z + d, zcount)
        return remote(
            z_buf.at[zz, slot], z_in.at[z, slot],
            z_send.at[d - 1, slot], z_recv.at[d - 1, slot], (2 * zz + y, c),
        )

    pair_high = (z == 1) | (z == 2)
    for d in (1, 2, 3, 0):
        zz = lax.rem(z + d, zcount)
        for slot in range(2):
            theirs = has_low(other_p) if slot == 0 else has_high(other_p)
            there = pair_high if slot else (z >= 0)

            @pl.when(theirs)
            def _():
                y_copy(zz, slot).wait_recv()
                z_buf[zz, slot] = (
                    parts[2 * zz + y, slot].astype(F32) + y_in[zz, slot].astype(F32)
                ).astype(BF)

            @pl.when(jnp.logical_not(theirs))
            def _():
                z_buf[zz, slot] = parts[2 * zz + y, slot]

            if d > 0:

                @pl.when(there)
                def _():
                    z_copy(d, slot).start()

    lax.fori_loop(0, SEGS * TAPS, square_rows, 0)
    for slot in range(2):
        z_in[z, slot] = z_buf[z, slot]
    for d in range(1, zcount):
        source = lax.rem(z + zcount - d, zcount)
        for slot in range(2):
            has = (source == 1) | (source == 2) if slot else (source >= 0)

            @pl.when(has)
            def _():
                z_copy(d, slot).wait_recv()

    def task_grads(rows):
        first = z_in[0, 0, rows, :].astype(F32) + z_in[1, 0, rows, :].astype(F32)
        second = z_in[1, 1, rows, :].astype(F32) + z_in[2, 0, rows, :].astype(F32)
        third = z_in[2, 1, rows, :].astype(F32) + z_in[3, 0, rows, :].astype(F32)
        return first, second, third

    pairs = ((0, 0), (0, 1), (0, 2), (1, 1), (1, 2), (2, 2))
    gram_own[...] = jnp.zeros_like(gram_own)

    def gram_rows(m, carry):
        rows = pl.ds(pl.multiple_of(m * 32, 32), 32)
        grads = task_grads(rows)
        for i, (a, b) in enumerate(pairs):
            product = grads[a] * grads[b]
            gram_own[i] += fold(product)
        return carry

    lax.fori_loop(0, CIN // 32, gram_rows, 0)

    def gc_copy(d):
        return remote(gram_own, gram_ch.at[d - 1], gc_send.at[d - 1], gc_recv.at[d - 1], ch_targets[d - 1])

    for d in range(1, NCH):
        gc_copy(d).start()
    for d in range(1, NCH):
        gc_copy(d).wait()
    gsum[...] = gram_own[...] + gram_ch[0] + gram_ch[1] + gram_ch[2]

    def gp_copy(d):
        return remote(gsum, gram_px.at[d - 1], gp_send.at[d - 1], gp_recv.at[d - 1], pix_targets[d - 1])

    for d in range(1, NPIX):
        gp_copy(d).start()
    for d in range(1, NPIX):
        gp_copy(d).wait()
    entry = {}
    for i, (a, b) in enumerate(pairs):
        total = gsum[i]
        for d in range(NPIX - 1):
            total = total + gram_px[d, i]
        value = jnp.sum(total, axis=0, keepdims=True)
        value = jnp.sum(value, axis=1, keepdims=True)
        entry[(a, b)] = value
        entry[(b, a)] = value
    lengths = [jnp.sqrt(entry[(t, t)] + 1e-12) for t in range(3)]

    def pairing(row_task, col_task):
        return (
            entry[(0, 0)] / lengths[0]
            - entry[(0, col_task)] / lengths[col_task]
            - entry[(row_task, 0)] / lengths[0]
            + entry[(row_task, col_task)] / lengths[col_task]
        )

    right_one = entry[(0, 0)] / lengths[0] - entry[(0, 1)] / lengths[1]
    right_two = entry[(0, 0)] / lengths[0] - entry[(0, 2)] / lengths[2]
    upper_left, upper_right = pairing(1, 1), pairing(1, 2)
    lower_left, lower_right = pairing(2, 1), pairing(2, 2)
    determinant = upper_left * lower_right - upper_right * lower_left
    alpha_one = (right_one * lower_right - right_two * lower_left) / determinant
    alpha_two = (right_two * upper_left - right_one * upper_right) / determinant
    alpha_zero = 1.0 - alpha_one - alpha_two

    for m in range(CIN // 128):
        first, second, third = task_grads(pl.ds(m * 128, 128))
        mixed = alpha_zero * first + alpha_one * second + alpha_two * third
        gz_ref[:, m * 128 : (m + 1) * 128] = jnp.transpose(mixed)

    for d in range(1, NPIX):
        row_copy(d).wait_send()
    for d in range(NPIX):
        b = lax.rem(p + NPIX - d, NPIX)
        x_copy(d, b, c).wait_send()
        ca_copy(d, b, c).wait_send()
        cb_copy(d, b, far).wait_send()
    for zz in range(zcount):

        @pl.when(has_low(p))
        def _():
            y_copy(zz, 0).wait_send()

        @pl.when(has_high(p))
        def _():
            y_copy(zz, 1).wait_send()

    for d in range(1, zcount):
        z_copy(d, 0).wait_send()

        @pl.when(pair_high)
        def _():
            z_copy(d, 1).wait_send()


def heads_backward(dq, xall, w_seg):
    dma = pltpu.SemaphoreType.DMA
    zc = NPIX // 2
    return pl.pallas_call(
        heads_backward_kernel,
        out_shape=(
            jax.ShapeDtypeStruct((SEGS, SEG_ROWS, CIN), F32),
            jax.ShapeDtypeStruct((PX, CIN), F32),
            jax.ShapeDtypeStruct((8, 128), F32),
        ),
        in_specs=[whole_vmem()] * 3,
        out_specs=[whole_vmem()] * 3,
        scratch_shapes=[
            pltpu.VMEM((NPIX, NCH, 4, COLS, WIDTH), BF),
            pltpu.VMEM((SEGS, CIN, SEG_ROWS), BF),
            pltpu.VMEM((SEGS, SEG_ROWS, PX), BF),
            pltpu.VMEM((NPIX, 2, CIN, PX), BF),
            pltpu.VMEM((zc, 2, CIN, PX), BF),
            pltpu.VMEM((zc, 2, CIN, PX), BF),
            pltpu.VMEM((zc, 2, CIN, PX), BF),
            pltpu.VMEM((6, 8, 128), F32),
            pltpu.VMEM((NCH - 1, 6, 8, 128), F32),
            pltpu.VMEM((NPIX - 1, 6, 8, 128), F32),
            pltpu.VMEM((6, 8, 128), F32),
            dma((1,)),
            dma((NPIX - 1,)), dma((NPIX - 1,)),
            dma((NPIX,)), dma((NPIX,)), dma((NPIX,)), dma((NPIX,)), dma((NPIX,)), dma((NPIX,)),
            dma((zc, 2)), dma((zc, 2)),
            dma((zc - 1, 2)), dma((zc - 1, 2)),
            dma((NCH - 1,)), dma((NCH - 1,)),
            dma((NPIX - 1,)), dma((NPIX - 1,)),
        ],
        compiler_params=pltpu.CompilerParams(
            collective_id=2, has_side_effects=True, vmem_limit_bytes=VMEM_LIMIT
        ),
        name="heads_backward",
    )(dq, xall, w_seg)


def tap_weights(head_weight, head_rates):
    rates = head_rates.astype(BF)
    pieces = [jnp.transpose(head_weight.astype(BF))[None]]
    for rate_index, step in GROUPS:
        pieces.append(rates[rate_index, 3 * (step + 1) : 3 * (step + 2)])
    taps = jnp.concatenate(pieces, axis=0)
    taps = taps.reshape(TAPS, SEGS, 32, CIN).transpose(1, 0, 2, 3)
    return taps.reshape(SEGS, SEG_ROWS, CIN)


def tap_grads(dw):
    taps = dw.reshape(SEGS, TAPS, 32, CIN).transpose(1, 0, 2, 3).reshape(TAPS, COLS, CIN)
    head = jnp.transpose(taps[0])
    rates = []
    for rate_index in range(3):
        for step in (-1, 0, 1):
            if (rate_index, step) in GROUPS:
                g = GROUPS.index((rate_index, step))
                rates.append(taps[1 + 3 * g : 4 + 3 * g])
            else:
                rates.append(jnp.zeros((3, COLS, CIN), F32))
    return head, jnp.stack(rates).reshape(3, 9, COLS, CIN)


MID = M // NCH
WPART = M // NPIX
TAP_LANES = 9 * MID
W_REDUCE = slice(0, CIN)
W_DILATED = slice(CIN, CIN + TAP_LANES)
W_EXPAND = slice(CIN + TAP_LANES, 2 * CIN + TAP_LANES)
W_LANES = 2 * CIN + TAP_LANES
SMALL_ROWS = 80


def slide_rows(tile, steps):
    if steps == 0:
        return tile
    line = lax.broadcasted_iota(jnp.int32, (WIDTH, tile.shape[1]), 0)
    keep = line >= steps if steps > 0 else line < WIDTH + steps
    pieces = []
    for r in range(ROWS):
        rolled = pltpu.roll(tile[r * WIDTH : (r + 1) * WIDTH], steps % WIDTH, 0)
        pieces.append(jnp.where(keep, rolled, 0.0))
    return jnp.concatenate(pieces, axis=0)


def column_sums(values):
    return jnp.sum(values, axis=0, keepdims=True)


def pix_copies(inbox, send_sem, recv_sem):
    p, c = lax.axis_index("pix"), lax.axis_index("ch")
    return [
        remote(inbox.at[p], inbox.at[p], send_sem.at[d - 1], recv_sem.at[d - 1], (lax.rem(p + d, NPIX), c))
        for d in range(1, NPIX)
    ]


def ch_copies(source, inbox, send_sem, recv_sem):
    p, c = lax.axis_index("pix"), lax.axis_index("ch")
    copies = []
    for d in range(1, NCH):
        other = lax.rem(c + d, NCH)
        copies.append(remote(source(other), inbox.at[c], send_sem.at[d - 1], recv_sem.at[d - 1], (p, other)))
    return copies


def start_all(copies):
    for copy in copies:
        copy.start()


def wait_all(copies):
    for copy in copies:
        copy.wait()


def add_up(inbox):
    total = inbox[0]
    for i in range(1, inbox.shape[0]):
        total = total + inbox[i]
    return total


def block_forward_kernel(
    x_ref, mask_ref, w_ref, proj_ref, narrow_ref, wide_ref,
    out_ref, hat_one_ref, hat_two_ref, hat_three_ref, wall_ref, first_ref, second_ref, stats_ref, stats_wide_ref, wpt_ref,
    work, ch_buf, ch_in, halo_buf, halo_in, stat_one, stat_two, stat_three,
    local_sem, wz_send, wz_recv, wy_send, wy_recv, c_send, c_recv, s_send, s_recv, h_send, h_recv,
):
    p, c, z, y, x, core = place()
    zcount = NPIX // 2
    other_y = (2 * z + 1 - y, c)
    pix_targets = [(lax.rem(p + d, NPIX), c) for d in range(1, NPIX)]
    ch_targets = [(p, lax.rem(c + d, NCH)) for d in range(1, NCH)]
    greet(pix_targets + ch_targets)
    parts = (pl.ds(0, CIN), pl.ds(CIN, TAP_LANES), pl.ds(CIN + TAP_LANES, CIN))

    def shard(part):
        return w_ref.at[:, parts[part]] if part < 3 else proj_ref

    def spot(part, source):
        if part < 3:
            return wall_ref.at[source, :, parts[part]]
        return wpt_ref.at[:, :, pl.ds(pl.multiple_of(source * 128, 128), 128)]

    def wz_copy(part, d):
        target = (2 * lax.rem(z + d, zcount) + y, c)
        return remote(
            shard(part), spot(part, p),
            wz_send.at[part, d - 1], wz_recv.at[part, d - 1], target,
        )

    def wy_copy(part, d):
        source = 2 * lax.rem(z + zcount - d, zcount) + y
        src = shard(part) if d == 0 else spot(part, source)
        return remote(
            src, spot(part, source), wy_send.at[part, d], wy_recv.at[part, d], other_y
        )

    for part in range(4):
        wy_copy(part, 0).start()
        for d in range(1, zcount):
            wz_copy(part, d).start()
    own = pltpu.make_async_copy(w_ref, wall_ref.at[p], local_sem.at[0])
    own.start()
    own_proj = pltpu.make_async_copy(proj_ref, spot(3, p), local_sem.at[1])
    own_proj.start()
    own.wait()
    own_proj.wait()

    def forward_part(part):
        for d in range(1, zcount):
            wz_copy(part, d).wait_recv()
            wy_copy(part, d).start()

    def receive_part(part):
        for d in range(zcount):
            wy_copy(part, d).wait_recv()

    def weights(lanes):
        return wall_ref[:, :, lanes].reshape(M, lanes.stop - lanes.start)

    def stat_round(index, inbox, values):
        if index > 0:
            inbox[p] = jnp.zeros_like(inbox[p])
        inbox[p, 0:1, :] = column_sums(values)
        inbox[p, 1:2, :] = column_sums(values * values)
        copies = pix_copies(inbox, s_send.at[index], s_recv.at[index])
        start_all(copies)
        wait_all(copies)
        return add_up(inbox)

    count_all = float(NPIX * PX)

    def norm_of(values, sums, gain, shift):
        mean = sums[0:1] / count_all
        scale = lax.rsqrt(sums[1:2] / count_all - mean * mean + EPS_NORM)
        hat = (values - mean) * scale
        return hat, hat * gain + shift, scale

    forward_part(0)
    receive_part(0)
    for m in range(NCH):
        wanted = wall_ref[2 * m : 2 * m + 2, :, W_REDUCE].reshape(MID, CIN)
        value = nt_dot(x_ref[...], wanted)
        ch_buf[0, m] = value.astype(BF)

        @pl.when(m == c)
        def _():
            work[...] = value

    reduce_copies = ch_copies(lambda other: ch_buf.at[0, other], ch_in, c_send.at[0], c_recv.at[0])
    start_all(reduce_copies)
    wait_all(reduce_copies)
    reduced = work[...]
    for d in range(1, NCH):
        reduced = reduced + ch_in[lax.rem(c + d, NCH)].astype(F32)
    stat_one[p] = jnp.zeros((8, MID), F32)
    stat_one[p, 2:3, :] = narrow_ref[4:5, :]
    sums = stat_round(0, stat_one, reduced)
    hat, normed, scale = norm_of(reduced, sums, narrow_ref[0:1, :], narrow_ref[1:2, :])
    hat_one_ref[...] = hat
    stats_ref[...] = jnp.zeros_like(stats_ref)
    stats_ref[0:1, :] = scale
    stats_ref[2:3, :] = jnp.maximum(sums[2:3], 1.0)

    def own_lanes():
        return pl.ds(pl.multiple_of(c * MID, MID), MID)

    def gather_copies(ref, index):
        copies = []
        for d in range(1, NCH):
            copies.append(
                remote(
                    ref.at[:, own_lanes()], ref.at[:, own_lanes()],
                    c_send.at[index, d - 1], c_recv.at[index, d - 1], ch_targets[d - 1],
                )
            )
        return copies

    first_ref[:, own_lanes()] = (gelu_of(normed) * mask_ref[...]).astype(BF)
    copies = gather_copies(first_ref, 1)
    start_all(copies)
    forward_part(1)
    wait_all(copies)
    receive_part(1)

    def row_part(step):
        total = jnp.zeros((PX, MID), F32)
        for col in range(3):
            tap = 3 * (step + 1) + col
            lanes = slice(CIN + tap * MID, CIN + (tap + 1) * MID)
            total = total + slide_rows(nn_dot(first_ref[...], weights(lanes)), -DILATION_RATE * (col - 1))
        return total

    def halo_copy(side):
        target = (p - 1, c) if side == 0 else (p + 1, c)
        return remote(halo_buf.at[side], halo_in.at[side], h_send.at[side], h_recv.at[side], target)

    halo_buf[0] = row_part(1).astype(BF)

    @pl.when(p > 0)
    def _():
        halo_copy(0).start()

    halo_buf[1] = row_part(-1).astype(BF)

    @pl.when(p < NPIX - 1)
    def _():
        halo_copy(1).start()

    work[...] = row_part(0)

    @pl.when(p < NPIX - 1)
    def _():
        halo_copy(0).wait_recv()
        work[...] += halo_in[0].astype(F32)

    @pl.when(p > 0)
    def _():
        halo_copy(1).wait_recv()
        work[...] += halo_in[1].astype(F32)

    forward_part(2)
    middle = work[...]
    sums = stat_round(1, stat_two, middle)
    hat, normed, scale = norm_of(middle, sums, narrow_ref[2:3, :], narrow_ref[3:4, :])
    hat_two_ref[...] = hat
    stats_ref[1:2, :] = scale
    second_ref[:, own_lanes()] = gelu_of(normed).astype(BF)
    copies = gather_copies(second_ref, 2)
    start_all(copies)
    wait_all(copies)

    receive_part(2)
    hat_three_ref[...] = nn_dot(second_ref[...], weights(W_EXPAND))
    expanded = hat_three_ref[...]
    forward_part(3)
    sums = stat_round(2, stat_three, expanded)
    hat, normed, scale = norm_of(expanded, sums, wide_ref[0:1, :], wide_ref[1:2, :])
    hat_three_ref[...] = hat
    stats_wide_ref[...] = jnp.broadcast_to(scale, stats_wide_ref.shape)
    out_ref[...] = gelu_of(normed + x_ref[...].astype(F32)).astype(BF)
    receive_part(3)

    for part in range(4):
        for d in range(zcount):
            wy_copy(part, d).wait_send()
        for d in range(1, zcount):
            wz_copy(part, d).wait_send()

    @pl.when(p > 0)
    def _():
        halo_copy(0).wait_send()

    @pl.when(p < NPIX - 1)
    def _():
        halo_copy(1).wait_send()


def block_forward(flat_in, mask, w_shard, proj_shard, narrow, wide):
    dma = pltpu.SemaphoreType.DMA
    zc = NPIX // 2
    shape = jax.ShapeDtypeStruct
    return pl.pallas_call(
        block_forward_kernel,
        out_shape=(
            shape((PX, CIN), BF),
            shape((PX, MID), F32),
            shape((PX, MID), F32),
            shape((PX, CIN), F32),
            shape((NPIX, WPART, W_LANES), BF),
            shape((PX, M), BF),
            shape((PX, M), BF),
            shape((8, MID), F32),
            shape((8, CIN), F32),
            shape((3, HID, 4 * HID), BF),
        ),
        in_specs=[whole_vmem()] * 6,
        out_specs=[whole_vmem()] * 10,
        scratch_shapes=[
            pltpu.VMEM((PX, MID), F32),
            pltpu.VMEM((1, NCH, PX, MID), BF),
            pltpu.VMEM((NCH, PX, MID), BF),
            pltpu.VMEM((2, PX, MID), BF),
            pltpu.VMEM((2, PX, MID), BF),
            pltpu.VMEM((NPIX, 8, MID), F32),
            pltpu.VMEM((NPIX, 8, MID), F32),
            pltpu.VMEM((NPIX, 8, CIN), F32),
            dma((2,)),
            dma((4, zc - 1)), dma((4, zc - 1)), dma((4, zc)), dma((4, zc)),
            dma((3, NCH - 1)), dma((3, NCH - 1)),
            dma((3, NPIX - 1)), dma((3, NPIX - 1)),
            dma((2,)), dma((2,)),
        ],
        compiler_params=pltpu.CompilerParams(
            collective_id=0, has_side_effects=True, vmem_limit_bytes=VMEM_LIMIT
        ),
        name="block_forward",
    )(flat_in, mask, w_shard, proj_shard, narrow, wide)


def block_backward_kernel(
    gz_ref, x_ref, mask_ref, wall_ref, hat_one_ref, hat_two_ref, hat_three_ref, first_ref, second_ref,
    narrow_ref, wide_ref, stats_ref, stats_wide_ref, dwp_ref, small_ref, square_ref,
    ingrad_ref, wgrad_ref, pgrad_ref, sgrad_ref, ngrad_ref, ngrad_wide_ref, total_ref,
    ds, ds_low, turned, ch_buf, ch_in, halo_in, taps, back_t, stat_three, stat_two, stat_one,
    we_buf, we_in, wd_buf, wd_in, wr_buf, wr_in, pc_buf, pc_in, pr_buf, pr_in, pg_in,
    small_ch, small_px, sq_ch, sq_px, norm_in, norm_wide_in,
    c_send, c_recv, s_send, s_recv, h_send, h_recv, g_send, g_recv,
    pc_send, pc_recv, pg_send, pg_recv, t_send, t_recv, u_send, u_recv, n_send, n_recv,
):
    p, c, z, y, x, core = place()
    pix_targets = [(lax.rem(p + d, NPIX), c) for d in range(1, NPIX)]
    ch_targets = [(p, lax.rem(c + d, NCH)) for d in range(1, NCH)]
    greet(pix_targets + ch_targets)
    count_all = float(NPIX * PX)

    def weights(lanes):
        return wall_ref[:, :, lanes].reshape(M, lanes.stop - lanes.start)

    def own_lanes():
        return pl.ds(pl.multiple_of(c * MID, MID), MID)

    def stat_round(index, inbox, upstream, hat):
        inbox[p] = jnp.zeros_like(inbox[p])
        inbox[p, 0:1, :] = column_sums(upstream)
        inbox[p, 1:2, :] = column_sums(upstream * hat)
        copies = pix_copies(inbox, s_send.at[index], s_recv.at[index])
        start_all(copies)
        return copies

    def stat_end(copies, inbox):
        wait_all(copies)
        return add_up(inbox)

    def norm_back(upstream, hat, sums, gain, scale):
        return gain * scale * (upstream - sums[0:1] / count_all - hat * (sums[1:2] / count_all))

    def own_ch_copies(ref, inbox_index):
        copies = []
        for d in range(1, NCH):
            copies.append(
                remote(ref.at[c], ref.at[c], n_send.at[inbox_index, d - 1], n_recv.at[inbox_index, d - 1], ch_targets[d - 1])
            )
        return copies

    small_ch[c] = small_ref[...]
    small_copies = own_ch_copies(small_ch, 0)
    start_all(small_copies)

    for other in range(NCH):
        for t in range(3):
            for b in range(NPIX):
                start = b * 128 + other * 32
                pc_buf[other, t, b] = dwp_ref[t, start : start + 32, :].astype(BF)
    proj_copies = ch_copies(lambda other: pc_buf.at[other], pc_in, pc_send, pc_recv)

    wide_rows = 64

    def expand_rows(m, carry):
        rows = pl.ds(pl.multiple_of(m * wide_rows, wide_rows), wide_rows)
        summed = hat_three_ref[rows, :] * wide_ref[0:1, :] + wide_ref[1:2, :] + x_ref[rows, :].astype(F32)
        ds[rows, :] = gz_ref[rows, :] * gelu_slope(summed)
        return carry

    lax.fori_loop(0, PX // wide_rows, expand_rows, 0)
    copies = stat_round(0, stat_three, ds[...], hat_three_ref[...])
    start_all(proj_copies)
    turned[0] = jnp.transpose(second_ref[...].astype(F32)).astype(BF)
    turned[1] = jnp.transpose(first_ref[...].astype(F32)).astype(BF)
    sums = stat_end(copies, stat_three)
    norm_wide_in[c] = sums
    ds_low[...] = norm_back(ds[...], hat_three_ref[...], sums, wide_ref[0:1, :], stats_wide_ref[0:1, :]).astype(BF)

    def scatter_ch(index, product):
        for m in range(NCH):
            value = product(m)
            ch_buf[index, m] = value.astype(BF)
        copies = ch_copies(lambda other: ch_buf.at[index, other], ch_in.at[index], c_send.at[index], c_recv.at[index])
        start_all(copies)
        return copies

    def scatter_end(index, copies):
        wait_all(copies)
        total = ch_buf[index, c].astype(F32)
        for d in range(1, NCH):
            total = total + ch_in[index, lax.rem(c + d, NCH)].astype(F32)
        return total

    def grad_copies(index, buf, inbox):
        copies = []
        for d in range(1, NPIX):
            b = lax.rem(p + d, NPIX)
            copies.append(
                remote(buf.at[b], inbox.at[d - 1], g_send.at[index, d - 1], g_recv.at[index, d - 1], (b, c))
            )
        return copies

    def expand_back(m):
        wanted = wall_ref[2 * m : 2 * m + 2, :, W_EXPAND].reshape(MID, CIN)
        return nt_dot(ds_low[...], wanted)

    copies = scatter_ch(0, expand_back)
    we_buf[...] = nn_dot(turned[0], ds_low[...]).astype(BF).reshape(NPIX, WPART, CIN)
    we_copies = grad_copies(0, we_buf, we_in)
    start_all(we_copies)
    hat = hat_two_ref[...]
    slope = gelu_slope(hat * narrow_ref[2:3, :] + narrow_ref[3:4, :])
    upstream = scatter_end(0, copies) * slope
    copies = stat_round(1, stat_two, upstream, hat)
    wait_all(proj_copies)
    for t in range(3):
        total = pc_buf[c, t].astype(F32)
        for d in range(1, NCH):
            total = total + pc_in[lax.rem(c + d, NCH), t].astype(F32)
        pr_buf[:, t] = total.astype(BF)
    wait_all(small_copies)
    small_px[p] = add_up(small_ch)
    sums = stat_end(copies, stat_two)
    norm_in[c, 2:4, :] = sums[0:2]

    def halo_copy(side):
        target = (p - 1, c) if side == 0 else (p + 1, c)
        return remote(back_t.at[0], halo_in.at[side], h_send.at[side], h_recv.at[side], target)

    gradient = norm_back(upstream, hat, sums, narrow_ref[2:3, :], stats_ref[1:2, :])
    back_t[0] = gradient.astype(BF)

    @pl.when(p > 0)
    def _():
        halo_copy(0).start()

    @pl.when(p < NPIX - 1)
    def _():
        halo_copy(1).start()

    def fill_taps(step, source):
        for col in range(3):
            tap = 3 * (step + 1) + col
            moved = slide_rows(source.astype(F32), DILATION_RATE * (col - 1))
            taps[:, tap * MID : (tap + 1) * MID] = moved.astype(BF)

    fill_taps(0, back_t[0])

    @pl.when(p < NPIX - 1)
    def _():
        halo_copy(0).wait_recv()

    @pl.when(p == NPIX - 1)
    def _():
        halo_in[0] = jnp.zeros((PX, MID), BF)

    fill_taps(-1, halo_in[0])

    @pl.when(p > 0)
    def _():
        halo_copy(1).wait_recv()

    @pl.when(p == 0)
    def _():
        halo_in[1] = jnp.zeros((PX, MID), BF)

    fill_taps(1, halo_in[1])

    def dilated_back(m):
        wanted = wall_ref[2 * m : 2 * m + 2, :, W_DILATED].reshape(MID, TAP_LANES)
        return nt_dot(taps[...], wanted)

    copies = scatter_ch(1, dilated_back)
    proj_rows = grad_copies(3, pr_buf, pr_in)
    start_all(proj_rows)
    for m in range(NPIX):
        wd_buf[m] = nn_dot(turned[1, m * WPART : (m + 1) * WPART, :], taps[...]).astype(BF)
    wd_copies = grad_copies(1, wd_buf, wd_in)
    start_all(wd_copies)
    hat = hat_one_ref[...]
    slope = gelu_slope(hat * narrow_ref[0:1, :] + narrow_ref[1:2, :]) * mask_ref[...]
    upstream = scatter_end(1, copies) * slope
    copies = stat_round(2, stat_one, upstream, hat)
    small_rows = [
        remote(small_px.at[p], small_px.at[p], t_send.at[d - 1], t_recv.at[d - 1], pix_targets[d - 1])
        for d in range(1, NPIX)
    ]
    start_all(small_rows)
    sums = stat_end(copies, stat_one)
    norm_in[c, 0:2, :] = sums[0:2]
    norm_in[c, 4:8, :] = jnp.zeros((4, MID), F32)
    gradient = norm_back(upstream, hat, sums, narrow_ref[0:1, :], stats_ref[0:1, :])

    own_rows = pl.ds(pl.multiple_of(c * MID, MID), MID)
    turned[2, own_rows, :] = jnp.transpose(gradient).astype(BF)
    copies = [
        remote(
            turned.at[2, own_rows, :], turned.at[2, own_rows, :],
            c_send.at[2, d - 1], c_recv.at[2, d - 1], ch_targets[d - 1],
        )
        for d in range(1, NCH)
    ]
    start_all(copies)
    norm_copies = own_ch_copies(norm_in, 1) + own_ch_copies(norm_wide_in, 2)
    start_all(norm_copies)
    wait_all(copies)
    wr_buf[...] = nn_dot(turned[2], x_ref[...]).astype(BF).reshape(NPIX, WPART, CIN)
    wr_copies = grad_copies(2, wr_buf, wr_in)
    start_all(wr_copies)
    full = jnp.transpose(turned[2].astype(F32)).astype(BF)
    ingrad_ref[...] = nn_dot(full, weights(W_REDUCE)) + ds[...]
    wait_all(proj_rows)
    for t in range(3):
        total = pr_buf[p, t].astype(F32)
        for d in range(NPIX - 1):
            total = total + pr_in[d, t].astype(F32)
        pg_in[c, t] = total
    pg_copies = [
        remote(pg_in.at[c], pg_in.at[c], pg_send.at[d - 1], pg_recv.at[d - 1], ch_targets[d - 1])
        for d in range(1, NCH)
    ]
    start_all(pg_copies)

    def grad_end(copies, buf, inbox, lanes):
        wait_all(copies)
        total = buf[p].astype(F32)
        for d in range(NPIX - 1):
            total = total + inbox[d].astype(F32)
        wgrad_ref[:, lanes] = total
        return fold(total * total)

    squares = square_ref[...] + grad_end(we_copies, we_buf, we_in, W_EXPAND)
    squares = squares + grad_end(wd_copies, wd_buf, wd_in, W_DILATED)
    wait_all(pg_copies)
    for t in range(3):
        for other in range(NCH):
            pgrad_ref[t, other * 32 : (other + 1) * 32, :] = pg_in[other, t]
        squares = squares + fold(pg_in[c, t] * pg_in[c, t])
    wait_all(small_rows)
    sgrad_ref[...] = add_up(small_px)
    wait_all(norm_copies)
    ngrad_ref[...] = norm_in[...]
    ngrad_wide_ref[...] = norm_wide_in[...]
    shared = fold(sgrad_ref[...] * sgrad_ref[...])
    for other in range(NCH):
        shared = shared + fold(norm_in[other] * norm_in[other])
        piece = norm_wide_in[other]
        shared = shared + fold(piece * piece)
    squares = squares + grad_end(wr_copies, wr_buf, wr_in, W_REDUCE)
    sq_ch[c] = squares
    copies = [
        remote(sq_ch.at[c], sq_ch.at[c], u_send.at[0, d - 1], u_recv.at[0, d - 1], ch_targets[d - 1])
        for d in range(1, NCH)
    ]
    start_all(copies)
    wait_all(copies)
    sq_px[p] = add_up(sq_ch)
    copies = [
        remote(sq_px.at[p], sq_px.at[p], u_send.at[1, d - 1], u_recv.at[1, d - 1], pix_targets[d - 1])
        for d in range(1, NPIX)
    ]
    start_all(copies)
    wait_all(copies)
    everything = add_up(sq_px) + shared
    total = jnp.sum(jnp.sum(everything, axis=0, keepdims=True), axis=1, keepdims=True)
    norm = jnp.sqrt(total)
    factor = jnp.minimum(1.0, CLIP_NORM / (norm + 1e-06))
    line = lax.broadcasted_iota(jnp.int32, (8, 128), 0)
    total_ref[...] = jnp.where(line == 0, norm, factor)

    @pl.when(p > 0)
    def _():
        halo_copy(0).wait_send()

    @pl.when(p < NPIX - 1)
    def _():
        halo_copy(1).wait_send()


def block_backward(*operands):
    dma = pltpu.SemaphoreType.DMA
    shape = jax.ShapeDtypeStruct
    vmem = pltpu.VMEM
    return pl.pallas_call(
        block_backward_kernel,
        out_shape=(
            shape((PX, CIN), F32),
            shape((WPART, W_LANES), F32),
            shape((3, 128, HID), F32),
            shape((SMALL_ROWS, 128), F32),
            shape((NCH, 8, MID), F32),
            shape((NCH, 8, CIN), F32),
            shape((8, 128), F32),
        ),
        in_specs=[whole_vmem()] * 16,
        out_specs=[whole_vmem()] * 7,
        scratch_shapes=[
            vmem((PX, CIN), F32),
            vmem((PX, CIN), BF),
            vmem((3, M, PX), BF),
            vmem((2, NCH, PX, MID), BF),
            vmem((2, NCH, PX, MID), BF),
            vmem((2, PX, MID), BF),
            vmem((PX, TAP_LANES), BF),
            vmem((1, PX, MID), BF),
            vmem((NPIX, 8, CIN), F32),
            vmem((NPIX, 8, MID), F32),
            vmem((NPIX, 8, MID), F32),
            vmem((NPIX, WPART, CIN), BF),
            vmem((NPIX - 1, WPART, CIN), BF),
            vmem((NPIX, WPART, TAP_LANES), BF),
            vmem((NPIX - 1, WPART, TAP_LANES), BF),
            vmem((NPIX, WPART, CIN), BF),
            vmem((NPIX - 1, WPART, CIN), BF),
            vmem((NCH, 3, NPIX, 32, HID), BF),
            vmem((NCH, 3, NPIX, 32, HID), BF),
            vmem((NPIX, 3, 32, HID), BF),
            vmem((NPIX - 1, 3, 32, HID), BF),
            vmem((NCH, 3, 32, HID), F32),
            vmem((NCH, SMALL_ROWS, 128), F32),
            vmem((NPIX, SMALL_ROWS, 128), F32),
            vmem((NCH, 8, 128), F32),
            vmem((NPIX, 8, 128), F32),
            vmem((NCH, 8, MID), F32),
            vmem((NCH, 8, CIN), F32),
            dma((3, NCH - 1)), dma((3, NCH - 1)),
            dma((3, NPIX - 1)), dma((3, NPIX - 1)),
            dma((2,)), dma((2,)),
            dma((4, NPIX - 1)), dma((4, NPIX - 1)),
            dma((NCH - 1,)), dma((NCH - 1,)),
            dma((NCH - 1,)), dma((NCH - 1,)),
            dma((NPIX - 1,)), dma((NPIX - 1,)),
            dma((2, NPIX - 1)), dma((2, NPIX - 1)),
            dma((3, NCH - 1)), dma((3, NCH - 1)),
        ],
        compiler_params=pltpu.CompilerParams(
            collective_id=3, has_side_effects=True, vmem_limit_bytes=VMEM_LIMIT
        ),
        name="block_backward",
    )(*operands)


def per_device_rows(
    features,
    valid_mask,
    sem_label,
    depth_target,
    normal_target,
    label_mask,
    w_reduce,
    m_reduce,
    v_reduce,
    w_dilated,
    m_dilated,
    v_dilated,
    w_expand,
    m_expand,
    v_expand,
    head_weight,
    m_head,
    v_head,
    head_rates,
    m_rates,
    v_rates,
    head_proj,
    m_proj,
    v_proj,
    norm_params,
    norm_m,
    norm_v,
    head_small,
    small_m,
    small_v,
):

    block_id = lax.axis_index("ch")
    flat_in = features.reshape(PX, CIN)
    mask_column = valid_mask.reshape(PX, 1).astype(F32)
    gains = norm_params[0]
    shifts = norm_params[1]

    def owned(vector, offset, width):
        return lax.dynamic_slice_in_dim(vector, offset + block_id * width, width)

    def own_row(array, axis):
        return lax.dynamic_slice_in_dim(array, block_id, 1, axis=axis)

    w_shard = jnp.concatenate(
        [w_reduce.T, w_dilated.transpose(1, 0, 2).reshape(WPART, TAP_LANES), w_expand], axis=1
    ).astype(BF)
    w_seg = tap_weights(head_weight, head_rates)
    local_counts = jnp.sum(label_mask.astype(F32), axis=(1, 2))
    narrow = jnp.stack(
        [
            owned(gains, 0, MID),
            owned(shifts, 0, MID),
            owned(gains, M, MID),
            owned(shifts, M, MID),
            jnp.pad(local_counts, (0, MID - 3)),
        ]
        + [jnp.zeros((MID,), F32)] * 3
    )
    wide = jnp.stack([owned(gains, 2 * M, CIN), owned(shifts, 2 * M, CIN)] + [jnp.zeros((CIN,), F32)] * 6)
    shared, hat_one, hat_two, hat_three, w_all, first, second, stats, stats_wide, proj_t = block_forward(
        flat_in, mask_column, w_shard, jnp.transpose(head_proj, (0, 2, 1)).astype(BF), narrow, wide
    )
    branch_bias, proj_bias, sem_w, depth_w, normal_w, sem_b, depth_b, normal_b = unpack_small(
        head_small
    )
    out_stack = jnp.stack(
        [jnp.pad(weight.astype(BF), ((0, 0), (0, 32 - weight.shape[1]))) for weight in (sem_w, depth_w, normal_w)]
    )
    out_bias = jnp.stack(
        [jnp.pad(bias, (0, 32 - bias.shape[0])) for bias in (sem_b, depth_b, normal_b)], axis=1
    )
    q_rows, shared_all = heads_forward(shared, w_seg)
    targets = jnp.concatenate([own_row(depth_target, 0), own_row(normal_target, 1)[:, 0]], axis=0)
    pre_grad, proj_part, out_grad, bias_rows, out_bias_rows = heads_middle(
        q_rows,
        branch_bias.T,
        proj_bias.T,
        proj_t,
        out_stack,
        out_bias,
        own_row(sem_label, 0),
        targets,
        own_row(label_mask, 1)[:, 0].astype(F32),
        jnp.broadcast_to(stats[2, :3][:, None], (3, WIDTH)),
    )
    small_term = pack_small(
        [bias_rows[:4, 0], bias_rows[4, 0]]
        + [out_grad[0, :NCLS].T, out_grad[1, :1].T, out_grad[2, :3].T]
        + [out_bias_rows[0, 0, :NCLS], out_bias_rows[1, 0, :1], out_bias_rows[2, 0, :3]]
    )
    small_count = small_term.shape[0]
    small_term = jnp.pad(small_term, (0, SMALL_ROWS * 128 - small_count)).reshape(SMALL_ROWS, 128)
    tap_sums, combined, squares = heads_backward(pre_grad, shared_all, w_seg)
    head_shard, rates_shard = tap_grads(tap_sums)
    input_grad, w_grad, proj_shard, small_sum, norm_narrow, norm_wide, totals = block_backward(
        combined, flat_in, mask_column, w_all, hat_one, hat_two, hat_three, first, second,
        narrow, wide, stats, stats_wide, proj_part, small_term, squares,
    )
    reduce_shard = w_grad[:, W_REDUCE].T
    dilated_shard = w_grad[:, W_DILATED].reshape(WPART, 9, MID).transpose(1, 0, 2)
    expand_shard = w_grad[:, W_EXPAND]
    small_grad = small_sum.reshape(-1)[:small_count]
    norm_grad = jnp.stack(
        [
            jnp.concatenate([norm_narrow[:, 1].reshape(-1), norm_narrow[:, 3].reshape(-1), norm_wide[:, 1].reshape(-1)]),
            jnp.concatenate([norm_narrow[:, 0].reshape(-1), norm_narrow[:, 2].reshape(-1), norm_wide[:, 0].reshape(-1)]),
        ]
    )
    grad_norm = totals[0, 0]
    factor = totals[1, 0]
    reduce_new, reduce_first, reduce_second = adam_step(
        w_reduce, m_reduce, v_reduce, reduce_shard * factor, RATE_MATRIX, DECAY
    )
    dilated_new, dilated_first, dilated_second = adam_step(
        w_dilated, m_dilated, v_dilated, dilated_shard * factor, RATE_MATRIX, DECAY
    )
    expand_new, expand_first, expand_second = adam_step(
        w_expand, m_expand, v_expand, expand_shard * factor, RATE_MATRIX, DECAY
    )
    head_new, head_first, head_second = adam_step(
        head_weight, m_head, v_head, head_shard * factor, RATE_MATRIX, DECAY
    )
    rates_new, rates_first, rates_second = adam_step(
        head_rates, m_rates, v_rates, rates_shard * factor, RATE_MATRIX, DECAY
    )
    proj_new, proj_first, proj_second = adam_step(
        head_proj, m_proj, v_proj, proj_shard * factor, RATE_MATRIX, DECAY
    )
    norm_new, norm_first, norm_second = adam_step(
        norm_params, norm_m, norm_v, norm_grad * factor, RATE_SMALL, 0.0
    )
    small_new, small_first, small_second = adam_step(
        head_small, small_m, small_v, small_grad * factor, RATE_SMALL, 0.0
    )
    depth_bias_grad = small_grad[small_count - 4]
    return (
        shared.reshape(ROWS, WIDTH, CIN),
        input_grad.reshape(ROWS, WIDTH, CIN),
        grad_norm,
        reduce_new,
        reduce_first,
        reduce_second,
        reduce_new.astype(jnp.bfloat16),
        dilated_new,
        dilated_first,
        dilated_second,
        dilated_new.astype(jnp.bfloat16),
        expand_new,
        expand_first,
        expand_second,
        expand_new.astype(jnp.bfloat16),
        head_new,
        head_first,
        head_second,
        head_new.astype(jnp.bfloat16),
        rates_new,
        rates_first,
        rates_second,
        rates_new.astype(jnp.bfloat16),
        proj_new,
        proj_first,
        proj_second,
        proj_new.astype(jnp.bfloat16),
        norm_new,
        norm_first,
        norm_second,
        small_new,
        small_first,
        small_second,
        depth_bias_grad,
    )


def per_device(features, *rest):
    sizes = (lax.axis_size("pix"), lax.axis_size("ch"))
    if sizes == (NPIX, NCH) and features.shape == (ROWS, WIDTH, CIN):
        return per_device_rows(features, *rest)
    return per_device_plain(features, *rest)


def solution(mesh):
    placed = (
        P("pix", None, "ch"),
        P("pix", None),
        P("pix", None),
        P("pix", None),
        P(None, "pix", None),
        P(None, "pix", None),
        P("ch", "pix"),
        P("ch", "pix"),
        P("ch", "pix"),
        P(None, "pix", "ch"),
        P(None, "pix", "ch"),
        P(None, "pix", "ch"),
        P("pix", "ch"),
        P("pix", "ch"),
        P("pix", "ch"),
        P("ch", "pix"),
        P("ch", "pix"),
        P("ch", "pix"),
        P(None, None, "pix", "ch"),
        P(None, None, "pix", "ch"),
        P(None, None, "pix", "ch"),
        P(None, "pix", None),
        P(None, "pix", None),
        P(None, "pix", None),
        P(),
        P(),
        P(),
        P(),
        P(),
        P(),
    )
    return jax.shard_map(
        per_device,
        mesh=mesh,
        in_specs=placed,
        out_specs=(
            P("pix", None, "ch"),
            P("pix", None, "ch"),
            P(),
            P("ch", "pix"),
            P("ch", "pix"),
            P("ch", "pix"),
            P("ch", "pix"),
            P(None, "pix", "ch"),
            P(None, "pix", "ch"),
            P(None, "pix", "ch"),
            P(None, "pix", "ch"),
            P("pix", "ch"),
            P("pix", "ch"),
            P("pix", "ch"),
            P("pix", "ch"),
            P("ch", "pix"),
            P("ch", "pix"),
            P("ch", "pix"),
            P("ch", "pix"),
            P(None, None, "pix", "ch"),
            P(None, None, "pix", "ch"),
            P(None, None, "pix", "ch"),
            P(None, None, "pix", "ch"),
            P(None, "pix", None),
            P(None, "pix", None),
            P(None, "pix", None),
            P(None, "pix", None),
            P(),
            P(),
            P(),
            P(),
            P(),
            P(),
            P(),
        ),
        check_vma=False,
    )
```

```python
import jax
import jax.numpy as jnp
from jax import lax
from jax.experimental import pallas as pl
from jax.experimental.pallas import tpu as pltpu
from jax.sharding import PartitionSpec as P

C = 2048
M = 512
HID = 256
NCLS = 19
DILATION_RATE = 4
STEP = 10


EPS_NORM = 1e-05
BETA_ONE = 0.9
BETA_TWO = 0.999
ADAM_EPS = 1e-08
RATE_MATRIX = 0.02
RATE_SMALL = 0.2
DECAY = 0.01
CLIP_NORM = 0.01
aspp_rates = (12, 24, 36)


def shifted(value, axis, steps):
    count = lax.axis_size(axis)
    leading, last = (max(0, -steps), min(count, count - steps))
    return lax.ppermute(value, axis, [(source, source + steps) for source in range(leading, last)])


def with_halo(cells, sides, width):
    for axis, dim in sides:
        count = lax.axis_size(axis)
        ends = count - 1
        head = lax.slice_in_dim(cells, 0, width, axis=dim)
        tail = lax.slice_in_dim(cells, cells.shape[dim] - width, cells.shape[dim], axis=dim)
        cells = jnp.concatenate(
            [
                lax.ppermute(tail, axis, [(i, (i + 1) % count) for i in range(ends)]),
                cells,
                lax.ppermute(head, axis, [((i + 1) % count, i) for i in range(ends)]),
            ],
            axis=dim,
        )
    return cells


def smooth(values):
    return jax.nn.gelu(values, approximate=True)


def smooth_slope(values):
    return jax.vjp(smooth, values)[1](jnp.ones_like(values))[0]


def contract_first(left, right):
    return lax.dot_general(
        left, right, (((0,), (0,)), ((), ())), preferred_element_type=jnp.float32
    )


def contract_last(left, right):
    return lax.dot_general(
        left, right, (((1,), (1,)), ((), ())), preferred_element_type=jnp.float32
    )


def split_tasks(slopes, weight):
    pixels = slopes.shape[0]
    return lax.dot_general(
        slopes.reshape(pixels, 3, -1),
        weight.reshape(weight.shape[0], 3, -1),
        (((2,), (2,)), ((1,), (1,))),
        preferred_element_type=jnp.float32,
    )


def split_tasks_rows(slopes, weight):
    pixels = slopes.shape[0]
    return lax.dot_general(
        slopes.reshape(pixels, 3, -1),
        weight.reshape(3, -1, weight.shape[1]),
        (((2,), (1,)), ((1,), (0,))),
        preferred_element_type=jnp.float32,
    )


def unpack_small(vector):
    lengths = (12 * HID, 3 * HID, HID * NCLS, HID, HID * 3, NCLS, 1, 3)
    pieces = []
    offset = 0
    for length in lengths:
        pieces.append(lax.slice_in_dim(vector, offset, offset + length, axis=0))
        offset = offset + length
    return (
        pieces[0].reshape(4, 3 * HID),
        pieces[1].reshape(3, HID),
        pieces[2].reshape(HID, NCLS),
        pieces[3].reshape(HID, 1),
        pieces[4].reshape(HID, 3),
        pieces[5],
        pieces[6],
        pieces[7],
    )


def pack_small(pieces):
    return jnp.concatenate([piece.reshape(-1) for piece in pieces])


def fetch_rows(grid, step):
    if abs(step) >= lax.axis_size("pix"):
        return jnp.zeros_like(grid)
    return shifted(grid, "pix", -step)


def fetch_grads(grid, step):
    if abs(step) >= lax.axis_size("pix"):
        return jnp.zeros_like(grid)
    return shifted(grid, "pix", -step)


def row_view(grid, offset, fetch):
    height = grid.shape[0]
    lead, rest = divmod(offset, height)
    return fetch(grid, lead)


def column_view(grid, offset):
    width = grid.shape[1]
    reach = abs(offset)
    if reach == 0:
        return grid
    padded_canvas = jnp.pad(grid, ((0, 0), (reach, reach), (0, 0)))
    return padded_canvas[:, reach + offset : reach + offset + width]


def imtl_weights(gram):
    lengths = jnp.sqrt(jnp.diagonal(gram) + 1e-12)

    def pairing(row_task, col_task):
        return (
            gram[0, 0] / lengths[0]
            - gram[0, col_task] / lengths[col_task]
            - gram[row_task, 0] / lengths[0]
            + gram[row_task, col_task] / lengths[col_task]
        )

    right_one = gram[0, 0] / lengths[0] - gram[0, 1] / lengths[1]
    right_two = gram[0, 0] / lengths[0] - gram[0, 2] / lengths[2]
    upper_left = pairing(1, 1)
    upper_right = pairing(1, 2)
    lower_left = pairing(2, 1)
    lower_right = pairing(2, 2)
    determinant = upper_left * lower_right - upper_right * lower_left
    alpha_one = (right_one * lower_right - right_two * lower_left) / determinant
    alpha_two = (right_two * upper_left - right_one * upper_right) / determinant
    return jnp.stack([1.0 - alpha_one - alpha_two, alpha_one, alpha_two])


def adam_step(weight, first, second, grad, rate, decay):
    first_new = BETA_ONE * first + (1.0 - BETA_ONE) * grad
    second_new = BETA_TWO * second + (1.0 - BETA_TWO) * grad * grad
    first_hat = first_new / (1.0 - BETA_ONE**STEP)
    second_hat = second_new / (1.0 - BETA_TWO**STEP)
    weight_new = weight - rate * (first_hat / (jnp.sqrt(second_hat) + ADAM_EPS) + decay * weight)
    return (weight_new, first_new, second_new)


def pixel_sums(first, second):
    return lax.psum((first, second), "pix")


def back_pair(first, second):
    return lax.psum((first, second), "pix")


def channel_gather(piece):
    return lax.all_gather(piece, "ch", axis=1, tiled=True)


def channel_parts(partial_sum):
    return lax.psum_scatter(partial_sum, "ch", scatter_dimension=1, tiled=True)


def forward_norm(inputs, sums, squares, count, gain_row, shift_row):
    mean_row = sums / count
    scale_row = lax.rsqrt(squares / count - mean_row * mean_row + EPS_NORM)
    normed = (inputs - mean_row) * scale_row
    return (normed * gain_row + shift_row, normed, scale_row)


def backward_norm(upstream, normed, scale_row, count, gain_row):
    shift_grad, gain_grad = back_pair(jnp.sum(upstream, axis=0), jnp.sum(upstream * normed, axis=0))
    inner = gain_row * scale_row * (upstream - shift_grad / count - normed * (gain_grad / count))
    return (inner, gain_grad, shift_grad)


def loss_slopes(
    logits, depth_pred, normal_pred, sem_label, depth_target, normal_target, label_mask, counts
):
    masks = label_mask.reshape(3, -1).astype(jnp.float32)
    classes = lax.broadcasted_iota(jnp.int32, (1, NCLS), 1)
    onehot = (sem_label.reshape(-1, 1) == classes).astype(jnp.float32)
    highest = jnp.max(logits, axis=1, keepdims=True)
    raised = jnp.exp(logits - highest)
    probs = raised / jnp.sum(raised, axis=1, keepdims=True)
    sem_slope = masks[0][:, None] * (probs - onehot) / counts[0]
    depth_gap = depth_pred[:, 0] - depth_target.reshape(-1)
    depth_slope = (masks[1] * depth_gap / jnp.sqrt(depth_gap * depth_gap + 1.0) / counts[1])[
        :, None
    ]
    normal_slope = masks[2][:, None] * (normal_pred - normal_target.reshape(3, -1).T) / counts[2]
    return (
        sem_slope.astype(jnp.bfloat16),
        depth_slope.astype(jnp.bfloat16),
        normal_slope.astype(jnp.bfloat16),
    )


def per_device_plain(
    features,
    valid_mask,
    sem_label,
    depth_target,
    normal_target,
    label_mask,
    w_reduce,
    m_reduce,
    v_reduce,
    w_dilated,
    m_dilated,
    v_dilated,
    w_expand,
    m_expand,
    v_expand,
    head_weight,
    m_head,
    v_head,
    head_rates,
    m_rates,
    v_rates,
    head_proj,
    m_proj,
    v_proj,
    norm_params,
    norm_m,
    norm_v,
    head_small,
    small_m,
    small_v,
):
    rows_per_shard, columns_per_shard, wide_dev = features.shape
    pixels = rows_per_shard * columns_per_shard
    groups = lax.axis_size("ch")
    block_id = lax.axis_index("ch")
    pix_devices = lax.axis_size("pix")
    middle_per_shard = M // groups
    count_all = float(pixels * pix_devices)
    flat_in = features.reshape(pixels, wide_dev)
    mask_flat = valid_mask.reshape(pixels).astype(jnp.float32)
    gains = norm_params[0]
    shifts = norm_params[1]

    def owned(vector, offset, width):
        return lax.dynamic_slice_in_dim(vector, offset + block_id * width, width)

    reduce_w, dilated_w, expand_w, heads_w, rates_w, proj_w = (
        lax.all_gather(w_reduce.astype(jnp.bfloat16), "pix", axis=1, tiled=True),
        lax.all_gather(w_dilated.astype(jnp.bfloat16), "pix", axis=1, tiled=True),
        lax.all_gather(w_expand.astype(jnp.bfloat16), "pix", axis=0, tiled=True),
        lax.all_gather(head_weight.astype(jnp.bfloat16), "pix", axis=1, tiled=True),
        lax.all_gather(head_rates.astype(jnp.bfloat16), "pix", axis=2, tiled=True),
        lax.all_gather(head_proj.astype(jnp.bfloat16), "pix", axis=1, tiled=True),
    )
    reduced = lax.psum_scatter(
        jnp.dot(flat_in, reduce_w, preferred_element_type=jnp.float32),
        "ch",
        scatter_dimension=1,
        tiled=True,
    )
    local_counts = jnp.sum(label_mask.astype(jnp.float32), axis=(1, 2))
    reduced_sum = jnp.sum(reduced, axis=0)
    reduced_sq = jnp.sum(reduced * reduced, axis=0)
    reduced_sum, reduced_sq = lax.psum((reduced_sum, reduced_sq), "pix")
    task_counts = lax.psum(local_counts, "pix")
    task_counts = jnp.maximum(task_counts, 1.0)
    gain_one = owned(gains, 0, middle_per_shard)
    norm_one, hat_one, scale_one = forward_norm(
        reduced, reduced_sum, reduced_sq, count_all, gain_one, owned(shifts, 0, middle_per_shard)
    )
    first = (smooth(norm_one) * mask_flat[:, None]).astype(jnp.bfloat16)
    first_gathered = channel_gather(first).reshape(rows_per_shard, columns_per_shard, M)
    bordered_input = with_halo(first_gathered, (("pix", 0),), DILATION_RATE)
    bordered_input = jnp.pad(bordered_input, ((0, 0), (DILATION_RATE, DILATION_RATE), (0, 0)))
    middle = jnp.zeros((pixels, middle_per_shard), jnp.float32)
    for tap_index in range(9):
        kernel_row, kernel_column = divmod(tap_index, 3)
        sliding_patch = bordered_input[
            kernel_row * DILATION_RATE : kernel_row * DILATION_RATE + rows_per_shard,
            kernel_column * DILATION_RATE : kernel_column * DILATION_RATE + columns_per_shard,
        ].reshape(pixels, M)
        middle = middle + jnp.dot(
            sliding_patch, dilated_w[tap_index], preferred_element_type=jnp.float32
        )
    gain_two = owned(gains, M, middle_per_shard)
    middle_sum, middle_sq = pixel_sums(jnp.sum(middle, axis=0), jnp.sum(middle * middle, axis=0))
    norm_two, hat_two, scale_two = forward_norm(
        middle, middle_sum, middle_sq, count_all, gain_two, owned(shifts, M, middle_per_shard)
    )
    second = smooth(norm_two).astype(jnp.bfloat16)
    second_all = channel_gather(second)
    expanded = jnp.dot(second_all, expand_w, preferred_element_type=jnp.float32)
    gain_three = owned(gains, 2 * M, wide_dev)
    expand_sum, expand_sq = pixel_sums(
        jnp.sum(expanded, axis=0), jnp.sum(expanded * expanded, axis=0)
    )
    norm_three, hat_three, scale_three = forward_norm(
        expanded, expand_sum, expand_sq, count_all, gain_three, owned(shifts, 2 * M, wide_dev)
    )
    summed_in = norm_three + flat_in.astype(jnp.float32)
    shared = smooth(summed_in).astype(jnp.bfloat16)
    branch_bias, proj_bias, sem_w, depth_w, normal_w, sem_b, depth_b, normal_b = unpack_small(
        head_small
    )
    out_weights = (
        sem_w.astype(jnp.bfloat16),
        depth_w.astype(jnp.bfloat16),
        normal_w.astype(jnp.bfloat16),
    )
    grid_shared = shared.reshape(rows_per_shard, columns_per_shard, wide_dev)
    row_views = []
    pre_list = [jnp.dot(shared, heads_w, preferred_element_type=jnp.float32)]
    for rate_index, rate in enumerate(aspp_rates):
        views = (
            row_view(grid_shared, -rate, fetch_rows),
            grid_shared,
            row_view(grid_shared, rate, fetch_rows),
        )
        row_views.append(views)
        summed = jnp.zeros((pixels, 3 * HID), jnp.float32)
        for tap_index in range(9):
            kernel_row, kernel_column = divmod(tap_index, 3)
            sliding_patch = column_view(views[kernel_row], (kernel_column - 1) * rate).reshape(
                pixels, wide_dev
            )
            summed = summed + contract_last(sliding_patch, rates_w[rate_index, tap_index])
        pre_list.append(summed)
    pre_parts = jnp.stack(pre_list, axis=1)
    before = lax.psum(pre_parts, "ch") + branch_bias[None]
    hidden = smooth(before).astype(jnp.bfloat16)
    branch_slope = smooth_slope(before).reshape(pixels, 4, 3, HID)
    joined_list = []
    projected_list = []
    top_list = []
    produced = []
    for task_index in range(3):
        joined = hidden[:, :, task_index * HID : (task_index + 1) * HID].reshape(pixels, 4 * HID)
        projected = (
            jnp.dot(joined, proj_w[task_index], preferred_element_type=jnp.float32)
            + proj_bias[task_index]
        )
        top = smooth(projected).astype(jnp.bfloat16)
        produced.append(jnp.dot(top, out_weights[task_index], preferred_element_type=jnp.float32))
        joined_list.append(joined)
        projected_list.append(projected)
        top_list.append(top)
    logits = produced[0] + sem_b
    depth_pred = produced[1] + depth_b
    normal_pred = produced[2] + normal_b
    slopes = loss_slopes(
        logits,
        depth_pred,
        normal_pred,
        sem_label,
        depth_target,
        normal_target,
        label_mask,
        task_counts,
    )
    out_grads = []
    out_bias_grads = []
    proj_grads = []
    proj_bias_grads = []
    joined_backs = []
    for task_index in range(3):
        top_back = contract_last(slopes[task_index], out_weights[task_index])
        proj_back = (top_back * smooth_slope(projected_list[task_index])).astype(jnp.bfloat16)
        out_grads.append(contract_first(top_list[task_index], slopes[task_index]))
        out_bias_grads.append(jnp.sum(slopes[task_index], axis=0, dtype=jnp.float32))
        proj_grads.append(contract_first(joined_list[task_index], proj_back))
        proj_bias_grads.append(jnp.sum(proj_back, axis=0, dtype=jnp.float32))
        joined_backs.append(contract_last(proj_back, proj_w[task_index]).reshape(pixels, 4, HID))
    joined_back = jnp.stack(joined_backs, axis=2)
    pre_grad = (joined_back * branch_slope).astype(jnp.bfloat16).reshape(pixels, 4, 3 * HID)
    small_term = (
        pack_small(
            [jnp.sum(pre_grad, axis=0, dtype=jnp.float32), jnp.stack(proj_bias_grads)]
            + out_grads
            + out_bias_grads
        )
        / groups
    )
    proj_grad = jnp.stack(proj_grads)
    first_branch = pre_grad[:, 0]
    task_sum = split_tasks(first_branch, heads_w)
    rates_list = []
    for rate_index, rate in enumerate(aspp_rates):
        flat_back = pre_grad[:, rate_index + 1]
        rate_back = flat_back.reshape(rows_per_shard, columns_per_shard, 3 * HID)
        back_views = (
            row_view(rate_back, rate, fetch_grads),
            rate_back,
            row_view(rate_back, -rate, fetch_grads),
        )
        for tap_index in range(9):
            kernel_row, kernel_column = divmod(tap_index, 3)
            sliding_patch = column_view(
                row_views[rate_index][kernel_row], (kernel_column - 1) * rate
            ).reshape(pixels, wide_dev)
            rates_list.append(contract_first(flat_back, sliding_patch))
            spread = column_view(back_views[kernel_row], (1 - kernel_column) * rate).reshape(
                pixels, 3 * HID
            )
            task_sum = task_sum + split_tasks_rows(spread, rates_w[rate_index, tap_index])
    rates_grad = jnp.stack(rates_list).reshape(3, 9, 3 * HID, wide_dev)
    task_grads = [task_sum[0], task_sum[1], task_sum[2]]
    head_grad = contract_first(shared, first_branch)
    local_gram = jnp.stack(
        [
            jnp.stack(
                [jnp.sum(task_grads[row_task] * task_grads[col_task]) for col_task in range(3)]
            )
            for row_task in range(3)
        ]
    )
    gram = lax.psum(local_gram, ("pix", "ch"))
    alphas = imtl_weights(gram)
    combined = alphas[0] * task_grads[0] + alphas[1] * task_grads[1] + alphas[2] * task_grads[2]
    shared_slope = combined * smooth_slope(summed_in)
    expand_up, gain_three_grad, shift_three_grad = backward_norm(
        shared_slope, hat_three, scale_three, count_all, gain_three
    )
    expand_back = expand_up.astype(jnp.bfloat16)
    expand_grad = contract_first(second_all, expand_back)
    second_back = channel_parts(contract_last(expand_back, expand_w))
    middle_up, gain_two_grad, shift_two_grad = backward_norm(
        second_back * smooth_slope(norm_two), hat_two, scale_two, count_all, gain_two
    )
    middle_gradient = middle_up.astype(jnp.bfloat16)
    dilated_list = []
    for tap_index in range(9):
        kernel_row, kernel_column = divmod(tap_index, 3)
        sliding_patch = bordered_input[
            kernel_row * DILATION_RATE : kernel_row * DILATION_RATE + rows_per_shard,
            kernel_column * DILATION_RATE : kernel_column * DILATION_RATE + columns_per_shard,
        ].reshape(pixels, M)
        dilated_list.append(contract_first(sliding_patch, middle_gradient))
    dilated_grad = jnp.stack(dilated_list)
    canvas_gradient = with_halo(
        middle_gradient.reshape(rows_per_shard, columns_per_shard, middle_per_shard),
        (("pix", 0),),
        DILATION_RATE,
    )
    canvas_gradient = jnp.pad(canvas_gradient, ((0, 0), (DILATION_RATE, DILATION_RATE), (0, 0)))
    first_part = jnp.zeros((pixels, M), jnp.float32)
    for tap_index in range(9):
        kernel_row, kernel_column = divmod(tap_index, 3)
        sliding_patch = canvas_gradient[
            (2 - kernel_row) * DILATION_RATE : (2 - kernel_row) * DILATION_RATE + rows_per_shard,
            (2 - kernel_column) * DILATION_RATE : (2 - kernel_column) * DILATION_RATE
            + columns_per_shard,
        ].reshape(pixels, middle_per_shard)
        first_part = first_part + contract_last(sliding_patch, dilated_w[tap_index])
    first_back = channel_parts(first_part) * mask_flat[:, None] * smooth_slope(norm_one)
    reduce_up, gain_one_grad, shift_one_grad = backward_norm(
        first_back, hat_one, scale_one, count_all, gain_one
    )
    reduce_all = channel_gather(reduce_up.astype(jnp.bfloat16))
    reduce_grad = contract_first(flat_in, reduce_all)
    input_grad = contract_last(reduce_all, reduce_w) + shared_slope
    reduce_shard, dilated_shard, expand_shard, head_shard, rates_shard, proj_shard = (
        lax.psum_scatter(reduce_grad, "pix", scatter_dimension=1, tiled=True),
        lax.psum_scatter(dilated_grad, "pix", scatter_dimension=1, tiled=True),
        lax.psum_scatter(expand_grad, "pix", scatter_dimension=0, tiled=True),
        lax.psum_scatter(head_grad, "pix", scatter_dimension=1, tiled=True),
        lax.psum_scatter(rates_grad, "pix", scatter_dimension=2, tiled=True),
        lax.psum_scatter(proj_grad, "pix", scatter_dimension=1, tiled=True),
    )
    norm_local = jnp.zeros((2, 2 * M + C), jnp.float32)
    for offset, width, gain_grad, shift_grad in (
        (0, middle_per_shard, gain_one_grad, shift_one_grad),
        (M, middle_per_shard, gain_two_grad, shift_two_grad),
        (2 * M, wide_dev, gain_three_grad, shift_three_grad),
    ):
        norm_local = lax.dynamic_update_slice(
            norm_local, jnp.stack([gain_grad, shift_grad]), (0, offset + block_id * width)
        )
    big_local = (
        jnp.sum(reduce_shard * reduce_shard)
        + jnp.sum(dilated_shard * dilated_shard)
        + jnp.sum(expand_shard * expand_shard)
        + jnp.sum(head_shard * head_shard)
        + jnp.sum(rates_shard * rates_shard)
        + jnp.sum(proj_shard * proj_shard) / groups
    )
    big_squares, norm_grad, small_grad = lax.psum(
        (big_local, norm_local / pix_devices, small_term), ("pix", "ch")
    )
    grad_norm = jnp.sqrt(
        big_squares + jnp.sum(norm_grad * norm_grad) + jnp.sum(small_grad * small_grad)
    )
    factor = jnp.minimum(1.0, CLIP_NORM / (grad_norm + 1e-06))
    reduce_new, reduce_first, reduce_second = adam_step(
        w_reduce, m_reduce, v_reduce, reduce_shard * factor, RATE_MATRIX, DECAY
    )
    dilated_new, dilated_first, dilated_second = adam_step(
        w_dilated, m_dilated, v_dilated, dilated_shard * factor, RATE_MATRIX, DECAY
    )
    expand_new, expand_first, expand_second = adam_step(
        w_expand, m_expand, v_expand, expand_shard * factor, RATE_MATRIX, DECAY
    )
    head_new, head_first, head_second = adam_step(
        head_weight, m_head, v_head, head_shard * factor, RATE_MATRIX, DECAY
    )
    rates_new, rates_first, rates_second = adam_step(
        head_rates, m_rates, v_rates, rates_shard * factor, RATE_MATRIX, DECAY
    )
    proj_new, proj_first, proj_second = adam_step(
        head_proj, m_proj, v_proj, proj_shard * factor, RATE_MATRIX, DECAY
    )
    norm_new, norm_first, norm_second = adam_step(
        norm_params, norm_m, norm_v, norm_grad * factor, RATE_SMALL, 0.0
    )
    small_new, small_first, small_second = adam_step(
        head_small, small_m, small_v, small_grad * factor, RATE_SMALL, 0.0
    )
    depth_bias_grad = small_grad[small_grad.shape[0] - 4]
    return (
        shared.reshape(rows_per_shard, columns_per_shard, wide_dev),
        input_grad.reshape(rows_per_shard, columns_per_shard, wide_dev),
        grad_norm,
        reduce_new,
        reduce_first,
        reduce_second,
        reduce_new.astype(jnp.bfloat16),
        dilated_new,
        dilated_first,
        dilated_second,
        dilated_new.astype(jnp.bfloat16),
        expand_new,
        expand_first,
        expand_second,
        expand_new.astype(jnp.bfloat16),
        head_new,
        head_first,
        head_second,
        head_new.astype(jnp.bfloat16),
        rates_new,
        rates_first,
        rates_second,
        rates_new.astype(jnp.bfloat16),
        proj_new,
        proj_first,
        proj_second,
        proj_new.astype(jnp.bfloat16),
        norm_new,
        norm_first,
        norm_second,
        small_new,
        small_first,
        small_second,
        depth_bias_grad,
    )


MESH = pl.DeviceIdType.MESH
BF = jnp.bfloat16
F32 = jnp.float32
NPIX = 8
NCH = 4
ROWS = 4
WIDTH = 128
PX = ROWS * WIDTH
CIN = C // NCH
COLS = 3 * HID // NPIX
SEGS = COLS // 32
VMEM_LIMIT = 60 * 2**20


REACH = tuple(rate // ROWS for rate in aspp_rates)


def tap_groups():
    groups = []
    first = 0
    for rate_index, step in ((1, -1), (0, -1), (None, 0), (0, 0), (1, 0), (2, 0), (0, 1), (1, 1)):
        if rate_index is None:
            groups.append((0, first, 0, 0, (0,)))
            first += 1
        else:
            rate = aspp_rates[rate_index]
            groups.append((rate_index + 1, first, step, REACH[rate_index], (rate, 0, -rate)))
            first += 3
    return groups


TAP_GROUPS = tap_groups()
TAPS = 22
SEG_ROWS = TAPS * 32
WINDOW = 16 * 32


def window_of(block):
    return jnp.where(block < NPIX - REACH[1], 0, jnp.where(block >= REACH[1], 2, 1))


def whole_vmem():
    return pl.BlockSpec(memory_space=pltpu.VMEM)


def slide(tile, steps):
    lane = lax.broadcasted_iota(jnp.int32, tile.shape, 1)
    if steps == 0:
        return tile
    rolled = pltpu.roll(tile, steps % WIDTH, 1)
    if steps > 0:
        return jnp.where(lane >= steps, rolled, 0.0)
    return jnp.where(lane < WIDTH + steps, rolled, 0.0)


def tanh_parts(values):
    root = 0.7978845608028654
    inner = jnp.tanh(root * (values + 0.044715 * values * values * values))
    return root, inner


def gelu_of(values):
    _, inner = tanh_parts(values)
    return 0.5 * values * (1.0 + inner)


def gelu_slope(values):
    root, inner = tanh_parts(values)
    return 0.5 * (1.0 + inner) + 0.5 * values * (1.0 - inner * inner) * root * (
        1.0 + 3.0 * 0.044715 * values * values
    )


def nt_dot(left, right):
    return lax.dot_general(left, right, (((1,), (1,)), ((), ())), preferred_element_type=F32)


def nn_dot(left, right):
    return lax.dot_general(left, right, (((1,), (0,)), ((), ())), preferred_element_type=F32)


def greet(targets):
    barrier = pltpu.get_barrier_semaphore()
    for target in targets:
        pl.semaphore_signal(barrier, inc=1, device_id=target, device_id_type=MESH)
    pl.semaphore_wait(barrier, len(targets))


def remote(src, dst, send_sem, recv_sem, target):
    return pltpu.make_async_remote_copy(
        src, dst, send_sem, recv_sem, device_id=target, device_id_type=MESH
    )


def place():
    p = lax.axis_index("pix")
    c = lax.axis_index("ch")
    return p, c, p // 2, lax.rem(p, 2), c // 2, lax.rem(c, 2)


def heads_forward_kernel(
    x_ref, w_ref, proj_ref, q_ref, xall_ref, wpt_ref,
    acc, y_tmp, core_buf, core_in, x_buf, x_in, row_buf, local_sem,
    zr_send, zl_send, z_recv, y_send, y_recv, core_send, core_recv, x_send, x_recv, row_send, row_recv,
    pj_send, pj_recv,
):
    p, c, z, y, x, core = place()
    zcount = NPIX // 2
    up = (2 * lax.rem(z + 1, zcount) + y, c)
    down = (2 * lax.rem(z + zcount - 1, zcount) + y, c)
    other_y = (2 * z + 1 - y, c)
    other_core = (p, 2 * x + 1 - core)
    other_x = (p, 2 * (1 - x) + core)
    row_targets = [(lax.rem(p + d, NPIX), c) for d in range(1, NPIX)]
    ch_targets = [(p, lax.rem(c + d, NCH)) for d in range(1, NCH)]
    greet(row_targets + ch_targets)

    own = pltpu.make_async_copy(x_ref, xall_ref.at[p], local_sem.at[0])
    own.start()
    wpt_ref[c] = proj_ref[...]
    proj_copies = [
        remote(proj_ref, wpt_ref.at[c], pj_send.at[d - 1], pj_recv.at[d - 1], ch_targets[d - 1])
        for d in range(1, NCH)
    ]
    for copy in proj_copies:
        copy.start()

    def to_up(source):
        return remote(xall_ref.at[source], xall_ref.at[source], zr_send.at[source // 2], z_recv.at[source // 2], up)

    def to_down(source):
        return remote(xall_ref.at[source], xall_ref.at[source], zl_send.at[source // 2], z_recv.at[source // 2], down)

    def to_y(source):
        return remote(xall_ref.at[source], xall_ref.at[source], y_send.at[source // 2], y_recv.at[source // 2], other_y)

    def step_of(i):
        near = jnp.where(z == 0, i, jnp.where(z == 3, 3 - i, 0))
        one = jnp.where(i == 0, 1, jnp.where(i == 1, 0, i))
        two = jnp.where(i == 0, 2, jnp.where(i == 1, 3, 3 - i))
        two = jnp.where(i == 2, 1, jnp.where(i == 3, 0, two))
        return jnp.where(z == 1, one, jnp.where(z == 2, two, near))

    acc[...] = jnp.zeros_like(acc)
    own.wait()

    def process(src):
        xb = xall_ref[src]

        first_row = pl.multiple_of(window_of(src) * 96, 32)

        def one_seg(s, carry):
            y_tmp[pl.ds(first_row, WINDOW), :] = nt_dot(w_ref[s, pl.ds(first_row, WINDOW), :], xb)

            def add_group(dest, branch, first_tap, shifts):
                rows = pl.ds(pl.multiple_of(branch * COLS + s * 32, 32), 32)
                for r in range(ROWS):
                    lanes = pl.ds(r * WIDTH, WIDTH)
                    total = acc[dest, rows, lanes]
                    for i, shift in enumerate(shifts):
                        tile = y_tmp[pl.ds((first_tap + i) * 32, 32), lanes]
                        total = total + slide(tile, shift)
                    acc[dest, rows, lanes] = total

            for branch, first_tap, step, reach, shifts in TAP_GROUPS:
                dest = src - step * reach
                if step == 0:
                    add_group(dest, branch, first_tap, shifts)
                else:

                    @pl.when((dest >= 0) & (dest < NPIX))
                    def _():
                        add_group(dest, branch, first_tap, shifts)

            return carry

        lax.fori_loop(0, SEGS, one_seg, 0)

    def gather_step(i, carry):
        zs = step_of(i)
        mine = 2 * zs + y
        theirs = 2 * zs + 1 - y

        @pl.when(i > 0)
        def _():
            to_up(mine).wait_recv()

        @pl.when((zs <= z) & (z < zcount - 1))
        def _():
            to_up(mine).start()

        @pl.when((zs >= z) & (z > 0))
        def _():
            to_down(mine).start()

        to_y(mine).start()
        process(mine)
        to_y(theirs).wait_recv()
        process(theirs)
        return carry

    lax.fori_loop(0, zcount, gather_step, 0)

    def drain(zs, carry):
        mine = 2 * zs + y

        @pl.when((zs <= z) & (z < zcount - 1))
        def _():
            to_up(mine).wait_send()

        @pl.when((zs >= z) & (z > 0))
        def _():
            to_down(mine).wait_send()

        to_y(mine).wait_send()
        return carry

    lax.fori_loop(0, zcount, drain, 0)

    def lanes_of(ch):
        return pl.ds(pl.multiple_of(ch * WIDTH, WIDTH), WIDTH)

    def core_copy(b):
        return remote(core_buf.at[b], core_in.at[b], core_send.at[b], core_recv.at[b], other_core)

    def x_copy(b):
        return remote(x_buf.at[b], x_in.at[b], x_send.at[b], x_recv.at[b], other_x)

    def row_copy(b, slot):
        return remote(
            row_buf.at[b],
            q_ref.at[:, pl.ds(pl.multiple_of(COLS * p, 32), COLS), :],
            row_send.at[slot],
            row_recv.at[slot],
            (b, c),
        )

    def core_step(d, carry):
        b = lax.rem(p + d, NPIX)
        for xx in range(2):
            core_buf[b, xx] = acc[b, :, lanes_of(2 * xx + 1 - core)].astype(BF)
        core_copy(b).start()
        return carry

    lax.fori_loop(0, NPIX, core_step, 0)

    def x_step(d, carry):
        b = lax.rem(p + d, NPIX)
        core_copy(b).wait_recv()
        x_buf[b] = (acc[b, :, lanes_of(2 * (1 - x) + core)] + core_in[b, 1 - x].astype(F32)).astype(BF)
        x_copy(b).start()
        return carry

    lax.fori_loop(0, NPIX, x_step, 0)

    def finish(b):
        x_copy(b).wait_recv()
        total = acc[b, :, lanes_of(c)] + core_in[b, x].astype(F32) + x_in[b].astype(F32)
        return total.astype(BF).reshape(4, COLS, WIDTH)

    def row_step(d, carry):
        b = lax.rem(p + d, NPIX)
        row_buf[b] = finish(b)
        row_copy(b, d - 1).start()
        return carry

    lax.fori_loop(1, NPIX, row_step, 0)
    q_ref[:, pl.ds(pl.multiple_of(COLS * p, 32), COLS), :] = finish(p)

    def settle(d, carry):
        b = lax.rem(p + d, NPIX)
        row_copy(b, d - 1).wait()
        return carry

    lax.fori_loop(1, NPIX, settle, 0)

    def settle_more(b, carry):
        core_copy(b).wait_send()
        x_copy(b).wait_send()
        return carry

    lax.fori_loop(0, NPIX, settle_more, 0)
    for copy in proj_copies:
        copy.wait()


def heads_forward(block_out, w_seg, proj_own):
    dma = pltpu.SemaphoreType.DMA
    zc = NPIX // 2
    return pl.pallas_call(
        heads_forward_kernel,
        out_shape=(
            jax.ShapeDtypeStruct((4, 3 * HID, WIDTH), BF),
            jax.ShapeDtypeStruct((NPIX, PX, CIN), BF),
            jax.ShapeDtypeStruct((NCH, 3, HID // NCH, 4 * HID), BF),
        ),
        in_specs=[whole_vmem()] * 3,
        out_specs=[whole_vmem()] * 3,
        scratch_shapes=[
            pltpu.VMEM((NPIX, 4 * COLS, PX), F32),
            pltpu.VMEM((SEG_ROWS, PX), F32),
            pltpu.VMEM((NPIX, 2, 4 * COLS, WIDTH), BF),
            pltpu.VMEM((NPIX, 2, 4 * COLS, WIDTH), BF),
            pltpu.VMEM((NPIX, 4 * COLS, WIDTH), BF),
            pltpu.VMEM((NPIX, 4 * COLS, WIDTH), BF),
            pltpu.VMEM((NPIX, 4, COLS, WIDTH), BF),
            dma((1,)),
            dma((zc,)), dma((zc,)), dma((zc,)), dma((zc,)), dma((zc,)),
            dma((NPIX,)), dma((NPIX,)), dma((NPIX,)), dma((NPIX,)),
            dma((NPIX - 1,)), dma((NPIX - 1,)),
            dma((NCH - 1,)), dma((NCH - 1,)),
        ],
        compiler_params=pltpu.CompilerParams(
            collective_id=1, has_side_effects=True, vmem_limit_bytes=VMEM_LIMIT
        ),
        name="heads_forward",
    )(block_out, w_seg, proj_own)


def heads_middle_kernel(
    q_ref, bias_ref, pbias_ref, wpt_ref, wot_ref, obias_ref, label_ref, target_ref, mask_ref, count_ref,
    dq_ref, dwp_ref, dwo_ref, rows_ref, obg_ref,
    hid,
):
    ones = jnp.ones((8, WIDTH), BF)
    for k in range(4):
        hid[k] = gelu_of(q_ref[k].astype(F32) + bias_ref[:, k : k + 1]).astype(BF)
    row = lax.broadcasted_iota(jnp.int32, (32, WIDTH), 0)
    for t in range(3):
        cols = slice(t * HID, (t + 1) * HID)
        wpt = wpt_ref[:, t].reshape(HID, 4 * HID)
        zt = pbias_ref[:, t : t + 1] + jnp.zeros((HID, WIDTH), F32)
        for k in range(4):
            zt = zt + nn_dot(wpt[:, k * HID : (k + 1) * HID], hid[k, cols, :])
        ut = gelu_of(zt).astype(BF)
        out = lax.dot_general(
            wot_ref[t], ut, (((0,), (0,)), ((), ())), preferred_element_type=F32
        ) + obias_ref[:, t : t + 1]
        scale = mask_ref[t : t + 1, :] / count_ref[t : t + 1, :]
        if t == 0:
            live = row < NCLS
            highest = jnp.max(jnp.where(live, out, -1e30), axis=0, keepdims=True)
            raised = jnp.where(live, jnp.exp(jnp.minimum(out - highest, 0.0)), 0.0)
            probs = raised / jnp.sum(raised, axis=0, keepdims=True)
            onehot = (row == label_ref[0:1, :]).astype(F32)
            slope = scale * (probs - onehot)
        elif t == 1:
            gap = out - target_ref[0:1, :]
            slope = jnp.where(row < 1, scale * gap / jnp.sqrt(gap * gap + 1.0), 0.0)
        else:
            target = jnp.zeros((32, WIDTH), F32)
            for i in range(3):
                target = jnp.where(row == i, target_ref[1 + i : 2 + i, :], target)
            slope = jnp.where(row < 3, scale * (out - target), 0.0)
        ot = slope.astype(BF)
        dwo_ref[t] = nt_dot(ot, ut)
        obg_ref[t] = nt_dot(ones, ot)
        dz = (nn_dot(wot_ref[t], ot) * gelu_slope(zt)).astype(BF)
        rows_ref[4, :, cols] = nt_dot(ones, dz)
        for k in range(4):
            part = hid[k, cols, :]
            dwp_ref[t, k * HID : (k + 1) * HID, :] = nt_dot(part, dz)
            dcat = lax.dot_general(
                wpt[:, k * HID : (k + 1) * HID], dz, (((0,), (0,)), ((), ())),
                preferred_element_type=F32,
            )
            before = q_ref[k, cols, :].astype(F32) + bias_ref[cols, k : k + 1]
            dq_ref[k, cols, :] = (dcat * gelu_slope(before)).astype(BF)
    for k in range(4):
        rows_ref[k] = nt_dot(ones, dq_ref[k])


def heads_middle(q, bias, pbias, wpt, wot, obias, label, target, mask, count):
    return pl.pallas_call(
        heads_middle_kernel,
        out_shape=(
            jax.ShapeDtypeStruct((4, 3 * HID, WIDTH), BF),
            jax.ShapeDtypeStruct((3, 4 * HID, HID), F32),
            jax.ShapeDtypeStruct((3, 32, HID), F32),
            jax.ShapeDtypeStruct((5, 8, 3 * HID), F32),
            jax.ShapeDtypeStruct((3, 8, 32), F32),
        ),
        in_specs=[whole_vmem()] * 10,
        out_specs=[whole_vmem()] * 5,
        scratch_shapes=[pltpu.VMEM((4, 3 * HID, WIDTH), BF)],
        compiler_params=pltpu.CompilerParams(vmem_limit_bytes=VMEM_LIMIT),
        name="heads_middle",
    )(q, bias, pbias, wpt, wot, obias, label, target, mask, count)


def fold(values):
    rows, lanes = values.shape
    total = values[0:8, 0:128]
    for r in range(rows // 8):
        for l in range(lanes // 128):
            if r or l:
                total = total + values[8 * r : 8 * r + 8, 128 * l : 128 * l + 128]
    return total


def moved_segments():
    moves = []
    for pair in range(NPIX // 2):
        tasks = [[(SEGS * (2 * pair + side) + s) * 32 // HID for s in range(SEGS)] for side in range(2)]
        low, high = tasks[0][0], tasks[1][-1]
        if low == high:
            continue
        for side, keeps in ((0, low), (1, high)):
            for s in range(SEGS):
                if tasks[side][s] != keeps:
                    moves.append((2 * pair + side, s, 2 * pair + 1 - side))
    return moves


MOVES = moved_segments()


def heads_backward_kernel(
    dq_ref, xall_ref, w_ref, dw_ref, gz_ref, square_ref,
    dq_all, dq_more, w_more, wt, dcol, dcol_more, work, buf, z_out, oi_in, ac_in, grads,
    gram_own, gram_ch, gram_px, gsum,
    local_sem, row_send, row_recv, x_send, x_recv, ca_send, ca_recv, cb_send, cb_recv,
    more_send, more_recv, fan_send, fan_recv, wm_send, wm_recv,
    y_send, y_recv, oi_send, oi_recv, ac_send, ac_recv, gc_send, gc_recv, gp_send, gp_recv,
):
    p, c, z, y, x, core = place()
    zcount = NPIX // 2
    other_y = (2 * z + 1 - y, c)
    other_core = (p, 2 * x + 1 - core)
    other_x = (p, 2 * (1 - x) + core)
    pix_targets = [(lax.rem(p + d, NPIX), c) for d in range(1, NPIX)]
    ch_targets = [(p, lax.rem(c + d, NCH)) for d in range(1, NCH)]
    greet(pix_targets + ch_targets)
    far = 2 * (1 - x) + core

    def cols_of(b):
        return pl.ds(pl.multiple_of(COLS * b, 32), COLS)

    def row_copy(d):
        b = lax.rem(p + d, NPIX)
        return remote(dq_ref.at[:, cols_of(b), :], dq_all.at[p, c], row_send.at[d - 1], row_recv.at[d - 1], (b, c))

    def more_copy(i, source):
        giver, s, receiver = MOVES[i]
        start = giver * COLS + s * 32
        return remote(
            dq_ref.at[:, start : start + 32, :], dq_more.at[source, c],
            more_send.at[i], more_recv.at[source], (receiver, c),
        )

    def weight_copy(i):
        return remote(w_ref.at[MOVES[i][1]], w_more, wm_send.at[0], wm_recv.at[0], other_y)

    def fan_copy(i, ch, target):
        return remote(dq_more.at[:, ch], dq_more.at[:, ch], fan_send.at[i], fan_recv.at[i], target)

    def any_of(flags):
        total = flags[0]
        for flag in flags[1:]:
            total = total | flag
        return total

    receives = any_of([p == move[2] for move in MOVES])

    for d in range(1, NPIX):
        row_copy(d).start()
    own = pltpu.make_async_copy(dq_ref.at[:, cols_of(p), :], dq_all.at[p, c], local_sem.at[0])
    own.start()
    for i, (giver, s, receiver) in enumerate(MOVES):
        start = giver * COLS + s * 32

        @pl.when(p == receiver)
        def _():
            dq_more[p, c] = dq_ref[:, start : start + 32, :]

        @pl.when(p != receiver)
        def _():
            more_copy(i, p).start()

        @pl.when(p == giver)
        def _():
            weight_copy(i).start()

    own.wait()

    def x_copy(d, b, ch):
        return remote(dq_all.at[b, ch], dq_all.at[b, ch], x_send.at[d], x_recv.at[d], other_x)

    def ca_copy(d, b, ch):
        return remote(dq_all.at[b, ch], dq_all.at[b, ch], ca_send.at[d], ca_recv.at[d], other_core)

    def cb_copy(d, b, ch):
        return remote(dq_all.at[b, ch], dq_all.at[b, ch], cb_send.at[d], cb_recv.at[d], other_core)

    def turn(win, s):
        value = jnp.transpose(w_ref[s, win * 96 : win * 96 + WINDOW, :].astype(F32)).astype(BF)
        lanes = slice(s * WINDOW, (s + 1) * WINDOW)
        givers = [move[0] for move in MOVES if move[1] == s]
        if givers:
            given = any_of([p == giver for giver in givers])
            wt[win, :, lanes] = jnp.where(given, jnp.zeros_like(value), value)
        else:
            wt[win, :, lanes] = value

    pieces = [(win, s) for win in range(3) for s in range(SEGS)]
    for d in range(NPIX):
        b = lax.rem(p + NPIX - d, NPIX)
        if d > 0:
            row_copy(d).wait_recv()
        x_copy(d, b, c).start()
        ca_copy(d, b, c).start()
        if d > 0:
            turn(*pieces[d - 1])
    for piece in pieces[NPIX - 1 :]:
        turn(*piece)

    @pl.when(receives)
    def _():
        for source in range(NPIX):

            @pl.when(p != source)
            def _():
                more_copy(0, source).wait_recv()

        fan_copy(0, c, other_x).start()
        fan_copy(1, c, other_core).start()

    for d in range(NPIX):
        b = lax.rem(p + NPIX - d, NPIX)
        x_copy(d, b, far).wait_recv()
        cb_copy(d, b, far).start()
    dw_ref[...] = jnp.zeros_like(dw_ref)

    @pl.when(receives)
    def _():
        weight_copy(0).wait_recv()
        for win in range(3):
            wt[win, :, SEGS * WINDOW :] = jnp.transpose(
                w_more[win * 96 : win * 96 + WINDOW, :].astype(F32)
            ).astype(BF)
        fan_copy(0, far, other_x).wait_recv()
        fan_copy(2, far, other_core).start()

    for d in range(NPIX):
        b = lax.rem(p + NPIX - d, NPIX)
        ca_copy(d, b, 2 * x + 1 - core).wait_recv()
        cb_copy(d, b, 2 * (1 - x) + 1 - core).wait_recv()

    @pl.when(receives)
    def _():
        fan_copy(1, 2 * x + 1 - core, other_core).wait_recv()
        fan_copy(2, 2 * (1 - x) + 1 - core, other_core).wait_recv()

    def one_block(b):
        win = window_of(b)

        def each_group(visit, clear):
            for branch, first_tap, step, reach, shifts in TAP_GROUPS:
                first_row = first_tap * 32 - win * 96
                source = b - step * reach
                if step == 0:
                    visit(source, branch, first_row, shifts)
                else:
                    in_window = win <= 1 if step < 0 else win >= 1
                    if reach == REACH[1]:
                        in_window = win == 1 + step
                    inside = (source >= 0) & (source < NPIX)

                    @pl.when(inside)
                    def _():
                        visit(source, branch, first_row, shifts)

                    @pl.when(in_window & jnp.logical_not(inside))
                    def _():
                        clear(first_row)

        def visit(source, branch, first_row, shifts):
            for r in range(ROWS):
                lanes = pl.ds(r * WIDTH, WIDTH)
                tile = dq_all[source, r, branch].astype(F32)
                for t, shift in enumerate(shifts):
                    moved = slide(tile, -shift).astype(BF)
                    for s in range(SEGS):
                        rows = pl.ds(pl.multiple_of(s * WINDOW + first_row + t * 32, 32), 32)
                        dcol[b, rows, lanes] = moved[s * 32 : (s + 1) * 32]

        def clear(first_row):
            for s in range(SEGS):
                rows = pl.ds(pl.multiple_of(s * WINDOW + first_row, 32), 96)
                dcol[b, rows, :] = jnp.zeros((96, PX), BF)

        def visit_more(source, branch, first_row, shifts):
            for r in range(ROWS):
                lanes = pl.ds(r * WIDTH, WIDTH)
                tile = dq_more[source, r, branch].astype(F32)
                for t, shift in enumerate(shifts):
                    rows = pl.ds(pl.multiple_of(first_row + t * 32, 32), 32)
                    dcol_more[rows, lanes] = slide(tile, -shift).astype(BF)

        def clear_more(first_row):
            dcol_more[pl.ds(pl.multiple_of(first_row, 32), 96), :] = jnp.zeros((96, PX), BF)

        each_group(visit, clear)
        work[...] = nn_dot(wt[win, :, : SEGS * WINDOW], dcol[b])

        @pl.when(receives)
        def _():
            each_group(visit_more, clear_more)
            work[...] += nn_dot(wt[win, :, SEGS * WINDOW :], dcol_more[...])

        buf[b] = work[...].astype(BF)

    mirrored = z >= 2
    outer = (z == 0) | (z == zcount - 1)
    inner = jnp.logical_not(outer)
    has_near = y == z - 1

    def true_z(e):
        return jnp.where(mirrored, zcount - 1 - e, e)

    def block_at(e):
        return 2 * true_z(e) + y

    def arrived_at(e):
        return NPIX + true_z(e)

    def near_at(e):
        return jnp.where(has_near, block_at(e), arrived_at(e))

    def mid_at(e):
        return jnp.where(has_near, arrived_at(e), block_at(e))

    def y_copy(zz):
        return remote(buf.at[2 * zz + 1 - y], buf.at[NPIX + zz], y_send.at[zz], y_recv.at[zz], other_y)

    oi_z = jnp.where(z == 0, 1, jnp.where(z == 1, 0, jnp.where(z == 2, 3, 2)))

    def oi_copy(i, source):
        return remote(source, oi_in.at[i], oi_send.at[i], oi_recv.at[i], (2 * oi_z + y, c))

    def ac_copy(i, source):
        return remote(source, ac_in.at[i], ac_send.at[i], ac_recv.at[i], (2 * (zcount - 1 - z) + y, c))

    def order(i):
        last = jnp.where(outer, zcount - 1 - i, i - 2)
        return jnp.where(i < 2, zcount - 1 - i, last)

    def sum_of(first, second):
        return (first.astype(F32) + second.astype(F32)).astype(BF)

    def block_pair(i, carry):
        zz = true_z(order(i))

        def either(j, inner_carry):
            one_block(2 * zz + jnp.where(j == 0, 1 - y, y))

            @pl.when(j == 0)
            def _():
                y_copy(zz).start()

            return inner_carry

        lax.fori_loop(0, 2, either, 0)

        @pl.when(i > 0)
        def _():
            y_copy(true_z(order(i - 1))).wait_recv()

        for step in range(1, zcount):

            @pl.when((i == step) & outer)
            def _():
                e = zcount - step
                z_out[step - 1] = sum_of(buf[block_at(e)], buf[arrived_at(e)])
                oi_copy(step - 1, z_out.at[step - 1]).start()

        @pl.when((i == 1) & inner)
        def _():
            ac_copy(0, buf.at[mid_at(3)]).start()

        @pl.when((i == 2) & inner)
        def _():
            ac_copy(1, buf.at[mid_at(2)]).start()
            oi_copy(0, z_out.at[0]).wait_recv()
            z_out[0] = sum_of(oi_in[0], buf[near_at(3)])
            ac_copy(2, z_out.at[0]).start()

        @pl.when((i == 3) & inner)
        def _():
            oi_copy(0, buf.at[near_at(0)]).start()
            oi_copy(1, z_out.at[0]).wait_recv()
            z_out[1] = sum_of(oi_in[1], buf[near_at(2)])
            ac_copy(3, z_out.at[1]).start()

        return carry

    lax.fori_loop(0, zcount, block_pair, 0)

    def weight_block(b, carry):
        first_row = pl.multiple_of(window_of(b) * 96, 32)

        def one_seg(s, inner_carry):
            rows = pl.ds(pl.multiple_of(s * WINDOW, WINDOW), WINDOW)
            dw_ref[s, pl.ds(first_row, WINDOW), :] += nn_dot(dcol[b, rows, :], xall_ref[b])
            return inner_carry

        return lax.fori_loop(0, SEGS, one_seg, carry)

    lax.fori_loop(0, NPIX // 2, weight_block, 0)

    @pl.when(inner)
    def _():
        ac_copy(0, z_out.at[0]).wait_recv()
        z_out[2] = sum_of(ac_in[0], buf[mid_at(0)])
        oi_copy(1, z_out.at[2]).start()
        ac_copy(2, z_out.at[0]).wait_recv()
        oi_copy(2, ac_in.at[2]).start()

    lax.fori_loop(NPIX // 2, NPIX, weight_block, 0)
    square_ref[...] = jnp.zeros_like(square_ref)

    def square_rows(m, carry):
        s = m // TAPS
        part = dw_ref[s, pl.ds(pl.multiple_of(lax.rem(m, TAPS) * 32, 32), 32), :]
        square_ref[...] += fold(part * part)
        return carry

    lax.fori_loop(0, SEGS * TAPS, square_rows, 0)

    near_task = jnp.where(mirrored, 2, 0)
    far_task = jnp.where(mirrored, 0, 2)
    y_copy(true_z(order(zcount - 1))).wait_recv()

    @pl.when(outer)
    def _():
        for i in range(3):
            oi_copy(i, z_out.at[0]).wait_recv()
        grads[near_task] = (
            buf[block_at(0)].astype(F32) + buf[arrived_at(0)].astype(F32) + oi_in[0].astype(F32)
        )
        grads[1] = oi_in[1].astype(F32)
        grads[far_task] = oi_in[2].astype(F32)

    @pl.when(inner)
    def _():
        oi_copy(2, z_out.at[0]).wait_recv()
        ac_copy(1, z_out.at[0]).wait_recv()
        ac_copy(3, z_out.at[0]).wait_recv()
        grads[near_task] = oi_in[2].astype(F32) + buf[near_at(1)].astype(F32)
        grads[1] = buf[mid_at(1)].astype(F32) + ac_in[1].astype(F32)
        grads[far_task] = ac_in[3].astype(F32)

    pairs = ((0, 0), (0, 1), (0, 2), (1, 1), (1, 2), (2, 2))
    gram_own[...] = jnp.zeros_like(gram_own)

    def gram_rows(m, carry):
        rows = pl.ds(pl.multiple_of(m * 32, 32), 32)
        tasks = [grads[t, rows, :] for t in range(3)]
        for i, (a, b) in enumerate(pairs):
            gram_own[i] += fold(tasks[a] * tasks[b])
        return carry

    lax.fori_loop(0, CIN // 32, gram_rows, 0)

    def gc_copy(d):
        return remote(gram_own, gram_ch.at[d - 1], gc_send.at[d - 1], gc_recv.at[d - 1], ch_targets[d - 1])

    for d in range(1, NCH):
        gc_copy(d).start()
    for d in range(1, NCH):
        gc_copy(d).wait()
    gsum[...] = gram_own[...] + gram_ch[0] + gram_ch[1] + gram_ch[2]

    def gp_copy(d):
        return remote(gsum, gram_px.at[d - 1], gp_send.at[d - 1], gp_recv.at[d - 1], pix_targets[d - 1])

    for d in range(1, NPIX):
        gp_copy(d).start()
    for d in range(1, NPIX):
        gp_copy(d).wait()
    entry = {}
    for i, (a, b) in enumerate(pairs):
        total = gsum[i]
        for d in range(NPIX - 1):
            total = total + gram_px[d, i]
        value = jnp.sum(total, axis=0, keepdims=True)
        value = jnp.sum(value, axis=1, keepdims=True)
        entry[(a, b)] = value
        entry[(b, a)] = value
    lengths = [jnp.sqrt(entry[(t, t)] + 1e-12) for t in range(3)]

    def pairing(row_task, col_task):
        return (
            entry[(0, 0)] / lengths[0]
            - entry[(0, col_task)] / lengths[col_task]
            - entry[(row_task, 0)] / lengths[0]
            + entry[(row_task, col_task)] / lengths[col_task]
        )

    right_one = entry[(0, 0)] / lengths[0] - entry[(0, 1)] / lengths[1]
    right_two = entry[(0, 0)] / lengths[0] - entry[(0, 2)] / lengths[2]
    upper_left, upper_right = pairing(1, 1), pairing(1, 2)
    lower_left, lower_right = pairing(2, 1), pairing(2, 2)
    determinant = upper_left * lower_right - upper_right * lower_left
    alpha_one = (right_one * lower_right - right_two * lower_left) / determinant
    alpha_two = (right_two * upper_left - right_one * upper_right) / determinant
    alpha_zero = 1.0 - alpha_one - alpha_two

    for m in range(CIN // 128):
        rows = pl.ds(m * 128, 128)
        mixed = alpha_zero * grads[0, rows, :] + alpha_one * grads[1, rows, :] + alpha_two * grads[2, rows, :]
        gz_ref[:, m * 128 : (m + 1) * 128] = jnp.transpose(mixed)

    for d in range(1, NPIX):
        row_copy(d).wait_send()
    for d in range(NPIX):
        b = lax.rem(p + NPIX - d, NPIX)
        x_copy(d, b, c).wait_send()
        ca_copy(d, b, c).wait_send()
        cb_copy(d, b, far).wait_send()
    for i, (giver, s, receiver) in enumerate(MOVES):

        @pl.when(p != receiver)
        def _():
            more_copy(i, p).wait_send()

        @pl.when(p == giver)
        def _():
            weight_copy(i).wait_send()

    @pl.when(receives)
    def _():
        fan_copy(0, c, other_x).wait_send()
        fan_copy(1, c, other_core).wait_send()
        fan_copy(2, far, other_core).wait_send()

    for i in range(zcount):
        y_copy(i).wait_send()
    for i in range(3):
        oi_copy(i, z_out.at[0]).wait_send()

    @pl.when(inner)
    def _():
        for i in range(4):
            ac_copy(i, z_out.at[0]).wait_send()


def heads_backward(dq, xall, w_seg):
    dma = pltpu.SemaphoreType.DMA
    zc = NPIX // 2
    return pl.pallas_call(
        heads_backward_kernel,
        out_shape=(
            jax.ShapeDtypeStruct((SEGS, SEG_ROWS, CIN), F32),
            jax.ShapeDtypeStruct((PX, CIN), F32),
            jax.ShapeDtypeStruct((8, 128), F32),
        ),
        in_specs=[whole_vmem()] * 3,
        out_specs=[whole_vmem()] * 3,
        scratch_shapes=[
            pltpu.VMEM((NPIX, NCH, 4, COLS, WIDTH), BF),
            pltpu.VMEM((NPIX, NCH, 4, 32, WIDTH), BF),
            pltpu.VMEM((SEG_ROWS, CIN), BF),
            pltpu.VMEM((3, CIN, (SEGS + 1) * WINDOW), BF),
            pltpu.VMEM((NPIX, SEGS * WINDOW, PX), BF),
            pltpu.VMEM((WINDOW, PX), BF),
            pltpu.VMEM((CIN, PX), F32),
            pltpu.VMEM((NPIX + zc, CIN, PX), BF),
            pltpu.VMEM((3, CIN, PX), BF),
            pltpu.VMEM((3, CIN, PX), BF),
            pltpu.VMEM((4, CIN, PX), BF),
            pltpu.VMEM((3, CIN, PX), F32),
            pltpu.VMEM((6, 8, 128), F32),
            pltpu.VMEM((NCH - 1, 6, 8, 128), F32),
            pltpu.VMEM((NPIX - 1, 6, 8, 128), F32),
            pltpu.VMEM((6, 8, 128), F32),
            dma((1,)),
            dma((NPIX - 1,)), dma((NPIX - 1,)),
            dma((NPIX,)), dma((NPIX,)), dma((NPIX,)), dma((NPIX,)), dma((NPIX,)), dma((NPIX,)),
            dma((len(MOVES),)), dma((NPIX,)), dma((3,)), dma((3,)), dma((1,)), dma((1,)),
            dma((zc,)), dma((zc,)), dma((3,)), dma((3,)), dma((4,)), dma((4,)),
            dma((NCH - 1,)), dma((NCH - 1,)),
            dma((NPIX - 1,)), dma((NPIX - 1,)),
        ],
        compiler_params=pltpu.CompilerParams(
            collective_id=2, has_side_effects=True, vmem_limit_bytes=VMEM_LIMIT
        ),
        name="heads_backward",
    )(dq, xall, w_seg)


def tap_weights(head_weight, head_rates):
    rates = head_rates.astype(BF)
    pieces = []
    for branch, first, step, reach, shifts in TAP_GROUPS:
        if branch == 0:
            pieces.append(jnp.transpose(head_weight.astype(BF))[None])
        else:
            pieces.append(rates[branch - 1, 3 * (step + 1) : 3 * (step + 2)])
    taps = jnp.concatenate(pieces, axis=0)
    taps = taps.reshape(TAPS, SEGS, 32, CIN).transpose(1, 0, 2, 3)
    return taps.reshape(SEGS, SEG_ROWS, CIN)


def tap_grads(dw):
    taps = dw.reshape(SEGS, TAPS, 32, CIN).transpose(1, 0, 2, 3).reshape(TAPS, COLS, CIN)
    at = {(group[0], group[2]): group[1] for group in TAP_GROUPS}
    head = jnp.transpose(taps[at[(0, 0)]])
    rates = []
    for rate_index in range(3):
        for step in (-1, 0, 1):
            first = at.get((rate_index + 1, step))
            rates.append(jnp.zeros((3, COLS, CIN), F32) if first is None else taps[first : first + 3])
    return head, jnp.stack(rates).reshape(3, 9, COLS, CIN)


MID = M // NCH
WPART = M // NPIX
TAP_LANES = 9 * MID
W_REDUCE = slice(0, CIN)
W_DILATED = slice(CIN, CIN + TAP_LANES)
W_EXPAND = slice(CIN + TAP_LANES, 2 * CIN + TAP_LANES)
W_LANES = 2 * CIN + TAP_LANES
SMALL_ROWS = 80


def slide_rows(tile, steps):
    if steps == 0:
        return tile
    line = lax.broadcasted_iota(jnp.int32, (WIDTH, tile.shape[1]), 0)
    keep = line >= steps if steps > 0 else line < WIDTH + steps
    pieces = []
    for r in range(ROWS):
        rolled = pltpu.roll(tile[r * WIDTH : (r + 1) * WIDTH], steps % WIDTH, 0)
        pieces.append(jnp.where(keep, rolled, 0.0))
    return jnp.concatenate(pieces, axis=0)


def column_sums(values):
    return jnp.sum(values, axis=0, keepdims=True)


def pix_copies(inbox, send_sem, recv_sem):
    p, c = lax.axis_index("pix"), lax.axis_index("ch")
    return [
        remote(inbox.at[p], inbox.at[p], send_sem.at[d - 1], recv_sem.at[d - 1], (lax.rem(p + d, NPIX), c))
        for d in range(1, NPIX)
    ]


def ch_copies(source, inbox, send_sem, recv_sem):
    p, c = lax.axis_index("pix"), lax.axis_index("ch")
    copies = []
    for d in range(1, NCH):
        other = lax.rem(c + d, NCH)
        copies.append(remote(source(other), inbox.at[c], send_sem.at[d - 1], recv_sem.at[d - 1], (p, other)))
    return copies


def start_all(copies):
    for copy in copies:
        copy.start()


def wait_all(copies):
    for copy in copies:
        copy.wait()


def add_up(inbox):
    total = inbox[0]
    for i in range(1, inbox.shape[0]):
        total = total + inbox[i]
    return total


def block_forward_kernel(
    x_ref, mask_ref, w_ref, proj_ref, narrow_ref, wide_ref,
    out_ref, hat_one_ref, hat_two_ref, hat_three_ref, wall_ref, first_ref, second_ref, stats_ref, stats_wide_ref, wpt_ref,
    work, ch_buf, ch_in, halo_buf, halo_in, stat_one, stat_two, stat_three,
    local_sem, wz_send, wz_recv, wy_send, wy_recv, c_send, c_recv, s_send, s_recv, h_send, h_recv,
):
    p, c, z, y, x, core = place()
    zcount = NPIX // 2
    other_y = (2 * z + 1 - y, c)
    pix_targets = [(lax.rem(p + d, NPIX), c) for d in range(1, NPIX)]
    ch_targets = [(p, lax.rem(c + d, NCH)) for d in range(1, NCH)]
    greet(pix_targets + ch_targets)
    parts = (pl.ds(0, CIN), pl.ds(CIN, TAP_LANES), pl.ds(CIN + TAP_LANES, CIN))

    def shard(part):
        return w_ref.at[:, parts[part]] if part < 3 else proj_ref

    def spot(part, source):
        if part < 3:
            return wall_ref.at[source, :, parts[part]]
        return wpt_ref.at[:, :, pl.ds(pl.multiple_of(source * 128, 128), 128)]

    def wz_copy(part, d):
        target = (2 * lax.rem(z + d, zcount) + y, c)
        return remote(
            shard(part), spot(part, p),
            wz_send.at[part, d - 1], wz_recv.at[part, d - 1], target,
        )

    def wy_copy(part, d):
        source = 2 * lax.rem(z + zcount - d, zcount) + y
        src = shard(part) if d == 0 else spot(part, source)
        return remote(
            src, spot(part, source), wy_send.at[part, d], wy_recv.at[part, d], other_y
        )

    for part in range(4):
        wy_copy(part, 0).start()
        for d in range(1, zcount):
            wz_copy(part, d).start()
    own = pltpu.make_async_copy(w_ref, wall_ref.at[p], local_sem.at[0])
    own.start()
    own_proj = pltpu.make_async_copy(proj_ref, spot(3, p), local_sem.at[1])
    own_proj.start()
    own.wait()
    own_proj.wait()

    def forward_part(part):
        for d in range(1, zcount):
            wz_copy(part, d).wait_recv()
            wy_copy(part, d).start()

    def receive_part(part):
        for d in range(zcount):
            wy_copy(part, d).wait_recv()

    def weights(lanes):
        return wall_ref[:, :, lanes].reshape(M, lanes.stop - lanes.start)

    def stat_round(index, inbox, values):
        if index > 0:
            inbox[p] = jnp.zeros_like(inbox[p])
        inbox[p, 0:1, :] = column_sums(values)
        inbox[p, 1:2, :] = column_sums(values * values)
        copies = pix_copies(inbox, s_send.at[index], s_recv.at[index])
        start_all(copies)
        wait_all(copies)
        return add_up(inbox)

    count_all = float(NPIX * PX)

    def norm_of(values, sums, gain, shift):
        mean = sums[0:1] / count_all
        scale = lax.rsqrt(sums[1:2] / count_all - mean * mean + EPS_NORM)
        hat = (values - mean) * scale
        return hat, hat * gain + shift, scale

    forward_part(0)
    receive_part(0)
    for m in range(NCH):
        wanted = wall_ref[2 * m : 2 * m + 2, :, W_REDUCE].reshape(MID, CIN)
        value = nt_dot(x_ref[...], wanted)
        ch_buf[0, m] = value.astype(BF)

        @pl.when(m == c)
        def _():
            work[...] = value

    reduce_copies = ch_copies(lambda other: ch_buf.at[0, other], ch_in, c_send.at[0], c_recv.at[0])
    start_all(reduce_copies)
    wait_all(reduce_copies)
    reduced = work[...]
    for d in range(1, NCH):
        reduced = reduced + ch_in[lax.rem(c + d, NCH)].astype(F32)
    stat_one[p] = jnp.zeros((8, MID), F32)
    stat_one[p, 2:3, :] = narrow_ref[4:5, :]
    sums = stat_round(0, stat_one, reduced)
    hat, normed, scale = norm_of(reduced, sums, narrow_ref[0:1, :], narrow_ref[1:2, :])
    hat_one_ref[...] = hat
    stats_ref[...] = jnp.zeros_like(stats_ref)
    stats_ref[0:1, :] = scale
    stats_ref[2:3, :] = jnp.maximum(sums[2:3], 1.0)

    def own_lanes():
        return pl.ds(pl.multiple_of(c * MID, MID), MID)

    def gather_copies(ref, index):
        copies = []
        for d in range(1, NCH):
            copies.append(
                remote(
                    ref.at[:, own_lanes()], ref.at[:, own_lanes()],
                    c_send.at[index, d - 1], c_recv.at[index, d - 1], ch_targets[d - 1],
                )
            )
        return copies

    first_ref[:, own_lanes()] = (gelu_of(normed) * mask_ref[...]).astype(BF)
    copies = gather_copies(first_ref, 1)
    start_all(copies)
    forward_part(1)
    wait_all(copies)
    receive_part(1)

    def row_part(step):
        total = jnp.zeros((PX, MID), F32)
        for col in range(3):
            tap = 3 * (step + 1) + col
            lanes = slice(CIN + tap * MID, CIN + (tap + 1) * MID)
            total = total + slide_rows(nn_dot(first_ref[...], weights(lanes)), -DILATION_RATE * (col - 1))
        return total

    def halo_copy(side):
        target = (p - 1, c) if side == 0 else (p + 1, c)
        return remote(halo_buf.at[side], halo_in.at[side], h_send.at[side], h_recv.at[side], target)

    halo_buf[0] = row_part(1).astype(BF)

    @pl.when(p > 0)
    def _():
        halo_copy(0).start()

    halo_buf[1] = row_part(-1).astype(BF)

    @pl.when(p < NPIX - 1)
    def _():
        halo_copy(1).start()

    work[...] = row_part(0)

    @pl.when(p < NPIX - 1)
    def _():
        halo_copy(0).wait_recv()
        work[...] += halo_in[0].astype(F32)

    @pl.when(p > 0)
    def _():
        halo_copy(1).wait_recv()
        work[...] += halo_in[1].astype(F32)

    forward_part(2)
    middle = work[...]
    sums = stat_round(1, stat_two, middle)
    hat, normed, scale = norm_of(middle, sums, narrow_ref[2:3, :], narrow_ref[3:4, :])
    hat_two_ref[...] = hat
    stats_ref[1:2, :] = scale
    second_ref[:, own_lanes()] = gelu_of(normed).astype(BF)
    copies = gather_copies(second_ref, 2)
    start_all(copies)
    wait_all(copies)

    receive_part(2)
    hat_three_ref[...] = nn_dot(second_ref[...], weights(W_EXPAND))
    expanded = hat_three_ref[...]
    forward_part(3)
    sums = stat_round(2, stat_three, expanded)
    hat, normed, scale = norm_of(expanded, sums, wide_ref[0:1, :], wide_ref[1:2, :])
    hat_three_ref[...] = hat
    stats_wide_ref[...] = jnp.broadcast_to(scale, stats_wide_ref.shape)
    out_ref[...] = gelu_of(normed + x_ref[...].astype(F32)).astype(BF)
    receive_part(3)

    for part in range(4):
        for d in range(zcount):
            wy_copy(part, d).wait_send()
        for d in range(1, zcount):
            wz_copy(part, d).wait_send()

    @pl.when(p > 0)
    def _():
        halo_copy(0).wait_send()

    @pl.when(p < NPIX - 1)
    def _():
        halo_copy(1).wait_send()


def block_forward(flat_in, mask, w_shard, proj_shard, narrow, wide):
    dma = pltpu.SemaphoreType.DMA
    zc = NPIX // 2
    shape = jax.ShapeDtypeStruct
    return pl.pallas_call(
        block_forward_kernel,
        out_shape=(
            shape((PX, CIN), BF),
            shape((PX, MID), F32),
            shape((PX, MID), F32),
            shape((PX, CIN), F32),
            shape((NPIX, WPART, W_LANES), BF),
            shape((PX, M), BF),
            shape((PX, M), BF),
            shape((8, MID), F32),
            shape((8, CIN), F32),
            shape((3, HID // NCH, 4 * HID), BF),
        ),
        in_specs=[whole_vmem()] * 6,
        out_specs=[whole_vmem()] * 10,
        scratch_shapes=[
            pltpu.VMEM((PX, MID), F32),
            pltpu.VMEM((1, NCH, PX, MID), BF),
            pltpu.VMEM((NCH, PX, MID), BF),
            pltpu.VMEM((2, PX, MID), BF),
            pltpu.VMEM((2, PX, MID), BF),
            pltpu.VMEM((NPIX, 8, MID), F32),
            pltpu.VMEM((NPIX, 8, MID), F32),
            pltpu.VMEM((NPIX, 8, CIN), F32),
            dma((2,)),
            dma((4, zc - 1)), dma((4, zc - 1)), dma((4, zc)), dma((4, zc)),
            dma((3, NCH - 1)), dma((3, NCH - 1)),
            dma((3, NPIX - 1)), dma((3, NPIX - 1)),
            dma((2,)), dma((2,)),
        ],
        compiler_params=pltpu.CompilerParams(
            collective_id=0, has_side_effects=True, vmem_limit_bytes=VMEM_LIMIT
        ),
        name="block_forward",
    )(flat_in, mask, w_shard, proj_shard, narrow, wide)


def block_backward_kernel(
    gz_ref, x_ref, mask_ref, wall_ref, hat_one_ref, hat_two_ref, hat_three_ref, first_ref, second_ref,
    narrow_ref, wide_ref, stats_ref, stats_wide_ref, dwp_ref, small_ref, square_ref,
    ingrad_ref, wgrad_ref, pgrad_ref, sgrad_ref, ngrad_ref, ngrad_wide_ref, total_ref,
    ds, ds_low, turned, ch_buf, ch_in, halo_in, taps, back_t, stat_three, stat_two, stat_one,
    we_buf, we_in, wd_buf, wd_in, wr_buf, wr_in, pc_buf, pc_in, pr_buf, pr_in, pg_in,
    small_ch, small_px, sq_ch, sq_px, norm_in, norm_wide_in,
    c_send, c_recv, s_send, s_recv, h_send, h_recv, g_send, g_recv,
    pc_send, pc_recv, pg_send, pg_recv, t_send, t_recv, u_send, u_recv, n_send, n_recv,
):
    p, c, z, y, x, core = place()
    pix_targets = [(lax.rem(p + d, NPIX), c) for d in range(1, NPIX)]
    ch_targets = [(p, lax.rem(c + d, NCH)) for d in range(1, NCH)]
    greet(pix_targets + ch_targets)
    count_all = float(NPIX * PX)

    def weights(lanes):
        return wall_ref[:, :, lanes].reshape(M, lanes.stop - lanes.start)

    def own_lanes():
        return pl.ds(pl.multiple_of(c * MID, MID), MID)

    def stat_round(index, inbox, upstream, hat):
        inbox[p] = jnp.zeros_like(inbox[p])
        inbox[p, 0:1, :] = column_sums(upstream)
        inbox[p, 1:2, :] = column_sums(upstream * hat)
        copies = pix_copies(inbox, s_send.at[index], s_recv.at[index])
        start_all(copies)
        return copies

    def stat_end(copies, inbox):
        wait_all(copies)
        return add_up(inbox)

    def norm_back(upstream, hat, sums, gain, scale):
        return gain * scale * (upstream - sums[0:1] / count_all - hat * (sums[1:2] / count_all))

    def own_ch_copies(ref, inbox_index):
        copies = []
        for d in range(1, NCH):
            copies.append(
                remote(ref.at[c], ref.at[c], n_send.at[inbox_index, d - 1], n_recv.at[inbox_index, d - 1], ch_targets[d - 1])
            )
        return copies

    small_ch[c] = small_ref[...]
    small_copies = own_ch_copies(small_ch, 0)
    start_all(small_copies)

    for other in range(NCH):
        for t in range(3):
            for b in range(NPIX):
                start = b * 128 + other * 32
                pc_buf[other, t, b] = dwp_ref[t, start : start + 32, :].astype(BF)
    proj_copies = ch_copies(lambda other: pc_buf.at[other], pc_in, pc_send, pc_recv)

    wide_rows = 64

    def expand_rows(m, carry):
        rows = pl.ds(pl.multiple_of(m * wide_rows, wide_rows), wide_rows)
        summed = hat_three_ref[rows, :] * wide_ref[0:1, :] + wide_ref[1:2, :] + x_ref[rows, :].astype(F32)
        ds[rows, :] = gz_ref[rows, :] * gelu_slope(summed)
        return carry

    lax.fori_loop(0, PX // wide_rows, expand_rows, 0)
    copies = stat_round(0, stat_three, ds[...], hat_three_ref[...])
    start_all(proj_copies)
    turned[0] = jnp.transpose(second_ref[...].astype(F32)).astype(BF)
    turned[1] = jnp.transpose(first_ref[...].astype(F32)).astype(BF)
    sums = stat_end(copies, stat_three)
    norm_wide_in[c] = sums
    ds_low[...] = norm_back(ds[...], hat_three_ref[...], sums, wide_ref[0:1, :], stats_wide_ref[0:1, :]).astype(BF)

    def scatter_ch(index, product):
        for m in range(NCH):
            value = product(m)
            ch_buf[index, m] = value.astype(BF)
        copies = ch_copies(lambda other: ch_buf.at[index, other], ch_in.at[index], c_send.at[index], c_recv.at[index])
        start_all(copies)
        return copies

    def scatter_end(index, copies):
        wait_all(copies)
        total = ch_buf[index, c].astype(F32)
        for d in range(1, NCH):
            total = total + ch_in[index, lax.rem(c + d, NCH)].astype(F32)
        return total

    def grad_copies(index, buf, inbox):
        copies = []
        for d in range(1, NPIX):
            b = lax.rem(p + d, NPIX)
            copies.append(
                remote(buf.at[b], inbox.at[d - 1], g_send.at[index, d - 1], g_recv.at[index, d - 1], (b, c))
            )
        return copies

    def expand_back(m):
        wanted = wall_ref[2 * m : 2 * m + 2, :, W_EXPAND].reshape(MID, CIN)
        return nt_dot(ds_low[...], wanted)

    copies = scatter_ch(0, expand_back)
    we_buf[...] = nn_dot(turned[0], ds_low[...]).astype(BF).reshape(NPIX, WPART, CIN)
    we_copies = grad_copies(0, we_buf, we_in)
    start_all(we_copies)
    hat = hat_two_ref[...]
    slope = gelu_slope(hat * narrow_ref[2:3, :] + narrow_ref[3:4, :])
    upstream = scatter_end(0, copies) * slope
    copies = stat_round(1, stat_two, upstream, hat)
    wait_all(proj_copies)
    for t in range(3):
        total = pc_buf[c, t].astype(F32)
        for d in range(1, NCH):
            total = total + pc_in[lax.rem(c + d, NCH), t].astype(F32)
        pr_buf[:, t] = total.astype(BF)
    wait_all(small_copies)
    small_px[p] = add_up(small_ch)
    sums = stat_end(copies, stat_two)
    norm_in[c, 2:4, :] = sums[0:2]

    def halo_copy(side):
        target = (p - 1, c) if side == 0 else (p + 1, c)
        return remote(back_t.at[0], halo_in.at[side], h_send.at[side], h_recv.at[side], target)

    gradient = norm_back(upstream, hat, sums, narrow_ref[2:3, :], stats_ref[1:2, :])
    back_t[0] = gradient.astype(BF)

    @pl.when(p > 0)
    def _():
        halo_copy(0).start()

    @pl.when(p < NPIX - 1)
    def _():
        halo_copy(1).start()

    def fill_taps(step, source):
        for col in range(3):
            tap = 3 * (step + 1) + col
            moved = slide_rows(source.astype(F32), DILATION_RATE * (col - 1))
            taps[:, tap * MID : (tap + 1) * MID] = moved.astype(BF)

    fill_taps(0, back_t[0])

    @pl.when(p < NPIX - 1)
    def _():
        halo_copy(0).wait_recv()

    @pl.when(p == NPIX - 1)
    def _():
        halo_in[0] = jnp.zeros((PX, MID), BF)

    fill_taps(-1, halo_in[0])

    @pl.when(p > 0)
    def _():
        halo_copy(1).wait_recv()

    @pl.when(p == 0)
    def _():
        halo_in[1] = jnp.zeros((PX, MID), BF)

    fill_taps(1, halo_in[1])

    def dilated_back(m):
        wanted = wall_ref[2 * m : 2 * m + 2, :, W_DILATED].reshape(MID, TAP_LANES)
        return nt_dot(taps[...], wanted)

    copies = scatter_ch(1, dilated_back)
    proj_rows = grad_copies(3, pr_buf, pr_in)
    start_all(proj_rows)
    for m in range(NPIX):
        wd_buf[m] = nn_dot(turned[1, m * WPART : (m + 1) * WPART, :], taps[...]).astype(BF)
    wd_copies = grad_copies(1, wd_buf, wd_in)
    start_all(wd_copies)
    hat = hat_one_ref[...]
    slope = gelu_slope(hat * narrow_ref[0:1, :] + narrow_ref[1:2, :]) * mask_ref[...]
    upstream = scatter_end(1, copies) * slope
    copies = stat_round(2, stat_one, upstream, hat)
    small_rows = [
        remote(small_px.at[p], small_px.at[p], t_send.at[d - 1], t_recv.at[d - 1], pix_targets[d - 1])
        for d in range(1, NPIX)
    ]
    start_all(small_rows)
    sums = stat_end(copies, stat_one)
    norm_in[c, 0:2, :] = sums[0:2]
    norm_in[c, 4:8, :] = jnp.zeros((4, MID), F32)
    gradient = norm_back(upstream, hat, sums, narrow_ref[0:1, :], stats_ref[0:1, :])

    own_rows = pl.ds(pl.multiple_of(c * MID, MID), MID)
    turned[2, own_rows, :] = jnp.transpose(gradient).astype(BF)
    copies = [
        remote(
            turned.at[2, own_rows, :], turned.at[2, own_rows, :],
            c_send.at[2, d - 1], c_recv.at[2, d - 1], ch_targets[d - 1],
        )
        for d in range(1, NCH)
    ]
    start_all(copies)
    norm_copies = own_ch_copies(norm_in, 1) + own_ch_copies(norm_wide_in, 2)
    start_all(norm_copies)
    wait_all(copies)
    wr_buf[...] = nn_dot(turned[2], x_ref[...]).astype(BF).reshape(NPIX, WPART, CIN)
    wr_copies = grad_copies(2, wr_buf, wr_in)
    start_all(wr_copies)
    full = jnp.transpose(turned[2].astype(F32)).astype(BF)
    ingrad_ref[...] = nn_dot(full, weights(W_REDUCE)) + ds[...]
    wait_all(proj_rows)
    for t in range(3):
        total = pr_buf[p, t].astype(F32)
        for d in range(NPIX - 1):
            total = total + pr_in[d, t].astype(F32)
        pg_in[c, t] = total
    pg_copies = [
        remote(pg_in.at[c], pg_in.at[c], pg_send.at[d - 1], pg_recv.at[d - 1], ch_targets[d - 1])
        for d in range(1, NCH)
    ]
    start_all(pg_copies)

    def grad_end(copies, buf, inbox, lanes):
        wait_all(copies)
        total = buf[p].astype(F32)
        for d in range(NPIX - 1):
            total = total + inbox[d].astype(F32)
        wgrad_ref[:, lanes] = total
        return fold(total * total)

    squares = square_ref[...] + grad_end(we_copies, we_buf, we_in, W_EXPAND)
    squares = squares + grad_end(wd_copies, wd_buf, wd_in, W_DILATED)
    wait_all(pg_copies)
    for t in range(3):
        for other in range(NCH):
            pgrad_ref[t, other * 32 : (other + 1) * 32, :] = pg_in[other, t]
        squares = squares + fold(pg_in[c, t] * pg_in[c, t])
    wait_all(small_rows)
    sgrad_ref[...] = add_up(small_px)
    wait_all(norm_copies)
    ngrad_ref[...] = norm_in[...]
    ngrad_wide_ref[...] = norm_wide_in[...]
    shared = fold(sgrad_ref[...] * sgrad_ref[...])
    for other in range(NCH):
        shared = shared + fold(norm_in[other] * norm_in[other])
        piece = norm_wide_in[other]
        shared = shared + fold(piece * piece)
    squares = squares + grad_end(wr_copies, wr_buf, wr_in, W_REDUCE)
    sq_ch[c] = squares
    copies = [
        remote(sq_ch.at[c], sq_ch.at[c], u_send.at[0, d - 1], u_recv.at[0, d - 1], ch_targets[d - 1])
        for d in range(1, NCH)
    ]
    start_all(copies)
    wait_all(copies)
    sq_px[p] = add_up(sq_ch)
    copies = [
        remote(sq_px.at[p], sq_px.at[p], u_send.at[1, d - 1], u_recv.at[1, d - 1], pix_targets[d - 1])
        for d in range(1, NPIX)
    ]
    start_all(copies)
    wait_all(copies)
    everything = add_up(sq_px) + shared
    total = jnp.sum(jnp.sum(everything, axis=0, keepdims=True), axis=1, keepdims=True)
    norm = jnp.sqrt(total)
    factor = jnp.minimum(1.0, CLIP_NORM / (norm + 1e-06))
    line = lax.broadcasted_iota(jnp.int32, (8, 128), 0)
    total_ref[...] = jnp.where(line == 0, norm, factor)

    @pl.when(p > 0)
    def _():
        halo_copy(0).wait_send()

    @pl.when(p < NPIX - 1)
    def _():
        halo_copy(1).wait_send()


def block_backward(*operands):
    dma = pltpu.SemaphoreType.DMA
    shape = jax.ShapeDtypeStruct
    vmem = pltpu.VMEM
    return pl.pallas_call(
        block_backward_kernel,
        out_shape=(
            shape((PX, CIN), F32),
            shape((WPART, W_LANES), F32),
            shape((3, 128, HID), F32),
            shape((SMALL_ROWS, 128), F32),
            shape((NCH, 8, MID), F32),
            shape((NCH, 8, CIN), F32),
            shape((8, 128), F32),
        ),
        in_specs=[whole_vmem()] * 16,
        out_specs=[whole_vmem()] * 7,
        scratch_shapes=[
            vmem((PX, CIN), F32),
            vmem((PX, CIN), BF),
            vmem((3, M, PX), BF),
            vmem((2, NCH, PX, MID), BF),
            vmem((2, NCH, PX, MID), BF),
            vmem((2, PX, MID), BF),
            vmem((PX, TAP_LANES), BF),
            vmem((1, PX, MID), BF),
            vmem((NPIX, 8, CIN), F32),
            vmem((NPIX, 8, MID), F32),
            vmem((NPIX, 8, MID), F32),
            vmem((NPIX, WPART, CIN), BF),
            vmem((NPIX - 1, WPART, CIN), BF),
            vmem((NPIX, WPART, TAP_LANES), BF),
            vmem((NPIX - 1, WPART, TAP_LANES), BF),
            vmem((NPIX, WPART, CIN), BF),
            vmem((NPIX - 1, WPART, CIN), BF),
            vmem((NCH, 3, NPIX, 32, HID), BF),
            vmem((NCH, 3, NPIX, 32, HID), BF),
            vmem((NPIX, 3, 32, HID), BF),
            vmem((NPIX - 1, 3, 32, HID), BF),
            vmem((NCH, 3, 32, HID), F32),
            vmem((NCH, SMALL_ROWS, 128), F32),
            vmem((NPIX, SMALL_ROWS, 128), F32),
            vmem((NCH, 8, 128), F32),
            vmem((NPIX, 8, 128), F32),
            vmem((NCH, 8, MID), F32),
            vmem((NCH, 8, CIN), F32),
            dma((3, NCH - 1)), dma((3, NCH - 1)),
            dma((3, NPIX - 1)), dma((3, NPIX - 1)),
            dma((2,)), dma((2,)),
            dma((4, NPIX - 1)), dma((4, NPIX - 1)),
            dma((NCH - 1,)), dma((NCH - 1,)),
            dma((NCH - 1,)), dma((NCH - 1,)),
            dma((NPIX - 1,)), dma((NPIX - 1,)),
            dma((2, NPIX - 1)), dma((2, NPIX - 1)),
            dma((3, NCH - 1)), dma((3, NCH - 1)),
        ],
        compiler_params=pltpu.CompilerParams(
            collective_id=3, has_side_effects=True, vmem_limit_bytes=VMEM_LIMIT
        ),
        name="block_backward",
    )(*operands)


def per_device_rows(
    features,
    valid_mask,
    sem_label,
    depth_target,
    normal_target,
    label_mask,
    w_reduce,
    m_reduce,
    v_reduce,
    w_dilated,
    m_dilated,
    v_dilated,
    w_expand,
    m_expand,
    v_expand,
    head_weight,
    m_head,
    v_head,
    head_rates,
    m_rates,
    v_rates,
    head_proj,
    m_proj,
    v_proj,
    norm_params,
    norm_m,
    norm_v,
    head_small,
    small_m,
    small_v,
):

    block_id = lax.axis_index("ch")
    flat_in = features.reshape(PX, CIN)
    mask_column = valid_mask.reshape(PX, 1).astype(F32)
    gains = norm_params[0]
    shifts = norm_params[1]

    def owned(vector, offset, width):
        return lax.dynamic_slice_in_dim(vector, offset + block_id * width, width)

    def own_row(array, axis):
        return lax.dynamic_slice_in_dim(array, block_id, 1, axis=axis)

    w_shard = jnp.concatenate(
        [w_reduce.T, w_dilated.transpose(1, 0, 2).reshape(WPART, TAP_LANES), w_expand], axis=1
    ).astype(BF)
    w_seg = tap_weights(head_weight, head_rates)
    local_counts = jnp.sum(label_mask.astype(F32), axis=(1, 2))
    narrow = jnp.stack(
        [
            owned(gains, 0, MID),
            owned(shifts, 0, MID),
            owned(gains, M, MID),
            owned(shifts, M, MID),
            jnp.pad(local_counts, (0, MID - 3)),
        ]
        + [jnp.zeros((MID,), F32)] * 3
    )
    wide = jnp.stack([owned(gains, 2 * M, CIN), owned(shifts, 2 * M, CIN)] + [jnp.zeros((CIN,), F32)] * 6)
    proj_shard_t = jnp.transpose(
        lax.dynamic_slice_in_dim(head_proj, block_id * (HID // NCH), HID // NCH, axis=2), (0, 2, 1)
    ).astype(BF)
    shared, hat_one, hat_two, hat_three, w_all, first, second, stats, stats_wide, proj_own = block_forward(
        flat_in, mask_column, w_shard, proj_shard_t, narrow, wide
    )
    branch_bias, proj_bias, sem_w, depth_w, normal_w, sem_b, depth_b, normal_b = unpack_small(
        head_small
    )
    out_stack = jnp.stack(
        [jnp.pad(weight.astype(BF), ((0, 0), (0, 32 - weight.shape[1]))) for weight in (sem_w, depth_w, normal_w)]
    )
    out_bias = jnp.stack(
        [jnp.pad(bias, (0, 32 - bias.shape[0])) for bias in (sem_b, depth_b, normal_b)], axis=1
    )
    q_rows, shared_all, proj_t = heads_forward(shared, w_seg, proj_own)
    targets = jnp.concatenate([own_row(depth_target, 0), own_row(normal_target, 1)[:, 0]], axis=0)
    pre_grad, proj_part, out_grad, bias_rows, out_bias_rows = heads_middle(
        q_rows,
        branch_bias.T,
        proj_bias.T,
        proj_t,
        out_stack,
        out_bias,
        own_row(sem_label, 0),
        targets,
        own_row(label_mask, 1)[:, 0].astype(F32),
        jnp.broadcast_to(stats[2, :3][:, None], (3, WIDTH)),
    )
    small_term = pack_small(
        [bias_rows[:4, 0], bias_rows[4, 0]]
        + [out_grad[0, :NCLS].T, out_grad[1, :1].T, out_grad[2, :3].T]
        + [out_bias_rows[0, 0, :NCLS], out_bias_rows[1, 0, :1], out_bias_rows[2, 0, :3]]
    )
    small_count = small_term.shape[0]
    small_term = jnp.pad(small_term, (0, SMALL_ROWS * 128 - small_count)).reshape(SMALL_ROWS, 128)
    tap_sums, combined, squares = heads_backward(pre_grad, shared_all, w_seg)
    head_shard, rates_shard = tap_grads(tap_sums)
    input_grad, w_grad, proj_shard, small_sum, norm_narrow, norm_wide, totals = block_backward(
        combined, flat_in, mask_column, w_all, hat_one, hat_two, hat_three, first, second,
        narrow, wide, stats, stats_wide, proj_part, small_term, squares,
    )
    reduce_shard = w_grad[:, W_REDUCE].T
    dilated_shard = w_grad[:, W_DILATED].reshape(WPART, 9, MID).transpose(1, 0, 2)
    expand_shard = w_grad[:, W_EXPAND]
    small_grad = small_sum.reshape(-1)[:small_count]
    norm_grad = jnp.stack(
        [
            jnp.concatenate([norm_narrow[:, 1].reshape(-1), norm_narrow[:, 3].reshape(-1), norm_wide[:, 1].reshape(-1)]),
            jnp.concatenate([norm_narrow[:, 0].reshape(-1), norm_narrow[:, 2].reshape(-1), norm_wide[:, 0].reshape(-1)]),
        ]
    )
    grad_norm = totals[0, 0]
    factor = totals[1, 0]
    reduce_new, reduce_first, reduce_second = adam_step(
        w_reduce, m_reduce, v_reduce, reduce_shard * factor, RATE_MATRIX, DECAY
    )
    dilated_new, dilated_first, dilated_second = adam_step(
        w_dilated, m_dilated, v_dilated, dilated_shard * factor, RATE_MATRIX, DECAY
    )
    expand_new, expand_first, expand_second = adam_step(
        w_expand, m_expand, v_expand, expand_shard * factor, RATE_MATRIX, DECAY
    )
    head_new, head_first, head_second = adam_step(
        head_weight, m_head, v_head, head_shard * factor, RATE_MATRIX, DECAY
    )
    rates_new, rates_first, rates_second = adam_step(
        head_rates, m_rates, v_rates, rates_shard * factor, RATE_MATRIX, DECAY
    )
    proj_new, proj_first, proj_second = adam_step(
        head_proj, m_proj, v_proj, proj_shard * factor, RATE_MATRIX, DECAY
    )
    norm_new, norm_first, norm_second = adam_step(
        norm_params, norm_m, norm_v, norm_grad * factor, RATE_SMALL, 0.0
    )
    small_new, small_first, small_second = adam_step(
        head_small, small_m, small_v, small_grad * factor, RATE_SMALL, 0.0
    )
    depth_bias_grad = small_grad[small_count - 4]
    return (
        shared.reshape(ROWS, WIDTH, CIN),
        input_grad.reshape(ROWS, WIDTH, CIN),
        grad_norm,
        reduce_new,
        reduce_first,
        reduce_second,
        reduce_new.astype(jnp.bfloat16),
        dilated_new,
        dilated_first,
        dilated_second,
        dilated_new.astype(jnp.bfloat16),
        expand_new,
        expand_first,
        expand_second,
        expand_new.astype(jnp.bfloat16),
        head_new,
        head_first,
        head_second,
        head_new.astype(jnp.bfloat16),
        rates_new,
        rates_first,
        rates_second,
        rates_new.astype(jnp.bfloat16),
        proj_new,
        proj_first,
        proj_second,
        proj_new.astype(jnp.bfloat16),
        norm_new,
        norm_first,
        norm_second,
        small_new,
        small_first,
        small_second,
        depth_bias_grad,
    )


def per_device(features, *rest):
    sizes = (lax.axis_size("pix"), lax.axis_size("ch"))
    if sizes == (NPIX, NCH) and features.shape == (ROWS, WIDTH, CIN):
        return per_device_rows(features, *rest)
    return per_device_plain(features, *rest)


def solution(mesh):
    placed = (
        P("pix", None, "ch"),
        P("pix", None),
        P("pix", None),
        P("pix", None),
        P(None, "pix", None),
        P(None, "pix", None),
        P("ch", "pix"),
        P("ch", "pix"),
        P("ch", "pix"),
        P(None, "pix", "ch"),
        P(None, "pix", "ch"),
        P(None, "pix", "ch"),
        P("pix", "ch"),
        P("pix", "ch"),
        P("pix", "ch"),
        P("ch", "pix"),
        P("ch", "pix"),
        P("ch", "pix"),
        P(None, None, "pix", "ch"),
        P(None, None, "pix", "ch"),
        P(None, None, "pix", "ch"),
        P(None, "pix", None),
        P(None, "pix", None),
        P(None, "pix", None),
        P(),
        P(),
        P(),
        P(),
        P(),
        P(),
    )
    return jax.shard_map(
        per_device,
        mesh=mesh,
        in_specs=placed,
        out_specs=(
            P("pix", None, "ch"),
            P("pix", None, "ch"),
            P(),
            P("ch", "pix"),
            P("ch", "pix"),
            P("ch", "pix"),
            P("ch", "pix"),
            P(None, "pix", "ch"),
            P(None, "pix", "ch"),
            P(None, "pix", "ch"),
            P(None, "pix", "ch"),
            P("pix", "ch"),
            P("pix", "ch"),
            P("pix", "ch"),
            P("pix", "ch"),
            P("ch", "pix"),
            P("ch", "pix"),
            P("ch", "pix"),
            P("ch", "pix"),
            P(None, None, "pix", "ch"),
            P(None, None, "pix", "ch"),
            P(None, None, "pix", "ch"),
            P(None, None, "pix", "ch"),
            P(None, "pix", None),
            P(None, "pix", None),
            P(None, "pix", None),
            P(None, "pix", None),
            P(),
            P(),
            P(),
            P(),
            P(),
            P(),
            P(),
        ),
        check_vma=False,
    )
```

```python
import jax
import jax.numpy as jnp
from jax import lax
from jax.experimental import pallas as pl
from jax.experimental.pallas import tpu as pltpu
from jax.sharding import PartitionSpec as P

C = 2048
M = 512
HID = 256
NCLS = 19
DILATION_RATE = 4
STEP = 10


EPS_NORM = 1e-05
BETA_ONE = 0.9
BETA_TWO = 0.999
ADAM_EPS = 1e-08
RATE_MATRIX = 0.02
RATE_SMALL = 0.2
DECAY = 0.01
CLIP_NORM = 0.01
aspp_rates = (12, 24, 36)


def shifted(value, axis, steps):
    count = lax.axis_size(axis)
    leading, last = (max(0, -steps), min(count, count - steps))
    return lax.ppermute(value, axis, [(source, source + steps) for source in range(leading, last)])


def with_halo(cells, sides, width):
    for axis, dim in sides:
        count = lax.axis_size(axis)
        ends = count - 1
        head = lax.slice_in_dim(cells, 0, width, axis=dim)
        tail = lax.slice_in_dim(cells, cells.shape[dim] - width, cells.shape[dim], axis=dim)
        cells = jnp.concatenate(
            [
                lax.ppermute(tail, axis, [(i, (i + 1) % count) for i in range(ends)]),
                cells,
                lax.ppermute(head, axis, [((i + 1) % count, i) for i in range(ends)]),
            ],
            axis=dim,
        )
    return cells


def smooth(values):
    return jax.nn.gelu(values, approximate=True)


def smooth_slope(values):
    return jax.vjp(smooth, values)[1](jnp.ones_like(values))[0]


def contract_first(left, right):
    return lax.dot_general(
        left, right, (((0,), (0,)), ((), ())), preferred_element_type=jnp.float32
    )


def contract_last(left, right):
    return lax.dot_general(
        left, right, (((1,), (1,)), ((), ())), preferred_element_type=jnp.float32
    )


def split_tasks(slopes, weight):
    pixels = slopes.shape[0]
    return lax.dot_general(
        slopes.reshape(pixels, 3, -1),
        weight.reshape(weight.shape[0], 3, -1),
        (((2,), (2,)), ((1,), (1,))),
        preferred_element_type=jnp.float32,
    )


def split_tasks_rows(slopes, weight):
    pixels = slopes.shape[0]
    return lax.dot_general(
        slopes.reshape(pixels, 3, -1),
        weight.reshape(3, -1, weight.shape[1]),
        (((2,), (1,)), ((1,), (0,))),
        preferred_element_type=jnp.float32,
    )


def unpack_small(vector):
    lengths = (12 * HID, 3 * HID, HID * NCLS, HID, HID * 3, NCLS, 1, 3)
    pieces = []
    offset = 0
    for length in lengths:
        pieces.append(lax.slice_in_dim(vector, offset, offset + length, axis=0))
        offset = offset + length
    return (
        pieces[0].reshape(4, 3 * HID),
        pieces[1].reshape(3, HID),
        pieces[2].reshape(HID, NCLS),
        pieces[3].reshape(HID, 1),
        pieces[4].reshape(HID, 3),
        pieces[5],
        pieces[6],
        pieces[7],
    )


def pack_small(pieces):
    return jnp.concatenate([piece.reshape(-1) for piece in pieces])


def fetch_rows(grid, step):
    if abs(step) >= lax.axis_size("pix"):
        return jnp.zeros_like(grid)
    return shifted(grid, "pix", -step)


def fetch_grads(grid, step):
    if abs(step) >= lax.axis_size("pix"):
        return jnp.zeros_like(grid)
    return shifted(grid, "pix", -step)


def row_view(grid, offset, fetch):
    height = grid.shape[0]
    lead, rest = divmod(offset, height)
    return fetch(grid, lead)


def column_view(grid, offset):
    width = grid.shape[1]
    reach = abs(offset)
    if reach == 0:
        return grid
    padded_canvas = jnp.pad(grid, ((0, 0), (reach, reach), (0, 0)))
    return padded_canvas[:, reach + offset : reach + offset + width]


def imtl_weights(gram):
    lengths = jnp.sqrt(jnp.diagonal(gram) + 1e-12)

    def pairing(row_task, col_task):
        return (
            gram[0, 0] / lengths[0]
            - gram[0, col_task] / lengths[col_task]
            - gram[row_task, 0] / lengths[0]
            + gram[row_task, col_task] / lengths[col_task]
        )

    right_one = gram[0, 0] / lengths[0] - gram[0, 1] / lengths[1]
    right_two = gram[0, 0] / lengths[0] - gram[0, 2] / lengths[2]
    upper_left = pairing(1, 1)
    upper_right = pairing(1, 2)
    lower_left = pairing(2, 1)
    lower_right = pairing(2, 2)
    determinant = upper_left * lower_right - upper_right * lower_left
    alpha_one = (right_one * lower_right - right_two * lower_left) / determinant
    alpha_two = (right_two * upper_left - right_one * upper_right) / determinant
    return jnp.stack([1.0 - alpha_one - alpha_two, alpha_one, alpha_two])


def adam_step(weight, first, second, grad, rate, decay):
    first_new = BETA_ONE * first + (1.0 - BETA_ONE) * grad
    second_new = BETA_TWO * second + (1.0 - BETA_TWO) * grad * grad
    first_hat = first_new / (1.0 - BETA_ONE**STEP)
    second_hat = second_new / (1.0 - BETA_TWO**STEP)
    weight_new = weight - rate * (first_hat / (jnp.sqrt(second_hat) + ADAM_EPS) + decay * weight)
    return (weight_new, first_new, second_new)


def pixel_sums(first, second):
    return lax.psum((first, second), "pix")


def back_pair(first, second):
    return lax.psum((first, second), "pix")


def channel_gather(piece):
    return lax.all_gather(piece, "ch", axis=1, tiled=True)


def channel_parts(partial_sum):
    return lax.psum_scatter(partial_sum, "ch", scatter_dimension=1, tiled=True)


def forward_norm(inputs, sums, squares, count, gain_row, shift_row):
    mean_row = sums / count
    scale_row = lax.rsqrt(squares / count - mean_row * mean_row + EPS_NORM)
    normed = (inputs - mean_row) * scale_row
    return (normed * gain_row + shift_row, normed, scale_row)


def backward_norm(upstream, normed, scale_row, count, gain_row):
    shift_grad, gain_grad = back_pair(jnp.sum(upstream, axis=0), jnp.sum(upstream * normed, axis=0))
    inner = gain_row * scale_row * (upstream - shift_grad / count - normed * (gain_grad / count))
    return (inner, gain_grad, shift_grad)


def loss_slopes(
    logits, depth_pred, normal_pred, sem_label, depth_target, normal_target, label_mask, counts
):
    masks = label_mask.reshape(3, -1).astype(jnp.float32)
    classes = lax.broadcasted_iota(jnp.int32, (1, NCLS), 1)
    onehot = (sem_label.reshape(-1, 1) == classes).astype(jnp.float32)
    highest = jnp.max(logits, axis=1, keepdims=True)
    raised = jnp.exp(logits - highest)
    probs = raised / jnp.sum(raised, axis=1, keepdims=True)
    sem_slope = masks[0][:, None] * (probs - onehot) / counts[0]
    depth_gap = depth_pred[:, 0] - depth_target.reshape(-1)
    depth_slope = (masks[1] * depth_gap / jnp.sqrt(depth_gap * depth_gap + 1.0) / counts[1])[
        :, None
    ]
    normal_slope = masks[2][:, None] * (normal_pred - normal_target.reshape(3, -1).T) / counts[2]
    return (
        sem_slope.astype(jnp.bfloat16),
        depth_slope.astype(jnp.bfloat16),
        normal_slope.astype(jnp.bfloat16),
    )


def per_device_plain(
    features,
    valid_mask,
    sem_label,
    depth_target,
    normal_target,
    label_mask,
    w_reduce,
    m_reduce,
    v_reduce,
    w_dilated,
    m_dilated,
    v_dilated,
    w_expand,
    m_expand,
    v_expand,
    head_weight,
    m_head,
    v_head,
    head_rates,
    m_rates,
    v_rates,
    head_proj,
    m_proj,
    v_proj,
    norm_params,
    norm_m,
    norm_v,
    head_small,
    small_m,
    small_v,
):
    rows_per_shard, columns_per_shard, wide_dev = features.shape
    pixels = rows_per_shard * columns_per_shard
    groups = lax.axis_size("ch")
    block_id = lax.axis_index("ch")
    pix_devices = lax.axis_size("pix")
    middle_per_shard = M // groups
    count_all = float(pixels * pix_devices)
    flat_in = features.reshape(pixels, wide_dev)
    mask_flat = valid_mask.reshape(pixels).astype(jnp.float32)
    gains = norm_params[0]
    shifts = norm_params[1]

    def owned(vector, offset, width):
        return lax.dynamic_slice_in_dim(vector, offset + block_id * width, width)

    reduce_w, dilated_w, expand_w, heads_w, rates_w, proj_w = (
        lax.all_gather(w_reduce.astype(jnp.bfloat16), "pix", axis=1, tiled=True),
        lax.all_gather(w_dilated.astype(jnp.bfloat16), "pix", axis=1, tiled=True),
        lax.all_gather(w_expand.astype(jnp.bfloat16), "pix", axis=0, tiled=True),
        lax.all_gather(head_weight.astype(jnp.bfloat16), "pix", axis=1, tiled=True),
        lax.all_gather(head_rates.astype(jnp.bfloat16), "pix", axis=2, tiled=True),
        lax.all_gather(head_proj.astype(jnp.bfloat16), "pix", axis=1, tiled=True),
    )
    reduced = lax.psum_scatter(
        jnp.dot(flat_in, reduce_w, preferred_element_type=jnp.float32),
        "ch",
        scatter_dimension=1,
        tiled=True,
    )
    local_counts = jnp.sum(label_mask.astype(jnp.float32), axis=(1, 2))
    reduced_sum = jnp.sum(reduced, axis=0)
    reduced_sq = jnp.sum(reduced * reduced, axis=0)
    reduced_sum, reduced_sq = lax.psum((reduced_sum, reduced_sq), "pix")
    task_counts = lax.psum(local_counts, "pix")
    task_counts = jnp.maximum(task_counts, 1.0)
    gain_one = owned(gains, 0, middle_per_shard)
    norm_one, hat_one, scale_one = forward_norm(
        reduced, reduced_sum, reduced_sq, count_all, gain_one, owned(shifts, 0, middle_per_shard)
    )
    first = (smooth(norm_one) * mask_flat[:, None]).astype(jnp.bfloat16)
    first_gathered = channel_gather(first).reshape(rows_per_shard, columns_per_shard, M)
    bordered_input = with_halo(first_gathered, (("pix", 0),), DILATION_RATE)
    bordered_input = jnp.pad(bordered_input, ((0, 0), (DILATION_RATE, DILATION_RATE), (0, 0)))
    middle = jnp.zeros((pixels, middle_per_shard), jnp.float32)
    for tap_index in range(9):
        kernel_row, kernel_column = divmod(tap_index, 3)
        sliding_patch = bordered_input[
            kernel_row * DILATION_RATE : kernel_row * DILATION_RATE + rows_per_shard,
            kernel_column * DILATION_RATE : kernel_column * DILATION_RATE + columns_per_shard,
        ].reshape(pixels, M)
        middle = middle + jnp.dot(
            sliding_patch, dilated_w[tap_index], preferred_element_type=jnp.float32
        )
    gain_two = owned(gains, M, middle_per_shard)
    middle_sum, middle_sq = pixel_sums(jnp.sum(middle, axis=0), jnp.sum(middle * middle, axis=0))
    norm_two, hat_two, scale_two = forward_norm(
        middle, middle_sum, middle_sq, count_all, gain_two, owned(shifts, M, middle_per_shard)
    )
    second = smooth(norm_two).astype(jnp.bfloat16)
    second_all = channel_gather(second)
    expanded = jnp.dot(second_all, expand_w, preferred_element_type=jnp.float32)
    gain_three = owned(gains, 2 * M, wide_dev)
    expand_sum, expand_sq = pixel_sums(
        jnp.sum(expanded, axis=0), jnp.sum(expanded * expanded, axis=0)
    )
    norm_three, hat_three, scale_three = forward_norm(
        expanded, expand_sum, expand_sq, count_all, gain_three, owned(shifts, 2 * M, wide_dev)
    )
    summed_in = norm_three + flat_in.astype(jnp.float32)
    shared = smooth(summed_in).astype(jnp.bfloat16)
    branch_bias, proj_bias, sem_w, depth_w, normal_w, sem_b, depth_b, normal_b = unpack_small(
        head_small
    )
    out_weights = (
        sem_w.astype(jnp.bfloat16),
        depth_w.astype(jnp.bfloat16),
        normal_w.astype(jnp.bfloat16),
    )
    grid_shared = shared.reshape(rows_per_shard, columns_per_shard, wide_dev)
    row_views = []
    pre_list = [jnp.dot(shared, heads_w, preferred_element_type=jnp.float32)]
    for rate_index, rate in enumerate(aspp_rates):
        views = (
            row_view(grid_shared, -rate, fetch_rows),
            grid_shared,
            row_view(grid_shared, rate, fetch_rows),
        )
        row_views.append(views)
        summed = jnp.zeros((pixels, 3 * HID), jnp.float32)
        for tap_index in range(9):
            kernel_row, kernel_column = divmod(tap_index, 3)
            sliding_patch = column_view(views[kernel_row], (kernel_column - 1) * rate).reshape(
                pixels, wide_dev
            )
            summed = summed + contract_last(sliding_patch, rates_w[rate_index, tap_index])
        pre_list.append(summed)
    pre_parts = jnp.stack(pre_list, axis=1)
    before = lax.psum(pre_parts, "ch") + branch_bias[None]
    hidden = smooth(before).astype(jnp.bfloat16)
    branch_slope = smooth_slope(before).reshape(pixels, 4, 3, HID)
    joined_list = []
    projected_list = []
    top_list = []
    produced = []
    for task_index in range(3):
        joined = hidden[:, :, task_index * HID : (task_index + 1) * HID].reshape(pixels, 4 * HID)
        projected = (
            jnp.dot(joined, proj_w[task_index], preferred_element_type=jnp.float32)
            + proj_bias[task_index]
        )
        top = smooth(projected).astype(jnp.bfloat16)
        produced.append(jnp.dot(top, out_weights[task_index], preferred_element_type=jnp.float32))
        joined_list.append(joined)
        projected_list.append(projected)
        top_list.append(top)
    logits = produced[0] + sem_b
    depth_pred = produced[1] + depth_b
    normal_pred = produced[2] + normal_b
    slopes = loss_slopes(
        logits,
        depth_pred,
        normal_pred,
        sem_label,
        depth_target,
        normal_target,
        label_mask,
        task_counts,
    )
    out_grads = []
    out_bias_grads = []
    proj_grads = []
    proj_bias_grads = []
    joined_backs = []
    for task_index in range(3):
        top_back = contract_last(slopes[task_index], out_weights[task_index])
        proj_back = (top_back * smooth_slope(projected_list[task_index])).astype(jnp.bfloat16)
        out_grads.append(contract_first(top_list[task_index], slopes[task_index]))
        out_bias_grads.append(jnp.sum(slopes[task_index], axis=0, dtype=jnp.float32))
        proj_grads.append(contract_first(joined_list[task_index], proj_back))
        proj_bias_grads.append(jnp.sum(proj_back, axis=0, dtype=jnp.float32))
        joined_backs.append(contract_last(proj_back, proj_w[task_index]).reshape(pixels, 4, HID))
    joined_back = jnp.stack(joined_backs, axis=2)
    pre_grad = (joined_back * branch_slope).astype(jnp.bfloat16).reshape(pixels, 4, 3 * HID)
    small_term = (
        pack_small(
            [jnp.sum(pre_grad, axis=0, dtype=jnp.float32), jnp.stack(proj_bias_grads)]
            + out_grads
            + out_bias_grads
        )
        / groups
    )
    proj_grad = jnp.stack(proj_grads)
    first_branch = pre_grad[:, 0]
    task_sum = split_tasks(first_branch, heads_w)
    rates_list = []
    for rate_index, rate in enumerate(aspp_rates):
        flat_back = pre_grad[:, rate_index + 1]
        rate_back = flat_back.reshape(rows_per_shard, columns_per_shard, 3 * HID)
        back_views = (
            row_view(rate_back, rate, fetch_grads),
            rate_back,
            row_view(rate_back, -rate, fetch_grads),
        )
        for tap_index in range(9):
            kernel_row, kernel_column = divmod(tap_index, 3)
            sliding_patch = column_view(
                row_views[rate_index][kernel_row], (kernel_column - 1) * rate
            ).reshape(pixels, wide_dev)
            rates_list.append(contract_first(flat_back, sliding_patch))
            spread = column_view(back_views[kernel_row], (1 - kernel_column) * rate).reshape(
                pixels, 3 * HID
            )
            task_sum = task_sum + split_tasks_rows(spread, rates_w[rate_index, tap_index])
    rates_grad = jnp.stack(rates_list).reshape(3, 9, 3 * HID, wide_dev)
    task_grads = [task_sum[0], task_sum[1], task_sum[2]]
    head_grad = contract_first(shared, first_branch)
    local_gram = jnp.stack(
        [
            jnp.stack(
                [jnp.sum(task_grads[row_task] * task_grads[col_task]) for col_task in range(3)]
            )
            for row_task in range(3)
        ]
    )
    gram = lax.psum(local_gram, ("pix", "ch"))
    alphas = imtl_weights(gram)
    combined = alphas[0] * task_grads[0] + alphas[1] * task_grads[1] + alphas[2] * task_grads[2]
    shared_slope = combined * smooth_slope(summed_in)
    expand_up, gain_three_grad, shift_three_grad = backward_norm(
        shared_slope, hat_three, scale_three, count_all, gain_three
    )
    expand_back = expand_up.astype(jnp.bfloat16)
    expand_grad = contract_first(second_all, expand_back)
    second_back = channel_parts(contract_last(expand_back, expand_w))
    middle_up, gain_two_grad, shift_two_grad = backward_norm(
        second_back * smooth_slope(norm_two), hat_two, scale_two, count_all, gain_two
    )
    middle_gradient = middle_up.astype(jnp.bfloat16)
    dilated_list = []
    for tap_index in range(9):
        kernel_row, kernel_column = divmod(tap_index, 3)
        sliding_patch = bordered_input[
            kernel_row * DILATION_RATE : kernel_row * DILATION_RATE + rows_per_shard,
            kernel_column * DILATION_RATE : kernel_column * DILATION_RATE + columns_per_shard,
        ].reshape(pixels, M)
        dilated_list.append(contract_first(sliding_patch, middle_gradient))
    dilated_grad = jnp.stack(dilated_list)
    canvas_gradient = with_halo(
        middle_gradient.reshape(rows_per_shard, columns_per_shard, middle_per_shard),
        (("pix", 0),),
        DILATION_RATE,
    )
    canvas_gradient = jnp.pad(canvas_gradient, ((0, 0), (DILATION_RATE, DILATION_RATE), (0, 0)))
    first_part = jnp.zeros((pixels, M), jnp.float32)
    for tap_index in range(9):
        kernel_row, kernel_column = divmod(tap_index, 3)
        sliding_patch = canvas_gradient[
            (2 - kernel_row) * DILATION_RATE : (2 - kernel_row) * DILATION_RATE + rows_per_shard,
            (2 - kernel_column) * DILATION_RATE : (2 - kernel_column) * DILATION_RATE
            + columns_per_shard,
        ].reshape(pixels, middle_per_shard)
        first_part = first_part + contract_last(sliding_patch, dilated_w[tap_index])
    first_back = channel_parts(first_part) * mask_flat[:, None] * smooth_slope(norm_one)
    reduce_up, gain_one_grad, shift_one_grad = backward_norm(
        first_back, hat_one, scale_one, count_all, gain_one
    )
    reduce_all = channel_gather(reduce_up.astype(jnp.bfloat16))
    reduce_grad = contract_first(flat_in, reduce_all)
    input_grad = contract_last(reduce_all, reduce_w) + shared_slope
    reduce_shard, dilated_shard, expand_shard, head_shard, rates_shard, proj_shard = (
        lax.psum_scatter(reduce_grad, "pix", scatter_dimension=1, tiled=True),
        lax.psum_scatter(dilated_grad, "pix", scatter_dimension=1, tiled=True),
        lax.psum_scatter(expand_grad, "pix", scatter_dimension=0, tiled=True),
        lax.psum_scatter(head_grad, "pix", scatter_dimension=1, tiled=True),
        lax.psum_scatter(rates_grad, "pix", scatter_dimension=2, tiled=True),
        lax.psum_scatter(proj_grad, "pix", scatter_dimension=1, tiled=True),
    )
    norm_local = jnp.zeros((2, 2 * M + C), jnp.float32)
    for offset, width, gain_grad, shift_grad in (
        (0, middle_per_shard, gain_one_grad, shift_one_grad),
        (M, middle_per_shard, gain_two_grad, shift_two_grad),
        (2 * M, wide_dev, gain_three_grad, shift_three_grad),
    ):
        norm_local = lax.dynamic_update_slice(
            norm_local, jnp.stack([gain_grad, shift_grad]), (0, offset + block_id * width)
        )
    big_local = (
        jnp.sum(reduce_shard * reduce_shard)
        + jnp.sum(dilated_shard * dilated_shard)
        + jnp.sum(expand_shard * expand_shard)
        + jnp.sum(head_shard * head_shard)
        + jnp.sum(rates_shard * rates_shard)
        + jnp.sum(proj_shard * proj_shard) / groups
    )
    big_squares, norm_grad, small_grad = lax.psum(
        (big_local, norm_local / pix_devices, small_term), ("pix", "ch")
    )
    grad_norm = jnp.sqrt(
        big_squares + jnp.sum(norm_grad * norm_grad) + jnp.sum(small_grad * small_grad)
    )
    factor = jnp.minimum(1.0, CLIP_NORM / (grad_norm + 1e-06))
    reduce_new, reduce_first, reduce_second = adam_step(
        w_reduce, m_reduce, v_reduce, reduce_shard * factor, RATE_MATRIX, DECAY
    )
    dilated_new, dilated_first, dilated_second = adam_step(
        w_dilated, m_dilated, v_dilated, dilated_shard * factor, RATE_MATRIX, DECAY
    )
    expand_new, expand_first, expand_second = adam_step(
        w_expand, m_expand, v_expand, expand_shard * factor, RATE_MATRIX, DECAY
    )
    head_new, head_first, head_second = adam_step(
        head_weight, m_head, v_head, head_shard * factor, RATE_MATRIX, DECAY
    )
    rates_new, rates_first, rates_second = adam_step(
        head_rates, m_rates, v_rates, rates_shard * factor, RATE_MATRIX, DECAY
    )
    proj_new, proj_first, proj_second = adam_step(
        head_proj, m_proj, v_proj, proj_shard * factor, RATE_MATRIX, DECAY
    )
    norm_new, norm_first, norm_second = adam_step(
        norm_params, norm_m, norm_v, norm_grad * factor, RATE_SMALL, 0.0
    )
    small_new, small_first, small_second = adam_step(
        head_small, small_m, small_v, small_grad * factor, RATE_SMALL, 0.0
    )
    depth_bias_grad = small_grad[small_grad.shape[0] - 4]
    return (
        shared.reshape(rows_per_shard, columns_per_shard, wide_dev),
        input_grad.reshape(rows_per_shard, columns_per_shard, wide_dev),
        grad_norm,
        reduce_new,
        reduce_first,
        reduce_second,
        reduce_new.astype(jnp.bfloat16),
        dilated_new,
        dilated_first,
        dilated_second,
        dilated_new.astype(jnp.bfloat16),
        expand_new,
        expand_first,
        expand_second,
        expand_new.astype(jnp.bfloat16),
        head_new,
        head_first,
        head_second,
        head_new.astype(jnp.bfloat16),
        rates_new,
        rates_first,
        rates_second,
        rates_new.astype(jnp.bfloat16),
        proj_new,
        proj_first,
        proj_second,
        proj_new.astype(jnp.bfloat16),
        norm_new,
        norm_first,
        norm_second,
        small_new,
        small_first,
        small_second,
        depth_bias_grad,
    )


MESH = pl.DeviceIdType.MESH
BF = jnp.bfloat16
F32 = jnp.float32
NPIX = 8
NCH = 4
ROWS = 4
WIDTH = 128
PX = ROWS * WIDTH
CIN = C // NCH
COLS = 3 * HID // NPIX
SEGS = COLS // 32
VMEM_LIMIT = 60 * 2**20
SLOT = (0, 2, 3, 1)
ROWS_AHEAD = 3
BLOCK_VMEM = 60 * 2**20
SMALL_ROWS = 64
SMALL_PART = SMALL_ROWS // NCH
ROOT_TAP = 6


REACH = tuple(rate // ROWS for rate in aspp_rates)


def tap_groups():
    groups = []
    first = 0
    for rate_index, step in ((1, -1), (0, -1), (None, 0), (0, 0), (1, 0), (2, 0), (0, 1), (1, 1)):
        if rate_index is None:
            groups.append((0, first, 0, 0, (0,)))
            first += 1
        else:
            rate = aspp_rates[rate_index]
            groups.append((rate_index + 1, first, step, REACH[rate_index], (rate, 0, -rate)))
            first += 3
    return groups


TAP_GROUPS = tap_groups()
TAPS = 22
SEG_ROWS = TAPS * 32
WINDOW = 16 * 32


def window_of(block):
    return jnp.where(block < NPIX - REACH[1], 0, jnp.where(block >= REACH[1], 2, 1))


def whole_vmem():
    return pl.BlockSpec(memory_space=pltpu.VMEM)


def slide(tile, steps):
    lane = lax.broadcasted_iota(jnp.int32, tile.shape, 1)
    if steps == 0:
        return tile
    rolled = pltpu.roll(tile, steps % WIDTH, 1)
    if steps > 0:
        return jnp.where(lane >= steps, rolled, 0.0)
    return jnp.where(lane < WIDTH + steps, rolled, 0.0)


def tanh_parts(values):
    root = 0.7978845608028654
    inner = jnp.tanh(root * (values + 0.044715 * values * values * values))
    return root, inner


def gelu_of(values):
    _, inner = tanh_parts(values)
    return 0.5 * values * (1.0 + inner)


def gelu_slope(values):
    root, inner = tanh_parts(values)
    return 0.5 * (1.0 + inner) + 0.5 * values * (1.0 - inner * inner) * root * (
        1.0 + 3.0 * 0.044715 * values * values
    )


def nt_dot(left, right):
    return lax.dot_general(left, right, (((1,), (1,)), ((), ())), preferred_element_type=F32)


def nn_dot(left, right):
    return lax.dot_general(left, right, (((1,), (0,)), ((), ())), preferred_element_type=F32)


def greet(targets):
    barrier = pltpu.get_barrier_semaphore()
    for target in targets:
        pl.semaphore_signal(barrier, inc=1, device_id=target, device_id_type=MESH)
    return len(targets)


def await_greetings(count):
    pl.semaphore_wait(pltpu.get_barrier_semaphore(), count)


def from_hbm():
    return pl.BlockSpec(memory_space=pl.ANY)


def remote(src, dst, send_sem, recv_sem, target):
    return pltpu.make_async_remote_copy(
        src, dst, send_sem, recv_sem, device_id=target, device_id_type=MESH
    )


def place():
    p = lax.axis_index("pix")
    c = lax.axis_index("ch")
    return p, c, p // 2, lax.rem(p, 2), c // 2, lax.rem(c, 2)


def moved_segments():
    moves = []
    for pair in range(NPIX // 2):
        tasks = [[(SEGS * (2 * pair + side) + s) * 32 // HID for s in range(SEGS)] for side in range(2)]
        low, high = tasks[0][0], tasks[1][-1]
        if low == high:
            continue
        for side, keeps in ((0, low), (1, high)):
            for s in range(SEGS):
                if tasks[side][s] != keeps:
                    moves.append((2 * pair + side, s, 2 * pair + 1 - side))
    return moves


MOVES = moved_segments()


NALL = NPIX * NCH


def all_targets():
    me = lax.axis_index("pix") * NCH + lax.axis_index("ch")
    targets = []
    for d in range(1, NALL):
        other = lax.rem(me + d, NALL)
        targets.append((other // NCH, lax.rem(other, NCH)))
    return targets


def sum_everywhere(row, inbox, send_sem, recv_sem):
    me = lax.axis_index("pix") * NCH + lax.axis_index("ch")
    inbox[me, 0:1, :] = row
    view = inbox.at[me, 0:1]
    copies = [
        remote(view, view, send_sem.at[i], recv_sem.at[i], target) for i, target in enumerate(all_targets())
    ]
    for copy in copies:
        copy.start()
    for copy in copies:
        copy.wait()
    total = inbox[0, 0:1, :]
    for i in range(1, NALL):
        total = total + inbox[i, 0:1, :]
    return total


def heads_forward_kernel(
    x_ref, rates_hbm, root_ref, proj_ref, q_ref, xall_out, wpt_ref, w_out, w_more_ref,
    rates_ref, xall_ref, w_ref, acc, y_tmp, core_buf, core_in, x_buf, x_in, row_buf, local_sem,
    zr_send, zl_send, z_recv, y_send, y_recv, core_send, core_recv, x_send, x_recv, row_send, row_recv,
    pj_send, pj_recv, wm_send, wm_recv, eh_send, eh_recv,
):
    p, c, z, y, x, core = place()
    zcount = NPIX // 2
    up = (2 * lax.rem(z + 1, zcount) + y, c)
    down = (2 * lax.rem(z + zcount - 1, zcount) + y, c)
    other_y = (2 * z + 1 - y, c)
    other_core = (p, 2 * x + 1 - core)
    other_x = (p, 2 * (1 - x) + core)
    row_targets = [(lax.rem(p + d, NPIX), c) for d in range(1, NPIX)]
    ch_targets = [(p, lax.rem(c + d, NCH)) for d in range(1, NCH)]
    greeted = greet(row_targets + ch_targets)
    rates_in = pltpu.make_async_copy(rates_hbm, rates_ref, local_sem.at[3])
    rates_in.start()

    own = pltpu.make_async_copy(x_ref, xall_ref.at[p], local_sem.at[0])
    own.start()
    wpt_ref[c] = proj_ref[...]
    await_greetings(greeted)
    proj_copies = [
        remote(proj_ref, wpt_ref.at[c], pj_send.at[d - 1], pj_recv.at[d - 1], ch_targets[d - 1])
        for d in range(1, NCH)
    ]
    for copy in proj_copies:
        copy.start()

    def to_up(source):
        return remote(xall_ref.at[source], xall_ref.at[source], zr_send.at[source // 2], z_recv.at[source // 2], up)

    def to_down(source):
        return remote(xall_ref.at[source], xall_ref.at[source], zl_send.at[source // 2], z_recv.at[source // 2], down)

    def to_y(source):
        return remote(xall_ref.at[source], xall_ref.at[source], y_send.at[source // 2], y_recv.at[source // 2], other_y)

    def half_to(source, i, target):
        view = xall_ref.at[source, PX // 2 : PX]
        return remote(view, view, eh_send.at[i], eh_recv.at[i], target)

    def to_y_part(source):
        view = xall_ref.at[source, 0 : PX // 2]
        return remote(view, view, y_send.at[source // 2], y_recv.at[source // 2], other_y)

    def is_far_end(zs):
        return ((zs == 0) | (zs == zcount - 1)) & (zs != z)

    def step_of(i):
        near = jnp.where(z == 0, i, jnp.where(z == 3, 3 - i, 0))
        one = jnp.where(i == 0, 1, jnp.where(i == 1, 0, i))
        two = jnp.where(i == 0, 2, jnp.where(i == 1, 3, 3 - i))
        two = jnp.where(i == 2, 1, jnp.where(i == 3, 0, two))
        return jnp.where(z == 1, one, jnp.where(z == 2, two, near))

    own.wait()
    to_y(p).start()

    @pl.when(z < zcount - 1)
    def _():
        to_up(p).start()

    @pl.when(z > 0)
    def _():
        to_down(p).start()

    acc[...] = jnp.zeros_like(acc)
    root = root_ref[...]
    rates_in.wait()
    for s in range(SEGS):
        w_ref[s, ROOT_TAP * 32 : (ROOT_TAP + 1) * 32, :] = root[s * 32 : (s + 1) * 32].astype(BF)
        for branch, first, step, reach, shifts in TAP_GROUPS:
            if branch > 0:
                value = rates_ref[branch - 1, 3 * (step + 1) : 3 * (step + 2), s * 32 : (s + 1) * 32, :]
                w_ref[s, first * 32 : (first + 3) * 32, :] = value.astype(BF).reshape(96, CIN)

    def process(src):
        xb = xall_ref[src]

        first_row = pl.multiple_of(window_of(src) * 96, 32)

        def one_seg(s, carry):
            y_tmp[pl.ds(first_row, WINDOW), :] = nt_dot(w_ref[s, pl.ds(first_row, WINDOW), :], xb)

            def add_group(dest, branch, first_tap, shifts):
                rows = pl.ds(pl.multiple_of(SLOT[branch] * COLS + s * 32, 32), 32)
                for r in range(ROWS):
                    lanes = pl.ds(r * WIDTH, WIDTH)
                    total = acc[dest, rows, lanes]
                    for i, shift in enumerate(shifts):
                        tile = y_tmp[pl.ds((first_tap + i) * 32, 32), lanes]
                        total = total + slide(tile, shift)
                    acc[dest, rows, lanes] = total

            for branch, first_tap, step, reach, shifts in TAP_GROUPS:
                dest = src - step * reach
                if step == 0:
                    add_group(dest, branch, first_tap, shifts)
                else:

                    @pl.when((dest >= 0) & (dest < NPIX))
                    def _():
                        add_group(dest, branch, first_tap, shifts)

            return carry

        lax.fori_loop(0, SEGS, one_seg, 0)

    def lanes_of(ch):
        return pl.ds(pl.multiple_of(ch * WIDTH, WIDTH), WIDTH)

    half_rows = (slice(0, 2 * COLS), slice(2 * COLS, 4 * COLS))

    def core_copy(b, half):
        return remote(core_buf.at[half, b], core_in.at[half, b], core_send.at[half, b], core_recv.at[half, b], other_core)

    def x_copy(b, half):
        return remote(x_buf.at[half, b], x_in.at[half, b], x_send.at[half, b], x_recv.at[half, b], other_x)

    def row_copy(b, half, slot):
        return remote(
            row_buf.at[half, b],
            q_ref.at[2 * half : 2 * half + 2, pl.ds(pl.multiple_of(COLS * p, 32), COLS), :],
            row_send.at[half, slot],
            row_recv.at[half, slot],
            (b, c),
        )

    def core_start(b, half):
        for xx in range(2):
            core_buf[half, b, xx] = acc[b, half_rows[half], lanes_of(2 * xx + 1 - core)].astype(BF)
        core_copy(b, half).start()

    def x_start(b, half):
        core_copy(b, half).wait_recv()
        x_buf[half, b] = (
            acc[b, half_rows[half], lanes_of(2 * (1 - x) + core)] + core_in[half, b, 1 - x].astype(F32)
        ).astype(BF)
        x_copy(b, half).start()

    def finish(b, half):
        x_copy(b, half).wait_recv()
        total = (
            acc[b, half_rows[half], lanes_of(c)] + core_in[half, b, x].astype(F32) + x_in[half, b].astype(F32)
        )
        return total.astype(BF).reshape(2, COLS, WIDTH)

    def gather_step(i, carry):
        zs = step_of(i)
        mine = 2 * zs + y
        theirs = 2 * zs + 1 - y

        @pl.when(i > 0)
        def _():
            to_up(mine).wait_recv()

        @pl.when((zs < z) & (z < zcount - 1))
        def _():
            to_up(mine).start()

        @pl.when((zs > z) & (z > 0))
        def _():
            to_down(mine).start()

        far = is_far_end(zs)

        @pl.when((i > 0) & jnp.logical_not(far))
        def _():
            to_y(mine).start()

        @pl.when(far)
        def _():
            to_y_part(mine).start()

        process(mine)
        core_start(mine, 0)

        @pl.when(i > 0)
        def _():
            x_start(2 * step_of(i - 1) + 1 - y, 0)

        @pl.when(jnp.logical_not(far))
        def _():
            to_y(theirs).wait_recv()

        for end, i_end in ((0, 0), (zcount - 1, 1)):
            onward = up if end == 0 else down

            @pl.when((zs == end) & (z == end))
            def _():
                half_to(theirs, i_end, onward).start()

            @pl.when((zs == end) & (z != end))
            def _():
                to_y_part(theirs).wait_recv()
                half_to(theirs, i_end, onward).wait_recv()

            @pl.when((zs == end) & (z != end) & (z != zcount - 1 - end))
            def _():
                half_to(theirs, i_end, onward).start()

        process(theirs)
        core_start(theirs, 0)
        x_start(mine, 0)
        return carry

    lax.fori_loop(0, zcount, gather_step, 0)
    leaving = [
        pltpu.make_async_copy(xall_ref, xall_out, local_sem.at[1]),
        pltpu.make_async_copy(w_ref, w_out, local_sem.at[2]),
    ]
    for copy in leaving:
        copy.start()

    def weight_copy(i):
        return remote(w_ref.at[MOVES[i][1]], w_more_ref, wm_send.at[0], wm_recv.at[0], other_y)

    for i, (giver, s, receiver) in enumerate(MOVES):

        @pl.when(p == giver)
        def _():
            weight_copy(i).start()

    def block_after(d):
        return lax.rem(p + 1 + d, NPIX)

    def late_core(d, carry):
        core_start(block_after(d), 1)
        return carry

    lax.fori_loop(0, NPIX, late_core, 0)
    x_start(2 * step_of(zcount - 1) + 1 - y, 0)

    def late_x(d, carry):
        x_start(block_after(d), 1)
        return carry

    lax.fori_loop(0, NPIX, late_x, 0)
    own_rows = pl.ds(pl.multiple_of(COLS * p, 32), COLS)
    for half in range(2):

        def row_step(d, carry):
            b = block_after(d)
            row_buf[half, b] = finish(b, half)
            row_copy(b, half, d).start()
            return carry

        lax.fori_loop(0, NPIX - 1, row_step, 0)
        q_ref[2 * half : 2 * half + 2, own_rows, :] = finish(p, half)

    def drain(zs, carry):
        mine = 2 * zs + y

        @pl.when((zs <= z) & (z < zcount - 1))
        def _():
            to_up(mine).wait_send()

        @pl.when((zs >= z) & (z > 0))
        def _():
            to_down(mine).wait_send()

        far = is_far_end(zs)

        @pl.when(jnp.logical_not(far))
        def _():
            to_y(mine).wait_send()

        @pl.when(far)
        def _():
            to_y_part(mine).wait_send()

        return carry

    lax.fori_loop(0, zcount, drain, 0)
    for end, i_end in ((0, 0), (zcount - 1, 1)):

        @pl.when(z != zcount - 1 - end)
        def _():
            half_to(2 * end + 1 - y, i_end, up).wait_send()

    for half in range(2):

        def settle(d, carry):
            row_copy(block_after(d), half, d).wait()
            return carry

        lax.fori_loop(0, NPIX - 1, settle, 0)

        def settle_more(b, carry):
            core_copy(b, half).wait_send()
            x_copy(b, half).wait_send()
            return carry

        lax.fori_loop(0, NPIX, settle_more, 0)
    for copy in proj_copies + leaving:
        copy.wait()
    for i, (giver, s, receiver) in enumerate(MOVES):

        @pl.when(p == giver)
        def _():
            weight_copy(i).wait_send()

        @pl.when(p == receiver)
        def _():
            weight_copy(i).wait_recv()


def heads_forward(block_out, rates, root, proj_own):
    dma = pltpu.SemaphoreType.DMA
    zc = NPIX // 2
    return pl.pallas_call(
        heads_forward_kernel,
        out_shape=(
            jax.ShapeDtypeStruct((4, 3 * HID, WIDTH), BF),
            jax.ShapeDtypeStruct((NPIX, PX, CIN), BF),
            jax.ShapeDtypeStruct((NCH, 3, HID // NCH, 4 * HID), BF),
            jax.ShapeDtypeStruct((SEGS, SEG_ROWS, CIN), BF),
            jax.ShapeDtypeStruct((SEG_ROWS, CIN), BF),
        ),
        in_specs=[whole_vmem(), from_hbm(), whole_vmem(), whole_vmem()],
        out_specs=[whole_vmem(), from_hbm(), whole_vmem(), from_hbm(), whole_vmem()],
        scratch_shapes=[
            pltpu.VMEM((3, 9, COLS, CIN), F32),
            pltpu.VMEM((NPIX, PX, CIN), BF),
            pltpu.VMEM((SEGS, SEG_ROWS, CIN), BF),
            pltpu.VMEM((NPIX, 4 * COLS, PX), F32),
            pltpu.VMEM((SEG_ROWS, PX), F32),
            pltpu.VMEM((2, NPIX, 2, 2 * COLS, WIDTH), BF),
            pltpu.VMEM((2, NPIX, 2, 2 * COLS, WIDTH), BF),
            pltpu.VMEM((2, NPIX, 2 * COLS, WIDTH), BF),
            pltpu.VMEM((2, NPIX, 2 * COLS, WIDTH), BF),
            pltpu.VMEM((2, NPIX, 2, COLS, WIDTH), BF),
            dma((4,)),
            dma((zc,)), dma((zc,)), dma((zc,)), dma((zc,)), dma((zc,)),
            dma((2, NPIX)), dma((2, NPIX)), dma((2, NPIX)), dma((2, NPIX)),
            dma((2, NPIX - 1)), dma((2, NPIX - 1)),
            dma((NCH - 1,)), dma((NCH - 1,)), dma((1,)), dma((1,)), dma((2,)), dma((2,)),
        ],
        compiler_params=pltpu.CompilerParams(
            collective_id=1, has_side_effects=True, vmem_limit_bytes=VMEM_LIMIT
        ),
        name="heads_forward",
    )(block_out, rates, root, proj_own)


def heads_middle_part(
    q_ref, wpt_ref, small_ref, cols_ref, stats_ref, label_ref, depth_ref, normal_ref, mask_ref,
    dq_ref, dwp_ref, sums_ref, hid,
):
    c = lax.axis_index("ch")
    ones = jnp.ones((8, WIDTH), BF)
    columns = jnp.transpose(small_ref[...])
    out_w = jnp.transpose(cols_ref[...]).astype(BF)
    out_bias = columns[0:32, 15:16]
    sums_ref[...] = jnp.zeros_like(sums_ref)

    def spread(rows_8):
        return rows_8[0:1, :]

    for k in range(4):
        for t in range(3):
            cols = slice(t * HID, (t + 1) * HID)
            i = 3 * k + t
            hid[k, cols, :] = gelu_of(q_ref[SLOT[k], cols, :].astype(F32) + columns[:, i : i + 1]).astype(BF)
    row = lax.broadcasted_iota(jnp.int32, (32, WIDTH), 0)
    own_row = pl.ds(c, 1)
    out_sum = jnp.zeros((32, HID), F32)
    bias_sum = jnp.zeros((8, 32), F32)
    for t in range(3):
        cols = slice(t * HID, (t + 1) * HID)
        wpt = wpt_ref[:, t].reshape(HID, 4 * HID)
        zt = columns[:, 12 + t : 13 + t] + jnp.zeros((HID, WIDTH), F32)
        for k in range(4):
            zt = zt + nn_dot(wpt[:, k * HID : (k + 1) * HID], hid[k, cols, :])
        ut = gelu_of(zt).astype(BF)
        out = nn_dot(out_w, ut) + out_bias
        count = jnp.maximum(jnp.sum(stats_ref[2 + t : 3 + t, :], axis=1, keepdims=True), 1.0)
        scale = mask_ref[t, own_row, :].astype(F32) / count
        if t == 0:
            live = row < NCLS
            highest = jnp.max(jnp.where(live, out, -1e30), axis=0, keepdims=True)
            raised = jnp.where(live, jnp.exp(jnp.minimum(out - highest, 0.0)), 0.0)
            probs = raised / jnp.sum(raised, axis=0, keepdims=True)
            onehot = (row == label_ref[own_row, :]).astype(F32)
            slope = scale * (probs - onehot)
        elif t == 1:
            gap = out - depth_ref[own_row, :]
            slope = jnp.where(row == NCLS, scale * gap / jnp.sqrt(gap * gap + 1.0), 0.0)
        else:
            target = jnp.zeros((32, WIDTH), F32)
            for i in range(3):
                target = jnp.where(row == NCLS + 1 + i, normal_ref[i, own_row, :], target)
            slope = jnp.where((row > NCLS) & (row < NCLS + 4), scale * (out - target), 0.0)
        ot = slope.astype(BF)
        out_sum = out_sum + nt_dot(ot, ut)
        bias_sum = bias_sum + nt_dot(ones, ot)
        back = lax.dot_general(out_w, ot, (((0,), (0,)), ((), ())), preferred_element_type=F32)
        dz = (back * gelu_slope(zt)).astype(BF)
        sums_ref[12 + t : 13 + t, :] = spread(nt_dot(ones, dz))
        for k in range(4):
            part = hid[k, cols, :]
            product = nt_dot(part, dz).astype(BF)
            for half in range(2):
                for quarter in range(NCH):
                    start = half * 128 + quarter * 32
                    dwp_ref[quarter, t, 2 * k + half] = product[start : start + 32]
            dcat = lax.dot_general(
                wpt[:, k * HID : (k + 1) * HID], dz, (((0,), (0,)), ((), ())),
                preferred_element_type=F32,
            )
            i = 3 * k + t
            before = q_ref[SLOT[k], cols, :].astype(F32) + columns[:, i : i + 1]
            dq = (dcat * gelu_slope(before)).astype(BF)
            dq_ref[k, cols, :] = dq
            sums_ref[i : i + 1, :] = spread(nt_dot(ones, dq))
    sums_ref[15:16, 0:32] = spread(bias_sum)
    sums_ref[16:48, :] = out_sum


def fold(values):
    rows, lanes = values.shape
    total = values[0:8, 0:128]
    for r in range(rows // 8):
        for l in range(lanes // 128):
            if r or l:
                total = total + values[8 * r : 8 * r + 8, 128 * l : 128 * l + 128]
    return total


def heads_backward_kernel(
    q_ref, wpt_ref, small_ref, cols_ref, stats_ref, label_ref, depth_ref, normal_ref, mask_ref, xall_hbm, w_ref, w_more,
    rates_ref, gz_ref, square_ref, proj_out_ref, sums_out_ref, root_out_ref,
    dq_ref, dwp_ref, sums_ref, hid, dq_all, dq_more, wt, dcol, dcol_more, work, buf, z_out, oi_in, ac_in,
    gram_own, gram_all, proj_in, sums_in, dw_ref, blank, xall_ref,
    local_sem, out_sem, row_send, row_recv, x_send, x_recv, ca_send, ca_recv, cb_send, cb_recv,
    more_send, more_recv, fan_send, fan_recv,
    y_send, y_recv, oi_send, oi_recv, ac_send, ac_recv, gram_send, gram_recv, sp_send, sp_recv,
):
    p, c, z, y, x, core = place()
    zcount = NPIX // 2
    other_y = (2 * z + 1 - y, c)
    other_core = (p, 2 * x + 1 - core)
    other_x = (p, 2 * (1 - x) + core)
    pix_targets = [(lax.rem(p + d, NPIX), c) for d in range(1, NPIX)]
    ch_targets = [(p, lax.rem(c + d, NCH)) for d in range(1, NCH)]
    greeted = greet(all_targets())
    coming = pltpu.make_async_copy(xall_hbm, xall_ref, local_sem.at[1])
    coming.start()
    heads_middle_part(
        q_ref, wpt_ref, small_ref, cols_ref, stats_ref, label_ref, depth_ref, normal_ref, mask_ref,
        dq_ref, dwp_ref, sums_ref, hid,
    )
    await_greetings(greeted)
    far = 2 * (1 - x) + core

    def cols_of(b):
        return pl.ds(pl.multiple_of(COLS * b, 32), COLS)

    def row_copy(d):
        b = lax.rem(p + d, NPIX)
        return remote(dq_ref.at[:, cols_of(b), :], dq_all.at[p, c], row_send.at[d - 1], row_recv.at[d - 1], (b, c))

    def more_copy(i, source):
        giver, s, receiver = MOVES[i]
        start = giver * COLS + s * 32
        return remote(
            dq_ref.at[:, start : start + 32, :], dq_more.at[source, c],
            more_send.at[i], more_recv.at[source], (receiver, c),
        )

    def fan_copy(i, ch, target):
        return remote(dq_more.at[:, ch], dq_more.at[:, ch], fan_send.at[i], fan_recv.at[i], target)

    def any_of(flags):
        total = flags[0]
        for flag in flags[1:]:
            total = total | flag
        return total

    receives = any_of([p == move[2] for move in MOVES])

    for d in range(1, 1 + ROWS_AHEAD):
        row_copy(d).start()
    own = pltpu.make_async_copy(dq_ref.at[:, cols_of(p), :], dq_all.at[p, c], local_sem.at[0])
    own.start()
    for i, (giver, s, receiver) in enumerate(MOVES):
        start = giver * COLS + s * 32

        @pl.when(p == receiver)
        def _():
            dq_more[p, c] = dq_ref[:, start : start + 32, :]

        @pl.when(p != receiver)
        def _():
            more_copy(i, p).start()

    own.wait()

    def x_copy(d, b, ch):
        return remote(dq_all.at[b, ch], dq_all.at[b, ch], x_send.at[d], x_recv.at[d], other_x)

    def ca_copy(d, b, ch):
        return remote(dq_all.at[b, ch], dq_all.at[b, ch], ca_send.at[d], ca_recv.at[d], other_core)

    def cb_copy(d, b, ch):
        return remote(dq_all.at[b, ch], dq_all.at[b, ch], cb_send.at[d], cb_recv.at[d], other_core)

    def turn(win, s):
        value = jnp.transpose(w_ref[s, win * 96 : win * 96 + WINDOW, :].astype(F32)).astype(BF)
        lanes = slice(s * WINDOW, (s + 1) * WINDOW)
        givers = [move[0] for move in MOVES if move[1] == s]
        if givers:
            given = any_of([p == giver for giver in givers])
            wt[win, :, lanes] = jnp.where(given, jnp.zeros_like(value), value)
        else:
            wt[win, :, lanes] = value

    pieces = [(win, s) for win in range(3) for s in range(SEGS)]
    for d in range(NPIX):
        b = lax.rem(p + NPIX - d, NPIX)
        if d > 0:
            row_copy(d).wait()
            if d + ROWS_AHEAD < NPIX:
                row_copy(d + ROWS_AHEAD).start()
        x_copy(d, b, c).start()
        ca_copy(d, b, c).start()
        if d > 0:
            turn(*pieces[d - 1])
    for piece in pieces[NPIX - 1 :]:
        turn(*piece)

    @pl.when(receives)
    def _():
        for source in range(NPIX):

            @pl.when(p != source)
            def _():
                more_copy(0, source).wait_recv()

        fan_copy(0, c, other_x).start()
        fan_copy(1, c, other_core).start()

    for d in range(NPIX):
        b = lax.rem(p + NPIX - d, NPIX)
        x_copy(d, b, far).wait_recv()
        cb_copy(d, b, far).start()
    dw_ref[...] = jnp.zeros_like(dw_ref)
    blank[...] = jnp.zeros_like(blank)

    @pl.when(receives)
    def _():
        for win in range(3):
            wt[win, :, SEGS * WINDOW :] = jnp.transpose(
                w_more[win * 96 : win * 96 + WINDOW, :].astype(F32)
            ).astype(BF)
        fan_copy(0, far, other_x).wait_recv()
        fan_copy(2, far, other_core).start()

    for d in range(NPIX):
        b = lax.rem(p + NPIX - d, NPIX)
        ca_copy(d, b, 2 * x + 1 - core).wait_recv()
        cb_copy(d, b, 2 * (1 - x) + 1 - core).wait_recv()

    @pl.when(receives)
    def _():
        fan_copy(1, 2 * x + 1 - core, other_core).wait_recv()
        fan_copy(2, 2 * (1 - x) + 1 - core, other_core).wait_recv()

    ride = []
    for d in range(1, NCH):
        other = lax.rem(c + d, NCH)
        part = pl.ds(pl.multiple_of(other * SMALL_PART, SMALL_PART), SMALL_PART)
        ride.append(remote(dwp_ref.at[other], proj_in.at[c], sp_send.at[0, d - 1], sp_recv.at[0, d - 1], (p, other)))
        ride.append(remote(sums_ref.at[part], sums_in.at[c], sp_send.at[1, d - 1], sp_recv.at[1, d - 1], (p, other)))
    for copy in ride:
        copy.start()

    def one_block(b):
        win = window_of(b)

        def each_group(visit, clear):
            for branch, first_tap, step, reach, shifts in TAP_GROUPS:
                first_row = first_tap * 32 - win * 96
                source = b - step * reach
                if step == 0:
                    visit(source, branch, first_row, shifts)
                else:
                    in_window = win <= 1 if step < 0 else win >= 1
                    if reach == REACH[1]:
                        in_window = win == 1 + step
                    inside = (source >= 0) & (source < NPIX)

                    @pl.when(inside)
                    def _():
                        visit(source, branch, first_row, shifts)

                    @pl.when(in_window & jnp.logical_not(inside))
                    def _():
                        clear(first_row)

        def visit(source, branch, first_row, shifts):
            for r in range(ROWS):
                lanes = pl.ds(r * WIDTH, WIDTH)
                tile = dq_all[source, r, branch].astype(F32)
                for t, shift in enumerate(shifts):
                    moved = slide(tile, -shift).astype(BF)
                    for s in range(SEGS):
                        rows = pl.ds(pl.multiple_of(s * WINDOW + first_row + t * 32, 32), 32)
                        dcol[b, rows, lanes] = moved[s * 32 : (s + 1) * 32]

        def clear(first_row):
            for s in range(SEGS):
                rows = pl.ds(pl.multiple_of(s * WINDOW + first_row, 32), 96)
                dcol[b, rows, :] = jnp.zeros((96, PX), BF)

        def visit_more(source, branch, first_row, shifts):
            for r in range(ROWS):
                lanes = pl.ds(r * WIDTH, WIDTH)
                tile = dq_more[source, r, branch].astype(F32)
                for t, shift in enumerate(shifts):
                    rows = pl.ds(pl.multiple_of(first_row + t * 32, 32), 32)
                    dcol_more[rows, lanes] = slide(tile, -shift).astype(BF)

        def clear_more(first_row):
            dcol_more[pl.ds(pl.multiple_of(first_row, 32), 96), :] = jnp.zeros((96, PX), BF)

        each_group(visit, clear)
        work[...] = nn_dot(wt[win, :, : SEGS * WINDOW], dcol[b])

        @pl.when(receives)
        def _():
            each_group(visit_more, clear_more)
            work[...] += nn_dot(wt[win, :, SEGS * WINDOW :], dcol_more[...])

        buf[b] = work[...].astype(BF)

    mirrored = z >= 2
    outer = (z == 0) | (z == zcount - 1)
    inner = jnp.logical_not(outer)
    has_near = y == z - 1

    def true_z(e):
        return jnp.where(mirrored, zcount - 1 - e, e)

    def block_at(e):
        return 2 * true_z(e) + y

    def arrived_at(e):
        return NPIX + true_z(e)

    def near_at(e):
        return jnp.where(has_near, block_at(e), arrived_at(e))

    def mid_at(e):
        return jnp.where(has_near, arrived_at(e), block_at(e))

    def y_copy(zz):
        return remote(buf.at[2 * zz + 1 - y], buf.at[NPIX + zz], y_send.at[zz], y_recv.at[zz], other_y)

    oi_z = jnp.where(z == 0, 1, jnp.where(z == 1, 0, jnp.where(z == 2, 3, 2)))

    def oi_copy(i, source):
        return remote(source, oi_in.at[i], oi_send.at[i], oi_recv.at[i], (2 * oi_z + y, c))

    def ac_copy(i, source):
        return remote(source, ac_in.at[i], ac_send.at[i], ac_recv.at[i], (2 * (zcount - 1 - z) + y, c))

    def order(i):
        last = jnp.where(outer, zcount - 1 - i, i - 2)
        return jnp.where(i < 2, zcount - 1 - i, last)

    def sum_of(first, second):
        return (first.astype(F32) + second.astype(F32)).astype(BF)

    def block_pair(i, carry):
        zz = true_z(order(i))

        def either(j, inner_carry):
            one_block(2 * zz + jnp.where(j == 0, 1 - y, y))

            @pl.when(j == 0)
            def _():
                y_copy(zz).start()

            return inner_carry

        lax.fori_loop(0, 2, either, 0)

        @pl.when(i > 0)
        def _():
            y_copy(true_z(order(i - 1))).wait_recv()

        for step in range(1, zcount):

            @pl.when((i == step) & outer)
            def _():
                e = zcount - step
                z_out[step - 1] = sum_of(buf[block_at(e)], buf[arrived_at(e)])
                oi_copy(step - 1, z_out.at[step - 1]).start()

        @pl.when((i == 1) & inner)
        def _():
            ac_copy(0, buf.at[mid_at(3)]).start()

        @pl.when((i == 2) & inner)
        def _():
            ac_copy(1, buf.at[mid_at(2)]).start()
            oi_copy(0, z_out.at[0]).wait_recv()
            z_out[0] = sum_of(oi_in[0], buf[near_at(3)])
            ac_copy(2, z_out.at[0]).start()

        @pl.when((i == 3) & inner)
        def _():
            oi_copy(0, buf.at[near_at(0)]).start()
            oi_copy(1, z_out.at[0]).wait_recv()
            z_out[1] = sum_of(oi_in[1], buf[near_at(2)])
            ac_copy(3, z_out.at[1]).start()

        return carry

    lax.fori_loop(0, zcount, block_pair, 0)

    def weight_block(b, carry):
        first_tap = window_of(b) * 3

        def one_seg(s, inner_carry):
            rows = pl.ds(pl.multiple_of(s * WINDOW, WINDOW), WINDOW)
            taps = pl.ds(first_tap, WINDOW // 32)
            dw_ref[s, taps] += nn_dot(dcol[b, rows, :], xall_ref[b]).reshape(WINDOW // 32, 32, CIN)
            return inner_carry

        return lax.fori_loop(0, SEGS, one_seg, carry)

    coming.wait()
    lax.fori_loop(0, NPIX // 2, weight_block, 0)

    @pl.when(inner)
    def _():
        ac_copy(0, z_out.at[0]).wait_recv()
        z_out[2] = sum_of(ac_in[0], buf[mid_at(0)])
        oi_copy(1, z_out.at[2]).start()
        ac_copy(2, z_out.at[0]).wait_recv()
        oi_copy(2, ac_in.at[2]).start()

    lax.fori_loop(NPIX // 2, NPIX, weight_block, 0)
    out_copies = []
    at = {(group[0] - 1, group[2]): group[1] for group in TAP_GROUPS if group[0] > 0}
    for rate_index in range(3):
        for step in (-1, 0, 1):
            first = at.get((rate_index, step))
            for s in range(SEGS):
                source = blank if first is None else dw_ref.at[s, first : first + 3]
                out_copies.append(
                    pltpu.make_async_copy(
                        source,
                        rates_ref.at[rate_index, 3 * (step + 1) : 3 * (step + 2), s * 32 : (s + 1) * 32, :],
                        out_sem.at[len(out_copies)],
                    )
                )
    for copy in out_copies:
        copy.start()
    square_ref[...] = jnp.zeros_like(square_ref)

    def square_rows(m, carry):
        s = m // TAPS
        part = dw_ref[s, lax.rem(m, TAPS)]
        square_ref[...] += fold(part * part)
        return carry

    lax.fori_loop(0, SEGS * TAPS, square_rows, 0)

    for copy in ride:
        copy.wait()
    for t in range(3):
        total = dwp_ref[c, t].astype(F32)
        for d in range(1, NCH):
            total = total + proj_in[lax.rem(c + d, NCH), t].astype(F32)
        total = total.astype(BF)
        for b in range(NPIX):
            proj_out_ref[b, t] = total[b]
    total = sums_ref[pl.ds(pl.multiple_of(c * SMALL_PART, SMALL_PART), SMALL_PART), :]
    for d in range(1, NCH):
        total = total + sums_in[lax.rem(c + d, NCH)]
    sums_out_ref[...] = total
    for s in range(SEGS):
        root_out_ref[s * 32 : (s + 1) * 32, :] = dw_ref[s, ROOT_TAP]

    for copy in out_copies:
        copy.wait()
    near_task = jnp.where(mirrored, 2, 0)
    far_task = jnp.where(mirrored, 0, 2)
    y_copy(true_z(order(zcount - 1))).wait_recv()

    def keep(task, value):
        dw_ref[task, 0:16] = value.reshape(16, 32, PX)

    @pl.when(outer)
    def _():
        for i in range(3):
            oi_copy(i, z_out.at[0]).wait_recv()
        keep(near_task, buf[block_at(0)].astype(F32) + buf[arrived_at(0)].astype(F32) + oi_in[0].astype(F32))
        keep(1, oi_in[1].astype(F32))
        keep(far_task, oi_in[2].astype(F32))

    @pl.when(inner)
    def _():
        oi_copy(2, z_out.at[0]).wait_recv()
        ac_copy(1, z_out.at[0]).wait_recv()
        ac_copy(3, z_out.at[0]).wait_recv()
        keep(near_task, oi_in[2].astype(F32) + buf[near_at(1)].astype(F32))
        keep(1, buf[mid_at(1)].astype(F32) + ac_in[1].astype(F32))
        keep(far_task, ac_in[3].astype(F32))

    pairs = ((0, 0), (0, 1), (0, 2), (1, 1), (1, 2), (2, 2))
    gram_own[...] = jnp.zeros_like(gram_own)

    def gram_rows(m, carry):
        tasks = [dw_ref[t, m] for t in range(3)]
        for i, (a, b) in enumerate(pairs):
            gram_own[i] += fold(tasks[a] * tasks[b])
        return carry

    lax.fori_loop(0, CIN // 32, gram_rows, 0)

    lane = lax.broadcasted_iota(jnp.int32, (1, 128), 1)
    row = jnp.zeros((1, 128), F32)
    for i in range(6):
        value = jnp.sum(column_sums(gram_own[i]), axis=1, keepdims=True)
        row = row + jnp.where(lane == i, value, 0.0)
    row = sum_everywhere(row, gram_all, gram_send, gram_recv)
    entry = {}
    for i, (a, b) in enumerate(pairs):
        value = jnp.sum(jnp.where(lane == i, row, 0.0), axis=1, keepdims=True)
        entry[(a, b)] = value
        entry[(b, a)] = value
    lengths = [jnp.sqrt(entry[(t, t)] + 1e-12) for t in range(3)]

    def pairing(row_task, col_task):
        return (
            entry[(0, 0)] / lengths[0]
            - entry[(0, col_task)] / lengths[col_task]
            - entry[(row_task, 0)] / lengths[0]
            + entry[(row_task, col_task)] / lengths[col_task]
        )

    right_one = entry[(0, 0)] / lengths[0] - entry[(0, 1)] / lengths[1]
    right_two = entry[(0, 0)] / lengths[0] - entry[(0, 2)] / lengths[2]
    upper_left, upper_right = pairing(1, 1), pairing(1, 2)
    lower_left, lower_right = pairing(2, 1), pairing(2, 2)
    determinant = upper_left * lower_right - upper_right * lower_left
    alpha_one = (right_one * lower_right - right_two * lower_left) / determinant
    alpha_two = (right_two * upper_left - right_one * upper_right) / determinant
    alpha_zero = 1.0 - alpha_one - alpha_two

    for m in range(CIN // 128):
        tasks = [dw_ref[t, 4 * m : 4 * m + 4].reshape(128, PX) for t in range(3)]
        mixed = alpha_zero * tasks[0] + alpha_one * tasks[1] + alpha_two * tasks[2]
        gz_ref[:, m * 128 : (m + 1) * 128] = jnp.transpose(mixed)

    for d in range(NPIX):
        b = lax.rem(p + NPIX - d, NPIX)
        x_copy(d, b, c).wait_send()
        ca_copy(d, b, c).wait_send()
        cb_copy(d, b, far).wait_send()
    for i, (giver, s, receiver) in enumerate(MOVES):

        @pl.when(p != receiver)
        def _():
            more_copy(i, p).wait_send()

    @pl.when(receives)
    def _():
        fan_copy(0, c, other_x).wait_send()
        fan_copy(1, c, other_core).wait_send()
        fan_copy(2, far, other_core).wait_send()

    for i in range(zcount):
        y_copy(i).wait_send()
    for i in range(3):
        oi_copy(i, z_out.at[0]).wait_send()

    @pl.when(inner)
    def _():
        for i in range(4):
            ac_copy(i, z_out.at[0]).wait_send()


def heads_backward(*operands):
    dma = pltpu.SemaphoreType.DMA
    zc = NPIX // 2
    return pl.pallas_call(
        heads_backward_kernel,
        out_shape=(
            jax.ShapeDtypeStruct((3, 9, COLS, CIN), F32),
            jax.ShapeDtypeStruct((PX, CIN), F32),
            jax.ShapeDtypeStruct((8, 128), F32),
            jax.ShapeDtypeStruct((NPIX, 3, 32, HID), BF),
            jax.ShapeDtypeStruct((SMALL_PART, HID), F32),
            jax.ShapeDtypeStruct((COLS, CIN), F32),
        ),
        in_specs=[whole_vmem()] * 9 + [from_hbm()] + [whole_vmem()] * 2,
        out_specs=[pl.BlockSpec(memory_space=pl.ANY)] + [whole_vmem()] * 5,
        scratch_shapes=[
            pltpu.VMEM((4, 3 * HID, WIDTH), BF),
            pltpu.VMEM((NCH, 3, NPIX, 32, HID), BF),
            pltpu.VMEM((SMALL_ROWS, HID), F32),
            pltpu.VMEM((4, 3 * HID, WIDTH), BF),
            pltpu.VMEM((NPIX, NCH, 4, COLS, WIDTH), BF),
            pltpu.VMEM((NPIX, NCH, 4, 32, WIDTH), BF),
            pltpu.VMEM((3, CIN, (SEGS + 1) * WINDOW), BF),
            pltpu.VMEM((NPIX, SEGS * WINDOW, PX), BF),
            pltpu.VMEM((WINDOW, PX), BF),
            pltpu.VMEM((CIN, PX), F32),
            pltpu.VMEM((NPIX + zc, CIN, PX), BF),
            pltpu.VMEM((3, CIN, PX), BF),
            pltpu.VMEM((3, CIN, PX), BF),
            pltpu.VMEM((4, CIN, PX), BF),
            pltpu.VMEM((6, 8, 128), F32),
            pltpu.VMEM((NALL, 8, 128), F32),
            pltpu.VMEM((NCH, 3, NPIX, 32, HID), BF),
            pltpu.VMEM((NCH, SMALL_PART, HID), F32),
            pltpu.VMEM((SEGS, TAPS, 32, CIN), F32),
            pltpu.VMEM((3, 32, CIN), F32),
            pltpu.VMEM((NPIX, PX, CIN), BF),
            dma((2,)), dma((9 * SEGS,)),
            dma((NPIX - 1,)), dma((NPIX - 1,)),
            dma((NPIX,)), dma((NPIX,)), dma((NPIX,)), dma((NPIX,)), dma((NPIX,)), dma((NPIX,)),
            dma((len(MOVES),)), dma((NPIX,)), dma((3,)), dma((3,)),
            dma((zc,)), dma((zc,)), dma((3,)), dma((3,)), dma((4,)), dma((4,)),
            dma((NALL - 1,)), dma((NALL - 1,)),
            dma((2, NCH - 1)), dma((2, NCH - 1)),
        ],
        compiler_params=pltpu.CompilerParams(
            collective_id=2, has_side_effects=True, vmem_limit_bytes=VMEM_LIMIT
        ),
        name="heads_backward",
    )(*operands)


MID = M // NCH
WPART = M // NPIX
TAP_LANES = 9 * MID
W_REDUCE = slice(0, CIN)
W_DILATED = slice(CIN, CIN + TAP_LANES)
W_EXPAND = slice(CIN + TAP_LANES, 2 * CIN + TAP_LANES)
W_LANES = 2 * CIN + TAP_LANES


def slide_rows(tile, steps):
    if steps == 0:
        return tile
    line = lax.broadcasted_iota(jnp.int32, (WIDTH, tile.shape[1]), 0)
    keep = line >= steps if steps > 0 else line < WIDTH + steps
    pieces = []
    for r in range(ROWS):
        rolled = pltpu.roll(tile[r * WIDTH : (r + 1) * WIDTH], steps % WIDTH, 0)
        pieces.append(jnp.where(keep, rolled, 0.0))
    return jnp.concatenate(pieces, axis=0)


def column_sums(values):
    return jnp.sum(values, axis=0, keepdims=True)


def pix_copies(inbox, send_sem, recv_sem, rows=8):
    p, c = lax.axis_index("pix"), lax.axis_index("ch")
    view = inbox.at[p] if rows == 8 else inbox.at[p, 0:rows]
    return [
        remote(view, view, send_sem.at[d - 1], recv_sem.at[d - 1], (lax.rem(p + d, NPIX), c))
        for d in range(1, NPIX)
    ]


def ch_copies(source, inbox, send_sem, recv_sem):
    p, c = lax.axis_index("pix"), lax.axis_index("ch")
    copies = []
    for d in range(1, NCH):
        other = lax.rem(c + d, NCH)
        copies.append(remote(source(other), inbox.at[c], send_sem.at[d - 1], recv_sem.at[d - 1], (p, other)))
    return copies


def start_all(copies):
    for copy in copies:
        copy.start()


def wait_all(copies):
    for copy in copies:
        copy.wait()


def add_up(inbox):
    total = inbox[0]
    for i in range(1, inbox.shape[0]):
        total = total + inbox[i]
    return total


def block_forward_kernel(
    x_ref, mask_ref, label_ref, reduce_ref, dilated_ref, expand_ref, head_proj_ref, norm_ref,
    out_ref, hat_one_out, hat_two_out, hat_three_ref, wall_out, first_out, second_out, stats_ref, stats_wide_ref, wpt_ref,
    hat_one_ref, hat_two_ref, wall_ref, first_ref, second_ref, out_sem,
    w_ref, proj_ref, turned, mask_t, work, ch_buf, ch_in, halo_buf, halo_in, stat_one, stat_two, stat_three,
    local_sem, wz_send, wz_recv, wy_send, wy_recv, c_send, c_recv, s_send, s_recv, h_send, h_recv,
):
    p, c, z, y, x, core = place()
    zcount = NPIX // 2
    other_y = (2 * z + 1 - y, c)
    pix_targets = [(lax.rem(p + d, NPIX), c) for d in range(1, NPIX)]
    ch_targets = [(p, lax.rem(c + d, NCH)) for d in range(1, NCH)]
    greeted = greet(pix_targets + ch_targets)
    w_ref[:, W_REDUCE] = reduce_ref[...].astype(BF)
    for tap in range(9):
        w_ref[:, CIN + tap * MID : CIN + (tap + 1) * MID] = dilated_ref[tap].astype(BF)
    w_ref[:, W_EXPAND] = expand_ref[...].astype(BF)
    for t in range(3):
        turned[...] = jnp.transpose(head_proj_ref[t])
        quarter = pl.ds(pl.multiple_of(c * (HID // NCH), HID // NCH), HID // NCH)
        proj_ref[t] = turned[quarter, :].astype(BF)
    mask_t[...] = jnp.zeros_like(mask_t)
    mask_t[0:ROWS, :] = mask_ref[...].astype(F32)

    def param(row, offset, width):
        return norm_ref[row : row + 1, pl.ds(pl.multiple_of(offset + c * width, 128), width)]

    await_greetings(greeted)
    parts = (pl.ds(0, CIN), pl.ds(CIN, TAP_LANES), pl.ds(CIN + TAP_LANES, CIN))

    def shard(part):
        return w_ref.at[:, parts[part]] if part < 3 else proj_ref

    def spot(part, source):
        if part < 3:
            return wall_ref.at[source, :, parts[part]]
        return wpt_ref.at[:, :, pl.ds(pl.multiple_of(source * 128, 128), 128)]

    def wz_copy(part, d):
        target = (2 * lax.rem(z + d, zcount) + y, c)
        return remote(
            shard(part), spot(part, p),
            wz_send.at[part, d - 1], wz_recv.at[part, d - 1], target,
        )

    def wy_copy(part, d):
        source = 2 * lax.rem(z + zcount - d, zcount) + y
        src = shard(part) if d == 0 else spot(part, source)
        return remote(
            src, spot(part, source), wy_send.at[part, d], wy_recv.at[part, d], other_y
        )

    def send_z(part):
        for d in range(1, zcount):
            wz_copy(part, d).start()

    wy_copy(0, 0).start()
    send_z(0)
    own = pltpu.make_async_copy(w_ref, wall_ref.at[p], local_sem.at[0])
    own.start()
    own_proj = pltpu.make_async_copy(proj_ref, spot(3, p), local_sem.at[1])
    own_proj.start()
    own.wait()
    own_proj.wait()

    def forward_part(part):
        for d in range(1, zcount):
            wz_copy(part, d).wait_recv()
            wy_copy(part, d).start()

    def receive_part(part):
        for d in range(zcount):
            wy_copy(part, d).wait_recv()

    def weights(lanes):
        return wall_ref[:, :, lanes].reshape(M, lanes.stop - lanes.start)

    def stat_round(index, inbox, values):
        inbox[p, 0:1, :] = column_sums(values)
        inbox[p, 1:2, :] = column_sums(values * values)
        rows = 8 if index == 0 else 2
        copies = pix_copies(inbox, s_send.at[index], s_recv.at[index], rows)
        start_all(copies)
        wait_all(copies)
        return add_up(inbox[:, 0:rows])

    count_all = float(NPIX * PX)

    def norm_of(values, sums, gain, shift):
        mean = sums[0:1] / count_all
        scale = lax.rsqrt(sums[1:2] / count_all - mean * mean + EPS_NORM)
        hat = (values - mean) * scale
        return hat, hat * gain + shift, scale

    forward_part(0)
    send_z(1)
    receive_part(0)
    wy_copy(1, 0).start()
    for m in range(NCH):
        wanted = wall_ref[2 * m : 2 * m + 2, :, W_REDUCE].reshape(MID, CIN)
        value = nt_dot(x_ref[...], wanted)
        ch_buf[0, m] = value.astype(BF)

        @pl.when(m == c)
        def _():
            work[...] = value

    reduce_copies = ch_copies(lambda other: ch_buf.at[0, other], ch_in, c_send.at[0], c_recv.at[0])
    start_all(reduce_copies)
    wait_all(reduce_copies)
    forward_part(1)
    reduced = work[...]
    for d in range(1, NCH):
        reduced = reduced + ch_in[lax.rem(c + d, NCH)].astype(F32)
    stat_one[p] = jnp.zeros((8, MID), F32)
    for t in range(3):
        stat_one[p, 2 + t : 3 + t, :] = column_sums(label_ref[t].astype(F32))
    sums = stat_round(0, stat_one, reduced)
    hat, normed, scale = norm_of(reduced, sums, param(0, 0, MID), param(1, 0, MID))
    hat_one_ref[...] = hat
    stats_ref[...] = jnp.zeros_like(stats_ref)
    stats_ref[0:1, :] = scale
    stats_ref[2:5, :] = sums[2:5]

    def own_lanes():
        return pl.ds(pl.multiple_of(c * MID, MID), MID)

    def gather_copies(ref, index):
        copies = []
        for d in range(1, NCH):
            copies.append(
                remote(
                    ref.at[:, own_lanes()], ref.at[:, own_lanes()],
                    c_send.at[index, d - 1], c_recv.at[index, d - 1], ch_targets[d - 1],
                )
            )
        return copies

    mask = jnp.transpose(mask_t[...])
    mask = jnp.concatenate(
        [jnp.broadcast_to(mask[:, r : r + 1], (WIDTH, MID)) for r in range(ROWS)], axis=0
    )
    first_ref[:, own_lanes()] = (gelu_of(normed) * mask).astype(BF)
    copies = gather_copies(first_ref, 1)
    start_all(copies)
    send_z(2)
    wait_all(copies)
    receive_part(1)
    wy_copy(2, 0).start()

    def row_part(step):
        total = jnp.zeros((PX, MID), F32)
        for col in range(3):
            tap = 3 * (step + 1) + col
            lanes = slice(CIN + tap * MID, CIN + (tap + 1) * MID)
            total = total + slide_rows(nn_dot(first_ref[...], weights(lanes)), -DILATION_RATE * (col - 1))
        return total

    def halo_copy(side):
        target = (p - 1, c) if side == 0 else (p + 1, c)
        return remote(halo_buf.at[side], halo_in.at[side], h_send.at[side], h_recv.at[side], target)

    halo_buf[0] = row_part(1).astype(BF)

    @pl.when(p > 0)
    def _():
        halo_copy(0).start()

    halo_buf[1] = row_part(-1).astype(BF)

    @pl.when(p < NPIX - 1)
    def _():
        halo_copy(1).start()

    work[...] = row_part(0)

    @pl.when(p < NPIX - 1)
    def _():
        halo_copy(0).wait_recv()
        work[...] += halo_in[0].astype(F32)

    @pl.when(p > 0)
    def _():
        halo_copy(1).wait_recv()
        work[...] += halo_in[1].astype(F32)

    forward_part(2)
    send_z(3)
    wy_copy(3, 0).start()
    middle = work[...]
    sums = stat_round(1, stat_two, middle)
    hat, normed, scale = norm_of(middle, sums, param(0, M, MID), param(1, M, MID))
    hat_two_ref[...] = hat
    stats_ref[1:2, :] = scale
    second_ref[:, own_lanes()] = gelu_of(normed).astype(BF)
    copies = gather_copies(second_ref, 2)
    start_all(copies)
    wait_all(copies)

    receive_part(2)
    hat_three_ref[...] = nn_dot(second_ref[...], weights(W_EXPAND))
    expanded = hat_three_ref[...]
    leaving = [
        pltpu.make_async_copy(ref, out, out_sem.at[i])
        for i, (ref, out) in enumerate(
            (
                (hat_one_ref, hat_one_out), (hat_two_ref, hat_two_out), (wall_ref, wall_out),
                (first_ref, first_out), (second_ref, second_out),
            )
        )
    ]
    start_all(leaving)
    forward_part(3)
    sums = stat_round(2, stat_three, expanded)
    hat, normed, scale = norm_of(expanded, sums, param(0, 2 * M, CIN), param(1, 2 * M, CIN))
    hat_three_ref[...] = hat
    stats_wide_ref[...] = jnp.broadcast_to(scale, stats_wide_ref.shape)
    out_ref[...] = gelu_of(normed + x_ref[...].astype(F32)).astype(BF)
    receive_part(3)
    wait_all(leaving)

    for part in range(4):
        for d in range(zcount):
            wy_copy(part, d).wait_send()
        for d in range(1, zcount):
            wz_copy(part, d).wait_send()

    @pl.when(p > 0)
    def _():
        halo_copy(0).wait_send()

    @pl.when(p < NPIX - 1)
    def _():
        halo_copy(1).wait_send()


def block_forward(*operands):
    dma = pltpu.SemaphoreType.DMA
    zc = NPIX // 2
    shape = jax.ShapeDtypeStruct
    return pl.pallas_call(
        block_forward_kernel,
        out_shape=(
            shape((PX, CIN), BF),
            shape((PX, MID), F32),
            shape((PX, MID), F32),
            shape((PX, CIN), F32),
            shape((NPIX, WPART, W_LANES), BF),
            shape((PX, M), BF),
            shape((PX, M), BF),
            shape((8, MID), F32),
            shape((8, CIN), F32),
            shape((3, HID // NCH, 4 * HID), BF),
        ),
        in_specs=[whole_vmem()] * 8,
        out_specs=[whole_vmem()] + [from_hbm()] * 2 + [whole_vmem()] + [from_hbm()] * 3 + [whole_vmem()] * 3,
        scratch_shapes=[
            pltpu.VMEM((PX, MID), F32),
            pltpu.VMEM((PX, MID), F32),
            pltpu.VMEM((NPIX, WPART, W_LANES), BF),
            pltpu.VMEM((PX, M), BF),
            pltpu.VMEM((PX, M), BF),
            dma((5,)),
            pltpu.VMEM((WPART, W_LANES), BF),
            pltpu.VMEM((3, HID // NCH, 128), BF),
            pltpu.VMEM((HID, 128), F32),
            pltpu.VMEM((8, WIDTH), F32),
            pltpu.VMEM((PX, MID), F32),
            pltpu.VMEM((1, NCH, PX, MID), BF),
            pltpu.VMEM((NCH, PX, MID), BF),
            pltpu.VMEM((2, PX, MID), BF),
            pltpu.VMEM((2, PX, MID), BF),
            pltpu.VMEM((NPIX, 8, MID), F32),
            pltpu.VMEM((NPIX, 8, MID), F32),
            pltpu.VMEM((NPIX, 8, CIN), F32),
            dma((2,)),
            dma((4, zc - 1)), dma((4, zc - 1)), dma((4, zc)), dma((4, zc)),
            dma((3, NCH - 1)), dma((3, NCH - 1)),
            dma((3, NPIX - 1)), dma((3, NPIX - 1)),
            dma((2,)), dma((2,)),
        ],
        compiler_params=pltpu.CompilerParams(
            collective_id=0, has_side_effects=True, vmem_limit_bytes=BLOCK_VMEM
        ),
        name="block_forward",
    )(*operands)


def block_backward_kernel(
    gz_hbm, x_hbm, mask_ref, wall_hbm, hat_one_hbm, hat_two_hbm, hat_three_hbm, first_hbm, second_hbm,
    norm_ref, stats_ref, stats_wide_ref, proj_hbm, small_ref, square_ref,
    ingrad_ref, wgrad_ref, pgrad_ref, sgrad_ref, ngrad_ref, total_ref,
    gz_ref, x_ref, hat_three_ref, second_ref, first_ref, wall_ref, proj_ref, hat_two_ref, hat_one_ref, in_sem,
    ds, ds_low, turned, ch_buf, ch_in, halo_in, taps, back_t, mask_t, stat_three, stat_two, stat_one,
    we_buf, we_y, we_z, we_in, wd_buf, wd_y, wd_z, wd_in, wr_buf, wr_y, wr_z, wr_in, pr_in, pg_in,
    small_px, sq_all, norm_in, norm_wide_in,
    c_send, c_recv, s_send, s_recv, h_send, h_recv, gy_send, gy_recv, gz_send, gz_recv,
    pr_send, pr_recv, pg_send, pg_recv, t_send, t_recv, u_send, u_recv, n_send, n_recv,
):
    p, c, z, y, x, core = place()
    zcount = NPIX // 2
    other_y = (2 * z + 1 - y, c)
    pix_targets = [(lax.rem(p + d, NPIX), c) for d in range(1, NPIX)]
    ch_targets = [(p, lax.rem(c + d, NCH)) for d in range(1, NCH)]
    greeted = greet(all_targets())
    coming = [
        pltpu.make_async_copy(source, ref, in_sem.at[i])
        for i, (source, ref) in enumerate(
            (
                (gz_hbm, gz_ref), (x_hbm, x_ref), (hat_three_hbm, hat_three_ref), (second_hbm, second_ref),
                (first_hbm, first_ref), (wall_hbm, wall_ref), (proj_hbm, proj_ref), (hat_two_hbm, hat_two_ref),
                (hat_one_hbm, hat_one_ref),
            )
        )
    ]
    start_all(coming)
    count_all = float(NPIX * PX)

    def param(row, offset, width):
        return norm_ref[row : row + 1, pl.ds(pl.multiple_of(offset + c * width, 128), width)]

    gain_one, shift_one = param(0, 0, MID), param(1, 0, MID)
    gain_two, shift_two = param(0, M, MID), param(1, M, MID)
    gain_three, shift_three = param(0, 2 * M, CIN), param(1, 2 * M, CIN)

    def weights(lanes):
        return wall_ref[:, :, lanes].reshape(M, lanes.stop - lanes.start)

    def stat_round(index, inbox, upstream, hat):
        inbox[p, 0:1, :] = column_sums(upstream)
        inbox[p, 1:2, :] = column_sums(upstream * hat)
        copies = pix_copies(inbox, s_send.at[index], s_recv.at[index], 2)
        start_all(copies)
        return copies

    def stat_end(copies, inbox):
        wait_all(copies)
        return add_up(inbox[:, 0:2])

    def norm_back(upstream, hat, sums, gain, scale):
        return gain * scale * (upstream - sums[0:1] / count_all - hat * (sums[1:2] / count_all))

    def own_ch_copies(ref, inbox_index):
        return [
            remote(
                ref.at[c], ref.at[c], n_send.at[inbox_index, d - 1], n_recv.at[inbox_index, d - 1],
                ch_targets[d - 1],
            )
            for d in range(1, NCH)
        ]

    def sum_y(index, buf, y_in):
        return remote(buf.at[:, 1 - y], y_in, gy_send.at[index], gy_recv.at[index], other_y)

    def sum_z(index, z_buf, z_in):
        copies = []
        for d in range(1, zcount):
            zz = lax.rem(z + d, zcount)
            copies.append(
                remote(
                    z_buf.at[zz], z_in.at[d - 1], gz_send.at[index, d - 1], gz_recv.at[index, d - 1],
                    (2 * zz + y, c),
                )
            )
        return copies

    def sum_middle(index, buf, y_in, z_buf, z_in):
        sum_y(index, buf, y_in).wait()
        for zz in range(zcount):
            z_buf[zz] = (buf[zz, y].astype(F32) + y_in[zz].astype(F32)).astype(BF)
        start_all(sum_z(index, z_buf, z_in))

    def sum_end(index, z_buf, z_in, lanes):
        wait_all(sum_z(index, z_buf, z_in))
        total = z_buf[z].astype(F32)
        for d in range(zcount - 1):
            total = total + z_in[d].astype(F32)
        wgrad_ref[:, lanes] = total
        return fold(total * total)

    wide_rows = 64

    def expand_rows(m, carry):
        rows = pl.ds(pl.multiple_of(m * wide_rows, wide_rows), wide_rows)
        summed = hat_three_ref[rows, :] * gain_three + shift_three + x_ref[rows, :].astype(F32)
        ds[rows, :] = gz_ref[rows, :] * gelu_slope(summed)
        return carry

    wait_all(coming[:3])
    lax.fori_loop(0, PX // wide_rows, expand_rows, 0)
    await_greetings(greeted)
    copies = stat_round(0, stat_three, ds[...], hat_three_ref[...])
    wait_all(coming[3:])
    turned[0] = jnp.transpose(second_ref[...].astype(F32)).astype(BF)
    turned[1] = jnp.transpose(first_ref[...].astype(F32)).astype(BF)
    mask_t[...] = jnp.zeros_like(mask_t)
    mask_t[0:ROWS, :] = mask_ref[...].astype(F32)
    sums = stat_end(copies, stat_three)
    norm_wide_in[c] = jnp.zeros((8, CIN), F32)
    norm_wide_in[c, 0:2, :] = sums
    ds_low[...] = norm_back(ds[...], hat_three_ref[...], sums, gain_three, stats_wide_ref[0:1, :]).astype(BF)

    def scatter_ch(index, product):
        for m in range(NCH):
            ch_buf[index, m] = product(m).astype(BF)
        copies = ch_copies(lambda other: ch_buf.at[index, other], ch_in.at[index], c_send.at[index], c_recv.at[index])
        start_all(copies)
        return copies

    def scatter_end(index, copies):
        wait_all(copies)
        total = ch_buf[index, c].astype(F32)
        for d in range(1, NCH):
            total = total + ch_in[index, lax.rem(c + d, NCH)].astype(F32)
        return total

    def expand_back(m):
        wanted = wall_ref[2 * m : 2 * m + 2, :, W_EXPAND].reshape(MID, CIN)
        return nt_dot(ds_low[...], wanted)

    copies = scatter_ch(0, expand_back)
    proj_copies = []
    for d in range(1, NPIX):
        b = lax.rem(p + d, NPIX)
        proj_copies.append(remote(proj_ref.at[b], pr_in.at[d - 1], pr_send.at[d - 1], pr_recv.at[d - 1], (b, c)))
    start_all(proj_copies)
    small_px[p] = small_ref[...]
    small_copies = pix_copies(small_px, t_send, t_recv)
    start_all(small_copies)
    we_buf[...] = nn_dot(turned[0], ds_low[...]).astype(BF).reshape(zcount, 2, WPART, CIN)
    sum_y(0, we_buf, we_y).start()
    hat = hat_two_ref[...]
    slope = gelu_slope(hat * gain_two + shift_two)
    upstream = scatter_end(0, copies) * slope
    copies = stat_round(1, stat_two, upstream, hat)
    sums = stat_end(copies, stat_two)
    norm_in[c, 2:4, :] = sums[0:2]

    def halo_copy(side):
        target = (p - 1, c) if side == 0 else (p + 1, c)
        return remote(back_t, halo_in.at[side], h_send.at[side], h_recv.at[side], target)

    gradient = norm_back(upstream, hat, sums, gain_two, stats_ref[1:2, :])
    back_t[...] = gradient.astype(BF)

    @pl.when(p > 0)
    def _():
        halo_copy(0).start()

    @pl.when(p < NPIX - 1)
    def _():
        halo_copy(1).start()

    def fill_taps(step, source):
        for col in range(3):
            tap = 3 * (step + 1) + col
            moved = slide_rows(source.astype(F32), DILATION_RATE * (col - 1))
            taps[:, tap * MID : (tap + 1) * MID] = moved.astype(BF)

    fill_taps(0, back_t[...])

    @pl.when(p < NPIX - 1)
    def _():
        halo_copy(0).wait_recv()

    @pl.when(p == NPIX - 1)
    def _():
        halo_in[0] = jnp.zeros((PX, MID), BF)

    fill_taps(-1, halo_in[0])

    @pl.when(p > 0)
    def _():
        halo_copy(1).wait_recv()

    @pl.when(p == 0)
    def _():
        halo_in[1] = jnp.zeros((PX, MID), BF)

    fill_taps(1, halo_in[1])

    def dilated_back(m):
        wanted = wall_ref[2 * m : 2 * m + 2, :, W_DILATED].reshape(MID, TAP_LANES)
        return nt_dot(taps[...], wanted)

    copies = scatter_ch(1, dilated_back)
    sum_middle(0, we_buf, we_y, we_z, we_in)
    for m in range(NPIX):
        wd_buf[m // 2, m % 2] = nn_dot(turned[1, m * WPART : (m + 1) * WPART, :], taps[...]).astype(BF)
    sum_y(1, wd_buf, wd_y).start()
    hat = hat_one_ref[...]
    mask = jnp.transpose(mask_t[...])
    mask = jnp.concatenate(
        [jnp.broadcast_to(mask[:, r : r + 1], (WIDTH, MID)) for r in range(ROWS)], axis=0
    )
    slope = gelu_slope(hat * gain_one + shift_one) * mask
    upstream = scatter_end(1, copies) * slope
    copies = stat_round(2, stat_one, upstream, hat)
    sums = stat_end(copies, stat_one)
    norm_in[c, 0:2, :] = sums[0:2]
    norm_in[c, 4:8, :] = jnp.zeros((4, MID), F32)
    gradient = norm_back(upstream, hat, sums, gain_one, stats_ref[0:1, :])

    own_rows = pl.ds(pl.multiple_of(c * MID, MID), MID)
    turned[2, own_rows, :] = jnp.transpose(gradient).astype(BF)
    copies = [
        remote(
            turned.at[2, own_rows, :], turned.at[2, own_rows, :],
            c_send.at[2, d - 1], c_recv.at[2, d - 1], ch_targets[d - 1],
        )
        for d in range(1, NCH)
    ]
    start_all(copies)
    norm_copies = own_ch_copies(norm_in, 0) + own_ch_copies(norm_wide_in, 1)
    start_all(norm_copies)
    sum_middle(1, wd_buf, wd_y, wd_z, wd_in)
    wait_all(copies)
    wr_buf[...] = nn_dot(turned[2], x_ref[...]).astype(BF).reshape(zcount, 2, WPART, CIN)
    sum_y(2, wr_buf, wr_y).start()
    wait_all(proj_copies)
    for t in range(3):
        total = proj_ref[p, t].astype(F32)
        for d in range(NPIX - 1):
            total = total + pr_in[d, t].astype(F32)
        pg_in[c, t] = total
    wait_all(small_copies)
    sgrad_ref[c] = add_up(small_px)
    ch_final = [
        remote(pg_in.at[c], pg_in.at[c], pg_send.at[0, d - 1], pg_recv.at[0, d - 1], ch_targets[d - 1])
        for d in range(1, NCH)
    ] + [
        remote(sgrad_ref.at[c], sgrad_ref.at[c], pg_send.at[1, d - 1], pg_recv.at[1, d - 1], ch_targets[d - 1])
        for d in range(1, NCH)
    ]
    start_all(ch_final)
    sum_middle(2, wr_buf, wr_y, wr_z, wr_in)
    full = jnp.transpose(turned[2].astype(F32)).astype(BF)
    ingrad_ref[...] = nn_dot(full, weights(W_REDUCE)) + ds[...]
    squares = square_ref[...] + sum_end(0, we_z, we_in, W_EXPAND)
    squares = squares + sum_end(1, wd_z, wd_in, W_DILATED)
    wait_all(ch_final)
    for t in range(3):
        for other in range(NCH):
            pgrad_ref[t, other * 32 : (other + 1) * 32, :] = pg_in[other, t]
        squares = squares + fold(pg_in[c, t] * pg_in[c, t])
    wait_all(norm_copies)
    for other in range(NCH):
        for row in range(2):
            for offset, width, value in (
                (0, MID, norm_in[other, 1 - row : 2 - row, :]),
                (M, MID, norm_in[other, 3 - row : 4 - row, :]),
                (2 * M, CIN, norm_wide_in[other, 1 - row : 2 - row, :]),
            ):
                start = offset + other * width
                ngrad_ref[row : row + 1, start : start + width] = value
    shared = jnp.zeros((8, 128), F32)
    for other in range(NCH):
        shared = shared + fold(sgrad_ref[other] * sgrad_ref[other])
        shared = shared + fold(norm_in[other] * norm_in[other])
        shared = shared + fold(norm_wide_in[other] * norm_wide_in[other])
    squares = squares + sum_end(2, wr_z, wr_in, W_REDUCE)
    summed = sum_everywhere(column_sums(squares), sq_all, u_send, u_recv)
    everything = summed + column_sums(shared)
    total = jnp.sum(everything, axis=1, keepdims=True)
    norm = jnp.sqrt(total)
    factor = jnp.minimum(1.0, CLIP_NORM / (norm + 1e-06))
    line = lax.broadcasted_iota(jnp.int32, (8, 128), 0)
    total_ref[...] = jnp.where(line == 0, norm, factor)

    @pl.when(p > 0)
    def _():
        halo_copy(0).wait_send()

    @pl.when(p < NPIX - 1)
    def _():
        halo_copy(1).wait_send()


def block_backward(*operands):
    dma = pltpu.SemaphoreType.DMA
    shape = jax.ShapeDtypeStruct
    vmem = pltpu.VMEM
    zc = NPIX // 2

    def sum_buffers(lanes):
        return [
            vmem((zc, 2, WPART, lanes), BF),
            vmem((zc, WPART, lanes), BF),
            vmem((zc, WPART, lanes), BF),
            vmem((zc - 1, WPART, lanes), BF),
        ]

    return pl.pallas_call(
        block_backward_kernel,
        out_shape=(
            shape((PX, CIN), F32),
            shape((WPART, W_LANES), F32),
            shape((3, 128, HID), F32),
            shape((NCH, SMALL_PART, HID), F32),
            shape((2, 2 * M + C), F32),
            shape((8, 128), F32),
        ),
        in_specs=[from_hbm()] * 2 + [whole_vmem()] + [from_hbm()] * 6 + [whole_vmem()] * 3 + [from_hbm()] + [whole_vmem()] * 2,
        out_specs=[whole_vmem()] * 6,
        scratch_shapes=[
            vmem((PX, CIN), F32),
            vmem((PX, CIN), BF),
            vmem((PX, CIN), F32),
            vmem((PX, M), BF),
            vmem((PX, M), BF),
            vmem((NPIX, WPART, W_LANES), BF),
            vmem((NPIX, 3, 32, HID), BF),
            vmem((PX, MID), F32),
            vmem((PX, MID), F32),
            dma((9,)),
            vmem((PX, CIN), F32),
            vmem((PX, CIN), BF),
            vmem((3, M, PX), BF),
            vmem((2, NCH, PX, MID), BF),
            vmem((2, NCH, PX, MID), BF),
            vmem((2, PX, MID), BF),
            vmem((PX, TAP_LANES), BF),
            vmem((PX, MID), BF),
            vmem((8, WIDTH), F32),
            vmem((NPIX, 8, CIN), F32),
            vmem((NPIX, 8, MID), F32),
            vmem((NPIX, 8, MID), F32),
        ]
        + sum_buffers(CIN)
        + sum_buffers(TAP_LANES)
        + sum_buffers(CIN)
        + [
            vmem((NPIX - 1, 3, 32, HID), BF),
            vmem((NCH, 3, 32, HID), F32),
            vmem((NPIX, SMALL_PART, HID), F32),
            vmem((NALL, 8, 128), F32),
            vmem((NCH, 8, MID), F32),
            vmem((NCH, 8, CIN), F32),
            dma((3, NCH - 1)), dma((3, NCH - 1)),
            dma((3, NPIX - 1)), dma((3, NPIX - 1)),
            dma((2,)), dma((2,)),
            dma((3,)), dma((3,)), dma((3, zc - 1)), dma((3, zc - 1)),
            dma((NPIX - 1,)), dma((NPIX - 1,)),
            dma((2, NCH - 1)), dma((2, NCH - 1)),
            dma((NPIX - 1,)), dma((NPIX - 1,)),
            dma((NALL - 1,)), dma((NALL - 1,)),
            dma((2, NCH - 1)), dma((2, NCH - 1)),
        ],
        compiler_params=pltpu.CompilerParams(
            collective_id=3, has_side_effects=True, vmem_limit_bytes=BLOCK_VMEM
        ),
        name="block_backward",
    )(*operands)


def adam_parts(weight, first, second, grad, rate=RATE_MATRIX, decay=DECAY):
    first_new = BETA_ONE * first + (1.0 - BETA_ONE) * grad
    second_new = BETA_TWO * second + (1.0 - BETA_TWO) * grad * grad
    first_hat = first_new * (1.0 / (1.0 - BETA_ONE**STEP))
    second_hat = second_new * (1.0 / (1.0 - BETA_TWO**STEP))
    weight_new = weight - rate * (first_hat / (jnp.sqrt(second_hat) + ADAM_EPS) + decay * weight)
    return weight_new, first_new, second_new


def adam_store(olds, news, at, grad):
    weight, first, second = adam_parts(olds[0][at], olds[1][at], olds[2][at], grad)
    news[0][at] = weight
    news[1][at] = first
    news[2][at] = second
    news[3][at] = weight.astype(BF)


def adam_matrices_kernel(*refs):
    total_ref, w_ref, tap_ref, p_ref, n_ref = refs[:5]
    olds = [refs[5 + 3 * i : 8 + 3 * i] for i in range(6)]
    news = [refs[23 + 4 * i : 27 + 4 * i] for i in range(6)]
    factor = total_ref[1:2, 0:1]
    every = (slice(None), slice(None))
    adam_store(olds[0], news[0], every, w_ref[:, W_REDUCE] * factor)
    for tap in range(9):
        lanes = slice(CIN + tap * MID, CIN + (tap + 1) * MID)
        adam_store(olds[1], news[1], (tap, slice(None), slice(None)), w_ref[:, lanes] * factor)
    adam_store(olds[2], news[2], every, w_ref[:, W_EXPAND] * factor)
    adam_store(olds[3], news[3], every, tap_ref[...] * factor)
    for t in range(3):
        adam_store(olds[4], news[4], (t, slice(None), slice(None)), p_ref[t] * factor)
    values = adam_parts(
        olds[5][0][...], olds[5][1][...], olds[5][2][...], n_ref[...] * factor, RATE_SMALL, 0.0
    )
    for ref, value in zip(news[5], values):
        ref[...] = value


def adam_matrices(totals, w_grad, tap_grad, proj_grad, norm_grad, states):
    flat = [array for state in states for array in state]
    outs = []
    for state in states[:5]:
        outs += [jax.ShapeDtypeStruct(state[0].shape, F32)] * 3 + [jax.ShapeDtypeStruct(state[0].shape, BF)]
    outs += [jax.ShapeDtypeStruct(states[5][0].shape, F32)] * 3
    return pl.pallas_call(
        adam_matrices_kernel,
        out_shape=tuple(outs),
        in_specs=[whole_vmem()] * (5 + len(flat)),
        out_specs=[whole_vmem()] * len(outs),
        compiler_params=pltpu.CompilerParams(vmem_limit_bytes=VMEM_LIMIT),
        name="adam_matrices",
    )(totals, w_grad, tap_grad, proj_grad, norm_grad, *flat)


def per_device_rows(
    features,
    valid_mask,
    sem_label,
    depth_target,
    normal_target,
    label_mask,
    w_reduce,
    m_reduce,
    v_reduce,
    w_dilated,
    m_dilated,
    v_dilated,
    w_expand,
    m_expand,
    v_expand,
    head_weight,
    m_head,
    v_head,
    head_rates,
    m_rates,
    v_rates,
    head_proj,
    m_proj,
    v_proj,
    norm_params,
    norm_m,
    norm_v,
    head_small,
    small_m,
    small_v,
):

    flat_in = features.reshape(PX, CIN)
    shared, hat_one, hat_two, hat_three, w_all, first, second, stats, stats_wide, proj_own = block_forward(
        flat_in, valid_mask, label_mask, w_reduce.T, w_dilated, w_expand, head_proj, norm_params
    )
    q_rows, shared_all, proj_t, w_seg, w_more = heads_forward(shared, head_rates, head_weight.T, proj_own)
    at_out = 15 * HID
    rest = at_out + HID * NCLS
    small_cols = jnp.concatenate(
        [
            head_small[at_out:rest].reshape(HID, NCLS),
            head_small[rest : rest + HID].reshape(HID, 1),
            head_small[rest + HID : rest + 4 * HID].reshape(HID, 3),
            jnp.zeros((HID, 32 - NCLS - 4), F32),
        ],
        axis=1,
    )
    out_bias = jnp.pad(head_small[rest + 4 * HID :], (0, HID - NCLS - 4))
    small_rows = jnp.concatenate([head_small[:at_out], out_bias]).reshape(16, HID)
    rates_shard, combined, squares, proj_sums, small_sums, root_sums = heads_backward(
        q_rows, proj_t, small_rows, small_cols, stats, sem_label, depth_target, normal_target, label_mask,
        shared_all, w_seg, w_more,
    )
    input_grad, w_grad, proj_shard, small_total, norm_grad, totals = block_backward(
        combined, flat_in, valid_mask, w_all, hat_one, hat_two, hat_three, first, second,
        norm_params, stats, stats_wide, proj_sums, small_sums, squares,
    )
    (
        reduce_new, reduce_first, reduce_second, reduce_copy,
        dilated_new, dilated_first, dilated_second, dilated_copy,
        expand_new, expand_first, expand_second, expand_copy,
        head_new, head_first, head_second, head_copy,
        proj_new, proj_first, proj_second, proj_copy,
        norm_new, norm_first, norm_second,
    ) = adam_matrices(
        totals, w_grad, root_sums, proj_shard, norm_grad,
        (
            (w_reduce.T, m_reduce.T, v_reduce.T),
            (w_dilated, m_dilated, v_dilated),
            (w_expand, m_expand, v_expand),
            (head_weight.T, m_head.T, v_head.T),
            (head_proj, m_proj, v_proj),
            (norm_params, norm_m, norm_v),
        ),
    )
    small_total = small_total.reshape(SMALL_ROWS, HID)
    small_grad = jnp.concatenate(
        [
            small_total[:15].reshape(-1),
            small_total[16 : 16 + NCLS].T.reshape(-1),
            small_total[16 + NCLS],
            small_total[17 + NCLS : 20 + NCLS].T.reshape(-1),
            small_total[15, : NCLS + 4],
        ]
    )
    grad_norm = totals[0, 0]
    factor = totals[1, 0]
    rates_new, rates_first, rates_second = adam_step(
        head_rates, m_rates, v_rates, rates_shard * factor, RATE_MATRIX, DECAY
    )
    small_new, small_first, small_second = adam_step(
        head_small, small_m, small_v, small_grad * factor, RATE_SMALL, 0.0
    )
    depth_bias_grad = small_total[15, NCLS]
    return (
        shared.reshape(ROWS, WIDTH, CIN),
        input_grad.reshape(ROWS, WIDTH, CIN),
        grad_norm,
        reduce_new.T,
        reduce_first.T,
        reduce_second.T,
        reduce_copy.T,
        dilated_new,
        dilated_first,
        dilated_second,
        dilated_copy,
        expand_new,
        expand_first,
        expand_second,
        expand_copy,
        head_new.T,
        head_first.T,
        head_second.T,
        head_copy.T,
        rates_new,
        rates_first,
        rates_second,
        rates_new.astype(BF),
        proj_new,
        proj_first,
        proj_second,
        proj_copy,
        norm_new,
        norm_first,
        norm_second,
        small_new,
        small_first,
        small_second,
        depth_bias_grad,
    )


def per_device(features, *rest):
    sizes = (lax.axis_size("pix"), lax.axis_size("ch"))
    if sizes == (NPIX, NCH) and features.shape == (ROWS, WIDTH, CIN):
        return per_device_rows(features, *rest)
    return per_device_plain(features, *rest)


def solution(mesh):
    placed = (
        P("pix", None, "ch"),
        P("pix", None),
        P("pix", None),
        P("pix", None),
        P(None, "pix", None),
        P(None, "pix", None),
        P("ch", "pix"),
        P("ch", "pix"),
        P("ch", "pix"),
        P(None, "pix", "ch"),
        P(None, "pix", "ch"),
        P(None, "pix", "ch"),
        P("pix", "ch"),
        P("pix", "ch"),
        P("pix", "ch"),
        P("ch", "pix"),
        P("ch", "pix"),
        P("ch", "pix"),
        P(None, None, "pix", "ch"),
        P(None, None, "pix", "ch"),
        P(None, None, "pix", "ch"),
        P(None, "pix", None),
        P(None, "pix", None),
        P(None, "pix", None),
        P(),
        P(),
        P(),
        P(),
        P(),
        P(),
    )
    return jax.shard_map(
        per_device,
        mesh=mesh,
        in_specs=placed,
        out_specs=(
            P("pix", None, "ch"),
            P("pix", None, "ch"),
            P(),
            P("ch", "pix"),
            P("ch", "pix"),
            P("ch", "pix"),
            P("ch", "pix"),
            P(None, "pix", "ch"),
            P(None, "pix", "ch"),
            P(None, "pix", "ch"),
            P(None, "pix", "ch"),
            P("pix", "ch"),
            P("pix", "ch"),
            P("pix", "ch"),
            P("pix", "ch"),
            P("ch", "pix"),
            P("ch", "pix"),
            P("ch", "pix"),
            P("ch", "pix"),
            P(None, None, "pix", "ch"),
            P(None, None, "pix", "ch"),
            P(None, None, "pix", "ch"),
            P(None, None, "pix", "ch"),
            P(None, "pix", None),
            P(None, "pix", None),
            P(None, "pix", None),
            P(None, "pix", None),
            P(),
            P(),
            P(),
            P(),
            P(),
            P(),
            P(),
        ),
        check_vma=False,
    )
```

```python
import jax
import jax.numpy as jnp
from jax import lax
from jax.experimental import pallas as pl
from jax.experimental.pallas import tpu as pltpu
from jax.sharding import PartitionSpec as P

C = 2048
M = 512
HID = 256
NCLS = 19
DILATION_RATE = 4
STEP = 10


EPS_NORM = 1e-05
BETA_ONE = 0.9
BETA_TWO = 0.999
ADAM_EPS = 1e-08
RATE_MATRIX = 0.02
RATE_SMALL = 0.2
DECAY = 0.01
CLIP_NORM = 0.01
aspp_rates = (12, 24, 36)


def shifted(value, axis, steps):
    count = lax.axis_size(axis)
    leading, last = (max(0, -steps), min(count, count - steps))
    return lax.ppermute(value, axis, [(source, source + steps) for source in range(leading, last)])


def with_halo(cells, sides, width):
    for axis, dim in sides:
        count = lax.axis_size(axis)
        ends = count - 1
        head = lax.slice_in_dim(cells, 0, width, axis=dim)
        tail = lax.slice_in_dim(cells, cells.shape[dim] - width, cells.shape[dim], axis=dim)
        cells = jnp.concatenate(
            [
                lax.ppermute(tail, axis, [(i, (i + 1) % count) for i in range(ends)]),
                cells,
                lax.ppermute(head, axis, [((i + 1) % count, i) for i in range(ends)]),
            ],
            axis=dim,
        )
    return cells


def smooth(values):
    return jax.nn.gelu(values, approximate=True)


def smooth_slope(values):
    return jax.vjp(smooth, values)[1](jnp.ones_like(values))[0]


def contract_first(left, right):
    return lax.dot_general(
        left, right, (((0,), (0,)), ((), ())), preferred_element_type=jnp.float32
    )


def contract_last(left, right):
    return lax.dot_general(
        left, right, (((1,), (1,)), ((), ())), preferred_element_type=jnp.float32
    )


def split_tasks(slopes, weight):
    pixels = slopes.shape[0]
    return lax.dot_general(
        slopes.reshape(pixels, 3, -1),
        weight.reshape(weight.shape[0], 3, -1),
        (((2,), (2,)), ((1,), (1,))),
        preferred_element_type=jnp.float32,
    )


def split_tasks_rows(slopes, weight):
    pixels = slopes.shape[0]
    return lax.dot_general(
        slopes.reshape(pixels, 3, -1),
        weight.reshape(3, -1, weight.shape[1]),
        (((2,), (1,)), ((1,), (0,))),
        preferred_element_type=jnp.float32,
    )


def unpack_small(vector):
    lengths = (12 * HID, 3 * HID, HID * NCLS, HID, HID * 3, NCLS, 1, 3)
    pieces = []
    offset = 0
    for length in lengths:
        pieces.append(lax.slice_in_dim(vector, offset, offset + length, axis=0))
        offset = offset + length
    return (
        pieces[0].reshape(4, 3 * HID),
        pieces[1].reshape(3, HID),
        pieces[2].reshape(HID, NCLS),
        pieces[3].reshape(HID, 1),
        pieces[4].reshape(HID, 3),
        pieces[5],
        pieces[6],
        pieces[7],
    )


def pack_small(pieces):
    return jnp.concatenate([piece.reshape(-1) for piece in pieces])


def fetch_rows(grid, step):
    if abs(step) >= lax.axis_size("pix"):
        return jnp.zeros_like(grid)
    return shifted(grid, "pix", -step)


def fetch_grads(grid, step):
    if abs(step) >= lax.axis_size("pix"):
        return jnp.zeros_like(grid)
    return shifted(grid, "pix", -step)


def row_view(grid, offset, fetch):
    height = grid.shape[0]
    lead, rest = divmod(offset, height)
    return fetch(grid, lead)


def column_view(grid, offset):
    width = grid.shape[1]
    reach = abs(offset)
    if reach == 0:
        return grid
    padded_canvas = jnp.pad(grid, ((0, 0), (reach, reach), (0, 0)))
    return padded_canvas[:, reach + offset : reach + offset + width]


def imtl_weights(gram):
    lengths = jnp.sqrt(jnp.diagonal(gram) + 1e-12)

    def pairing(row_task, col_task):
        return (
            gram[0, 0] / lengths[0]
            - gram[0, col_task] / lengths[col_task]
            - gram[row_task, 0] / lengths[0]
            + gram[row_task, col_task] / lengths[col_task]
        )

    right_one = gram[0, 0] / lengths[0] - gram[0, 1] / lengths[1]
    right_two = gram[0, 0] / lengths[0] - gram[0, 2] / lengths[2]
    upper_left = pairing(1, 1)
    upper_right = pairing(1, 2)
    lower_left = pairing(2, 1)
    lower_right = pairing(2, 2)
    determinant = upper_left * lower_right - upper_right * lower_left
    alpha_one = (right_one * lower_right - right_two * lower_left) / determinant
    alpha_two = (right_two * upper_left - right_one * upper_right) / determinant
    return jnp.stack([1.0 - alpha_one - alpha_two, alpha_one, alpha_two])


def adam_step(weight, first, second, grad, rate, decay):
    first_new = BETA_ONE * first + (1.0 - BETA_ONE) * grad
    second_new = BETA_TWO * second + (1.0 - BETA_TWO) * grad * grad
    first_hat = first_new / (1.0 - BETA_ONE**STEP)
    second_hat = second_new / (1.0 - BETA_TWO**STEP)
    weight_new = weight - rate * (first_hat / (jnp.sqrt(second_hat) + ADAM_EPS) + decay * weight)
    return (weight_new, first_new, second_new)


def pixel_sums(first, second):
    return lax.psum((first, second), "pix")


def back_pair(first, second):
    return lax.psum((first, second), "pix")


def channel_gather(piece):
    return lax.all_gather(piece, "ch", axis=1, tiled=True)


def channel_parts(partial_sum):
    return lax.psum_scatter(partial_sum, "ch", scatter_dimension=1, tiled=True)


def forward_norm(inputs, sums, squares, count, gain_row, shift_row):
    mean_row = sums / count
    scale_row = lax.rsqrt(squares / count - mean_row * mean_row + EPS_NORM)
    normed = (inputs - mean_row) * scale_row
    return (normed * gain_row + shift_row, normed, scale_row)


def backward_norm(upstream, normed, scale_row, count, gain_row):
    shift_grad, gain_grad = back_pair(jnp.sum(upstream, axis=0), jnp.sum(upstream * normed, axis=0))
    inner = gain_row * scale_row * (upstream - shift_grad / count - normed * (gain_grad / count))
    return (inner, gain_grad, shift_grad)


def loss_slopes(
    logits, depth_pred, normal_pred, sem_label, depth_target, normal_target, label_mask, counts
):
    masks = label_mask.reshape(3, -1).astype(jnp.float32)
    classes = lax.broadcasted_iota(jnp.int32, (1, NCLS), 1)
    onehot = (sem_label.reshape(-1, 1) == classes).astype(jnp.float32)
    highest = jnp.max(logits, axis=1, keepdims=True)
    raised = jnp.exp(logits - highest)
    probs = raised / jnp.sum(raised, axis=1, keepdims=True)
    sem_slope = masks[0][:, None] * (probs - onehot) / counts[0]
    depth_gap = depth_pred[:, 0] - depth_target.reshape(-1)
    depth_slope = (masks[1] * depth_gap / jnp.sqrt(depth_gap * depth_gap + 1.0) / counts[1])[
        :, None
    ]
    normal_slope = masks[2][:, None] * (normal_pred - normal_target.reshape(3, -1).T) / counts[2]
    return (
        sem_slope.astype(jnp.bfloat16),
        depth_slope.astype(jnp.bfloat16),
        normal_slope.astype(jnp.bfloat16),
    )


def per_device_plain(
    features,
    valid_mask,
    sem_label,
    depth_target,
    normal_target,
    label_mask,
    w_reduce,
    m_reduce,
    v_reduce,
    w_dilated,
    m_dilated,
    v_dilated,
    w_expand,
    m_expand,
    v_expand,
    head_weight,
    m_head,
    v_head,
    head_rates,
    m_rates,
    v_rates,
    head_proj,
    m_proj,
    v_proj,
    norm_params,
    norm_m,
    norm_v,
    head_small,
    small_m,
    small_v,
):
    rows_per_shard, columns_per_shard, wide_dev = features.shape
    pixels = rows_per_shard * columns_per_shard
    groups = lax.axis_size("ch")
    block_id = lax.axis_index("ch")
    pix_devices = lax.axis_size("pix")
    middle_per_shard = M // groups
    count_all = float(pixels * pix_devices)
    flat_in = features.reshape(pixels, wide_dev)
    mask_flat = valid_mask.reshape(pixels).astype(jnp.float32)
    gains = norm_params[0]
    shifts = norm_params[1]

    def owned(vector, offset, width):
        return lax.dynamic_slice_in_dim(vector, offset + block_id * width, width)

    reduce_w, dilated_w, expand_w, heads_w, rates_w, proj_w = (
        lax.all_gather(w_reduce.astype(jnp.bfloat16), "pix", axis=1, tiled=True),
        lax.all_gather(w_dilated.astype(jnp.bfloat16), "pix", axis=1, tiled=True),
        lax.all_gather(w_expand.astype(jnp.bfloat16), "pix", axis=0, tiled=True),
        lax.all_gather(head_weight.astype(jnp.bfloat16), "pix", axis=1, tiled=True),
        lax.all_gather(head_rates.astype(jnp.bfloat16), "pix", axis=2, tiled=True),
        lax.all_gather(head_proj.astype(jnp.bfloat16), "pix", axis=1, tiled=True),
    )
    reduced = lax.psum_scatter(
        jnp.dot(flat_in, reduce_w, preferred_element_type=jnp.float32),
        "ch",
        scatter_dimension=1,
        tiled=True,
    )
    local_counts = jnp.sum(label_mask.astype(jnp.float32), axis=(1, 2))
    reduced_sum = jnp.sum(reduced, axis=0)
    reduced_sq = jnp.sum(reduced * reduced, axis=0)
    reduced_sum, reduced_sq = lax.psum((reduced_sum, reduced_sq), "pix")
    task_counts = lax.psum(local_counts, "pix")
    task_counts = jnp.maximum(task_counts, 1.0)
    gain_one = owned(gains, 0, middle_per_shard)
    norm_one, hat_one, scale_one = forward_norm(
        reduced, reduced_sum, reduced_sq, count_all, gain_one, owned(shifts, 0, middle_per_shard)
    )
    first = (smooth(norm_one) * mask_flat[:, None]).astype(jnp.bfloat16)
    first_gathered = channel_gather(first).reshape(rows_per_shard, columns_per_shard, M)
    bordered_input = with_halo(first_gathered, (("pix", 0),), DILATION_RATE)
    bordered_input = jnp.pad(bordered_input, ((0, 0), (DILATION_RATE, DILATION_RATE), (0, 0)))
    middle = jnp.zeros((pixels, middle_per_shard), jnp.float32)
    for tap_index in range(9):
        kernel_row, kernel_column = divmod(tap_index, 3)
        sliding_patch = bordered_input[
            kernel_row * DILATION_RATE : kernel_row * DILATION_RATE + rows_per_shard,
            kernel_column * DILATION_RATE : kernel_column * DILATION_RATE + columns_per_shard,
        ].reshape(pixels, M)
        middle = middle + jnp.dot(
            sliding_patch, dilated_w[tap_index], preferred_element_type=jnp.float32
        )
    gain_two = owned(gains, M, middle_per_shard)
    middle_sum, middle_sq = pixel_sums(jnp.sum(middle, axis=0), jnp.sum(middle * middle, axis=0))
    norm_two, hat_two, scale_two = forward_norm(
        middle, middle_sum, middle_sq, count_all, gain_two, owned(shifts, M, middle_per_shard)
    )
    second = smooth(norm_two).astype(jnp.bfloat16)
    second_all = channel_gather(second)
    expanded = jnp.dot(second_all, expand_w, preferred_element_type=jnp.float32)
    gain_three = owned(gains, 2 * M, wide_dev)
    expand_sum, expand_sq = pixel_sums(
        jnp.sum(expanded, axis=0), jnp.sum(expanded * expanded, axis=0)
    )
    norm_three, hat_three, scale_three = forward_norm(
        expanded, expand_sum, expand_sq, count_all, gain_three, owned(shifts, 2 * M, wide_dev)
    )
    summed_in = norm_three + flat_in.astype(jnp.float32)
    shared = smooth(summed_in).astype(jnp.bfloat16)
    branch_bias, proj_bias, sem_w, depth_w, normal_w, sem_b, depth_b, normal_b = unpack_small(
        head_small
    )
    out_weights = (
        sem_w.astype(jnp.bfloat16),
        depth_w.astype(jnp.bfloat16),
        normal_w.astype(jnp.bfloat16),
    )
    grid_shared = shared.reshape(rows_per_shard, columns_per_shard, wide_dev)
    row_views = []
    pre_list = [jnp.dot(shared, heads_w, preferred_element_type=jnp.float32)]
    for rate_index, rate in enumerate(aspp_rates):
        views = (
            row_view(grid_shared, -rate, fetch_rows),
            grid_shared,
            row_view(grid_shared, rate, fetch_rows),
        )
        row_views.append(views)
        summed = jnp.zeros((pixels, 3 * HID), jnp.float32)
        for tap_index in range(9):
            kernel_row, kernel_column = divmod(tap_index, 3)
            sliding_patch = column_view(views[kernel_row], (kernel_column - 1) * rate).reshape(
                pixels, wide_dev
            )
            summed = summed + contract_last(sliding_patch, rates_w[rate_index, tap_index])
        pre_list.append(summed)
    pre_parts = jnp.stack(pre_list, axis=1)
    before = lax.psum(pre_parts, "ch") + branch_bias[None]
    hidden = smooth(before).astype(jnp.bfloat16)
    branch_slope = smooth_slope(before).reshape(pixels, 4, 3, HID)
    joined_list = []
    projected_list = []
    top_list = []
    produced = []
    for task_index in range(3):
        joined = hidden[:, :, task_index * HID : (task_index + 1) * HID].reshape(pixels, 4 * HID)
        projected = (
            jnp.dot(joined, proj_w[task_index], preferred_element_type=jnp.float32)
            + proj_bias[task_index]
        )
        top = smooth(projected).astype(jnp.bfloat16)
        produced.append(jnp.dot(top, out_weights[task_index], preferred_element_type=jnp.float32))
        joined_list.append(joined)
        projected_list.append(projected)
        top_list.append(top)
    logits = produced[0] + sem_b
    depth_pred = produced[1] + depth_b
    normal_pred = produced[2] + normal_b
    slopes = loss_slopes(
        logits,
        depth_pred,
        normal_pred,
        sem_label,
        depth_target,
        normal_target,
        label_mask,
        task_counts,
    )
    out_grads = []
    out_bias_grads = []
    proj_grads = []
    proj_bias_grads = []
    joined_backs = []
    for task_index in range(3):
        top_back = contract_last(slopes[task_index], out_weights[task_index])
        proj_back = (top_back * smooth_slope(projected_list[task_index])).astype(jnp.bfloat16)
        out_grads.append(contract_first(top_list[task_index], slopes[task_index]))
        out_bias_grads.append(jnp.sum(slopes[task_index], axis=0, dtype=jnp.float32))
        proj_grads.append(contract_first(joined_list[task_index], proj_back))
        proj_bias_grads.append(jnp.sum(proj_back, axis=0, dtype=jnp.float32))
        joined_backs.append(contract_last(proj_back, proj_w[task_index]).reshape(pixels, 4, HID))
    joined_back = jnp.stack(joined_backs, axis=2)
    pre_grad = (joined_back * branch_slope).astype(jnp.bfloat16).reshape(pixels, 4, 3 * HID)
    small_term = (
        pack_small(
            [jnp.sum(pre_grad, axis=0, dtype=jnp.float32), jnp.stack(proj_bias_grads)]
            + out_grads
            + out_bias_grads
        )
        / groups
    )
    proj_grad = jnp.stack(proj_grads)
    first_branch = pre_grad[:, 0]
    task_sum = split_tasks(first_branch, heads_w)
    rates_list = []
    for rate_index, rate in enumerate(aspp_rates):
        flat_back = pre_grad[:, rate_index + 1]
        rate_back = flat_back.reshape(rows_per_shard, columns_per_shard, 3 * HID)
        back_views = (
            row_view(rate_back, rate, fetch_grads),
            rate_back,
            row_view(rate_back, -rate, fetch_grads),
        )
        for tap_index in range(9):
            kernel_row, kernel_column = divmod(tap_index, 3)
            sliding_patch = column_view(
                row_views[rate_index][kernel_row], (kernel_column - 1) * rate
            ).reshape(pixels, wide_dev)
            rates_list.append(contract_first(flat_back, sliding_patch))
            spread = column_view(back_views[kernel_row], (1 - kernel_column) * rate).reshape(
                pixels, 3 * HID
            )
            task_sum = task_sum + split_tasks_rows(spread, rates_w[rate_index, tap_index])
    rates_grad = jnp.stack(rates_list).reshape(3, 9, 3 * HID, wide_dev)
    task_grads = [task_sum[0], task_sum[1], task_sum[2]]
    head_grad = contract_first(shared, first_branch)
    local_gram = jnp.stack(
        [
            jnp.stack(
                [jnp.sum(task_grads[row_task] * task_grads[col_task]) for col_task in range(3)]
            )
            for row_task in range(3)
        ]
    )
    gram = lax.psum(local_gram, ("pix", "ch"))
    alphas = imtl_weights(gram)
    combined = alphas[0] * task_grads[0] + alphas[1] * task_grads[1] + alphas[2] * task_grads[2]
    shared_slope = combined * smooth_slope(summed_in)
    expand_up, gain_three_grad, shift_three_grad = backward_norm(
        shared_slope, hat_three, scale_three, count_all, gain_three
    )
    expand_back = expand_up.astype(jnp.bfloat16)
    expand_grad = contract_first(second_all, expand_back)
    second_back = channel_parts(contract_last(expand_back, expand_w))
    middle_up, gain_two_grad, shift_two_grad = backward_norm(
        second_back * smooth_slope(norm_two), hat_two, scale_two, count_all, gain_two
    )
    middle_gradient = middle_up.astype(jnp.bfloat16)
    dilated_list = []
    for tap_index in range(9):
        kernel_row, kernel_column = divmod(tap_index, 3)
        sliding_patch = bordered_input[
            kernel_row * DILATION_RATE : kernel_row * DILATION_RATE + rows_per_shard,
            kernel_column * DILATION_RATE : kernel_column * DILATION_RATE + columns_per_shard,
        ].reshape(pixels, M)
        dilated_list.append(contract_first(sliding_patch, middle_gradient))
    dilated_grad = jnp.stack(dilated_list)
    canvas_gradient = with_halo(
        middle_gradient.reshape(rows_per_shard, columns_per_shard, middle_per_shard),
        (("pix", 0),),
        DILATION_RATE,
    )
    canvas_gradient = jnp.pad(canvas_gradient, ((0, 0), (DILATION_RATE, DILATION_RATE), (0, 0)))
    first_part = jnp.zeros((pixels, M), jnp.float32)
    for tap_index in range(9):
        kernel_row, kernel_column = divmod(tap_index, 3)
        sliding_patch = canvas_gradient[
            (2 - kernel_row) * DILATION_RATE : (2 - kernel_row) * DILATION_RATE + rows_per_shard,
            (2 - kernel_column) * DILATION_RATE : (2 - kernel_column) * DILATION_RATE
            + columns_per_shard,
        ].reshape(pixels, middle_per_shard)
        first_part = first_part + contract_last(sliding_patch, dilated_w[tap_index])
    first_back = channel_parts(first_part) * mask_flat[:, None] * smooth_slope(norm_one)
    reduce_up, gain_one_grad, shift_one_grad = backward_norm(
        first_back, hat_one, scale_one, count_all, gain_one
    )
    reduce_all = channel_gather(reduce_up.astype(jnp.bfloat16))
    reduce_grad = contract_first(flat_in, reduce_all)
    input_grad = contract_last(reduce_all, reduce_w) + shared_slope
    reduce_shard, dilated_shard, expand_shard, head_shard, rates_shard, proj_shard = (
        lax.psum_scatter(reduce_grad, "pix", scatter_dimension=1, tiled=True),
        lax.psum_scatter(dilated_grad, "pix", scatter_dimension=1, tiled=True),
        lax.psum_scatter(expand_grad, "pix", scatter_dimension=0, tiled=True),
        lax.psum_scatter(head_grad, "pix", scatter_dimension=1, tiled=True),
        lax.psum_scatter(rates_grad, "pix", scatter_dimension=2, tiled=True),
        lax.psum_scatter(proj_grad, "pix", scatter_dimension=1, tiled=True),
    )
    norm_local = jnp.zeros((2, 2 * M + C), jnp.float32)
    for offset, width, gain_grad, shift_grad in (
        (0, middle_per_shard, gain_one_grad, shift_one_grad),
        (M, middle_per_shard, gain_two_grad, shift_two_grad),
        (2 * M, wide_dev, gain_three_grad, shift_three_grad),
    ):
        norm_local = lax.dynamic_update_slice(
            norm_local, jnp.stack([gain_grad, shift_grad]), (0, offset + block_id * width)
        )
    big_local = (
        jnp.sum(reduce_shard * reduce_shard)
        + jnp.sum(dilated_shard * dilated_shard)
        + jnp.sum(expand_shard * expand_shard)
        + jnp.sum(head_shard * head_shard)
        + jnp.sum(rates_shard * rates_shard)
        + jnp.sum(proj_shard * proj_shard) / groups
    )
    big_squares, norm_grad, small_grad = lax.psum(
        (big_local, norm_local / pix_devices, small_term), ("pix", "ch")
    )
    grad_norm = jnp.sqrt(
        big_squares + jnp.sum(norm_grad * norm_grad) + jnp.sum(small_grad * small_grad)
    )
    factor = jnp.minimum(1.0, CLIP_NORM / (grad_norm + 1e-06))
    reduce_new, reduce_first, reduce_second = adam_step(
        w_reduce, m_reduce, v_reduce, reduce_shard * factor, RATE_MATRIX, DECAY
    )
    dilated_new, dilated_first, dilated_second = adam_step(
        w_dilated, m_dilated, v_dilated, dilated_shard * factor, RATE_MATRIX, DECAY
    )
    expand_new, expand_first, expand_second = adam_step(
        w_expand, m_expand, v_expand, expand_shard * factor, RATE_MATRIX, DECAY
    )
    head_new, head_first, head_second = adam_step(
        head_weight, m_head, v_head, head_shard * factor, RATE_MATRIX, DECAY
    )
    rates_new, rates_first, rates_second = adam_step(
        head_rates, m_rates, v_rates, rates_shard * factor, RATE_MATRIX, DECAY
    )
    proj_new, proj_first, proj_second = adam_step(
        head_proj, m_proj, v_proj, proj_shard * factor, RATE_MATRIX, DECAY
    )
    norm_new, norm_first, norm_second = adam_step(
        norm_params, norm_m, norm_v, norm_grad * factor, RATE_SMALL, 0.0
    )
    small_new, small_first, small_second = adam_step(
        head_small, small_m, small_v, small_grad * factor, RATE_SMALL, 0.0
    )
    depth_bias_grad = small_grad[small_grad.shape[0] - 4]
    return (
        shared.reshape(rows_per_shard, columns_per_shard, wide_dev),
        input_grad.reshape(rows_per_shard, columns_per_shard, wide_dev),
        grad_norm,
        reduce_new,
        reduce_first,
        reduce_second,
        reduce_new.astype(jnp.bfloat16),
        dilated_new,
        dilated_first,
        dilated_second,
        dilated_new.astype(jnp.bfloat16),
        expand_new,
        expand_first,
        expand_second,
        expand_new.astype(jnp.bfloat16),
        head_new,
        head_first,
        head_second,
        head_new.astype(jnp.bfloat16),
        rates_new,
        rates_first,
        rates_second,
        rates_new.astype(jnp.bfloat16),
        proj_new,
        proj_first,
        proj_second,
        proj_new.astype(jnp.bfloat16),
        norm_new,
        norm_first,
        norm_second,
        small_new,
        small_first,
        small_second,
        depth_bias_grad,
    )


MESH = pl.DeviceIdType.MESH
BF = jnp.bfloat16
F32 = jnp.float32
NPIX = 8
NCH = 4
ROWS = 4
WIDTH = 128
PX = ROWS * WIDTH
CIN = C // NCH
COLS = 3 * HID // NPIX
SEGS = COLS // 32
VMEM_LIMIT = 60 * 2**20
SLOT = (0, 2, 3, 1)
ROWS_AHEAD = 3
BLOCK_VMEM = 60 * 2**20
SMALL_ROWS = 64
SMALL_PART = SMALL_ROWS // NCH
ROOT_TAP = 6


REACH = tuple(rate // ROWS for rate in aspp_rates)


def tap_groups():
    groups = []
    first = 0
    for rate_index, step in ((1, -1), (0, -1), (None, 0), (0, 0), (1, 0), (2, 0), (0, 1), (1, 1)):
        if rate_index is None:
            groups.append((0, first, 0, 0, (0,)))
            first += 1
        else:
            rate = aspp_rates[rate_index]
            groups.append((rate_index + 1, first, step, REACH[rate_index], (rate, 0, -rate)))
            first += 3
    return groups


TAP_GROUPS = tap_groups()
TAPS = 22
SEG_ROWS = TAPS * 32
WINDOW = 16 * 32


def window_of(block):
    return jnp.where(block < NPIX - REACH[1], 0, jnp.where(block >= REACH[1], 2, 1))


def whole_vmem():
    return pl.BlockSpec(memory_space=pltpu.VMEM)


def slide(tile, steps):
    lane = lax.broadcasted_iota(jnp.int32, tile.shape, 1)
    if steps == 0:
        return tile
    rolled = pltpu.roll(tile, steps % WIDTH, 1)
    if steps > 0:
        return jnp.where(lane >= steps, rolled, 0.0)
    return jnp.where(lane < WIDTH + steps, rolled, 0.0)


def tanh_parts(values):
    root = 0.7978845608028654
    inner = jnp.tanh(root * (values + 0.044715 * values * values * values))
    return root, inner


def gelu_of(values):
    _, inner = tanh_parts(values)
    return 0.5 * values * (1.0 + inner)


def gelu_slope(values):
    root, inner = tanh_parts(values)
    return 0.5 * (1.0 + inner) + 0.5 * values * (1.0 - inner * inner) * root * (
        1.0 + 3.0 * 0.044715 * values * values
    )


def nt_dot(left, right):
    return lax.dot_general(left, right, (((1,), (1,)), ((), ())), preferred_element_type=F32)


def nn_dot(left, right):
    return lax.dot_general(left, right, (((1,), (0,)), ((), ())), preferred_element_type=F32)


def greet(targets):
    barrier = pltpu.get_barrier_semaphore()
    for target in targets:
        pl.semaphore_signal(barrier, inc=1, device_id=target, device_id_type=MESH)
    return len(targets)


def await_greetings(count):
    pl.semaphore_wait(pltpu.get_barrier_semaphore(), count)


def from_hbm():
    return pl.BlockSpec(memory_space=pl.ANY)


def remote(src, dst, send_sem, recv_sem, target):
    return pltpu.make_async_remote_copy(
        src, dst, send_sem, recv_sem, device_id=target, device_id_type=MESH
    )


def place():
    p = lax.axis_index("pix")
    c = lax.axis_index("ch")
    return p, c, p // 2, lax.rem(p, 2), c // 2, lax.rem(c, 2)


def moved_segments():
    moves = []
    for pair in range(NPIX // 2):
        tasks = [[(SEGS * (2 * pair + side) + s) * 32 // HID for s in range(SEGS)] for side in range(2)]
        low, high = tasks[0][0], tasks[1][-1]
        if low == high:
            continue
        for side, keeps in ((0, low), (1, high)):
            for s in range(SEGS):
                if tasks[side][s] != keeps:
                    moves.append((2 * pair + side, s, 2 * pair + 1 - side))
    return moves


MOVES = moved_segments()


NALL = NPIX * NCH


def all_targets():
    me = lax.axis_index("pix") * NCH + lax.axis_index("ch")
    targets = []
    for d in range(1, NALL):
        other = lax.rem(me + d, NALL)
        targets.append((other // NCH, lax.rem(other, NCH)))
    return targets


def sum_everywhere(row, inbox, send_sem, recv_sem):
    me = lax.axis_index("pix") * NCH + lax.axis_index("ch")
    inbox[me, 0:1, :] = row
    view = inbox.at[me, 0:1]
    copies = [
        remote(view, view, send_sem.at[i], recv_sem.at[i], target) for i, target in enumerate(all_targets())
    ]
    for copy in copies:
        copy.start()
    for copy in copies:
        copy.wait()
    total = inbox[0, 0:1, :]
    for i in range(1, NALL):
        total = total + inbox[i, 0:1, :]
    return total


def heads_forward_kernel(
    x_ref, rates_hbm, root_ref, proj_ref, q_ref, xall_out, wpt_ref, w_out, w_more_ref,
    rates_ref, xall_ref, w_ref, acc, y_tmp, core_buf, core_in, x_buf, x_in, row_buf, local_sem,
    zr_send, zl_send, z_recv, y_send, y_recv, core_send, core_recv, x_send, x_recv, row_send, row_recv,
    pj_send, pj_recv, wm_send, wm_recv, eh_send, eh_recv,
):
    p, c, z, y, x, core = place()
    zcount = NPIX // 2
    up = (2 * lax.rem(z + 1, zcount) + y, c)
    down = (2 * lax.rem(z + zcount - 1, zcount) + y, c)
    other_y = (2 * z + 1 - y, c)
    other_core = (p, 2 * x + 1 - core)
    other_x = (p, 2 * (1 - x) + core)
    row_targets = [(lax.rem(p + d, NPIX), c) for d in range(1, NPIX)]
    ch_targets = [(p, lax.rem(c + d, NCH)) for d in range(1, NCH)]
    greeted = greet(row_targets + ch_targets)
    rates_in = pltpu.make_async_copy(rates_hbm, rates_ref, local_sem.at[3])
    rates_in.start()

    own = pltpu.make_async_copy(x_ref, xall_ref.at[p], local_sem.at[0])
    own.start()
    wpt_ref[c] = proj_ref[...]
    await_greetings(greeted)
    proj_copies = [
        remote(proj_ref, wpt_ref.at[c], pj_send.at[d - 1], pj_recv.at[d - 1], ch_targets[d - 1])
        for d in range(1, NCH)
    ]
    for copy in proj_copies:
        copy.start()

    def to_up(source):
        return remote(xall_ref.at[source], xall_ref.at[source], zr_send.at[source // 2], z_recv.at[source // 2], up)

    def to_down(source):
        return remote(xall_ref.at[source], xall_ref.at[source], zl_send.at[source // 2], z_recv.at[source // 2], down)

    def to_y(source):
        return remote(xall_ref.at[source], xall_ref.at[source], y_send.at[source // 2], y_recv.at[source // 2], other_y)

    def half_to(source, i, target):
        view = xall_ref.at[source, PX // 2 : PX]
        return remote(view, view, eh_send.at[i], eh_recv.at[i], target)

    def to_y_part(source):
        view = xall_ref.at[source, 0 : PX // 2]
        return remote(view, view, y_send.at[source // 2], y_recv.at[source // 2], other_y)

    def is_far_end(zs):
        return ((zs == 0) | (zs == zcount - 1)) & (zs != z)

    def step_of(i):
        near = jnp.where(z == 0, i, jnp.where(z == 3, 3 - i, 0))
        one = jnp.where(i == 0, 1, jnp.where(i == 1, 0, i))
        two = jnp.where(i == 0, 2, jnp.where(i == 1, 3, 3 - i))
        two = jnp.where(i == 2, 1, jnp.where(i == 3, 0, two))
        return jnp.where(z == 1, one, jnp.where(z == 2, two, near))

    own.wait()
    to_y(p).start()

    @pl.when(z < zcount - 1)
    def _():
        to_up(p).start()

    @pl.when(z > 0)
    def _():
        to_down(p).start()

    acc[...] = jnp.zeros_like(acc)
    root = root_ref[...]
    rates_in.wait()
    for s in range(SEGS):
        w_ref[s, ROOT_TAP * 32 : (ROOT_TAP + 1) * 32, :] = root[s * 32 : (s + 1) * 32].astype(BF)
        for branch, first, step, reach, shifts in TAP_GROUPS:
            if branch > 0:
                value = rates_ref[branch - 1, 3 * (step + 1) : 3 * (step + 2), s * 32 : (s + 1) * 32, :]
                w_ref[s, first * 32 : (first + 3) * 32, :] = value.astype(BF).reshape(96, CIN)

    def process(src):
        xb = xall_ref[src]

        first_row = pl.multiple_of(window_of(src) * 96, 32)

        def one_seg(s, carry):
            y_tmp[pl.ds(first_row, WINDOW), :] = nt_dot(w_ref[s, pl.ds(first_row, WINDOW), :], xb)

            def add_group(dest, branch, first_tap, shifts):
                rows = pl.ds(pl.multiple_of(SLOT[branch] * COLS + s * 32, 32), 32)
                for r in range(ROWS):
                    lanes = pl.ds(r * WIDTH, WIDTH)
                    total = acc[dest, rows, lanes]
                    for i, shift in enumerate(shifts):
                        tile = y_tmp[pl.ds((first_tap + i) * 32, 32), lanes]
                        total = total + slide(tile, shift)
                    acc[dest, rows, lanes] = total

            for branch, first_tap, step, reach, shifts in TAP_GROUPS:
                dest = src - step * reach
                if step == 0:
                    add_group(dest, branch, first_tap, shifts)
                else:

                    @pl.when((dest >= 0) & (dest < NPIX))
                    def _():
                        add_group(dest, branch, first_tap, shifts)

            return carry

        lax.fori_loop(0, SEGS, one_seg, 0)

    def lanes_of(ch):
        return pl.ds(pl.multiple_of(ch * WIDTH, WIDTH), WIDTH)

    half_rows = (slice(0, 2 * COLS), slice(2 * COLS, 4 * COLS))

    def core_copy(b, half):
        return remote(core_buf.at[half, b], core_in.at[half, b], core_send.at[half, b], core_recv.at[half, b], other_core)

    def x_copy(b, half):
        return remote(x_buf.at[half, b], x_in.at[half, b], x_send.at[half, b], x_recv.at[half, b], other_x)

    def row_copy(b, half, slot):
        return remote(
            row_buf.at[half, b],
            q_ref.at[2 * half : 2 * half + 2, pl.ds(pl.multiple_of(COLS * p, 32), COLS), :],
            row_send.at[half, slot],
            row_recv.at[half, slot],
            (b, c),
        )

    def core_start(b, half):
        for xx in range(2):
            core_buf[half, b, xx] = acc[b, half_rows[half], lanes_of(2 * xx + 1 - core)].astype(BF)
        core_copy(b, half).start()

    def x_start(b, half):
        core_copy(b, half).wait_recv()
        x_buf[half, b] = (
            acc[b, half_rows[half], lanes_of(2 * (1 - x) + core)] + core_in[half, b, 1 - x].astype(F32)
        ).astype(BF)
        x_copy(b, half).start()

    def finish(b, half):
        x_copy(b, half).wait_recv()
        total = (
            acc[b, half_rows[half], lanes_of(c)] + core_in[half, b, x].astype(F32) + x_in[half, b].astype(F32)
        )
        return total.astype(BF).reshape(2, COLS, WIDTH)

    def gather_step(i, carry):
        zs = step_of(i)
        mine = 2 * zs + y
        theirs = 2 * zs + 1 - y

        @pl.when(i > 0)
        def _():
            to_up(mine).wait_recv()

        @pl.when((zs < z) & (z < zcount - 1))
        def _():
            to_up(mine).start()

        @pl.when((zs > z) & (z > 0))
        def _():
            to_down(mine).start()

        far = is_far_end(zs)

        @pl.when((i > 0) & jnp.logical_not(far))
        def _():
            to_y(mine).start()

        @pl.when(far)
        def _():
            to_y_part(mine).start()

        process(mine)
        core_start(mine, 0)

        @pl.when(i > 0)
        def _():
            x_start(2 * step_of(i - 1) + 1 - y, 0)

        @pl.when(jnp.logical_not(far))
        def _():
            to_y(theirs).wait_recv()

        for end, i_end in ((0, 0), (zcount - 1, 1)):
            onward = up if end == 0 else down

            @pl.when((zs == end) & (z == end))
            def _():
                half_to(theirs, i_end, onward).start()

            @pl.when((zs == end) & (z != end))
            def _():
                to_y_part(theirs).wait_recv()
                half_to(theirs, i_end, onward).wait_recv()

            @pl.when((zs == end) & (z != end) & (z != zcount - 1 - end))
            def _():
                half_to(theirs, i_end, onward).start()

        process(theirs)
        core_start(theirs, 0)
        x_start(mine, 0)
        return carry

    lax.fori_loop(0, zcount, gather_step, 0)
    leaving = [
        pltpu.make_async_copy(xall_ref, xall_out, local_sem.at[1]),
        pltpu.make_async_copy(w_ref, w_out, local_sem.at[2]),
    ]
    for copy in leaving:
        copy.start()

    def weight_copy(i):
        return remote(w_ref.at[MOVES[i][1]], w_more_ref, wm_send.at[0], wm_recv.at[0], other_y)

    for i, (giver, s, receiver) in enumerate(MOVES):

        @pl.when(p == giver)
        def _():
            weight_copy(i).start()

    def block_after(d):
        return lax.rem(p + 1 + d, NPIX)

    def late_core(d, carry):
        core_start(block_after(d), 1)
        return carry

    lax.fori_loop(0, NPIX, late_core, 0)
    x_start(2 * step_of(zcount - 1) + 1 - y, 0)

    def late_x(d, carry):
        x_start(block_after(d), 1)
        return carry

    lax.fori_loop(0, NPIX, late_x, 0)
    own_rows = pl.ds(pl.multiple_of(COLS * p, 32), COLS)
    for half in range(2):

        def row_step(d, carry):
            b = block_after(d)
            row_buf[half, b] = finish(b, half)
            row_copy(b, half, d).start()
            return carry

        lax.fori_loop(0, NPIX - 1, row_step, 0)
        q_ref[2 * half : 2 * half + 2, own_rows, :] = finish(p, half)

    def drain(zs, carry):
        mine = 2 * zs + y

        @pl.when((zs <= z) & (z < zcount - 1))
        def _():
            to_up(mine).wait_send()

        @pl.when((zs >= z) & (z > 0))
        def _():
            to_down(mine).wait_send()

        far = is_far_end(zs)

        @pl.when(jnp.logical_not(far))
        def _():
            to_y(mine).wait_send()

        @pl.when(far)
        def _():
            to_y_part(mine).wait_send()

        return carry

    lax.fori_loop(0, zcount, drain, 0)
    for end, i_end in ((0, 0), (zcount - 1, 1)):

        @pl.when(z != zcount - 1 - end)
        def _():
            half_to(2 * end + 1 - y, i_end, up).wait_send()

    for half in range(2):

        def settle(d, carry):
            row_copy(block_after(d), half, d).wait()
            return carry

        lax.fori_loop(0, NPIX - 1, settle, 0)

        def settle_more(b, carry):
            core_copy(b, half).wait_send()
            x_copy(b, half).wait_send()
            return carry

        lax.fori_loop(0, NPIX, settle_more, 0)
    for copy in proj_copies + leaving:
        copy.wait()
    for i, (giver, s, receiver) in enumerate(MOVES):

        @pl.when(p == giver)
        def _():
            weight_copy(i).wait_send()

        @pl.when(p == receiver)
        def _():
            weight_copy(i).wait_recv()


def heads_forward(block_out, rates, root, proj_own):
    dma = pltpu.SemaphoreType.DMA
    zc = NPIX // 2
    return pl.pallas_call(
        heads_forward_kernel,
        out_shape=(
            jax.ShapeDtypeStruct((4, 3 * HID, WIDTH), BF),
            jax.ShapeDtypeStruct((NPIX, PX, CIN), BF),
            jax.ShapeDtypeStruct((NCH, 3, HID // NCH, 4 * HID), BF),
            jax.ShapeDtypeStruct((SEGS, SEG_ROWS, CIN), BF),
            jax.ShapeDtypeStruct((SEG_ROWS, CIN), BF),
        ),
        in_specs=[whole_vmem(), from_hbm(), whole_vmem(), whole_vmem()],
        out_specs=[whole_vmem(), from_hbm(), whole_vmem(), from_hbm(), whole_vmem()],
        scratch_shapes=[
            pltpu.VMEM((3, 9, COLS, CIN), F32),
            pltpu.VMEM((NPIX, PX, CIN), BF),
            pltpu.VMEM((SEGS, SEG_ROWS, CIN), BF),
            pltpu.VMEM((NPIX, 4 * COLS, PX), F32),
            pltpu.VMEM((SEG_ROWS, PX), F32),
            pltpu.VMEM((2, NPIX, 2, 2 * COLS, WIDTH), BF),
            pltpu.VMEM((2, NPIX, 2, 2 * COLS, WIDTH), BF),
            pltpu.VMEM((2, NPIX, 2 * COLS, WIDTH), BF),
            pltpu.VMEM((2, NPIX, 2 * COLS, WIDTH), BF),
            pltpu.VMEM((2, NPIX, 2, COLS, WIDTH), BF),
            dma((4,)),
            dma((zc,)), dma((zc,)), dma((zc,)), dma((zc,)), dma((zc,)),
            dma((2, NPIX)), dma((2, NPIX)), dma((2, NPIX)), dma((2, NPIX)),
            dma((2, NPIX - 1)), dma((2, NPIX - 1)),
            dma((NCH - 1,)), dma((NCH - 1,)), dma((1,)), dma((1,)), dma((2,)), dma((2,)),
        ],
        compiler_params=pltpu.CompilerParams(
            collective_id=1, has_side_effects=True, vmem_limit_bytes=VMEM_LIMIT
        ),
        name="heads_forward",
    )(block_out, rates, root, proj_own)


def heads_middle_part(
    q_ref, wpt_ref, small_ref, cols_ref, stats_ref, label_ref, depth_ref, normal_ref, mask_ref,
    dq_ref, dwp_ref, sums_ref, hid,
):
    c = lax.axis_index("ch")
    ones = jnp.ones((8, WIDTH), BF)
    columns = jnp.transpose(small_ref[...])
    out_w = jnp.transpose(cols_ref[...]).astype(BF)
    out_bias = columns[0:32, 15:16]
    sums_ref[...] = jnp.zeros_like(sums_ref)

    def spread(rows_8):
        return rows_8[0:1, :]

    for k in range(4):
        for t in range(3):
            cols = slice(t * HID, (t + 1) * HID)
            i = 3 * k + t
            hid[k, cols, :] = gelu_of(q_ref[SLOT[k], cols, :].astype(F32) + columns[:, i : i + 1]).astype(BF)
    row = lax.broadcasted_iota(jnp.int32, (32, WIDTH), 0)
    own_row = pl.ds(c, 1)
    out_sum = jnp.zeros((32, HID), F32)
    bias_sum = jnp.zeros((8, 32), F32)
    for t in range(3):
        cols = slice(t * HID, (t + 1) * HID)
        wpt = wpt_ref[:, t].reshape(HID, 4 * HID)
        zt = columns[:, 12 + t : 13 + t] + jnp.zeros((HID, WIDTH), F32)
        for k in range(4):
            zt = zt + nn_dot(wpt[:, k * HID : (k + 1) * HID], hid[k, cols, :])
        ut = gelu_of(zt).astype(BF)
        out = nn_dot(out_w, ut) + out_bias
        count = jnp.maximum(jnp.sum(stats_ref[2 + t : 3 + t, :], axis=1, keepdims=True), 1.0)
        scale = mask_ref[t, own_row, :].astype(F32) / count
        if t == 0:
            live = row < NCLS
            highest = jnp.max(jnp.where(live, out, -1e30), axis=0, keepdims=True)
            raised = jnp.where(live, jnp.exp(jnp.minimum(out - highest, 0.0)), 0.0)
            probs = raised / jnp.sum(raised, axis=0, keepdims=True)
            onehot = (row == label_ref[own_row, :]).astype(F32)
            slope = scale * (probs - onehot)
        elif t == 1:
            gap = out - depth_ref[own_row, :]
            slope = jnp.where(row == NCLS, scale * gap / jnp.sqrt(gap * gap + 1.0), 0.0)
        else:
            target = jnp.zeros((32, WIDTH), F32)
            for i in range(3):
                target = jnp.where(row == NCLS + 1 + i, normal_ref[i, own_row, :], target)
            slope = jnp.where((row > NCLS) & (row < NCLS + 4), scale * (out - target), 0.0)
        ot = slope.astype(BF)
        out_sum = out_sum + nt_dot(ot, ut)
        bias_sum = bias_sum + nt_dot(ones, ot)
        back = lax.dot_general(out_w, ot, (((0,), (0,)), ((), ())), preferred_element_type=F32)
        dz = (back * gelu_slope(zt)).astype(BF)
        sums_ref[12 + t : 13 + t, :] = spread(nt_dot(ones, dz))
        for k in range(4):
            part = hid[k, cols, :]
            product = nt_dot(part, dz).astype(BF)
            for half in range(2):
                for quarter in range(NCH):
                    start = half * 128 + quarter * 32
                    dwp_ref[quarter, t, 2 * k + half] = product[start : start + 32]
            dcat = lax.dot_general(
                wpt[:, k * HID : (k + 1) * HID], dz, (((0,), (0,)), ((), ())),
                preferred_element_type=F32,
            )
            i = 3 * k + t
            before = q_ref[SLOT[k], cols, :].astype(F32) + columns[:, i : i + 1]
            dq = (dcat * gelu_slope(before)).astype(BF)
            dq_ref[k, cols, :] = dq
            sums_ref[i : i + 1, :] = spread(nt_dot(ones, dq))
    sums_ref[15:16, 0:32] = spread(bias_sum)
    sums_ref[16:48, :] = out_sum


def fold(values):
    rows, lanes = values.shape
    total = values[0:8, 0:128]
    for r in range(rows // 8):
        for l in range(lanes // 128):
            if r or l:
                total = total + values[8 * r : 8 * r + 8, 128 * l : 128 * l + 128]
    return total


def heads_backward_kernel(
    q_ref, wpt_ref, small_ref, cols_ref, stats_ref, label_ref, depth_ref, normal_ref, mask_ref, xall_hbm, w_ref, w_more,
    rates_ref, gz_ref, square_ref, proj_out_ref, sums_out_ref, root_out_ref,
    dq_ref, dwp_ref, sums_ref, hid, dq_all, dq_more, wt, dcol, dcol_more, work, buf, z_out, oi_in, ac_in,
    gram_own, gram_all, proj_in, sums_in, dw_ref, blank, xall_ref,
    local_sem, out_sem, row_send, row_recv, x_send, x_recv, ca_send, ca_recv, cb_send, cb_recv,
    more_send, more_recv, fan_send, fan_recv,
    y_send, y_recv, oi_send, oi_recv, ac_send, ac_recv, gram_send, gram_recv, sp_send, sp_recv,
):
    p, c, z, y, x, core = place()
    zcount = NPIX // 2
    other_y = (2 * z + 1 - y, c)
    other_core = (p, 2 * x + 1 - core)
    other_x = (p, 2 * (1 - x) + core)
    pix_targets = [(lax.rem(p + d, NPIX), c) for d in range(1, NPIX)]
    ch_targets = [(p, lax.rem(c + d, NCH)) for d in range(1, NCH)]
    greeted = greet(all_targets())
    coming = pltpu.make_async_copy(xall_hbm, xall_ref, local_sem.at[1])
    coming.start()
    heads_middle_part(
        q_ref, wpt_ref, small_ref, cols_ref, stats_ref, label_ref, depth_ref, normal_ref, mask_ref,
        dq_ref, dwp_ref, sums_ref, hid,
    )
    await_greetings(greeted)
    far = 2 * (1 - x) + core

    def cols_of(b):
        return pl.ds(pl.multiple_of(COLS * b, 32), COLS)

    def row_copy(d):
        b = lax.rem(p + d, NPIX)
        return remote(dq_ref.at[:, cols_of(b), :], dq_all.at[p, c], row_send.at[d - 1], row_recv.at[d - 1], (b, c))

    def more_copy(i, source):
        giver, s, receiver = MOVES[i]
        start = giver * COLS + s * 32
        return remote(
            dq_ref.at[:, start : start + 32, :], dq_more.at[source, c],
            more_send.at[i], more_recv.at[source], (receiver, c),
        )

    def fan_copy(i, ch, target):
        return remote(dq_more.at[:, ch], dq_more.at[:, ch], fan_send.at[i], fan_recv.at[i], target)

    def any_of(flags):
        total = flags[0]
        for flag in flags[1:]:
            total = total | flag
        return total

    receives = any_of([p == move[2] for move in MOVES])

    for d in range(1, 1 + ROWS_AHEAD):
        row_copy(d).start()
    own = pltpu.make_async_copy(dq_ref.at[:, cols_of(p), :], dq_all.at[p, c], local_sem.at[0])
    own.start()
    for i, (giver, s, receiver) in enumerate(MOVES):
        start = giver * COLS + s * 32

        @pl.when(p == receiver)
        def _():
            dq_more[p, c] = dq_ref[:, start : start + 32, :]

        @pl.when(p != receiver)
        def _():
            more_copy(i, p).start()

    own.wait()

    def x_copy(d, b, ch):
        return remote(dq_all.at[b, ch], dq_all.at[b, ch], x_send.at[d], x_recv.at[d], other_x)

    def ca_copy(d, b, ch):
        return remote(dq_all.at[b, ch], dq_all.at[b, ch], ca_send.at[d], ca_recv.at[d], other_core)

    def cb_copy(d, b, ch):
        return remote(dq_all.at[b, ch], dq_all.at[b, ch], cb_send.at[d], cb_recv.at[d], other_core)

    def turn(win, s):
        value = jnp.transpose(w_ref[s, win * 96 : win * 96 + WINDOW, :].astype(F32)).astype(BF)
        lanes = slice(s * WINDOW, (s + 1) * WINDOW)
        givers = [move[0] for move in MOVES if move[1] == s]
        if givers:
            given = any_of([p == giver for giver in givers])
            wt[win, :, lanes] = jnp.where(given, jnp.zeros_like(value), value)
        else:
            wt[win, :, lanes] = value

    pieces = [(win, s) for win in range(3) for s in range(SEGS)]
    for d in range(NPIX):
        b = lax.rem(p + NPIX - d, NPIX)
        if d > 0:
            row_copy(d).wait()
            if d + ROWS_AHEAD < NPIX:
                row_copy(d + ROWS_AHEAD).start()
        x_copy(d, b, c).start()
        ca_copy(d, b, c).start()
        if d > 0:
            turn(*pieces[d - 1])
    for piece in pieces[NPIX - 1 :]:
        turn(*piece)

    @pl.when(receives)
    def _():
        for source in range(NPIX):

            @pl.when(p != source)
            def _():
                more_copy(0, source).wait_recv()

        fan_copy(0, c, other_x).start()
        fan_copy(1, c, other_core).start()

    for d in range(NPIX):
        b = lax.rem(p + NPIX - d, NPIX)
        x_copy(d, b, far).wait_recv()
        cb_copy(d, b, far).start()
    dw_ref[...] = jnp.zeros_like(dw_ref)
    blank[...] = jnp.zeros_like(blank)

    @pl.when(receives)
    def _():
        for win in range(3):
            wt[win, :, SEGS * WINDOW :] = jnp.transpose(
                w_more[win * 96 : win * 96 + WINDOW, :].astype(F32)
            ).astype(BF)
        fan_copy(0, far, other_x).wait_recv()
        fan_copy(2, far, other_core).start()

    for d in range(NPIX):
        b = lax.rem(p + NPIX - d, NPIX)
        ca_copy(d, b, 2 * x + 1 - core).wait_recv()
        cb_copy(d, b, 2 * (1 - x) + 1 - core).wait_recv()

    @pl.when(receives)
    def _():
        fan_copy(1, 2 * x + 1 - core, other_core).wait_recv()
        fan_copy(2, 2 * (1 - x) + 1 - core, other_core).wait_recv()

    ride = []
    for d in range(1, NCH):
        other = lax.rem(c + d, NCH)
        part = pl.ds(pl.multiple_of(other * SMALL_PART, SMALL_PART), SMALL_PART)
        ride.append(remote(dwp_ref.at[other], proj_in.at[c], sp_send.at[0, d - 1], sp_recv.at[0, d - 1], (p, other)))
        ride.append(remote(sums_ref.at[part], sums_in.at[c], sp_send.at[1, d - 1], sp_recv.at[1, d - 1], (p, other)))
    for copy in ride:
        copy.start()

    def one_block(b):
        win = window_of(b)

        def each_group(visit, clear):
            for branch, first_tap, step, reach, shifts in TAP_GROUPS:
                first_row = first_tap * 32 - win * 96
                source = b - step * reach
                if step == 0:
                    visit(source, branch, first_row, shifts)
                else:
                    in_window = win <= 1 if step < 0 else win >= 1
                    if reach == REACH[1]:
                        in_window = win == 1 + step
                    inside = (source >= 0) & (source < NPIX)

                    @pl.when(inside)
                    def _():
                        visit(source, branch, first_row, shifts)

                    @pl.when(in_window & jnp.logical_not(inside))
                    def _():
                        clear(first_row)

        def visit(source, branch, first_row, shifts):
            for r in range(ROWS):
                lanes = pl.ds(r * WIDTH, WIDTH)
                tile = dq_all[source, r, branch].astype(F32)
                for t, shift in enumerate(shifts):
                    moved = slide(tile, -shift).astype(BF)
                    for s in range(SEGS):
                        rows = pl.ds(pl.multiple_of(s * WINDOW + first_row + t * 32, 32), 32)
                        dcol[b, rows, lanes] = moved[s * 32 : (s + 1) * 32]

        def clear(first_row):
            for s in range(SEGS):
                rows = pl.ds(pl.multiple_of(s * WINDOW + first_row, 32), 96)
                dcol[b, rows, :] = jnp.zeros((96, PX), BF)

        def visit_more(source, branch, first_row, shifts):
            for r in range(ROWS):
                lanes = pl.ds(r * WIDTH, WIDTH)
                tile = dq_more[source, r, branch].astype(F32)
                for t, shift in enumerate(shifts):
                    rows = pl.ds(pl.multiple_of(first_row + t * 32, 32), 32)
                    dcol_more[rows, lanes] = slide(tile, -shift).astype(BF)

        def clear_more(first_row):
            dcol_more[pl.ds(pl.multiple_of(first_row, 32), 96), :] = jnp.zeros((96, PX), BF)

        each_group(visit, clear)
        work[...] = nn_dot(wt[win, :, : SEGS * WINDOW], dcol[b])

        @pl.when(receives)
        def _():
            each_group(visit_more, clear_more)
            work[...] += nn_dot(wt[win, :, SEGS * WINDOW :], dcol_more[...])

        buf[b] = work[...].astype(BF)

    mirrored = z >= 2
    outer = (z == 0) | (z == zcount - 1)
    inner = jnp.logical_not(outer)
    has_near = y == z - 1

    def true_z(e):
        return jnp.where(mirrored, zcount - 1 - e, e)

    def block_at(e):
        return 2 * true_z(e) + y

    def arrived_at(e):
        return NPIX + true_z(e)

    def near_at(e):
        return jnp.where(has_near, block_at(e), arrived_at(e))

    def mid_at(e):
        return jnp.where(has_near, arrived_at(e), block_at(e))

    def y_copy(zz):
        return remote(buf.at[2 * zz + 1 - y], buf.at[NPIX + zz], y_send.at[zz], y_recv.at[zz], other_y)

    oi_z = jnp.where(z == 0, 1, jnp.where(z == 1, 0, jnp.where(z == 2, 3, 2)))

    def oi_copy(i, source):
        return remote(source, oi_in.at[i], oi_send.at[i], oi_recv.at[i], (2 * oi_z + y, c))

    def ac_copy(i, source):
        return remote(source, ac_in.at[i], ac_send.at[i], ac_recv.at[i], (2 * (zcount - 1 - z) + y, c))

    def order(i):
        last = jnp.where(outer, zcount - 1 - i, i - 2)
        return jnp.where(i < 2, zcount - 1 - i, last)

    def sum_of(first, second):
        return (first.astype(F32) + second.astype(F32)).astype(BF)

    def block_pair(i, carry):
        zz = true_z(order(i))

        def either(j, inner_carry):
            one_block(2 * zz + jnp.where(j == 0, 1 - y, y))

            @pl.when(j == 0)
            def _():
                y_copy(zz).start()

            return inner_carry

        lax.fori_loop(0, 2, either, 0)

        @pl.when(i > 0)
        def _():
            y_copy(true_z(order(i - 1))).wait_recv()

        for step in range(1, zcount):

            @pl.when((i == step) & outer)
            def _():
                e = zcount - step
                z_out[step - 1] = sum_of(buf[block_at(e)], buf[arrived_at(e)])
                oi_copy(step - 1, z_out.at[step - 1]).start()

        @pl.when((i == 1) & inner)
        def _():
            ac_copy(0, buf.at[mid_at(3)]).start()

        @pl.when((i == 2) & inner)
        def _():
            ac_copy(1, buf.at[mid_at(2)]).start()
            oi_copy(0, z_out.at[0]).wait_recv()
            z_out[0] = sum_of(oi_in[0], buf[near_at(3)])
            ac_copy(2, z_out.at[0]).start()

        @pl.when((i == 3) & inner)
        def _():
            oi_copy(0, buf.at[near_at(0)]).start()
            oi_copy(1, z_out.at[0]).wait_recv()
            z_out[1] = sum_of(oi_in[1], buf[near_at(2)])
            ac_copy(3, z_out.at[1]).start()

        return carry

    lax.fori_loop(0, zcount, block_pair, 0)

    def weight_block(b, carry):
        first_tap = window_of(b) * 3

        def one_seg(s, inner_carry):
            rows = pl.ds(pl.multiple_of(s * WINDOW, WINDOW), WINDOW)
            taps = pl.ds(first_tap, WINDOW // 32)
            dw_ref[s, taps] += nn_dot(dcol[b, rows, :], xall_ref[b]).reshape(WINDOW // 32, 32, CIN)
            return inner_carry

        return lax.fori_loop(0, SEGS, one_seg, carry)

    coming.wait()
    lax.fori_loop(0, NPIX // 2, weight_block, 0)

    @pl.when(inner)
    def _():
        ac_copy(0, z_out.at[0]).wait_recv()
        z_out[2] = sum_of(ac_in[0], buf[mid_at(0)])
        oi_copy(1, z_out.at[2]).start()
        ac_copy(2, z_out.at[0]).wait_recv()
        oi_copy(2, ac_in.at[2]).start()

    lax.fori_loop(NPIX // 2, NPIX, weight_block, 0)
    out_copies = []
    at = {(group[0] - 1, group[2]): group[1] for group in TAP_GROUPS if group[0] > 0}
    for rate_index in range(3):
        for step in (-1, 0, 1):
            first = at.get((rate_index, step))
            for s in range(SEGS):
                source = blank if first is None else dw_ref.at[s, first : first + 3]
                out_copies.append(
                    pltpu.make_async_copy(
                        source,
                        rates_ref.at[rate_index, 3 * (step + 1) : 3 * (step + 2), s * 32 : (s + 1) * 32, :],
                        out_sem.at[len(out_copies)],
                    )
                )
    for copy in out_copies:
        copy.start()
    square_ref[...] = jnp.zeros_like(square_ref)

    def square_rows(m, carry):
        s = m // TAPS
        part = dw_ref[s, lax.rem(m, TAPS)]
        square_ref[...] += fold(part * part)
        return carry

    lax.fori_loop(0, SEGS * TAPS, square_rows, 0)

    for copy in ride:
        copy.wait()
    for t in range(3):
        total = dwp_ref[c, t].astype(F32)
        for d in range(1, NCH):
            total = total + proj_in[lax.rem(c + d, NCH), t].astype(F32)
        total = total.astype(BF)
        for b in range(NPIX):
            proj_out_ref[b, t] = total[b]
    total = sums_ref[pl.ds(pl.multiple_of(c * SMALL_PART, SMALL_PART), SMALL_PART), :]
    for d in range(1, NCH):
        total = total + sums_in[lax.rem(c + d, NCH)]
    sums_out_ref[...] = total
    for s in range(SEGS):
        root_out_ref[s * 32 : (s + 1) * 32, :] = dw_ref[s, ROOT_TAP]

    for copy in out_copies:
        copy.wait()
    near_task = jnp.where(mirrored, 2, 0)
    far_task = jnp.where(mirrored, 0, 2)
    y_copy(true_z(order(zcount - 1))).wait_recv()

    def keep(task, value):
        dw_ref[task, 0:16] = value.reshape(16, 32, PX)

    @pl.when(outer)
    def _():
        for i in range(3):
            oi_copy(i, z_out.at[0]).wait_recv()
        keep(near_task, buf[block_at(0)].astype(F32) + buf[arrived_at(0)].astype(F32) + oi_in[0].astype(F32))
        keep(1, oi_in[1].astype(F32))
        keep(far_task, oi_in[2].astype(F32))

    @pl.when(inner)
    def _():
        oi_copy(2, z_out.at[0]).wait_recv()
        ac_copy(1, z_out.at[0]).wait_recv()
        ac_copy(3, z_out.at[0]).wait_recv()
        keep(near_task, oi_in[2].astype(F32) + buf[near_at(1)].astype(F32))
        keep(1, buf[mid_at(1)].astype(F32) + ac_in[1].astype(F32))
        keep(far_task, ac_in[3].astype(F32))

    pairs = ((0, 0), (0, 1), (0, 2), (1, 1), (1, 2), (2, 2))
    gram_own[...] = jnp.zeros_like(gram_own)

    def gram_rows(m, carry):
        tasks = [dw_ref[t, m] for t in range(3)]
        for i, (a, b) in enumerate(pairs):
            gram_own[i] += fold(tasks[a] * tasks[b])
        return carry

    lax.fori_loop(0, CIN // 32, gram_rows, 0)

    lane = lax.broadcasted_iota(jnp.int32, (1, 128), 1)
    row = jnp.zeros((1, 128), F32)
    for i in range(6):
        value = jnp.sum(column_sums(gram_own[i]), axis=1, keepdims=True)
        row = row + jnp.where(lane == i, value, 0.0)
    row = sum_everywhere(row, gram_all, gram_send, gram_recv)
    entry = {}
    for i, (a, b) in enumerate(pairs):
        value = jnp.sum(jnp.where(lane == i, row, 0.0), axis=1, keepdims=True)
        entry[(a, b)] = value
        entry[(b, a)] = value
    lengths = [jnp.sqrt(entry[(t, t)] + 1e-12) for t in range(3)]

    def pairing(row_task, col_task):
        return (
            entry[(0, 0)] / lengths[0]
            - entry[(0, col_task)] / lengths[col_task]
            - entry[(row_task, 0)] / lengths[0]
            + entry[(row_task, col_task)] / lengths[col_task]
        )

    right_one = entry[(0, 0)] / lengths[0] - entry[(0, 1)] / lengths[1]
    right_two = entry[(0, 0)] / lengths[0] - entry[(0, 2)] / lengths[2]
    upper_left, upper_right = pairing(1, 1), pairing(1, 2)
    lower_left, lower_right = pairing(2, 1), pairing(2, 2)
    determinant = upper_left * lower_right - upper_right * lower_left
    alpha_one = (right_one * lower_right - right_two * lower_left) / determinant
    alpha_two = (right_two * upper_left - right_one * upper_right) / determinant
    alpha_zero = 1.0 - alpha_one - alpha_two

    for m in range(CIN // 128):
        tasks = [dw_ref[t, 4 * m : 4 * m + 4].reshape(128, PX) for t in range(3)]
        mixed = alpha_zero * tasks[0] + alpha_one * tasks[1] + alpha_two * tasks[2]
        gz_ref[:, m * 128 : (m + 1) * 128] = jnp.transpose(mixed)

    for d in range(NPIX):
        b = lax.rem(p + NPIX - d, NPIX)
        x_copy(d, b, c).wait_send()
        ca_copy(d, b, c).wait_send()
        cb_copy(d, b, far).wait_send()
    for i, (giver, s, receiver) in enumerate(MOVES):

        @pl.when(p != receiver)
        def _():
            more_copy(i, p).wait_send()

    @pl.when(receives)
    def _():
        fan_copy(0, c, other_x).wait_send()
        fan_copy(1, c, other_core).wait_send()
        fan_copy(2, far, other_core).wait_send()

    for i in range(zcount):
        y_copy(i).wait_send()
    for i in range(3):
        oi_copy(i, z_out.at[0]).wait_send()

    @pl.when(inner)
    def _():
        for i in range(4):
            ac_copy(i, z_out.at[0]).wait_send()


def heads_backward(*operands):
    dma = pltpu.SemaphoreType.DMA
    zc = NPIX // 2
    return pl.pallas_call(
        heads_backward_kernel,
        out_shape=(
            jax.ShapeDtypeStruct((3, 9, COLS, CIN), F32),
            jax.ShapeDtypeStruct((PX, CIN), F32),
            jax.ShapeDtypeStruct((8, 128), F32),
            jax.ShapeDtypeStruct((NPIX, 3, 32, HID), BF),
            jax.ShapeDtypeStruct((SMALL_PART, HID), F32),
            jax.ShapeDtypeStruct((COLS, CIN), F32),
        ),
        in_specs=[whole_vmem()] * 9 + [from_hbm()] + [whole_vmem()] * 2,
        out_specs=[pl.BlockSpec(memory_space=pl.ANY)] + [whole_vmem()] * 5,
        scratch_shapes=[
            pltpu.VMEM((4, 3 * HID, WIDTH), BF),
            pltpu.VMEM((NCH, 3, NPIX, 32, HID), BF),
            pltpu.VMEM((SMALL_ROWS, HID), F32),
            pltpu.VMEM((4, 3 * HID, WIDTH), BF),
            pltpu.VMEM((NPIX, NCH, 4, COLS, WIDTH), BF),
            pltpu.VMEM((NPIX, NCH, 4, 32, WIDTH), BF),
            pltpu.VMEM((3, CIN, (SEGS + 1) * WINDOW), BF),
            pltpu.VMEM((NPIX, SEGS * WINDOW, PX), BF),
            pltpu.VMEM((WINDOW, PX), BF),
            pltpu.VMEM((CIN, PX), F32),
            pltpu.VMEM((NPIX + zc, CIN, PX), BF),
            pltpu.VMEM((3, CIN, PX), BF),
            pltpu.VMEM((3, CIN, PX), BF),
            pltpu.VMEM((4, CIN, PX), BF),
            pltpu.VMEM((6, 8, 128), F32),
            pltpu.VMEM((NALL, 8, 128), F32),
            pltpu.VMEM((NCH, 3, NPIX, 32, HID), BF),
            pltpu.VMEM((NCH, SMALL_PART, HID), F32),
            pltpu.VMEM((SEGS, TAPS, 32, CIN), F32),
            pltpu.VMEM((3, 32, CIN), F32),
            pltpu.VMEM((NPIX, PX, CIN), BF),
            dma((2,)), dma((9 * SEGS,)),
            dma((NPIX - 1,)), dma((NPIX - 1,)),
            dma((NPIX,)), dma((NPIX,)), dma((NPIX,)), dma((NPIX,)), dma((NPIX,)), dma((NPIX,)),
            dma((len(MOVES),)), dma((NPIX,)), dma((3,)), dma((3,)),
            dma((zc,)), dma((zc,)), dma((3,)), dma((3,)), dma((4,)), dma((4,)),
            dma((NALL - 1,)), dma((NALL - 1,)),
            dma((2, NCH - 1)), dma((2, NCH - 1)),
        ],
        compiler_params=pltpu.CompilerParams(
            collective_id=2, has_side_effects=True, vmem_limit_bytes=VMEM_LIMIT
        ),
        name="heads_backward",
    )(*operands)


MID = M // NCH
WPART = M // NPIX
TAP_LANES = 9 * MID
W_REDUCE = slice(0, CIN)
W_DILATED = slice(CIN, CIN + TAP_LANES)
W_EXPAND = slice(CIN + TAP_LANES, 2 * CIN + TAP_LANES)
W_LANES = 2 * CIN + TAP_LANES


def slide_rows(tile, steps):
    if steps == 0:
        return tile
    line = lax.broadcasted_iota(jnp.int32, (WIDTH, tile.shape[1]), 0)
    keep = line >= steps if steps > 0 else line < WIDTH + steps
    pieces = []
    for r in range(ROWS):
        rolled = pltpu.roll(tile[r * WIDTH : (r + 1) * WIDTH], steps % WIDTH, 0)
        pieces.append(jnp.where(keep, rolled, 0.0))
    return jnp.concatenate(pieces, axis=0)


def column_sums(values):
    return jnp.sum(values, axis=0, keepdims=True)


def pix_copies(inbox, send_sem, recv_sem, rows=8):
    p, c = lax.axis_index("pix"), lax.axis_index("ch")
    view = inbox.at[p] if rows == 8 else inbox.at[p, 0:rows]
    return [
        remote(view, view, send_sem.at[d - 1], recv_sem.at[d - 1], (lax.rem(p + d, NPIX), c))
        for d in range(1, NPIX)
    ]


def ch_copies(source, inbox, send_sem, recv_sem):
    p, c = lax.axis_index("pix"), lax.axis_index("ch")
    copies = []
    for d in range(1, NCH):
        other = lax.rem(c + d, NCH)
        copies.append(remote(source(other), inbox.at[c], send_sem.at[d - 1], recv_sem.at[d - 1], (p, other)))
    return copies


def start_all(copies):
    for copy in copies:
        copy.start()


def wait_all(copies):
    for copy in copies:
        copy.wait()


def add_up(inbox):
    total = inbox[0]
    for i in range(1, inbox.shape[0]):
        total = total + inbox[i]
    return total


def block_forward_kernel(
    x_ref, mask_ref, label_ref, reduce_ref, dilated_ref, expand_ref, head_proj_ref, norm_ref,
    out_ref, hat_one_out, hat_two_out, hat_three_ref, wall_out, first_out, second_out, stats_ref, stats_wide_ref, wpt_ref,
    hat_one_ref, hat_two_ref, wall_ref, first_ref, second_ref, out_sem,
    w_ref, proj_ref, turned, mask_t, work, ch_buf, ch_in, halo_buf, halo_in, stat_one, stat_two, stat_three,
    local_sem, wz_send, wz_recv, wy_send, wy_recv, c_send, c_recv, s_send, s_recv, h_send, h_recv,
):
    p, c, z, y, x, core = place()
    zcount = NPIX // 2
    other_y = (2 * z + 1 - y, c)
    pix_targets = [(lax.rem(p + d, NPIX), c) for d in range(1, NPIX)]
    ch_targets = [(p, lax.rem(c + d, NCH)) for d in range(1, NCH)]
    greeted = greet(pix_targets + ch_targets)
    w_ref[:, W_REDUCE] = reduce_ref[...].astype(BF)
    for tap in range(9):
        w_ref[:, CIN + tap * MID : CIN + (tap + 1) * MID] = dilated_ref[tap].astype(BF)
    w_ref[:, W_EXPAND] = expand_ref[...].astype(BF)
    for t in range(3):
        turned[...] = jnp.transpose(head_proj_ref[t])
        quarter = pl.ds(pl.multiple_of(c * (HID // NCH), HID // NCH), HID // NCH)
        proj_ref[t] = turned[quarter, :].astype(BF)
    mask_t[...] = jnp.zeros_like(mask_t)
    mask_t[0:ROWS, :] = mask_ref[...].astype(F32)

    def param(row, offset, width):
        return norm_ref[row : row + 1, pl.ds(pl.multiple_of(offset + c * width, 128), width)]

    await_greetings(greeted)
    parts = (pl.ds(0, CIN), pl.ds(CIN, TAP_LANES), pl.ds(CIN + TAP_LANES, CIN))

    def shard(part):
        return w_ref.at[:, parts[part]] if part < 3 else proj_ref

    def spot(part, source):
        if part < 3:
            return wall_ref.at[source, :, parts[part]]
        return wpt_ref.at[:, :, pl.ds(pl.multiple_of(source * 128, 128), 128)]

    def wz_copy(part, d):
        target = (2 * lax.rem(z + d, zcount) + y, c)
        return remote(
            shard(part), spot(part, p),
            wz_send.at[part, d - 1], wz_recv.at[part, d - 1], target,
        )

    def wy_copy(part, d):
        source = 2 * lax.rem(z + zcount - d, zcount) + y
        src = shard(part) if d == 0 else spot(part, source)
        return remote(
            src, spot(part, source), wy_send.at[part, d], wy_recv.at[part, d], other_y
        )

    def send_z(part):
        for d in range(1, zcount):
            wz_copy(part, d).start()

    wy_copy(0, 0).start()
    send_z(0)
    own = pltpu.make_async_copy(w_ref, wall_ref.at[p], local_sem.at[0])
    own.start()
    own_proj = pltpu.make_async_copy(proj_ref, spot(3, p), local_sem.at[1])
    own_proj.start()
    own.wait()
    own_proj.wait()

    def forward_part(part):
        for d in range(1, zcount):
            wz_copy(part, d).wait_recv()
            wy_copy(part, d).start()

    def receive_part(part):
        for d in range(zcount):
            wy_copy(part, d).wait_recv()

    def weights(lanes):
        return wall_ref[:, :, lanes].reshape(M, lanes.stop - lanes.start)

    def stat_round(index, inbox, values):
        inbox[p, 0:1, :] = column_sums(values)
        inbox[p, 1:2, :] = column_sums(values * values)
        rows = 8 if index == 0 else 2
        copies = pix_copies(inbox, s_send.at[index], s_recv.at[index], rows)
        start_all(copies)
        wait_all(copies)
        return add_up(inbox[:, 0:rows])

    count_all = float(NPIX * PX)

    def norm_of(values, sums, gain, shift):
        mean = sums[0:1] / count_all
        scale = lax.rsqrt(sums[1:2] / count_all - mean * mean + EPS_NORM)
        hat = (values - mean) * scale
        return hat, hat * gain + shift, scale

    forward_part(0)
    send_z(1)
    receive_part(0)
    wy_copy(1, 0).start()
    for m in range(NCH):
        wanted = wall_ref[2 * m : 2 * m + 2, :, W_REDUCE].reshape(MID, CIN)
        value = nt_dot(x_ref[...], wanted)
        ch_buf[0, m] = value.astype(BF)

        @pl.when(m == c)
        def _():
            work[...] = value

    reduce_copies = ch_copies(lambda other: ch_buf.at[0, other], ch_in, c_send.at[0], c_recv.at[0])
    start_all(reduce_copies)
    wait_all(reduce_copies)
    forward_part(1)
    reduced = work[...]
    for d in range(1, NCH):
        reduced = reduced + ch_in[lax.rem(c + d, NCH)].astype(F32)
    stat_one[p] = jnp.zeros((8, MID), F32)
    for t in range(3):
        stat_one[p, 2 + t : 3 + t, :] = column_sums(label_ref[t].astype(F32))
    sums = stat_round(0, stat_one, reduced)
    hat, normed, scale = norm_of(reduced, sums, param(0, 0, MID), param(1, 0, MID))
    hat_one_ref[...] = hat
    stats_ref[...] = jnp.zeros_like(stats_ref)
    stats_ref[0:1, :] = scale
    stats_ref[2:5, :] = sums[2:5]

    def own_lanes():
        return pl.ds(pl.multiple_of(c * MID, MID), MID)

    def gather_copies(ref, index):
        copies = []
        for d in range(1, NCH):
            copies.append(
                remote(
                    ref.at[:, own_lanes()], ref.at[:, own_lanes()],
                    c_send.at[index, d - 1], c_recv.at[index, d - 1], ch_targets[d - 1],
                )
            )
        return copies

    mask = jnp.transpose(mask_t[...])
    mask = jnp.concatenate(
        [jnp.broadcast_to(mask[:, r : r + 1], (WIDTH, MID)) for r in range(ROWS)], axis=0
    )
    first_ref[:, own_lanes()] = (gelu_of(normed) * mask).astype(BF)
    copies = gather_copies(first_ref, 1)
    start_all(copies)
    send_z(2)
    wait_all(copies)
    receive_part(1)
    wy_copy(2, 0).start()

    def row_part(step):
        total = jnp.zeros((PX, MID), F32)
        for col in range(3):
            tap = 3 * (step + 1) + col
            lanes = slice(CIN + tap * MID, CIN + (tap + 1) * MID)
            total = total + slide_rows(nn_dot(first_ref[...], weights(lanes)), -DILATION_RATE * (col - 1))
        return total

    def halo_copy(side):
        target = (p - 1, c) if side == 0 else (p + 1, c)
        return remote(halo_buf.at[side], halo_in.at[side], h_send.at[side], h_recv.at[side], target)

    halo_buf[0] = row_part(1).astype(BF)

    @pl.when(p > 0)
    def _():
        halo_copy(0).start()

    halo_buf[1] = row_part(-1).astype(BF)

    @pl.when(p < NPIX - 1)
    def _():
        halo_copy(1).start()

    work[...] = row_part(0)

    @pl.when(p < NPIX - 1)
    def _():
        halo_copy(0).wait_recv()
        work[...] += halo_in[0].astype(F32)

    @pl.when(p > 0)
    def _():
        halo_copy(1).wait_recv()
        work[...] += halo_in[1].astype(F32)

    forward_part(2)
    send_z(3)
    wy_copy(3, 0).start()
    middle = work[...]
    sums = stat_round(1, stat_two, middle)
    hat, normed, scale = norm_of(middle, sums, param(0, M, MID), param(1, M, MID))
    hat_two_ref[...] = hat
    stats_ref[1:2, :] = scale
    second_ref[:, own_lanes()] = gelu_of(normed).astype(BF)
    copies = gather_copies(second_ref, 2)
    start_all(copies)
    wait_all(copies)

    receive_part(2)
    hat_three_ref[...] = nn_dot(second_ref[...], weights(W_EXPAND))
    expanded = hat_three_ref[...]
    leaving = [
        pltpu.make_async_copy(ref, out, out_sem.at[i])
        for i, (ref, out) in enumerate(
            (
                (hat_one_ref, hat_one_out), (hat_two_ref, hat_two_out), (wall_ref, wall_out),
                (first_ref, first_out), (second_ref, second_out),
            )
        )
    ]
    start_all(leaving)
    forward_part(3)
    sums = stat_round(2, stat_three, expanded)
    hat, normed, scale = norm_of(expanded, sums, param(0, 2 * M, CIN), param(1, 2 * M, CIN))
    hat_three_ref[...] = hat
    stats_wide_ref[...] = jnp.broadcast_to(scale, stats_wide_ref.shape)
    out_ref[...] = gelu_of(normed + x_ref[...].astype(F32)).astype(BF)
    receive_part(3)
    wait_all(leaving)

    for part in range(4):
        for d in range(zcount):
            wy_copy(part, d).wait_send()
        for d in range(1, zcount):
            wz_copy(part, d).wait_send()

    @pl.when(p > 0)
    def _():
        halo_copy(0).wait_send()

    @pl.when(p < NPIX - 1)
    def _():
        halo_copy(1).wait_send()


def block_forward(*operands):
    dma = pltpu.SemaphoreType.DMA
    zc = NPIX // 2
    shape = jax.ShapeDtypeStruct
    return pl.pallas_call(
        block_forward_kernel,
        out_shape=(
            shape((PX, CIN), BF),
            shape((PX, MID), F32),
            shape((PX, MID), F32),
            shape((PX, CIN), F32),
            shape((NPIX, WPART, W_LANES), BF),
            shape((PX, M), BF),
            shape((PX, M), BF),
            shape((8, MID), F32),
            shape((8, CIN), F32),
            shape((3, HID // NCH, 4 * HID), BF),
        ),
        in_specs=[whole_vmem()] * 8,
        out_specs=[whole_vmem()] + [from_hbm()] * 2 + [whole_vmem()] + [from_hbm()] * 3 + [whole_vmem()] * 3,
        scratch_shapes=[
            pltpu.VMEM((PX, MID), F32),
            pltpu.VMEM((PX, MID), F32),
            pltpu.VMEM((NPIX, WPART, W_LANES), BF),
            pltpu.VMEM((PX, M), BF),
            pltpu.VMEM((PX, M), BF),
            dma((5,)),
            pltpu.VMEM((WPART, W_LANES), BF),
            pltpu.VMEM((3, HID // NCH, 128), BF),
            pltpu.VMEM((HID, 128), F32),
            pltpu.VMEM((8, WIDTH), F32),
            pltpu.VMEM((PX, MID), F32),
            pltpu.VMEM((1, NCH, PX, MID), BF),
            pltpu.VMEM((NCH, PX, MID), BF),
            pltpu.VMEM((2, PX, MID), BF),
            pltpu.VMEM((2, PX, MID), BF),
            pltpu.VMEM((NPIX, 8, MID), F32),
            pltpu.VMEM((NPIX, 8, MID), F32),
            pltpu.VMEM((NPIX, 8, CIN), F32),
            dma((2,)),
            dma((4, zc - 1)), dma((4, zc - 1)), dma((4, zc)), dma((4, zc)),
            dma((3, NCH - 1)), dma((3, NCH - 1)),
            dma((3, NPIX - 1)), dma((3, NPIX - 1)),
            dma((2,)), dma((2,)),
        ],
        compiler_params=pltpu.CompilerParams(
            collective_id=0, has_side_effects=True, vmem_limit_bytes=BLOCK_VMEM
        ),
        name="block_forward",
    )(*operands)


def block_backward_kernel(
    gz_hbm, x_hbm, mask_ref, wall_hbm, hat_one_hbm, hat_two_hbm, hat_three_hbm, first_hbm, second_hbm,
    norm_ref, stats_ref, stats_wide_ref, proj_hbm, small_ref, square_ref,
    ingrad_ref, wgrad_ref, pgrad_ref, sgrad_ref, ngrad_ref, total_ref,
    gz_ref, x_ref, hat_three_ref, second_ref, first_ref, wall_ref, proj_ref, hat_two_ref, hat_one_ref, in_sem,
    ds, ds_low, turned, ch_buf, ch_in, halo_in, taps, back_t, mask_t, stat_three, stat_two, stat_one,
    we_buf, we_y, we_z, we_in, wd_buf, wd_y, wd_z, wd_in, wr_buf, wr_y, wr_z, wr_in, pr_in, pg_in,
    small_px, sq_all, norm_in, norm_wide_in,
    c_send, c_recv, s_send, s_recv, h_send, h_recv, gy_send, gy_recv, gz_send, gz_recv,
    pr_send, pr_recv, pg_send, pg_recv, t_send, t_recv, u_send, u_recv, n_send, n_recv,
):
    p, c, z, y, x, core = place()
    zcount = NPIX // 2
    other_y = (2 * z + 1 - y, c)
    pix_targets = [(lax.rem(p + d, NPIX), c) for d in range(1, NPIX)]
    ch_targets = [(p, lax.rem(c + d, NCH)) for d in range(1, NCH)]
    greeted = greet(all_targets())
    coming = [
        pltpu.make_async_copy(source, ref, in_sem.at[i])
        for i, (source, ref) in enumerate(
            (
                (gz_hbm, gz_ref), (x_hbm, x_ref), (hat_three_hbm, hat_three_ref), (second_hbm, second_ref),
                (first_hbm, first_ref), (wall_hbm, wall_ref), (proj_hbm, proj_ref), (hat_two_hbm, hat_two_ref),
                (hat_one_hbm, hat_one_ref),
            )
        )
    ]
    start_all(coming)
    count_all = float(NPIX * PX)

    def param(row, offset, width):
        return norm_ref[row : row + 1, pl.ds(pl.multiple_of(offset + c * width, 128), width)]

    gain_one, shift_one = param(0, 0, MID), param(1, 0, MID)
    gain_two, shift_two = param(0, M, MID), param(1, M, MID)
    gain_three, shift_three = param(0, 2 * M, CIN), param(1, 2 * M, CIN)

    def weights(lanes):
        return wall_ref[:, :, lanes].reshape(M, lanes.stop - lanes.start)

    def stat_round(index, inbox, upstream, hat):
        inbox[p, 0:1, :] = column_sums(upstream)
        inbox[p, 1:2, :] = column_sums(upstream * hat)
        copies = pix_copies(inbox, s_send.at[index], s_recv.at[index], 2)
        start_all(copies)
        return copies

    def stat_end(copies, inbox):
        wait_all(copies)
        return add_up(inbox[:, 0:2])

    def norm_back(upstream, hat, sums, gain, scale):
        return gain * scale * (upstream - sums[0:1] / count_all - hat * (sums[1:2] / count_all))

    def own_ch_copies(ref, inbox_index):
        return [
            remote(
                ref.at[c], ref.at[c], n_send.at[inbox_index, d - 1], n_recv.at[inbox_index, d - 1],
                ch_targets[d - 1],
            )
            for d in range(1, NCH)
        ]

    def sum_y(index, buf, y_in):
        return remote(buf.at[:, 1 - y], y_in, gy_send.at[index], gy_recv.at[index], other_y)

    def sum_z(index, z_buf, z_in):
        copies = []
        for d in range(1, zcount):
            zz = lax.rem(z + d, zcount)
            copies.append(
                remote(
                    z_buf.at[zz], z_in.at[d - 1], gz_send.at[index, d - 1], gz_recv.at[index, d - 1],
                    (2 * zz + y, c),
                )
            )
        return copies

    def sum_middle(index, buf, y_in, z_buf, z_in):
        sum_y(index, buf, y_in).wait()
        for zz in range(zcount):
            z_buf[zz] = (buf[zz, y].astype(F32) + y_in[zz].astype(F32)).astype(BF)
        start_all(sum_z(index, z_buf, z_in))

    def sum_end(index, z_buf, z_in, lanes):
        wait_all(sum_z(index, z_buf, z_in))
        total = z_buf[z].astype(F32)
        for d in range(zcount - 1):
            total = total + z_in[d].astype(F32)
        wgrad_ref[:, lanes] = total
        return fold(total * total)

    wide_rows = 64

    def expand_rows(m, carry):
        rows = pl.ds(pl.multiple_of(m * wide_rows, wide_rows), wide_rows)
        summed = hat_three_ref[rows, :] * gain_three + shift_three + x_ref[rows, :].astype(F32)
        ds[rows, :] = gz_ref[rows, :] * gelu_slope(summed)
        return carry

    wait_all(coming[:3])
    lax.fori_loop(0, PX // wide_rows, expand_rows, 0)
    await_greetings(greeted)
    copies = stat_round(0, stat_three, ds[...], hat_three_ref[...])
    wait_all(coming[3:])
    turned[0] = jnp.transpose(second_ref[...].astype(F32)).astype(BF)
    turned[1] = jnp.transpose(first_ref[...].astype(F32)).astype(BF)
    mask_t[...] = jnp.zeros_like(mask_t)
    mask_t[0:ROWS, :] = mask_ref[...].astype(F32)
    sums = stat_end(copies, stat_three)
    norm_wide_in[c] = jnp.zeros((8, CIN), F32)
    norm_wide_in[c, 0:2, :] = sums
    ds_low[...] = norm_back(ds[...], hat_three_ref[...], sums, gain_three, stats_wide_ref[0:1, :]).astype(BF)

    def scatter_ch(index, product):
        for m in range(NCH):
            ch_buf[index, m] = product(m).astype(BF)
        copies = ch_copies(lambda other: ch_buf.at[index, other], ch_in.at[index], c_send.at[index], c_recv.at[index])
        start_all(copies)
        return copies

    def scatter_end(index, copies):
        wait_all(copies)
        total = ch_buf[index, c].astype(F32)
        for d in range(1, NCH):
            total = total + ch_in[index, lax.rem(c + d, NCH)].astype(F32)
        return total

    def expand_back(m):
        wanted = wall_ref[2 * m : 2 * m + 2, :, W_EXPAND].reshape(MID, CIN)
        return nt_dot(ds_low[...], wanted)

    copies = scatter_ch(0, expand_back)
    proj_copies = []
    for d in range(1, NPIX):
        b = lax.rem(p + d, NPIX)
        proj_copies.append(remote(proj_ref.at[b], pr_in.at[d - 1], pr_send.at[d - 1], pr_recv.at[d - 1], (b, c)))
    start_all(proj_copies)
    small_px[p] = small_ref[...]
    small_copies = pix_copies(small_px, t_send, t_recv)
    start_all(small_copies)
    we_buf[...] = nn_dot(turned[0], ds_low[...]).astype(BF).reshape(zcount, 2, WPART, CIN)
    sum_y(0, we_buf, we_y).start()
    hat = hat_two_ref[...]
    slope = gelu_slope(hat * gain_two + shift_two)
    upstream = scatter_end(0, copies) * slope
    copies = stat_round(1, stat_two, upstream, hat)
    sums = stat_end(copies, stat_two)
    norm_in[c, 2:4, :] = sums[0:2]

    def halo_copy(side):
        target = (p - 1, c) if side == 0 else (p + 1, c)
        return remote(back_t, halo_in.at[side], h_send.at[side], h_recv.at[side], target)

    gradient = norm_back(upstream, hat, sums, gain_two, stats_ref[1:2, :])
    back_t[...] = gradient.astype(BF)

    @pl.when(p > 0)
    def _():
        halo_copy(0).start()

    @pl.when(p < NPIX - 1)
    def _():
        halo_copy(1).start()

    def fill_taps(step, source):
        for col in range(3):
            tap = 3 * (step + 1) + col
            moved = slide_rows(source.astype(F32), DILATION_RATE * (col - 1))
            taps[:, tap * MID : (tap + 1) * MID] = moved.astype(BF)

    fill_taps(0, back_t[...])

    @pl.when(p < NPIX - 1)
    def _():
        halo_copy(0).wait_recv()

    @pl.when(p == NPIX - 1)
    def _():
        halo_in[0] = jnp.zeros((PX, MID), BF)

    fill_taps(-1, halo_in[0])

    @pl.when(p > 0)
    def _():
        halo_copy(1).wait_recv()

    @pl.when(p == 0)
    def _():
        halo_in[1] = jnp.zeros((PX, MID), BF)

    fill_taps(1, halo_in[1])

    def dilated_back(m):
        wanted = wall_ref[2 * m : 2 * m + 2, :, W_DILATED].reshape(MID, TAP_LANES)
        return nt_dot(taps[...], wanted)

    copies = scatter_ch(1, dilated_back)
    sum_middle(0, we_buf, we_y, we_z, we_in)
    for m in range(NPIX):
        wd_buf[m // 2, m % 2] = nn_dot(turned[1, m * WPART : (m + 1) * WPART, :], taps[...]).astype(BF)
    sum_y(1, wd_buf, wd_y).start()
    hat = hat_one_ref[...]
    mask = jnp.transpose(mask_t[...])
    mask = jnp.concatenate(
        [jnp.broadcast_to(mask[:, r : r + 1], (WIDTH, MID)) for r in range(ROWS)], axis=0
    )
    slope = gelu_slope(hat * gain_one + shift_one) * mask
    upstream = scatter_end(1, copies) * slope
    copies = stat_round(2, stat_one, upstream, hat)
    sums = stat_end(copies, stat_one)
    norm_in[c, 0:2, :] = sums[0:2]
    norm_in[c, 4:8, :] = jnp.zeros((4, MID), F32)
    gradient = norm_back(upstream, hat, sums, gain_one, stats_ref[0:1, :])

    own_rows = pl.ds(pl.multiple_of(c * MID, MID), MID)
    turned[2, own_rows, :] = jnp.transpose(gradient).astype(BF)
    copies = [
        remote(
            turned.at[2, own_rows, :], turned.at[2, own_rows, :],
            c_send.at[2, d - 1], c_recv.at[2, d - 1], ch_targets[d - 1],
        )
        for d in range(1, NCH)
    ]
    start_all(copies)
    norm_copies = own_ch_copies(norm_in, 0) + own_ch_copies(norm_wide_in, 1)
    start_all(norm_copies)
    sum_middle(1, wd_buf, wd_y, wd_z, wd_in)
    wait_all(copies)
    wr_buf[...] = nn_dot(turned[2], x_ref[...]).astype(BF).reshape(zcount, 2, WPART, CIN)
    sum_y(2, wr_buf, wr_y).start()
    wait_all(proj_copies)
    for t in range(3):
        total = proj_ref[p, t].astype(F32)
        for d in range(NPIX - 1):
            total = total + pr_in[d, t].astype(F32)
        pg_in[c, t] = total
    wait_all(small_copies)
    sgrad_ref[c] = add_up(small_px)
    ch_final = [
        remote(pg_in.at[c], pg_in.at[c], pg_send.at[0, d - 1], pg_recv.at[0, d - 1], ch_targets[d - 1])
        for d in range(1, NCH)
    ] + [
        remote(sgrad_ref.at[c], sgrad_ref.at[c], pg_send.at[1, d - 1], pg_recv.at[1, d - 1], ch_targets[d - 1])
        for d in range(1, NCH)
    ]
    start_all(ch_final)
    sum_middle(2, wr_buf, wr_y, wr_z, wr_in)
    full = jnp.transpose(turned[2].astype(F32)).astype(BF)
    ingrad_ref[...] = nn_dot(full, weights(W_REDUCE)) + ds[...]
    squares = square_ref[...] + sum_end(0, we_z, we_in, W_EXPAND)
    squares = squares + sum_end(1, wd_z, wd_in, W_DILATED)
    wait_all(ch_final)
    for t in range(3):
        for other in range(NCH):
            pgrad_ref[t, other * 32 : (other + 1) * 32, :] = pg_in[other, t]
        squares = squares + fold(pg_in[c, t] * pg_in[c, t])
    wait_all(norm_copies)
    for other in range(NCH):
        for row in range(2):
            for offset, width, value in (
                (0, MID, norm_in[other, 1 - row : 2 - row, :]),
                (M, MID, norm_in[other, 3 - row : 4 - row, :]),
                (2 * M, CIN, norm_wide_in[other, 1 - row : 2 - row, :]),
            ):
                start = offset + other * width
                ngrad_ref[row : row + 1, start : start + width] = value
    shared = jnp.zeros((8, 128), F32)
    for other in range(NCH):
        shared = shared + fold(sgrad_ref[other] * sgrad_ref[other])
        shared = shared + fold(norm_in[other] * norm_in[other])
        shared = shared + fold(norm_wide_in[other] * norm_wide_in[other])
    squares = squares + sum_end(2, wr_z, wr_in, W_REDUCE)
    summed = sum_everywhere(column_sums(squares), sq_all, u_send, u_recv)
    everything = summed + column_sums(shared)
    total = jnp.sum(everything, axis=1, keepdims=True)
    norm = jnp.sqrt(total)
    factor = jnp.minimum(1.0, CLIP_NORM / (norm + 1e-06))
    line = lax.broadcasted_iota(jnp.int32, (8, 128), 0)
    total_ref[...] = jnp.where(line == 0, norm, factor)

    @pl.when(p > 0)
    def _():
        halo_copy(0).wait_send()

    @pl.when(p < NPIX - 1)
    def _():
        halo_copy(1).wait_send()


def block_backward(*operands):
    dma = pltpu.SemaphoreType.DMA
    shape = jax.ShapeDtypeStruct
    vmem = pltpu.VMEM
    zc = NPIX // 2

    def sum_buffers(lanes):
        return [
            vmem((zc, 2, WPART, lanes), BF),
            vmem((zc, WPART, lanes), BF),
            vmem((zc, WPART, lanes), BF),
            vmem((zc - 1, WPART, lanes), BF),
        ]

    return pl.pallas_call(
        block_backward_kernel,
        out_shape=(
            shape((PX, CIN), F32),
            shape((WPART, W_LANES), F32),
            shape((3, 128, HID), F32),
            shape((NCH, SMALL_PART, HID), F32),
            shape((2, 2 * M + C), F32),
            shape((8, 128), F32),
        ),
        in_specs=[from_hbm()] * 2 + [whole_vmem()] + [from_hbm()] * 6 + [whole_vmem()] * 3 + [from_hbm()] + [whole_vmem()] * 2,
        out_specs=[whole_vmem()] * 6,
        scratch_shapes=[
            vmem((PX, CIN), F32),
            vmem((PX, CIN), BF),
            vmem((PX, CIN), F32),
            vmem((PX, M), BF),
            vmem((PX, M), BF),
            vmem((NPIX, WPART, W_LANES), BF),
            vmem((NPIX, 3, 32, HID), BF),
            vmem((PX, MID), F32),
            vmem((PX, MID), F32),
            dma((9,)),
            vmem((PX, CIN), F32),
            vmem((PX, CIN), BF),
            vmem((3, M, PX), BF),
            vmem((2, NCH, PX, MID), BF),
            vmem((2, NCH, PX, MID), BF),
            vmem((2, PX, MID), BF),
            vmem((PX, TAP_LANES), BF),
            vmem((PX, MID), BF),
            vmem((8, WIDTH), F32),
            vmem((NPIX, 8, CIN), F32),
            vmem((NPIX, 8, MID), F32),
            vmem((NPIX, 8, MID), F32),
        ]
        + sum_buffers(CIN)
        + sum_buffers(TAP_LANES)
        + sum_buffers(CIN)
        + [
            vmem((NPIX - 1, 3, 32, HID), BF),
            vmem((NCH, 3, 32, HID), F32),
            vmem((NPIX, SMALL_PART, HID), F32),
            vmem((NALL, 8, 128), F32),
            vmem((NCH, 8, MID), F32),
            vmem((NCH, 8, CIN), F32),
            dma((3, NCH - 1)), dma((3, NCH - 1)),
            dma((3, NPIX - 1)), dma((3, NPIX - 1)),
            dma((2,)), dma((2,)),
            dma((3,)), dma((3,)), dma((3, zc - 1)), dma((3, zc - 1)),
            dma((NPIX - 1,)), dma((NPIX - 1,)),
            dma((2, NCH - 1)), dma((2, NCH - 1)),
            dma((NPIX - 1,)), dma((NPIX - 1,)),
            dma((NALL - 1,)), dma((NALL - 1,)),
            dma((2, NCH - 1)), dma((2, NCH - 1)),
        ],
        compiler_params=pltpu.CompilerParams(
            collective_id=3, has_side_effects=True, vmem_limit_bytes=BLOCK_VMEM
        ),
        name="block_backward",
    )(*operands)


def adam_parts(weight, first, second, grad, rate=RATE_MATRIX, decay=DECAY):
    first_new = BETA_ONE * first + (1.0 - BETA_ONE) * grad
    second_new = BETA_TWO * second + (1.0 - BETA_TWO) * grad * grad
    first_hat = first_new * (1.0 / (1.0 - BETA_ONE**STEP))
    second_hat = second_new * (1.0 / (1.0 - BETA_TWO**STEP))
    weight_new = weight - rate * (first_hat / (jnp.sqrt(second_hat) + ADAM_EPS) + decay * weight)
    return weight_new, first_new, second_new


def adam_store(olds, news, at, grad):
    weight, first, second = adam_parts(olds[0][at], olds[1][at], olds[2][at], grad)
    news[0][at] = weight
    news[1][at] = first
    news[2][at] = second
    news[3][at] = weight.astype(BF)


def adam_matrices_kernel(*refs):
    total_ref, w_ref, tap_ref, p_ref, n_ref = refs[:5]
    olds = [refs[5 + 3 * i : 8 + 3 * i] for i in range(6)]
    news = [refs[25 + 4 * i : 29 + 4 * i] for i in range(5)] + [refs[45:48]]
    for i in range(2):
        refs[48 + i][...] = refs[23 + i][...]
    factor = total_ref[1:2, 0:1]
    every = (slice(None), slice(None))
    adam_store(olds[0], news[0], every, w_ref[:, W_REDUCE] * factor)
    for tap in range(9):
        lanes = slice(CIN + tap * MID, CIN + (tap + 1) * MID)
        adam_store(olds[1], news[1], (tap, slice(None), slice(None)), w_ref[:, lanes] * factor)
    adam_store(olds[2], news[2], every, w_ref[:, W_EXPAND] * factor)
    adam_store(olds[3], news[3], every, tap_ref[...] * factor)
    for t in range(3):
        adam_store(olds[4], news[4], (t, slice(None), slice(None)), p_ref[t] * factor)
    values = adam_parts(
        olds[5][0][...], olds[5][1][...], olds[5][2][...], n_ref[...] * factor, RATE_SMALL, 0.0
    )
    for ref, value in zip(news[5], values):
        ref[...] = value


def adam_matrices(totals, w_grad, tap_grad, proj_grad, norm_grad, states, results):
    flat = [array for state in states for array in state]
    outs = []
    for state in states[:5]:
        outs += [jax.ShapeDtypeStruct(state[0].shape, F32)] * 3 + [jax.ShapeDtypeStruct(state[0].shape, BF)]
    outs += [jax.ShapeDtypeStruct(states[5][0].shape, F32)] * 3
    outs += [jax.ShapeDtypeStruct(result.shape, result.dtype) for result in results]
    return pl.pallas_call(
        adam_matrices_kernel,
        out_shape=tuple(outs),
        in_specs=[whole_vmem()] * (7 + len(flat)),
        out_specs=[whole_vmem()] * len(outs),
        compiler_params=pltpu.CompilerParams(vmem_limit_bytes=VMEM_LIMIT),
        name="adam_matrices",
    )(totals, w_grad, tap_grad, proj_grad, norm_grad, *flat, *results)


def per_device_rows(
    features,
    valid_mask,
    sem_label,
    depth_target,
    normal_target,
    label_mask,
    w_reduce,
    m_reduce,
    v_reduce,
    w_dilated,
    m_dilated,
    v_dilated,
    w_expand,
    m_expand,
    v_expand,
    head_weight,
    m_head,
    v_head,
    head_rates,
    m_rates,
    v_rates,
    head_proj,
    m_proj,
    v_proj,
    norm_params,
    norm_m,
    norm_v,
    head_small,
    small_m,
    small_v,
):

    flat_in = features.reshape(PX, CIN)
    shared, hat_one, hat_two, hat_three, w_all, first, second, stats, stats_wide, proj_own = block_forward(
        flat_in, valid_mask, label_mask, w_reduce.T, w_dilated, w_expand, head_proj, norm_params
    )
    q_rows, shared_all, proj_t, w_seg, w_more = heads_forward(shared, head_rates, head_weight.T, proj_own)
    at_out = 15 * HID
    rest = at_out + HID * NCLS
    small_cols = jnp.concatenate(
        [
            head_small[at_out:rest].reshape(HID, NCLS),
            head_small[rest : rest + HID].reshape(HID, 1),
            head_small[rest + HID : rest + 4 * HID].reshape(HID, 3),
            jnp.zeros((HID, 32 - NCLS - 4), F32),
        ],
        axis=1,
    )
    out_bias = jnp.pad(head_small[rest + 4 * HID :], (0, HID - NCLS - 4))
    small_rows = jnp.concatenate([head_small[:at_out], out_bias]).reshape(16, HID)
    rates_shard, combined, squares, proj_sums, small_sums, root_sums = heads_backward(
        q_rows, proj_t, small_rows, small_cols, stats, sem_label, depth_target, normal_target, label_mask,
        shared_all, w_seg, w_more,
    )
    input_grad, w_grad, proj_shard, small_total, norm_grad, totals = block_backward(
        combined, flat_in, valid_mask, w_all, hat_one, hat_two, hat_three, first, second,
        norm_params, stats, stats_wide, proj_sums, small_sums, squares,
    )
    (
        reduce_new, reduce_first, reduce_second, reduce_copy,
        dilated_new, dilated_first, dilated_second, dilated_copy,
        expand_new, expand_first, expand_second, expand_copy,
        head_new, head_first, head_second, head_copy,
        proj_new, proj_first, proj_second, proj_copy,
        norm_new, norm_first, norm_second, shared, input_grad,
    ) = adam_matrices(
        totals, w_grad, root_sums, proj_shard, norm_grad,
        (
            (w_reduce.T, m_reduce.T, v_reduce.T),
            (w_dilated, m_dilated, v_dilated),
            (w_expand, m_expand, v_expand),
            (head_weight.T, m_head.T, v_head.T),
            (head_proj, m_proj, v_proj),
            (norm_params, norm_m, norm_v),
        ),
        (shared, input_grad),
    )
    small_total = small_total.reshape(SMALL_ROWS, HID)
    small_grad = jnp.concatenate(
        [
            small_total[:15].reshape(-1),
            small_total[16 : 16 + NCLS].T.reshape(-1),
            small_total[16 + NCLS],
            small_total[17 + NCLS : 20 + NCLS].T.reshape(-1),
            small_total[15, : NCLS + 4],
        ]
    )
    grad_norm = totals[0, 0]
    factor = totals[1, 0]
    rates_new, rates_first, rates_second = adam_step(
        head_rates, m_rates, v_rates, rates_shard * factor, RATE_MATRIX, DECAY
    )
    small_new, small_first, small_second = adam_step(
        head_small, small_m, small_v, small_grad * factor, RATE_SMALL, 0.0
    )
    depth_bias_grad = small_total[15, NCLS]
    return (
        shared.reshape(ROWS, WIDTH, CIN),
        input_grad.reshape(ROWS, WIDTH, CIN),
        grad_norm,
        reduce_new.T,
        reduce_first.T,
        reduce_second.T,
        reduce_copy.T,
        dilated_new,
        dilated_first,
        dilated_second,
        dilated_copy,
        expand_new,
        expand_first,
        expand_second,
        expand_copy,
        head_new.T,
        head_first.T,
        head_second.T,
        head_copy.T,
        rates_new,
        rates_first,
        rates_second,
        rates_new.astype(BF),
        proj_new,
        proj_first,
        proj_second,
        proj_copy,
        norm_new,
        norm_first,
        norm_second,
        small_new,
        small_first,
        small_second,
        depth_bias_grad,
    )


def per_device(features, *rest):
    sizes = (lax.axis_size("pix"), lax.axis_size("ch"))
    if sizes == (NPIX, NCH) and features.shape == (ROWS, WIDTH, CIN):
        return per_device_rows(features, *rest)
    return per_device_plain(features, *rest)


def solution(mesh):
    placed = (
        P("pix", None, "ch"),
        P("pix", None),
        P("pix", None),
        P("pix", None),
        P(None, "pix", None),
        P(None, "pix", None),
        P("ch", "pix"),
        P("ch", "pix"),
        P("ch", "pix"),
        P(None, "pix", "ch"),
        P(None, "pix", "ch"),
        P(None, "pix", "ch"),
        P("pix", "ch"),
        P("pix", "ch"),
        P("pix", "ch"),
        P("ch", "pix"),
        P("ch", "pix"),
        P("ch", "pix"),
        P(None, None, "pix", "ch"),
        P(None, None, "pix", "ch"),
        P(None, None, "pix", "ch"),
        P(None, "pix", None),
        P(None, "pix", None),
        P(None, "pix", None),
        P(),
        P(),
        P(),
        P(),
        P(),
        P(),
    )
    return jax.shard_map(
        per_device,
        mesh=mesh,
        in_specs=placed,
        out_specs=(
            P("pix", None, "ch"),
            P("pix", None, "ch"),
            P(),
            P("ch", "pix"),
            P("ch", "pix"),
            P("ch", "pix"),
            P("ch", "pix"),
            P(None, "pix", "ch"),
            P(None, "pix", "ch"),
            P(None, "pix", "ch"),
            P(None, "pix", "ch"),
            P("pix", "ch"),
            P("pix", "ch"),
            P("pix", "ch"),
            P("pix", "ch"),
            P("ch", "pix"),
            P("ch", "pix"),
            P("ch", "pix"),
            P("ch", "pix"),
            P(None, None, "pix", "ch"),
            P(None, None, "pix", "ch"),
            P(None, None, "pix", "ch"),
            P(None, None, "pix", "ch"),
            P(None, "pix", None),
            P(None, "pix", None),
            P(None, "pix", None),
            P(None, "pix", None),
            P(),
            P(),
            P(),
            P(),
            P(),
            P(),
            P(),
        ),
        check_vma=False,
    )
```
